32 devices in a mesh: space: 8 (over y, x, core), dp: 4 (over z).
Axes of the slice: x: 2, y: 2, z: 4, core: 2. Of those that a mesh axis runs over, the one named last changes fastest.
Arguments:
- volume: bfloat16 [4, 32, 96, 512], P('dp', 'space'), may hold values from -6 to 6
- neighbours: int32 [4, 32, 26], P('dp'), may hold values from -1 to 31, as said below
- active: int32 [4, 32], P('dp'), may hold values from 0 to 1, as said below
- cotangent: bfloat16 [4, 32, 96, 512], P('dp', 'space'), may hold values from -0.0234375 to 0.0234375
- weight_one: bfloat16 [96, 2592], replicated, may hold values from -0.125 to 0.125
- weight_two: bfloat16 [96, 2592], replicated, may hold values from -0.125 to 0.125
- bias_one: float32 [96], replicated, may hold values from -3 to 3
- bias_two: float32 [96], replicated, may hold values from -3 to 3
Outputs:
- output: bfloat16 [4, 32, 96, 512], P('dp', 'space')
- grad_weight_one: float32 [96, 2592], replicated
- grad_weight_two: float32 [96, 2592], replicated
- grad_bias_one: float32 [96], replicated
- grad_bias_two: float32 [96], replicated
The draws below stay inside these ranges and needn't reach their ends.
Inputs may be any that keep to these rules, and one draw needn't show every extreme that they name: `neighbours`: each volume is a grid of 8 x 2 x 2 bricks; brick (l, y, z) sits in one slot, and slot g lies on space index g // 4. Entry k of a slot is the slot of the brick at the k-th offset, -1 where the offset leaves the grid. The bricks of brick layers 2m and 2m + 1 lie on space indices 2m and 2m + 1, one brick of each (y, z) on each of the two. `active`: the bricks on space indices 0 and 1 are all live.
All inputs are finite; a program needn't handle non-finite values.
Results may differ from the reference program's by a relative error of at most 0.0065.
Values may be sent and summed in bfloat16 or wider, within the bound.
No kernel may reach another device: no remote copies, remote signals or barrier semaphores. Data moves between devices by JAX's collectives and lax.ppermute only.
A program may use at most 128 MiB of HBM per device.

```python
import jax
import jax.numpy as jnp
from jax import lax

C = 96
EDGE = 8
LY = 2
LZ = 2
BPD = 4
SLOTS = 32
VOLS = 4
CELLS = 512
N_SPACE = 8


OFFSETS = [(a, b, c) for a in (-1, 0, 1) for b in (-1, 0, 1) for c in (-1, 0, 1) if (a, b, c) != (0, 0, 0)]


def brick_layout(key):
    first_key, second_key = jax.random.split(key)
    swapped = jax.random.randint(first_key, (VOLS, N_SPACE // 2, BPD), 0, 2)
    many_keys = jax.random.split(second_key, VOLS * N_SPACE)
    orders = jax.vmap(lambda single: jax.random.permutation(single, BPD))(many_keys).reshape(VOLS, N_SPACE, BPD).astype(jnp.int32)
    layer_ids = jnp.arange(N_SPACE, dtype=jnp.int32)[None, :, None]
    owners = jnp.bitwise_xor(layer_ids, jnp.repeat(swapped, 2, axis=1)).astype(jnp.int32)
    return owners * BPD + jnp.take_along_axis(orders, owners, axis=1)


def by_slot(slot_of, values):
    flat_slots = slot_of.reshape(VOLS, SLOTS)
    flat_values = values.reshape(VOLS, SLOTS, -1)

    def place_one(slots_one, values_one):
        return jnp.zeros((SLOTS, values_one.shape[1]), jnp.int32).at[slots_one].set(values_one)
    return jax.vmap(place_one)(flat_slots, flat_values)


def draw_neighbours(key, part):
    slot_of = brick_layout(jax.random.fold_in(key, 7))
    grid = slot_of.reshape(VOLS, N_SPACE, LY, LZ)
    framed = jnp.pad(grid, ((0, 0), (1, 1), (1, 1), (1, 1)), constant_values=-1)
    columns = []
    for a, b, c in OFFSETS:
        columns.append(framed[:, 1 + a:1 + a + N_SPACE, 1 + b:1 + b + LY, 1 + c:1 + c + LZ])
    stacked = jnp.stack(columns, axis=-1)
    return by_slot(slot_of, stacked)


def draw_active(key, part):
    slot_of = brick_layout(jax.random.fold_in(key, 7))
    layer_ids = jnp.broadcast_to(jnp.arange(N_SPACE, dtype=jnp.int32)[None, :, None], (VOLS, N_SPACE, BPD))
    base_layer = layer_ids - layer_ids % 2
    scores = jax.random.randint(jax.random.fold_in(key, 11), (VOLS, N_SPACE, BPD), 0, 8 * N_SPACE)
    alive_bricks = (scores >= 7 * base_layer).astype(jnp.int32)
    return by_slot(slot_of, alive_bricks)[:, :, 0]


def shard_levels(key, extent, cuts, smallest, top_value):
    level, own = 1.0, jax.random.fold_in(key, 6)
    for axis_at, shards_of in cuts:
        steps = jnp.exp(jax.random.uniform(jax.random.fold_in(own, axis_at), (shards_of,), jnp.float32, smallest / len(cuts), top_value / len(cuts)))
        level = level * jnp.repeat(steps, extent[axis_at] // shards_of).reshape([-1 if axis == axis_at else 1 for axis in range(len(extent))])
    return level


def normal_values(stream_key, extent, scale, most, cuts=(), held_as=jnp.bfloat16):
    entries = jax.random.normal(stream_key, extent, jnp.float32) * scale
    if len(cuts) > 0:
        entries = shard_levels(stream_key, extent, cuts, -0.22, 0.18) * entries
    return jnp.clip(entries, min=-most, max=most).astype(held_as)


def setup_inputs(seed: int = 0) -> dict:
    keys = jax.random.split(jax.random.key(seed), 9)
    volume = normal_values(keys[0], (VOLS, SLOTS, C, CELLS), 1.0, 6.0, ((0, 4), (1, 8)))
    neighbours = draw_neighbours(jax.random.fold_in(keys[8], 71), 0)
    active = draw_active(jax.random.fold_in(keys[8], 71), 0)
    cotangent = normal_values(keys[3], (VOLS, SLOTS, C, CELLS), (VOLS * SLOTS * CELLS) ** -0.5, 0.0234375, ((0, 4), (1, 8)))
    weight_one = normal_values(keys[4], (C, 27 * C), (27 * C) ** -0.5, 0.125)
    weight_two = normal_values(keys[5], (C, 27 * C), (27 * C) ** -0.5, 0.125)
    bias_one = normal_values(keys[6], (C,), 0.5, 3.0, (), jnp.float32)
    bias_two = normal_values(keys[7], (C,), 0.5, 3.0, (), jnp.float32)
    return {"volume": volume, "neighbours": neighbours, "active": active, "cotangent": cotangent, "weight_one": weight_one, "weight_two": weight_two, "bias_one": bias_one, "bias_two": bias_two}


OFFSETS = [(a, b, c) for a in (-1, 0, 1) for b in (-1, 0, 1) for c in (-1, 0, 1) if (a, b, c) != (0, 0, 0)]

def collect_faces(bricks):
    edge_len = bricks.shape[-1]
    sides = [bricks[:, :, 0], bricks[:, :, edge_len - 1], bricks[:, :, :, 0], bricks[:, :, :, edge_len - 1], bricks[:, :, :, :, 0], bricks[:, :, :, :, edge_len - 1]]
    stacked = jnp.stack(sides, axis=2)
    return stacked.reshape(bricks.shape[0], bricks.shape[1], 6 * edge_len * edge_len)

def face_index(offset):
    if offset[0] != 0:
        return 1 if offset[0] < 0 else 0
    if offset[1] != 0:
        return 3 if offset[1] < 0 else 2
    return 5 if offset[2] < 0 else 4

def face_span(shift_by, edge_len):
    if shift_by < 0:
        return slice(edge_len - 1, edge_len)
    if shift_by > 0:
        return slice(0, 1)
    return slice(0, edge_len)

def target(shift_by, edge_len):
    if shift_by < 0:
        return slice(0, 1)
    if shift_by > 0:
        return slice(edge_len + 1, edge_len + 2)
    return slice(1, edge_len + 1)

def pad_bricks(center, pool, pool_rows):
    brick_count, channels, edge_len = (center.shape[0], center.shape[1], center.shape[2])
    face_area = edge_len * edge_len
    padded = jnp.zeros((brick_count, channels, edge_len + 2, edge_len + 2, edge_len + 2), center.dtype)
    padded = padded.at[:, :, 1:edge_len + 1, 1:edge_len + 1, 1:edge_len + 1].set(center)
    for k, offset in enumerate(OFFSETS):
        a, b, c = offset
        side_index = face_index(offset)
        source = pool[:, :, side_index * face_area:(side_index + 1) * face_area]
        face_cells = jnp.take(source, pool_rows[:, k], axis=0).reshape(brick_count, channels, edge_len, edge_len)
        if a != 0:
            piece_cells = face_cells[:, :, face_span(b, edge_len), face_span(c, edge_len)][:, :, None]
        elif b != 0:
            piece_cells = face_cells[:, :, :, face_span(c, edge_len)][:, :, :, None]
        else:
            piece_cells = face_cells[:, :, :, :, None]
        padded = padded.at[:, :, target(a, edge_len), target(b, edge_len), target(c, edge_len)].set(piece_cells)
    return padded

def pad_volume(flat_bricks, pool_rows):
    slot_count, channels, cell_count = flat_bricks.shape
    edge_len = EDGE
    center = flat_bricks.reshape(slot_count, channels, edge_len, edge_len, edge_len)
    outer_faces = collect_faces(center)
    zero_row = jnp.zeros((1, channels, outer_faces.shape[2]), outer_faces.dtype)
    pool = jnp.concatenate([outer_faces, zero_row], axis=0)
    return pad_bricks(center, pool, pool_rows)

def tap_slice(padded_wide, tap_index, edge_len):
    a, b, c = (tap_index // 9, tap_index // 3 % 3, tap_index % 3)
    window = padded_wide[:, :, a:a + edge_len, b:b + edge_len, c:c + edge_len]
    return window.reshape(padded_wide.shape[0], padded_wide.shape[1], edge_len ** 3)

def convolve(padded, weight_taps):
    padded_wide = padded.astype(jnp.float32)
    summed = jnp.zeros((padded.shape[0], weight_taps.shape[0], EDGE ** 3), jnp.float32)
    for tap_index in range(27):
        piece_cells = tap_slice(padded_wide, tap_index, EDGE)
        summed = summed + jnp.einsum('oi,sip->sop', weight_taps[:, tap_index], piece_cells, precision=lax.Precision.HIGHEST)
    return summed

def convolve_back(padded, weight_taps):
    padded_wide = padded.astype(jnp.float32)
    summed = jnp.zeros((padded.shape[0], weight_taps.shape[2], EDGE ** 3), jnp.float32)
    for tap_index in range(27):
        piece_cells = tap_slice(padded_wide, tap_index, EDGE)
        summed = summed + jnp.einsum('oi,sop->sip', weight_taps[:, 26 - tap_index], piece_cells, precision=lax.Precision.HIGHEST)
    return summed

def weight_grad(grad_cells, padded):
    padded_wide = padded.astype(jnp.float32)
    grad_wide = grad_cells.astype(jnp.float32)
    per_tap = []
    for tap_index in range(27):
        piece_cells = tap_slice(padded_wide, tap_index, EDGE)
        per_tap.append(jnp.einsum('sop,sip->oi', grad_wide, piece_cells, precision=lax.Precision.HIGHEST))
    return jnp.stack(per_tap, axis=1)

def silu_slope(values):
    sigma = jax.nn.sigmoid(values)
    return sigma * (1.0 + values * (1.0 - sigma))

def reference(volume, neighbours, active, cotangent, weight_one, weight_two, bias_one, bias_two):
    channels = volume.shape[2]
    taps_one = weight_one.astype(jnp.float32).reshape(channels, 27, channels)
    taps_two = weight_two.astype(jnp.float32).reshape(channels, 27, channels)

    def one_volume(carry, inputs):
        bricks, near_table, alive_slots, upstream = inputs
        slot_count = bricks.shape[0]
        live_mask = alive_slots.astype(jnp.float32)[:, None, None]
        masked = bricks * live_mask.astype(jnp.bfloat16)
        pool_rows = jnp.where(near_table < 0, slot_count, near_table).astype(jnp.int32)
        padded_x = pad_volume(masked, pool_rows)
        hidden_pre = convolve(padded_x, taps_one) + bias_one[None, :, None]
        hidden = (jax.nn.silu(hidden_pre) * live_mask).astype(jnp.bfloat16)
        padded_h = pad_volume(hidden, pool_rows)
        out_pre = convolve(padded_h, taps_two) + bias_two[None, :, None]
        result = (jax.nn.silu(out_pre) * live_mask).astype(jnp.bfloat16)
        grad_out = (upstream.astype(jnp.float32) * live_mask * silu_slope(out_pre)).astype(jnp.bfloat16)
        grad_w_two = weight_grad(grad_out, padded_h)
        grad_b_two = lax.optimization_barrier(jnp.sum(grad_out.astype(jnp.float32), axis=(0, 2)))
        padded_g = pad_volume(grad_out, pool_rows)
        hidden_grad = convolve_back(padded_g, taps_two)
        grad_hidden = (hidden_grad * live_mask * silu_slope(hidden_pre)).astype(jnp.bfloat16)
        grad_w_one = weight_grad(grad_hidden, padded_x)
        grad_b_one = lax.optimization_barrier(jnp.sum(grad_hidden.astype(jnp.float32), axis=(0, 2)))
        carry = (carry[0] + grad_w_one, carry[1] + grad_w_two, carry[2] + grad_b_one, carry[3] + grad_b_two)
        return (carry, result)
    start = (jnp.zeros((channels, 27, channels), jnp.float32), jnp.zeros((channels, 27, channels), jnp.float32), jnp.zeros((channels,), jnp.float32), jnp.zeros((channels,), jnp.float32))
    totals, outputs = lax.scan(one_volume, start, (volume, neighbours, active, cotangent))
    return (outputs, totals[0].reshape(channels, 27 * channels), totals[1].reshape(channels, 27 * channels), totals[2], totals[3])
```

```python
import jax
import jax.numpy as jnp
import numpy as np
from jax import lax
from jax.experimental import pallas as pl
from jax.experimental.pallas import tpu as pltpu
from jax.sharding import PartitionSpec as P

EDGE = 8
PLANE = 256
CELLS = 512
KDIM = 896
TILES = 24
NEAR_Y, NEAR_Z, NEAR_UP = 10, 12, 21
F32 = jnp.float32
BF16 = jnp.bfloat16


def spread_matrix():
    move = np.zeros((256, 256), np.float32)
    for z in range(2):
        for p in range(2):
            for q in range(8):
                for r in range(8):
                    move[z * 128 + p * 64 + q * 8 + r, p * 128 + q * 16 + z * 8 + r] = 1.0
    return move


def tap_masks():
    masks = np.zeros((9, 16, 256), np.float32)
    for b in range(3):
        for c in range(3):
            for q in range(16):
                for r in range(16):
                    inside = 0 <= q + b - 1 < 16 and 0 <= r + c - 1 < 16
                    masks[b * 3 + c, :, q * 16 + r] = float(inside)
    return masks


def write_taps(dst, plane, masks_ref):
    channels = plane.shape[0]
    wide = plane.astype(F32)
    for k in range(9):
        step = (k // 3 - 1) * 16 + (k % 3 - 1)
        if step == 0:
            moved = plane
        else:
            moved = pltpu.roll(wide, (-step) % PLANE, 1).astype(BF16)
            moved = moved * jnp.concatenate([masks_ref[k]] * (channels // 16), axis=0)
        dst[k * channels : (k + 1) * channels, :] = moved


def slot_place(near_ref, slot, pair_slots):
    shift = pair_slots.bit_length() - 1
    up = near_ref[slot, NEAR_UP]
    inside = jnp.logical_and(up >= 0, up >> shift == slot >> shift)
    parity = jnp.where(inside, 0, 1)
    column = jnp.where(near_ref[slot, NEAR_Y] >= 0, 2, 0) + jnp.where(
        near_ref[slot, NEAR_Z] >= 0, 1, 0
    )
    return parity, column


def lane_mask(scalars):
    lane = lax.broadcasted_iota(jnp.int32, (8, PLANE), 1)
    high_y = lane >= 128
    high_z = (lane & 8) != 0
    s = [jnp.full((8, PLANE), v, F32) for v in scalars]
    return jnp.where(high_y, jnp.where(high_z, s[3], s[2]), jnp.where(high_z, s[1], s[0]))


def plane_product(weight_ref, taps):
    return jnp.dot(weight_ref[...], taps, preferred_element_type=F32)


def add_planes(acc, at, product, channels):
    acc[at + 1] = product[:channels]
    acc[at] = acc[at] + product[channels : 2 * channels]
    acc[at - 1] = acc[at - 1] + product[2 * channels :]


def weight_products(total, grads, taps, first_grad, first_tap, pairs):
    for j in range(0, 2 * pairs, 2):
        left = jnp.concatenate([grads[first_grad + j], grads[first_grad + j + 1]], axis=1)
        right = jnp.concatenate([taps[first_tap + j], taps[first_tap + j + 1]], axis=1)
        part = lax.dot_general(left, right, (((1,), (1,)), ((), ())), preferred_element_type=F32)
        total[...] = part if j == 0 else total[...] + part


def write_tiles(out_ref, total, channels):
    lane = lax.broadcasted_iota(jnp.int32, (channels, 128), 1)
    blank = jnp.zeros((channels, 128), F32)
    first = total[:channels, :]
    second = jnp.concatenate([total[channels : 2 * channels, :], blank], axis=1)
    third = jnp.concatenate([total[2 * channels :, :], blank], axis=1)
    second = pltpu.roll(second, 96, 1)
    third = pltpu.roll(third, 64, 1)

    def cut(value, k):
        return value[:, k * 128 : (k + 1) * 128]

    tiles = [cut(first, k) for k in range(6)]
    tiles.append(jnp.where(lane < 96, cut(first, 6), cut(second, 0)))
    tiles += [cut(second, k) for k in range(1, 7)]
    tiles.append(jnp.where(lane < 64, cut(second, 7), cut(third, 0)))
    tiles += [cut(third, k) for k in range(1, 8)]
    for k in range(TILES):
        out_ref[k] = (tiles[k] if k < len(tiles) else blank).astype(out_ref.dtype)


def forward_kernel(
    place_ref, near_ref, active_ref, own_ref, pair_ref, near_a_ref, near_b_ref, cot_own_ref,
    cot_pair_ref, w1_ref, w2_ref, b1_ref, b2_ref, move_ref, back_ref, masks_ref,
    keep_ref, send_ref, grad_ref, g_ref, slope_ref, x_ref,
    bricks, cots, nears, planes, cot_planes, layer_mask, xc, hc, acc_one, acc_two, outs, gs, total,
):
    slots, channels = own_ref.shape[0], own_ref.shape[1]
    pair_slots = 2 * slots
    last = near_ref.shape[0] - slots
    me, other, from_a, from_b = (jnp.clip(place_ref[k], 0, last) for k in range(4))
    core = jnp.where(place_ref[4] == 1, 1, 0)
    alone = place_ref[5] == 1

    own_places, pair_places = [], []
    live = [[jnp.float32(0)] * 4 for _ in range(2)]
    live_near = [[jnp.float32(0)] * 4 for _ in range(2)]
    for device, source, cot_source, places in (
        (me, own_ref, cot_own_ref, own_places), (other, pair_ref, cot_pair_ref, pair_places),
    ):
        for s in range(slots):
            slot = device + s
            parity, column = slot_place(near_ref, slot, pair_slots)
            places.append((parity, column))
            alive = active_ref[slot].astype(F32)
            scale = jnp.full((channels, CELLS), alive, F32).astype(BF16)
            bricks[parity, column] = source[s] * scale
            cots[parity, column] = cot_source[s] * scale
            for p in range(2):
                for k in range(4):
                    here = jnp.logical_and(parity == p, column == k)
                    live[p][k] = jnp.where(here, alive, live[p][k])
    for device, source in ((from_a, near_a_ref), (from_b, near_b_ref)):
        for s in range(slots):
            slot = device + s
            parity, column = slot_place(near_ref, slot, pair_slots)
            alive = jnp.where(alone, 0.0, active_ref[slot].astype(F32))
            scale = jnp.full((channels, PLANE), alive, F32).astype(BF16)
            nears[parity, column] = source[s] * scale
            for p in range(2):
                for k in range(4):
                    here = jnp.logical_and(parity == p, column == k)
                    live_near[p][k] = jnp.where(here, alive, live_near[p][k])
    mine = [jnp.where(core == 0, live[0][k], live[1][k]) for k in range(4)]
    inner = [jnp.where(core == 0, live[1][k], live[0][k]) for k in range(4)]
    outer = [jnp.where(core == 0, live_near[1][k], live_near[0][k]) for k in range(4)]
    layer_mask[0] = lane_mask([jnp.where(core == 0, outer[k], inner[k]) for k in range(4)])
    layer_mask[1] = lane_mask(mine)
    layer_mask[2] = lane_mask([jnp.where(core == 0, inner[k], outer[k]) for k in range(4)])

    move = move_ref[...]

    def spread(left, right):
        two = jnp.concatenate([left, right], axis=1)
        return jnp.dot(two, move, preferred_element_type=F32).astype(BF16)

    for y in range(2):
        row = slice(y * 128, (y + 1) * 128)
        for j in range(4):
            pair = slice(j * 128, (j + 1) * 128)
            both = spread(bricks[core, 2 * y, :, pair], bricks[core, 2 * y + 1, :, pair])
            planes[4 + 2 * j, :, row] = both[:, :128]
            planes[5 + 2 * j, :, row] = both[:, 128:]
            both = spread(cots[core, 2 * y, :, pair], cots[core, 2 * y + 1, :, pair])
            cot_planes[1 + 2 * j, :, row] = both[:, :128]
            cot_planes[2 + 2 * j, :, row] = both[:, 128:]
        inner_at = jnp.where(core == 0, 12, 0)
        for j in range(2):
            start = pl.multiple_of(jnp.where(core == 0, j * 128, 256 + j * 128), 128)
            pair = pl.ds(start, 128)
            both = spread(
                bricks[1 - core, 2 * y, :, pair], bricks[1 - core, 2 * y + 1, :, pair]
            )
            planes[inner_at + 2 * j, :, row] = both[:, :128]
            planes[inner_at + 2 * j + 1, :, row] = both[:, 128:]
        pair = pl.ds(pl.multiple_of(jnp.where(core == 0, 0, 384), 128), 128)
        both = spread(cots[1 - core, 2 * y, :, pair], cots[1 - core, 2 * y + 1, :, pair])

        @pl.when(core == 0)
        def _(both=both, row=row):
            cot_planes[9, :, row] = both[:, :128]

        @pl.when(core == 1)
        def _(both=both, row=row):
            cot_planes[0, :, row] = both[:, 128:]

        outer_at = jnp.where(core == 0, 1, 12)
        first = spread(nears[1 - core, 2 * y, :, :128], nears[1 - core, 2 * y + 1, :, :128])
        second = spread(nears[1 - core, 2 * y, :, 128:], nears[1 - core, 2 * y + 1, :, 128:])
        planes[outer_at, :, row] = first[:, :128]
        planes[outer_at + 1, :, row] = first[:, 128:]
        planes[outer_at + 2, :, row] = second[:, :128]
        cot_planes[jnp.where(core == 0, 0, 9), :, row] = second[:, 128:]
    x_ref[...] = planes[3:13]

    ones = jnp.ones((KDIM - 9 * channels, PLANE), BF16)
    for k in range(2):
        xc[k, 9 * channels :, :] = ones
    for k in range(12):
        hc[k, 9 * channels :, :] = ones
    gs[1, 2 * channels :, :] = jnp.zeros((channels, PLANE), BF16)
    gs[10, :channels, :] = jnp.zeros((channels, PLANE), BF16)

    def which_layer(q):
        return 0 if q < 0 else 1 if q < EDGE else 2

    def finish_one(q):
        pre = acc_one[q + 4] + b1_ref[...]
        mask = layer_mask[which_layer(q)][:1]
        sigma = jax.nn.sigmoid(pre)
        slope_ref[q + 2] = sigma * (1.0 + pre * (1.0 - sigma)) * mask
        hidden = (pre * sigma * mask).astype(BF16)
        write_taps(hc.at[q + 2], hidden, masks_ref)

    def step_one(p, finish):
        now = (p + 3) & 1
        product = plane_product(w1_ref, xc[now])
        write_taps(xc.at[1 - now], planes[p + 5], masks_ref)
        if finish:
            finish_one(p - 2)
        add_planes(acc_one, p + 4, product, channels)

    write_taps(xc.at[0], planes[1], masks_ref)
    for p in range(-3, 0):
        step_one(p, False)
    for p in range(0, 11):
        step_one(p, True)
    finish_one(9)

    def finish_two(q):
        pre = acc_two[q + 3] + b2_ref[...]
        sigma = jax.nn.sigmoid(pre)
        outs[q + 1] = (pre * sigma * layer_mask[which_layer(q)][:1]).astype(BF16)
        grad = cot_planes[q + 1].astype(F32) * (sigma * (1.0 + pre * (1.0 - sigma)))
        g_ref[q + 1] = grad.astype(BF16)
        kept = grad.astype(BF16)
        if not 0 <= q < EDGE:
            kept = jnp.zeros_like(kept)
        gs[q + 1, :channels, :] = kept
        gs[q + 2, channels : 2 * channels, :] = kept
        gs[q + 3, 2 * channels :, :] = kept

    def step_two(p, finish):
        product = plane_product(w2_ref, hc[p + 2])
        if finish:
            finish_two(p - 2)
        add_planes(acc_two, p + 3, product, channels)

    for p in range(-2, 1):
        step_two(p, False)
    for p in range(1, 10):
        step_two(p, True)
    finish_two(8)

    weight_products(total, gs, hc, 1, 1, 5)
    write_tiles(grad_ref, total, channels)

    back = back_ref[...]
    for y in range(2):
        row = slice(y * 128, (y + 1) * 128)
        for j in range(4):
            two = jnp.concatenate([outs[1 + 2 * j, :, row], outs[2 + 2 * j, :, row]], axis=1)
            both = jnp.dot(two, back, preferred_element_type=F32).astype(BF16)
            pair = slice(j * 128, (j + 1) * 128)
            bricks[0, 2 * y, :, pair] = both[:, :128]
            bricks[0, 2 * y + 1, :, pair] = both[:, 128:]
    for target, places in ((keep_ref, own_places), (send_ref, pair_places)):
        for s, (parity, column) in enumerate(places):
            scale = jnp.where(parity == core, 1.0, 0.0)
            target[s] = bricks[0, column] * jnp.full((channels, CELLS), scale, F32).astype(BF16)


def backward_kernel(
    g_ref, slope_ref, x_ref, w2t_ref, masks_ref, grad_ref, gc, xc, acc, gs, total,
):
    channels = g_ref.shape[1]
    blank = jnp.zeros((channels, PLANE), BF16)
    ones = jnp.ones((KDIM - 9 * channels, PLANE), BF16)
    for k in range(2):
        gc[k, 9 * channels :, :] = ones
    for k in range(10):
        xc[k, 9 * channels :, :] = ones
    for at, a in ((1, 1), (1, 2), (2, 2), (9, 0), (10, 0), (10, 1)):
        gs[at, a * channels : (a + 1) * channels, :] = blank

    def finish(q):
        grad = (acc[q + 2] * slope_ref[q + 2]).astype(BF16)
        gs[q + 1, :channels, :] = grad
        gs[q + 2, channels : 2 * channels, :] = grad
        gs[q + 3, 2 * channels :, :] = grad

    def step(p, done):
        now = (p + 1) & 1
        product = plane_product(w2t_ref, gc[now])
        write_taps(gc.at[1 - now], g_ref[min(p + 2, 9)], masks_ref)
        write_taps(xc.at[p + 1], x_ref[p + 1], masks_ref)
        if done:
            finish(p - 2)
        add_planes(acc, p + 2, product, channels)

    write_taps(gc.at[0], g_ref[0], masks_ref)
    for p in range(-1, 2):
        step(p, False)
    for p in range(2, 9):
        step(p, True)
    finish(7)
    weight_products(total, gs, xc, 1, 0, 5)
    write_tiles(grad_ref, total, channels)


def gather_kernel(first_ref, second_ref, w_one_ref, w_two_ref, b_one_ref, b_two_ref):
    for source, weight, bias in (
        (first_ref, w_one_ref, b_one_ref), (second_ref, w_two_ref, b_two_ref),
    ):
        for k in range(20):
            weight[:, k * 128 : (k + 1) * 128] = source[k].astype(F32)
        last = source[20].astype(F32)
        weight[:, 2560:2592] = last[:, :32]
        bias[...] = last.T[32:33, :]


VMEM = pl.BlockSpec(memory_space=pltpu.VMEM)
SMEM = pl.BlockSpec(memory_space=pltpu.SMEM)
PARAMS = pltpu.CompilerParams(vmem_limit_bytes=56 * 2**20)


def shared_sum(tiles):
    group = lax.axis_size("space")
    volumes = lax.axis_size("dp")
    rows = tiles.shape[1]
    parts = tiles.reshape(group, -1, 128)
    parts = lax.all_to_all(parts, "space", 0, 0)
    part = jnp.sum(parts.astype(F32), axis=0).astype(BF16)
    copies = jnp.broadcast_to(part[None], (volumes, *part.shape))
    copies = lax.all_to_all(copies, "dp", 0, 0)
    part = jnp.sum(copies.astype(F32), axis=0).astype(BF16)
    copies = jnp.broadcast_to(part[None], (group, *part.shape))
    return lax.all_to_all(copies, "space", 0, 0).reshape(-1, rows, 128)


def local(volume, neighbours, active, cotangent, weight_one, weight_two, bias_one, bias_two):
    volume, cotangent = volume[0], cotangent[0]
    slots, channels = volume.shape[0], volume.shape[1]
    me = lax.axis_index("space")
    count = lax.axis_size("space")
    odd = me % 2 == 1

    swap = [(d, d ^ 1) for d in range(count)]
    hop_a = [(d, d + 1) for d in range(1, count - 1, 2)] + [(d, d - 1) for d in range(2, count, 2)]
    hop_b = [(d, d + 2) for d in range(0, count - 2, 2)] + [(d, d - 2) for d in range(3, count, 2)]
    top = jnp.concatenate([volume[:, :, 320:], cotangent[:, :, 448:]], axis=2)
    bottom = jnp.concatenate([volume[:, :, :192], cotangent[:, :, :64]], axis=2)
    near_a = lax.ppermute(jnp.where(odd, top, bottom), "space", hop_a)
    near_b = lax.ppermute(jnp.where(odd, bottom, top), "space", hop_b)
    pair_volume = lax.ppermute(volume, "space", swap)
    pair_cot = lax.ppermute(cotangent, "space", swap)

    def by_plane(weight):
        weight = weight.reshape(channels, 3, 9 * channels).transpose(1, 0, 2)
        weight = weight.reshape(3 * channels, 9 * channels)
        return jnp.pad(weight, ((0, 0), (0, KDIM - 9 * channels)))

    w1 = by_plane(weight_one)
    w2 = by_plane(weight_two)
    w2t = weight_two.reshape(channels, 3, 3, 3, channels)[:, ::-1, ::-1, ::-1]
    w2t = w2t.transpose(1, 4, 2, 3, 0).reshape(3 * channels, 9 * channels)
    w2t = jnp.pad(w2t, ((0, 0), (0, KDIM - 9 * channels)))
    move = spread_matrix()
    masks = jnp.asarray(tap_masks(), BF16)
    core = me & 1
    alone = jnp.where(odd, me == count - 1, me == 0)
    step = jnp.where(odd, 1, -1)
    from_a = jnp.where(alone, me, me + step)
    from_b = jnp.where(alone, me ^ 1, me + 2 * step)
    devices = jnp.stack([me, me ^ 1, from_a, from_b]) * slots
    place = jnp.concatenate([devices, jnp.stack([core, alone.astype(core.dtype)])])
    place = place.astype(jnp.int32)

    bricks = (slots, channels, CELLS)
    keep, send, tiles_two, grad_out, slope, planes = pl.pallas_call(
        forward_kernel,
        out_shape=(
            jax.ShapeDtypeStruct(bricks, BF16),
            jax.ShapeDtypeStruct(bricks, BF16),
            jax.ShapeDtypeStruct((TILES, channels, 128), BF16),
            jax.ShapeDtypeStruct((10, channels, PLANE), BF16),
            jax.ShapeDtypeStruct((12, channels, PLANE), F32),
            jax.ShapeDtypeStruct((10, channels, PLANE), BF16),
        ),
        in_specs=[SMEM] * 3 + [VMEM] * 13,
        out_specs=(VMEM,) * 6,
        scratch_shapes=[
            pltpu.VMEM((2, *bricks), BF16),
            pltpu.VMEM((2, *bricks), BF16),
            pltpu.VMEM((2, slots, channels, PLANE), BF16),
            pltpu.VMEM((16, channels, PLANE), BF16),
            pltpu.VMEM((10, channels, PLANE), BF16),
            pltpu.VMEM((3, 8, PLANE), F32),
            pltpu.VMEM((2, KDIM, PLANE), BF16),
            pltpu.VMEM((12, KDIM, PLANE), BF16),
            pltpu.VMEM((16, channels, PLANE), F32),
            pltpu.VMEM((14, channels, PLANE), F32),
            pltpu.VMEM((10, channels, PLANE), BF16),
            pltpu.VMEM((12, 3 * channels, PLANE), BF16),
            pltpu.VMEM((3 * channels, KDIM), F32),
        ],
        compiler_params=PARAMS,
        cost_estimate=pl.CostEstimate(flops=2**33, bytes_accessed=2**23, transcendentals=2**20),
        name="forward",
    )(
        place, neighbours[0], active[0], volume, pair_volume, near_a, near_b, cotangent, pair_cot,
        w1, w2, bias_one[:, None], bias_two[:, None], jnp.asarray(move, BF16),
        jnp.asarray(move.T, BF16), masks,
    )
    tiles_one = pl.pallas_call(
        backward_kernel,
        out_shape=jax.ShapeDtypeStruct((TILES, channels, 128), BF16),
        in_specs=[VMEM] * 5,
        out_specs=VMEM,
        scratch_shapes=[
            pltpu.VMEM((2, KDIM, PLANE), BF16),
            pltpu.VMEM((10, KDIM, PLANE), BF16),
            pltpu.VMEM((12, channels, PLANE), F32),
            pltpu.VMEM((12, 3 * channels, PLANE), BF16),
            pltpu.VMEM((3 * channels, KDIM), F32),
        ],
        compiler_params=PARAMS,
        cost_estimate=pl.CostEstimate(flops=2**32, bytes_accessed=2**22, transcendentals=0),
        name="backward",
    )(grad_out, slope, planes, w2t, masks)

    output = (keep + lax.ppermute(send, "space", swap))[None]
    all_two = shared_sum(tiles_two)
    all_one = shared_sum(tiles_one)
    width = 27 * channels
    weight_shape = jax.ShapeDtypeStruct((channels, width), F32)
    bias_shape = jax.ShapeDtypeStruct((1, channels), F32)
    total_w_one, total_w_two, total_b_one, total_b_two = pl.pallas_call(
        gather_kernel,
        out_shape=(weight_shape, weight_shape, bias_shape, bias_shape),
        in_specs=[VMEM] * 2,
        out_specs=(VMEM,) * 4,
        compiler_params=PARAMS,
        name="gather",
    )(all_one, all_two)
    return (output, total_w_one, total_w_two, total_b_one[0], total_b_two[0])


def solution(mesh):
    in_specs = (
        P("dp", "space", None, None),
        P("dp", None, None),
        P("dp", None),
        P("dp", "space", None, None),
        P(),
        P(),
        P(),
        P(),
    )
    out_specs = (P("dp", "space", None, None), P(), P(), P(), P())
    return jax.shard_map(local, mesh=mesh, in_specs=in_specs, out_specs=out_specs, check_vma=False)
```

```python
import jax
import jax.numpy as jnp
import numpy as np
from jax import lax
from jax.experimental import pallas as pl
from jax.experimental.pallas import tpu as pltpu
from jax.sharding import PartitionSpec as P

EDGE = 8
PLANE = 256
CELLS = 512
KDIM = 896
TILES = 21
ROWS = 2048
NEAR_DOWN, NEAR_Y, NEAR_Z, NEAR_UP = 4, 10, 12, 21
F32 = jnp.float32
BF16 = jnp.bfloat16


def spread_matrix():
    move = np.zeros((256, 256), np.float32)
    for z in range(2):
        for p in range(2):
            for q in range(8):
                for r in range(8):
                    move[z * 128 + p * 64 + q * 8 + r, p * 128 + q * 16 + z * 8 + r] = 1.0
    return move


def tap_masks():
    masks = np.zeros((9, 16, 256), np.float32)
    for b in range(3):
        for c in range(3):
            for q in range(16):
                for r in range(16):
                    inside = 0 <= q + b - 1 < 16 and 0 <= r + c - 1 < 16
                    masks[b * 3 + c, :, q * 16 + r] = float(inside)
    return masks


def write_taps(dst, plane, masks_ref):
    channels = plane.shape[0]
    wide = plane.astype(F32)
    for k in range(9):
        step = (k // 3 - 1) * 16 + (k % 3 - 1)
        if step == 0:
            moved = plane
        else:
            moved = pltpu.roll(wide, (-step) % PLANE, 1).astype(BF16)
            moved = moved * jnp.concatenate([masks_ref[k]] * (channels // 16), axis=0)
        dst[k * channels : (k + 1) * channels, :] = moved


def slot_place(near_ref, slot, pair_slots):
    shift = pair_slots.bit_length() - 1
    up = near_ref[slot, NEAR_UP]
    inside = jnp.logical_and(up >= 0, up >> shift == slot >> shift)
    parity = jnp.where(inside, 0, 1)
    column = jnp.where(near_ref[slot, NEAR_Y] >= 0, 2, 0) + jnp.where(
        near_ref[slot, NEAR_Z] >= 0, 1, 0
    )
    return parity, column


def lane_mask(scalars):
    lane = lax.broadcasted_iota(jnp.int32, (8, PLANE), 1)
    high_y = lane >= 128
    high_z = (lane & 8) != 0
    s = [jnp.full((8, PLANE), v, F32) for v in scalars]
    return jnp.where(high_y, jnp.where(high_z, s[3], s[2]), jnp.where(high_z, s[1], s[0]))


def plane_product(weight_ref, taps):
    return jnp.dot(weight_ref[...], taps, preferred_element_type=F32)


def add_planes(acc, at, product, channels):
    acc[at + 1] = product[:channels]
    acc[at] = acc[at] + product[channels : 2 * channels]
    acc[at - 1] = acc[at - 1] + product[2 * channels :]


def weight_products(total, grads, taps, first_grad, first_tap, pairs):
    for j in range(0, 2 * pairs, 2):
        left = jnp.concatenate([grads[first_grad + j], grads[first_grad + j + 1]], axis=1)
        right = jnp.concatenate([taps[first_tap + j], taps[first_tap + j + 1]], axis=1)
        part = lax.dot_general(left, right, (((1,), (1,)), ((), ())), preferred_element_type=F32)
        total[...] = part if j == 0 else total[...] + part


def write_tiles(flat, total, channels):
    lane = lax.broadcasted_iota(jnp.int32, (channels, 128), 1)
    blank = jnp.zeros((channels, 128), F32)
    first = total[:channels, :]
    second = jnp.concatenate([total[channels : 2 * channels, :], blank], axis=1)
    third = jnp.concatenate([total[2 * channels :, :], blank], axis=1)
    second = pltpu.roll(second, 96, 1)
    third = pltpu.roll(third, 64, 1)

    def cut(value, k):
        return value[:, k * 128 : (k + 1) * 128]

    tiles = [cut(first, k) for k in range(6)]
    tiles.append(jnp.where(lane < 96, cut(first, 6), cut(second, 0)))
    tiles += [cut(second, k) for k in range(1, 7)]
    tiles.append(jnp.where(lane < 64, cut(second, 7), cut(third, 0)))
    tiles += [cut(third, k) for k in range(1, 8)]
    for k in range(TILES):
        flat[k * channels : (k + 1) * channels, :] = tiles[k]
    flat[TILES * channels :, :] = jnp.zeros((ROWS - TILES * channels, 128), F32)


def split_tiles(keep_ref, send_ref, flat, me):
    chips, rows = keep_ref.shape[0], keep_ref.shape[1]
    core, chip = me & 1, me >> 1
    for r in range(chips):
        at = jnp.clip(chip ^ r, 0, chips - 1) * rows
        here = at + jnp.where(core == 1, chips * rows, 0)
        there = at + jnp.where(core == 1, 0, chips * rows)
        keep_ref[r] = flat[pl.ds(pl.multiple_of(here, rows), rows), :]
        send_ref[r] = flat[pl.ds(pl.multiple_of(there, rows), rows), :].astype(BF16)


def layout_kernel(
    me_ref, near_ref, active_ref, own_ref, pair_ref, cot_own_ref, cot_pair_ref, move_ref,
    x_ref, cot_ref, edge_ref, mask_ref, bricks, cots,
):
    slots, channels = own_ref.shape[0], own_ref.shape[1]
    all_slots = near_ref.shape[0]
    me = jnp.clip(me_ref[0], 0, all_slots // slots - 1)
    core = me & 1
    even = core == 0

    live = [[jnp.float32(0)] * 4 for _ in range(2)]
    beyond = [jnp.float32(0)] * 4
    for device, source, cot_source in (
        (me, own_ref, cot_own_ref), (me ^ 1, pair_ref, cot_pair_ref),
    ):
        for s in range(slots):
            slot = jnp.clip(device * slots + s, 0, all_slots - 1)
            parity, column = slot_place(near_ref, slot, 2 * slots)
            alive = active_ref[slot].astype(F32)
            scale = jnp.full((channels, CELLS), alive, F32).astype(BF16)
            bricks[parity, column] = source[s] * scale
            cots[parity, column] = cot_source[s] * scale
            outer = jnp.where(even, near_ref[slot, NEAR_DOWN], near_ref[slot, NEAR_UP])
            alive_outer = active_ref[jnp.clip(outer, 0, all_slots - 1)].astype(F32)
            alive_outer = jnp.where(outer >= 0, alive_outer, 0.0)
            for k in range(4):
                for p in range(2):
                    here = jnp.logical_and(parity == p, column == k)
                    live[p][k] = jnp.where(here, alive, live[p][k])
                here = jnp.logical_and(parity == core, column == k)
                beyond[k] = jnp.where(here, alive_outer, beyond[k])
    inner = [jnp.where(even, live[1][k], live[0][k]) for k in range(4)]
    mask_ref[0] = lane_mask([jnp.where(even, beyond[k], inner[k]) for k in range(4)])
    mask_ref[1] = lane_mask([jnp.where(even, live[0][k], live[1][k]) for k in range(4)])
    mask_ref[2] = lane_mask([jnp.where(even, inner[k], beyond[k]) for k in range(4)])

    move = move_ref[...]
    mine = jnp.where(even, 0, 1)

    def spread(left, right):
        two = jnp.concatenate([left, right], axis=1)
        return jnp.dot(two, move, preferred_element_type=F32).astype(BF16)

    for y in range(2):
        row = slice(y * 128, (y + 1) * 128)
        for j in range(4):
            pair = slice(j * 128, (j + 1) * 128)
            both = spread(bricks[mine, 2 * y, :, pair], bricks[mine, 2 * y + 1, :, pair])
            x_ref[4 + 2 * j, :, row] = both[:, :128]
            x_ref[5 + 2 * j, :, row] = both[:, 128:]
            both = spread(cots[mine, 2 * y, :, pair], cots[mine, 2 * y + 1, :, pair])
            cot_ref[1 + 2 * j, :, row] = both[:, :128]
            cot_ref[2 + 2 * j, :, row] = both[:, 128:]
        inner_at = jnp.where(even, 12, 0)
        for j in range(2):
            start = pl.multiple_of(jnp.where(even, j * 128, 256 + j * 128), 128)
            pair = pl.ds(start, 128)
            both = spread(
                bricks[1 - mine, 2 * y, :, pair], bricks[1 - mine, 2 * y + 1, :, pair]
            )
            x_ref[inner_at + 2 * j, :, row] = both[:, :128]
            x_ref[inner_at + 2 * j + 1, :, row] = both[:, 128:]
        pair = pl.ds(pl.multiple_of(jnp.where(even, 0, 384), 128), 128)
        both = spread(cots[1 - mine, 2 * y, :, pair], cots[1 - mine, 2 * y + 1, :, pair])

        @pl.when(even)
        def _(both=both, row=row):
            cot_ref[9, :, row] = both[:, :128]

        @pl.when(core == 1)
        def _(both=both, row=row):
            cot_ref[0, :, row] = both[:, 128:]

    edge_ref[:3] = x_ref[pl.ds(jnp.where(even, 4, 9), 3)]
    edge_ref[3] = cot_ref[jnp.where(even, 1, 8)]


def forward_kernel(
    me_ref, near_ref, x_in_ref, cot_in_ref, outer_ref, layer_mask, w1_ref, w2_ref, b1_ref, b2_ref,
    back_ref, masks_ref,
    keep_ref, send_ref, grad_keep_ref, grad_send_ref, g_ref, slope_ref, x_ref,
    bricks, planes, cot_planes, xc, hc, acc_one, acc_two, outs, gs, total, flat,
):
    slots, channels = keep_ref.shape[0], keep_ref.shape[1]
    me = jnp.clip(me_ref[0], 0, near_ref.shape[0] // slots - 1)
    core = me & 1
    even = core == 0
    planes[...] = x_in_ref[...]
    cot_planes[...] = cot_in_ref[...]
    planes[pl.ds(jnp.where(even, 1, 12), 3)] = outer_ref[:3]
    cot_planes[jnp.where(even, 0, 9)] = outer_ref[3]
    bias_one = jnp.broadcast_to(b1_ref[...], (8, channels)).T[:, :1]
    bias_two = jnp.broadcast_to(b2_ref[...], (8, channels)).T[:, :1]
    x_ref[...] = planes[3:13]

    ones = jnp.ones((KDIM - 9 * channels, PLANE), BF16)
    for k in range(2):
        xc[k, 9 * channels :, :] = ones
    for k in range(12):
        hc[k, 9 * channels :, :] = ones
    gs[1, 2 * channels :, :] = jnp.zeros((channels, PLANE), BF16)
    gs[10, :channels, :] = jnp.zeros((channels, PLANE), BF16)

    def which_layer(q):
        return 0 if q < 0 else 1 if q < EDGE else 2

    def finish_one(q):
        pre = acc_one[q + 4] + bias_one
        mask = layer_mask[which_layer(q)][:1]
        sigma = jax.nn.sigmoid(pre)
        slope_ref[q + 2] = sigma * (1.0 + pre * (1.0 - sigma)) * mask
        hidden = (pre * sigma * mask).astype(BF16)
        write_taps(hc.at[q + 2], hidden, masks_ref)

    def step_one(p, finish):
        now = (p + 3) & 1
        product = plane_product(w1_ref, xc[now])
        write_taps(xc.at[1 - now], planes[p + 5], masks_ref)
        if finish:
            finish_one(p - 2)
        add_planes(acc_one, p + 4, product, channels)

    write_taps(xc.at[0], planes[1], masks_ref)
    for p in range(-3, 0):
        step_one(p, False)
    for p in range(0, 11):
        step_one(p, True)
    finish_one(9)

    def finish_two(q):
        pre = acc_two[q + 3] + bias_two
        sigma = jax.nn.sigmoid(pre)
        outs[q + 1] = (pre * sigma * layer_mask[which_layer(q)][:1]).astype(BF16)
        grad = cot_planes[q + 1].astype(F32) * (sigma * (1.0 + pre * (1.0 - sigma)))
        g_ref[q + 1] = grad.astype(BF16)
        kept = grad.astype(BF16)
        if not 0 <= q < EDGE:
            kept = jnp.zeros_like(kept)
        gs[q + 1, :channels, :] = kept
        gs[q + 2, channels : 2 * channels, :] = kept
        gs[q + 3, 2 * channels :, :] = kept

    def step_two(p, finish):
        product = plane_product(w2_ref, hc[p + 2])
        if finish:
            finish_two(p - 2)
        add_planes(acc_two, p + 3, product, channels)

    for p in range(-2, 1):
        step_two(p, False)
    for p in range(1, 10):
        step_two(p, True)
    finish_two(8)

    weight_products(total, gs, hc, 1, 1, 5)
    write_tiles(flat, total, channels)
    split_tiles(grad_keep_ref, grad_send_ref, flat, me)

    back = back_ref[...]
    for y in range(2):
        row = slice(y * 128, (y + 1) * 128)
        for j in range(4):
            two = jnp.concatenate([outs[1 + 2 * j, :, row], outs[2 + 2 * j, :, row]], axis=1)
            both = jnp.dot(two, back, preferred_element_type=F32).astype(BF16)
            pair = slice(j * 128, (j + 1) * 128)
            bricks[2 * y, :, pair] = both[:, :128]
            bricks[2 * y + 1, :, pair] = both[:, 128:]
    for target, device in ((keep_ref, me), (send_ref, me ^ 1)):
        for s in range(slots):
            slot = jnp.clip(device * slots + s, 0, near_ref.shape[0] - 1)
            parity, column = slot_place(near_ref, slot, 2 * slots)
            scale = jnp.where(parity == core, 1.0, 0.0)
            target[s] = bricks[column] * jnp.full((channels, CELLS), scale, F32).astype(BF16)


def backward_kernel(
    me_ref, g_ref, slope_ref, x_ref, w2t_ref, masks_ref, grad_keep_ref, grad_send_ref,
    gc, xc, acc, gs, total, flat,
):
    channels = g_ref.shape[1]
    blank = jnp.zeros((channels, PLANE), BF16)
    ones = jnp.ones((KDIM - 9 * channels, PLANE), BF16)
    for k in range(2):
        gc[k, 9 * channels :, :] = ones
    for k in range(10):
        xc[k, 9 * channels :, :] = ones
    for at, a in ((1, 1), (1, 2), (2, 2), (9, 0), (10, 0), (10, 1)):
        gs[at, a * channels : (a + 1) * channels, :] = blank

    def finish(q):
        grad = (acc[q + 2] * slope_ref[q + 2]).astype(BF16)
        gs[q + 1, :channels, :] = grad
        gs[q + 2, channels : 2 * channels, :] = grad
        gs[q + 3, 2 * channels :, :] = grad

    def step(p, done):
        now = (p + 1) & 1
        product = plane_product(w2t_ref, gc[now])
        write_taps(gc.at[1 - now], g_ref[min(p + 2, 9)], masks_ref)
        write_taps(xc.at[p + 1], x_ref[p + 1], masks_ref)
        if done:
            finish(p - 2)
        add_planes(acc, p + 2, product, channels)

    write_taps(gc.at[0], g_ref[0], masks_ref)
    for p in range(-1, 2):
        step(p, False)
    for p in range(2, 9):
        step(p, True)
    finish(7)
    weight_products(total, gs, xc, 1, 0, 5)
    write_tiles(flat, total, channels)
    split_tiles(grad_keep_ref, grad_send_ref, flat, jnp.clip(me_ref[0], 0, 2**15))


def gather_kernel(me_ref, *refs):
    chips = (len(refs) - 5) // 2
    w_one_ref, w_two_ref, b_one_ref, b_two_ref, flat = refs[2 * chips :]
    rows = refs[0].shape[1]
    channels = w_one_ref.shape[0]
    me = jnp.clip(me_ref[0], 0, 2 * chips - 1)
    core, chip = me & 1, me >> 1
    for half in range(2):
        base = jnp.where(core == half, 0, chips * rows)
        for r in range(chips):
            at = base + jnp.clip(chip ^ r, 0, chips - 1) * rows
            flat[:, pl.ds(pl.multiple_of(at, rows), rows), :] = refs[half * chips + r][...]
    for n, (weight, bias) in enumerate(((w_one_ref, b_one_ref), (w_two_ref, b_two_ref))):
        for k in range(TILES - 1):
            tile = flat[n, k * channels : (k + 1) * channels, :]
            weight[:, k * 128 : (k + 1) * 128] = tile.astype(F32)
        last = flat[n, (TILES - 1) * channels : TILES * channels, :].astype(F32)
        weight[:, 2560:2592] = last[:, :32]
        bias[...] = last.T[32:33, :]


VMEM = pl.BlockSpec(memory_space=pltpu.VMEM)
SMEM = pl.BlockSpec(memory_space=pltpu.SMEM)
PARAMS = pltpu.CompilerParams(vmem_limit_bytes=56 * 2**20)


def shared_sum(keeps, sends, send_two_done):
    chips = keeps[0].shape[0]
    count = 2 * chips
    volumes = lax.axis_size("dp")
    swap = [(d, d ^ 1) for d in range(count)]
    halves = [keeps[0] + lax.ppermute(sends[0], "space", swap).astype(F32)]
    halves.append(keeps[1] + send_two_done.astype(F32))
    total = jnp.stack([half[0] for half in halves])
    for r in range(1, chips):
        part = jnp.stack([half[r] for half in halves]).astype(BF16)
        hop = [(d, d ^ (2 * r)) for d in range(count)]
        total = total + lax.ppermute(part, "space", hop).astype(F32)
    total = total.astype(BF16)
    step = 1
    while step < volumes:
        hop = [(d, d ^ step) for d in range(volumes)]
        moved = lax.ppermute(total, "dp", hop)
        total = (total.astype(F32) + moved.astype(F32)).astype(BF16)
        step *= 2
    parts = [total]
    for r in range(1, chips):
        parts.append(lax.ppermute(total, "space", [(d, d ^ (2 * r)) for d in range(count)]))
    return parts + [lax.ppermute(part, "space", swap) for part in parts]


def local(volume, neighbours, active, cotangent, weight_one, weight_two, bias_one, bias_two):
    volume, cotangent = volume[0], cotangent[0]
    slots, channels = volume.shape[0], volume.shape[1]
    near = neighbours[0]
    count = lax.axis_size("space")
    chips = count // 2
    me = lax.axis_index("space").astype(jnp.int32)[None]

    swap = [(d, d ^ 1) for d in range(count)]
    hop = [(d, d + 1) for d in range(1, count - 1, 2)] + [(d, d - 1) for d in range(2, count, 2)]
    pair_volume = lax.ppermute(volume, "space", swap)
    pair_cot = lax.ppermute(cotangent, "space", swap)

    def by_plane(weight):
        weight = weight.reshape(channels, 3, 9 * channels).transpose(1, 0, 2)
        weight = weight.reshape(3 * channels, 9 * channels)
        return jnp.pad(weight, ((0, 0), (0, KDIM - 9 * channels)))

    w1 = by_plane(weight_one)
    w2 = by_plane(weight_two)
    w2t = weight_two.reshape(channels, 3, 3, 3, channels)[:, ::-1, ::-1, ::-1]
    w2t = w2t.transpose(1, 4, 2, 3, 0).reshape(3 * channels, 9 * channels)
    w2t = jnp.pad(w2t, ((0, 0), (0, KDIM - 9 * channels)))
    move = spread_matrix()
    masks = jnp.asarray(tap_masks(), BF16)

    def planes(number, dtype=BF16):
        return jax.ShapeDtypeStruct((number, channels, PLANE), dtype)

    bricks = (slots, channels, CELLS)
    x_planes, cot_planes, edge, layer_mask = pl.pallas_call(
        layout_kernel,
        out_shape=(planes(16), planes(10), planes(4), jax.ShapeDtypeStruct((3, 8, PLANE), F32)),
        in_specs=[SMEM] * 3 + [VMEM] * 5,
        out_specs=(VMEM,) * 4,
        scratch_shapes=[pltpu.VMEM((2, *bricks), BF16), pltpu.VMEM((2, *bricks), BF16)],
        compiler_params=PARAMS,
        name="layout",
    )(me, near, active[0], volume, pair_volume, cotangent, pair_cot, jnp.asarray(move, BF16))
    outer = lax.ppermute(edge, "space", hop)

    half = (chips, ROWS // count, 128)
    keep, send, keep_two, send_two, grad_out, slope, x_inner = pl.pallas_call(
        forward_kernel,
        out_shape=(
            jax.ShapeDtypeStruct(bricks, BF16),
            jax.ShapeDtypeStruct(bricks, BF16),
            jax.ShapeDtypeStruct(half, F32),
            jax.ShapeDtypeStruct(half, BF16),
            planes(10),
            planes(12, F32),
            planes(10),
        ),
        in_specs=[SMEM] * 2 + [VMEM] * 10,
        out_specs=(VMEM,) * 7,
        scratch_shapes=[
            pltpu.VMEM(bricks, BF16),
            pltpu.VMEM((16, channels, PLANE), BF16),
            pltpu.VMEM((10, channels, PLANE), BF16),
            pltpu.VMEM((2, KDIM, PLANE), BF16),
            pltpu.VMEM((12, KDIM, PLANE), BF16),
            pltpu.VMEM((16, channels, PLANE), F32),
            pltpu.VMEM((14, channels, PLANE), F32),
            pltpu.VMEM((10, channels, PLANE), BF16),
            pltpu.VMEM((12, 3 * channels, PLANE), BF16),
            pltpu.VMEM((3 * channels, KDIM), F32),
            pltpu.VMEM((ROWS, 128), F32),
        ],
        compiler_params=PARAMS,
        cost_estimate=pl.CostEstimate(flops=2**33, bytes_accessed=2**23, transcendentals=2**20),
        name="forward",
    )(
        me, near, x_planes, cot_planes, outer, layer_mask, w1, w2, bias_one[None], bias_two[None],
        jnp.asarray(move.T, BF16), masks,
    )
    got_two = lax.ppermute(send_two, "space", swap)
    keep_one, send_one = pl.pallas_call(
        backward_kernel,
        out_shape=(jax.ShapeDtypeStruct(half, F32), jax.ShapeDtypeStruct(half, BF16)),
        in_specs=[SMEM] + [VMEM] * 5,
        out_specs=(VMEM,) * 2,
        scratch_shapes=[
            pltpu.VMEM((2, KDIM, PLANE), BF16),
            pltpu.VMEM((10, KDIM, PLANE), BF16),
            pltpu.VMEM((12, channels, PLANE), F32),
            pltpu.VMEM((12, 3 * channels, PLANE), BF16),
            pltpu.VMEM((3 * channels, KDIM), F32),
            pltpu.VMEM((ROWS, 128), F32),
        ],
        compiler_params=PARAMS,
        cost_estimate=pl.CostEstimate(flops=2**32, bytes_accessed=2**22, transcendentals=0),
        name="backward",
    )(me, grad_out, slope, x_inner, w2t, masks)

    output = (keep + lax.ppermute(send, "space", swap))[None]
    parts = shared_sum([keep_one, keep_two], [send_one, send_two], got_two)
    weight_shape = jax.ShapeDtypeStruct((channels, 27 * channels), F32)
    bias_shape = jax.ShapeDtypeStruct((1, channels), F32)
    total_w_one, total_w_two, total_b_one, total_b_two = pl.pallas_call(
        gather_kernel,
        out_shape=(weight_shape, weight_shape, bias_shape, bias_shape),
        in_specs=[SMEM] + [VMEM] * len(parts),
        out_specs=(VMEM,) * 4,
        scratch_shapes=[pltpu.VMEM((2, ROWS, 128), BF16)],
        compiler_params=PARAMS,
        name="gather",
    )(me, *parts)
    return (output, total_w_one, total_w_two, total_b_one[0], total_b_two[0])


def solution(mesh):
    in_specs = (
        P("dp", "space", None, None),
        P("dp", None, None),
        P("dp", None),
        P("dp", "space", None, None),
        P(),
        P(),
        P(),
        P(),
    )
    out_specs = (P("dp", "space", None, None), P(), P(), P(), P())
    return jax.shard_map(local, mesh=mesh, in_specs=in_specs, out_specs=out_specs, check_vma=False)
```

```python
import jax
import jax.numpy as jnp
import numpy as np
from jax import lax
from jax.experimental import pallas as pl
from jax.experimental.pallas import tpu as pltpu
from jax.sharding import PartitionSpec as P

EDGE = 8
PLANE = 256
CELLS = 512
KDIM = 896
TILES = 21
ROWS = 2048
NEAR_DOWN, NEAR_Y, NEAR_Z, NEAR_UP = 4, 10, 12, 21
F32 = jnp.float32
BF16 = jnp.bfloat16


def spread_matrix():
    move = np.zeros((256, 256), np.float32)
    for z in range(2):
        for p in range(2):
            for q in range(8):
                for r in range(8):
                    move[z * 128 + p * 64 + q * 8 + r, p * 128 + q * 16 + z * 8 + r] = 1.0
    return move


def tap_masks():
    masks = np.zeros((9, 16, 256), np.float32)
    for b in range(3):
        for c in range(3):
            for q in range(16):
                for r in range(16):
                    inside = 0 <= q + b - 1 < 16 and 0 <= r + c - 1 < 16
                    masks[b * 3 + c, :, q * 16 + r] = float(inside)
    return masks


def write_taps(dst, plane, masks_ref):
    channels = plane.shape[0]
    wide = plane.astype(F32)
    for k in range(9):
        step = (k // 3 - 1) * 16 + (k % 3 - 1)
        if step == 0:
            moved = plane
        else:
            moved = pltpu.roll(wide, (-step) % PLANE, 1).astype(BF16)
            moved = moved * jnp.concatenate([masks_ref[k]] * (channels // 16), axis=0)
        dst[k * channels : (k + 1) * channels, :] = moved


def slot_place(near_ref, slot, pair_slots):
    shift = pair_slots.bit_length() - 1
    up = near_ref[slot, NEAR_UP]
    inside = jnp.logical_and(up >= 0, up >> shift == slot >> shift)
    parity = jnp.where(inside, 0, 1)
    column = jnp.where(near_ref[slot, NEAR_Y] >= 0, 2, 0) + jnp.where(
        near_ref[slot, NEAR_Z] >= 0, 1, 0
    )
    return parity, column


def lane_mask(scalars):
    lane = lax.broadcasted_iota(jnp.int32, (8, PLANE), 1)
    high_y = lane >= 128
    high_z = (lane & 8) != 0
    s = [jnp.full((8, PLANE), v, F32) for v in scalars]
    return jnp.where(high_y, jnp.where(high_z, s[3], s[2]), jnp.where(high_z, s[1], s[0]))


def plane_product(weight_ref, taps):
    return jnp.dot(weight_ref[...], taps, preferred_element_type=F32)


def add_planes(acc, at, product, channels):
    acc[at + 1] = product[:channels]
    acc[at] = acc[at] + product[channels : 2 * channels]
    acc[at - 1] = acc[at - 1] + product[2 * channels :]


def weight_products(total, grads, taps, first_grad, first_tap, pairs):
    for j in range(0, 2 * pairs, 2):
        left = jnp.concatenate([grads[first_grad + j], grads[first_grad + j + 1]], axis=1)
        right = jnp.concatenate([taps[first_tap + j], taps[first_tap + j + 1]], axis=1)
        part = lax.dot_general(left, right, (((1,), (1,)), ((), ())), preferred_element_type=F32)
        total[...] = part if j == 0 else total[...] + part


def write_tiles(flat, total, channels):
    lane = lax.broadcasted_iota(jnp.int32, (channels, 128), 1)
    blank = jnp.zeros((channels, 128), F32)
    first = total[:channels, :]
    second = jnp.concatenate([total[channels : 2 * channels, :], blank], axis=1)
    third = jnp.concatenate([total[2 * channels :, :], blank], axis=1)
    second = pltpu.roll(second, 96, 1)
    third = pltpu.roll(third, 64, 1)

    def cut(value, k):
        return value[:, k * 128 : (k + 1) * 128]

    tiles = [cut(first, k) for k in range(6)]
    tiles.append(jnp.where(lane < 96, cut(first, 6), cut(second, 0)))
    tiles += [cut(second, k) for k in range(1, 7)]
    tiles.append(jnp.where(lane < 64, cut(second, 7), cut(third, 0)))
    tiles += [cut(third, k) for k in range(1, 8)]
    for k in range(TILES):
        flat[k * channels : (k + 1) * channels, :] = tiles[k]
    flat[TILES * channels :, :] = jnp.zeros((ROWS - TILES * channels, 128), F32)


def split_tiles(keep_ref, send_ref, flat, me):
    chips, rows = keep_ref.shape[0], keep_ref.shape[1]
    core, chip = me & 1, me >> 1
    for r in range(chips):
        at = jnp.clip(chip ^ r, 0, chips - 1) * rows
        here = at + jnp.where(core == 1, chips * rows, 0)
        there = at + jnp.where(core == 1, 0, chips * rows)
        keep_ref[r] = flat[pl.ds(pl.multiple_of(here, rows), rows), :]
        send_ref[r] = flat[pl.ds(pl.multiple_of(there, rows), rows), :]


def layout_kernel(
    me_ref, near_ref, active_ref, own_ref, pair_ref, cot_own_ref, cot_pair_ref, move_ref,
    x_ref, cot_ref, edge_ref, mask_ref, bricks, cots,
):
    slots, channels = own_ref.shape[0], own_ref.shape[1]
    all_slots = near_ref.shape[0]
    me = jnp.clip(me_ref[0], 0, all_slots // slots - 1)
    core = me & 1
    even = core == 0

    live = [[jnp.float32(0)] * 4 for _ in range(2)]
    beyond = [jnp.float32(0)] * 4
    for device, source, cot_source in (
        (me, own_ref, cot_own_ref), (me ^ 1, pair_ref, cot_pair_ref),
    ):
        for s in range(slots):
            slot = jnp.clip(device * slots + s, 0, all_slots - 1)
            parity, column = slot_place(near_ref, slot, 2 * slots)
            alive = active_ref[slot].astype(F32)
            scale = jnp.full((channels, CELLS), alive, F32).astype(BF16)
            bricks[parity, column] = source[s] * scale
            cots[parity, column] = cot_source[s] * scale
            outer = jnp.where(even, near_ref[slot, NEAR_DOWN], near_ref[slot, NEAR_UP])
            alive_outer = active_ref[jnp.clip(outer, 0, all_slots - 1)].astype(F32)
            alive_outer = jnp.where(outer >= 0, alive_outer, 0.0)
            for k in range(4):
                for p in range(2):
                    here = jnp.logical_and(parity == p, column == k)
                    live[p][k] = jnp.where(here, alive, live[p][k])
                here = jnp.logical_and(parity == core, column == k)
                beyond[k] = jnp.where(here, alive_outer, beyond[k])
    inner = [jnp.where(even, live[1][k], live[0][k]) for k in range(4)]
    mask_ref[0] = lane_mask([jnp.where(even, beyond[k], inner[k]) for k in range(4)])
    mask_ref[1] = lane_mask([jnp.where(even, live[0][k], live[1][k]) for k in range(4)])
    mask_ref[2] = lane_mask([jnp.where(even, inner[k], beyond[k]) for k in range(4)])

    move = move_ref[...]
    mine = jnp.where(even, 0, 1)

    def spread(left, right):
        two = jnp.concatenate([left, right], axis=1)
        return jnp.dot(two, move, preferred_element_type=F32).astype(BF16)

    for y in range(2):
        row = slice(y * 128, (y + 1) * 128)
        for j in range(4):
            pair = slice(j * 128, (j + 1) * 128)
            both = spread(bricks[mine, 2 * y, :, pair], bricks[mine, 2 * y + 1, :, pair])
            x_ref[4 + 2 * j, :, row] = both[:, :128]
            x_ref[5 + 2 * j, :, row] = both[:, 128:]
            both = spread(cots[mine, 2 * y, :, pair], cots[mine, 2 * y + 1, :, pair])
            cot_ref[1 + 2 * j, :, row] = both[:, :128]
            cot_ref[2 + 2 * j, :, row] = both[:, 128:]
        inner_at = jnp.where(even, 12, 0)
        for j in range(2):
            start = pl.multiple_of(jnp.where(even, j * 128, 256 + j * 128), 128)
            pair = pl.ds(start, 128)
            both = spread(
                bricks[1 - mine, 2 * y, :, pair], bricks[1 - mine, 2 * y + 1, :, pair]
            )
            x_ref[inner_at + 2 * j, :, row] = both[:, :128]
            x_ref[inner_at + 2 * j + 1, :, row] = both[:, 128:]
        pair = pl.ds(pl.multiple_of(jnp.where(even, 0, 384), 128), 128)
        both = spread(cots[1 - mine, 2 * y, :, pair], cots[1 - mine, 2 * y + 1, :, pair])

        @pl.when(even)
        def _(both=both, row=row):
            cot_ref[9, :, row] = both[:, :128]

        @pl.when(core == 1)
        def _(both=both, row=row):
            cot_ref[0, :, row] = both[:, 128:]

    edge_ref[:3] = x_ref[pl.ds(jnp.where(even, 4, 9), 3)]
    edge_ref[3] = cot_ref[jnp.where(even, 1, 8)]


def forward_kernel(
    me_ref, near_ref, x_in_ref, cot_in_ref, outer_ref, layer_mask, w1_ref, w2_ref, b1_ref, b2_ref,
    back_ref, masks_ref,
    keep_ref, send_ref, grad_keep_ref, grad_send_ref, g_ref, slope_ref, x_ref,
    bricks, planes, cot_planes, xc, hc, acc_one, acc_two, outs, gs, total, flat,
):
    slots, channels = keep_ref.shape[0], keep_ref.shape[1]
    me = jnp.clip(me_ref[0], 0, near_ref.shape[0] // slots - 1)
    core = me & 1
    even = core == 0
    planes[...] = x_in_ref[...]
    cot_planes[...] = cot_in_ref[...]
    planes[pl.ds(jnp.where(even, 1, 12), 3)] = outer_ref[:3]
    cot_planes[jnp.where(even, 0, 9)] = outer_ref[3]
    bias_one = jnp.broadcast_to(b1_ref[...], (8, channels)).T[:, :1]
    bias_two = jnp.broadcast_to(b2_ref[...], (8, channels)).T[:, :1]
    x_ref[...] = planes[3:13]

    ones = jnp.ones((KDIM - 9 * channels, PLANE), BF16)
    for k in range(2):
        xc[k, 9 * channels :, :] = ones
    for k in range(12):
        hc[k, 9 * channels :, :] = ones
    gs[1, 2 * channels :, :] = jnp.zeros((channels, PLANE), BF16)
    gs[10, :channels, :] = jnp.zeros((channels, PLANE), BF16)

    def which_layer(q):
        return 0 if q < 0 else 1 if q < EDGE else 2

    def finish_one(q):
        pre = acc_one[q + 4] + bias_one
        mask = layer_mask[which_layer(q)][:1]
        sigma = jax.nn.sigmoid(pre)
        slope_ref[q + 2] = sigma * (1.0 + pre * (1.0 - sigma)) * mask
        hidden = (pre * sigma * mask).astype(BF16)
        write_taps(hc.at[q + 2], hidden, masks_ref)

    def step_one(p, finish):
        now = (p + 3) & 1
        product = plane_product(w1_ref, xc[now])
        write_taps(xc.at[1 - now], planes[p + 5], masks_ref)
        if finish:
            finish_one(p - 2)
        add_planes(acc_one, p + 4, product, channels)

    write_taps(xc.at[0], planes[1], masks_ref)
    for p in range(-3, 0):
        step_one(p, False)
    for p in range(0, 11):
        step_one(p, True)
    finish_one(9)

    def finish_two(q):
        pre = acc_two[q + 3] + bias_two
        sigma = jax.nn.sigmoid(pre)
        outs[q + 1] = (pre * sigma * layer_mask[which_layer(q)][:1]).astype(BF16)
        grad = cot_planes[q + 1].astype(F32) * (sigma * (1.0 + pre * (1.0 - sigma)))
        g_ref[q + 1] = grad.astype(BF16)
        kept = grad.astype(BF16)
        if not 0 <= q < EDGE:
            kept = jnp.zeros_like(kept)
        gs[q + 1, :channels, :] = kept
        gs[q + 2, channels : 2 * channels, :] = kept
        gs[q + 3, 2 * channels :, :] = kept

    def step_two(p, finish):
        product = plane_product(w2_ref, hc[p + 2])
        if finish:
            finish_two(p - 2)
        add_planes(acc_two, p + 3, product, channels)

    for p in range(-2, 1):
        step_two(p, False)
    for p in range(1, 10):
        step_two(p, True)
    finish_two(8)

    weight_products(total, gs, hc, 1, 1, 5)
    write_tiles(flat, total, channels)
    split_tiles(grad_keep_ref, grad_send_ref, flat, me)

    back = back_ref[...]
    for y in range(2):
        row = slice(y * 128, (y + 1) * 128)
        for j in range(4):
            two = jnp.concatenate([outs[1 + 2 * j, :, row], outs[2 + 2 * j, :, row]], axis=1)
            both = jnp.dot(two, back, preferred_element_type=F32).astype(BF16)
            pair = slice(j * 128, (j + 1) * 128)
            bricks[2 * y, :, pair] = both[:, :128]
            bricks[2 * y + 1, :, pair] = both[:, 128:]
    for target, device in ((keep_ref, me), (send_ref, me ^ 1)):
        for s in range(slots):
            slot = jnp.clip(device * slots + s, 0, near_ref.shape[0] - 1)
            parity, column = slot_place(near_ref, slot, 2 * slots)
            scale = jnp.where(parity == core, 1.0, 0.0)
            target[s] = bricks[column] * jnp.full((channels, CELLS), scale, F32).astype(BF16)


def backward_kernel(
    me_ref, g_ref, slope_ref, x_ref, w2t_ref, masks_ref, grad_keep_ref, grad_send_ref,
    gc, xc, acc, gs, total, flat,
):
    channels = g_ref.shape[1]
    blank = jnp.zeros((channels, PLANE), BF16)
    ones = jnp.ones((KDIM - 9 * channels, PLANE), BF16)
    for k in range(2):
        gc[k, 9 * channels :, :] = ones
    for k in range(10):
        xc[k, 9 * channels :, :] = ones
    for at, a in ((1, 1), (1, 2), (2, 2), (9, 0), (10, 0), (10, 1)):
        gs[at, a * channels : (a + 1) * channels, :] = blank

    def finish(q):
        grad = (acc[q + 2] * slope_ref[q + 2]).astype(BF16)
        gs[q + 1, :channels, :] = grad
        gs[q + 2, channels : 2 * channels, :] = grad
        gs[q + 3, 2 * channels :, :] = grad

    def step(p, done):
        now = (p + 1) & 1
        product = plane_product(w2t_ref, gc[now])
        write_taps(gc.at[1 - now], g_ref[min(p + 2, 9)], masks_ref)
        write_taps(xc.at[p + 1], x_ref[p + 1], masks_ref)
        if done:
            finish(p - 2)
        add_planes(acc, p + 2, product, channels)

    write_taps(gc.at[0], g_ref[0], masks_ref)
    for p in range(-1, 2):
        step(p, False)
    for p in range(2, 9):
        step(p, True)
    finish(7)
    weight_products(total, gs, xc, 1, 0, 5)
    write_tiles(flat, total, channels)
    split_tiles(grad_keep_ref, grad_send_ref, flat, jnp.clip(me_ref[0], 0, 2**15))


def gather_kernel(me_ref, *refs):
    chips = (len(refs) - 5) // 2
    w_one_ref, w_two_ref, b_one_ref, b_two_ref, flat = refs[2 * chips :]
    rows = refs[0].shape[1]
    channels = w_one_ref.shape[0]
    me = jnp.clip(me_ref[0], 0, 2 * chips - 1)
    core, chip = me & 1, me >> 1
    for half in range(2):
        base = jnp.where(core == half, 0, chips * rows)
        for r in range(chips):
            at = base + jnp.clip(chip ^ r, 0, chips - 1) * rows
            flat[:, pl.ds(pl.multiple_of(at, rows), rows), :] = refs[half * chips + r][...]
    for n, (weight, bias) in enumerate(((w_one_ref, b_one_ref), (w_two_ref, b_two_ref))):
        for k in range(TILES - 1):
            tile = flat[n, k * channels : (k + 1) * channels, :]
            weight[:, k * 128 : (k + 1) * 128] = tile.astype(F32)
        last = flat[n, (TILES - 1) * channels : TILES * channels, :].astype(F32)
        weight[:, 2560:2592] = last[:, :32]
        bias[...] = last.T[32:33, :]


VMEM = pl.BlockSpec(memory_space=pltpu.VMEM)
SMEM = pl.BlockSpec(memory_space=pltpu.SMEM)


def vmem(mebibytes):
    return pltpu.CompilerParams(vmem_limit_bytes=mebibytes * 2**20)


def shared_sum(keeps, sends, send_two_done):
    chips = keeps[0].shape[0]
    count = 2 * chips
    volumes = lax.axis_size("dp")
    swap = [(d, d ^ 1) for d in range(count)]
    halves = [keeps[0] + lax.ppermute(sends[0], "space", swap)]
    halves.append(keeps[1] + send_two_done)
    total = jnp.stack([half[0] for half in halves])
    for r in range(chips - 1, 0, -1):
        part = jnp.stack([half[r] for half in halves]).astype(BF16)
        hop = [(d, d ^ (2 * r)) for d in range(count)]
        total = total + lax.ppermute(part, "space", hop).astype(F32)
    total = total.astype(BF16)
    step = 1
    while step < volumes:
        hop = [(d, d ^ step) for d in range(volumes)]
        moved = lax.ppermute(total, "dp", hop)
        total = (total.astype(F32) + moved.astype(F32)).astype(BF16)
        step *= 2
    parts = [total]
    for r in range(chips - 1, 0, -1):
        parts.insert(1, lax.ppermute(total, "space", [(d, d ^ (2 * r)) for d in range(count)]))
    return parts + [lax.ppermute(part, "space", swap) for part in parts]


def local(volume, neighbours, active, cotangent, weight_one, weight_two, bias_one, bias_two):
    volume, cotangent = volume[0], cotangent[0]
    slots, channels = volume.shape[0], volume.shape[1]
    near = neighbours[0]
    count = lax.axis_size("space")
    chips = count // 2
    me = lax.axis_index("space").astype(jnp.int32)[None]

    swap = [(d, d ^ 1) for d in range(count)]
    hop = [(d, d + 1) for d in range(1, count - 1, 2)] + [(d, d - 1) for d in range(2, count, 2)]
    pair_volume = lax.ppermute(volume, "space", swap)
    pair_cot = lax.ppermute(cotangent, "space", swap)

    def by_plane(weight):
        weight = weight.reshape(channels, 3, 9 * channels).transpose(1, 0, 2)
        weight = weight.reshape(3 * channels, 9 * channels)
        return jnp.pad(weight, ((0, 0), (0, KDIM - 9 * channels)))

    w1 = by_plane(weight_one)
    w2 = by_plane(weight_two)
    w2t = weight_two.reshape(channels, 3, 3, 3, channels)[:, ::-1, ::-1, ::-1]
    w2t = w2t.transpose(1, 4, 2, 3, 0).reshape(3 * channels, 9 * channels)
    w2t = jnp.pad(w2t, ((0, 0), (0, KDIM - 9 * channels)))
    move = spread_matrix()
    masks = jnp.asarray(tap_masks(), BF16)

    def planes(number, dtype=BF16):
        return jax.ShapeDtypeStruct((number, channels, PLANE), dtype)

    bricks = (slots, channels, CELLS)
    x_planes, cot_planes, edge, layer_mask = pl.pallas_call(
        layout_kernel,
        out_shape=(planes(16), planes(10), planes(4), jax.ShapeDtypeStruct((3, 8, PLANE), F32)),
        in_specs=[SMEM] * 3 + [VMEM] * 5,
        out_specs=(VMEM,) * 4,
        scratch_shapes=[pltpu.VMEM((2, *bricks), BF16), pltpu.VMEM((2, *bricks), BF16)],
        compiler_params=vmem(8),
        name="layout",
    )(me, near, active[0], volume, pair_volume, cotangent, pair_cot, jnp.asarray(move, BF16))
    outer = lax.ppermute(edge, "space", hop)

    half = (chips, ROWS // count, 128)
    keep, send, keep_two, send_two, grad_out, slope, x_inner = pl.pallas_call(
        forward_kernel,
        out_shape=(
            jax.ShapeDtypeStruct(bricks, BF16),
            jax.ShapeDtypeStruct(bricks, BF16),
            jax.ShapeDtypeStruct(half, F32),
            jax.ShapeDtypeStruct(half, F32),
            planes(10),
            planes(12, F32),
            planes(10),
        ),
        in_specs=[SMEM] * 2 + [VMEM] * 10,
        out_specs=(VMEM,) * 7,
        scratch_shapes=[
            pltpu.VMEM(bricks, BF16),
            pltpu.VMEM((16, channels, PLANE), BF16),
            pltpu.VMEM((10, channels, PLANE), BF16),
            pltpu.VMEM((2, KDIM, PLANE), BF16),
            pltpu.VMEM((12, KDIM, PLANE), BF16),
            pltpu.VMEM((16, channels, PLANE), F32),
            pltpu.VMEM((14, channels, PLANE), F32),
            pltpu.VMEM((10, channels, PLANE), BF16),
            pltpu.VMEM((12, 3 * channels, PLANE), BF16),
            pltpu.VMEM((3 * channels, KDIM), F32),
            pltpu.VMEM((ROWS, 128), F32),
        ],
        compiler_params=vmem(26),
        cost_estimate=pl.CostEstimate(flops=2**33, bytes_accessed=2**23, transcendentals=2**20),
        name="forward",
    )(
        me, near, x_planes, cot_planes, outer, layer_mask, w1, w2, bias_one[None], bias_two[None],
        jnp.asarray(move.T, BF16), masks,
    )
    got_two = lax.ppermute(send_two, "space", swap)
    keep_one, send_one = pl.pallas_call(
        backward_kernel,
        out_shape=(jax.ShapeDtypeStruct(half, F32), jax.ShapeDtypeStruct(half, F32)),
        in_specs=[SMEM] + [VMEM] * 5,
        out_specs=(VMEM,) * 2,
        scratch_shapes=[
            pltpu.VMEM((2, KDIM, PLANE), BF16),
            pltpu.VMEM((10, KDIM, PLANE), BF16),
            pltpu.VMEM((12, channels, PLANE), F32),
            pltpu.VMEM((12, 3 * channels, PLANE), BF16),
            pltpu.VMEM((3 * channels, KDIM), F32),
            pltpu.VMEM((ROWS, 128), F32),
        ],
        compiler_params=vmem(22),
        cost_estimate=pl.CostEstimate(flops=2**32, bytes_accessed=2**22, transcendentals=0),
        name="backward",
    )(me, grad_out, slope, x_inner, w2t, masks)

    output = (keep + lax.ppermute(send, "space", swap))[None]
    parts = shared_sum([keep_one, keep_two], [send_one, send_two], got_two)
    weight_shape = jax.ShapeDtypeStruct((channels, 27 * channels), F32)
    bias_shape = jax.ShapeDtypeStruct((1, channels), F32)
    total_w_one, total_w_two, total_b_one, total_b_two = pl.pallas_call(
        gather_kernel,
        out_shape=(weight_shape, weight_shape, bias_shape, bias_shape),
        in_specs=[SMEM] + [VMEM] * len(parts),
        out_specs=(VMEM,) * 4,
        scratch_shapes=[pltpu.VMEM((2, ROWS, 128), BF16)],
        compiler_params=vmem(8),
        name="gather",
    )(me, *parts)
    return (output, total_w_one, total_w_two, total_b_one[0], total_b_two[0])


def solution(mesh):
    in_specs = (
        P("dp", "space", None, None),
        P("dp", None, None),
        P("dp", None),
        P("dp", "space", None, None),
        P(),
        P(),
        P(),
        P(),
    )
    out_specs = (P("dp", "space", None, None), P(), P(), P(), P())
    return jax.shard_map(local, mesh=mesh, in_specs=in_specs, out_specs=out_specs, check_vma=False)
```

```python
import jax
import jax.numpy as jnp
import numpy as np
from jax import lax
from jax.experimental import pallas as pl
from jax.experimental.pallas import tpu as pltpu
from jax.sharding import PartitionSpec as P

EDGE = 8
PLANE = 256
CELLS = 512
KDIM = 896
TILES = 21
ROWS = 2048
OFFSETS = (4, 10, 12, 21)
DOWN, NEAR_Y, NEAR_Z, UP, LIVE, DEVICE = range(6)
F32 = jnp.float32
BF16 = jnp.bfloat16


def spread_matrix():
    move = np.zeros((256, 256), np.float32)
    for z in range(2):
        for p in range(2):
            for q in range(8):
                for r in range(8):
                    move[z * 128 + p * 64 + q * 8 + r, p * 128 + q * 16 + z * 8 + r] = 1.0
    return move


def tap_masks():
    masks = np.zeros((9, 16, 256), np.float32)
    for b in range(3):
        for c in range(3):
            for q in range(16):
                for r in range(16):
                    inside = 0 <= q + b - 1 < 16 and 0 <= r + c - 1 < 16
                    masks[b * 3 + c, :, q * 16 + r] = float(inside)
    return masks


def write_taps(dst, plane, masks_ref):
    channels = plane.shape[0]
    wide = plane.astype(F32)
    for k in range(9):
        step = (k // 3 - 1) * 16 + (k % 3 - 1)
        if step == 0:
            moved = plane
        else:
            moved = pltpu.roll(wide, (-step) % PLANE, 1).astype(BF16)
            moved = moved * jnp.concatenate([masks_ref[k]] * (channels // 16), axis=0)
        dst[k * channels : (k + 1) * channels, :] = moved


def slot_place(table, slot, pair_slots):
    shift = pair_slots.bit_length() - 1
    up = table[UP, slot]
    inside = jnp.logical_and(up >= 0, up >> shift == slot >> shift)
    parity = jnp.where(inside, 0, 1)
    place = jnp.where(table[NEAR_Y, slot] >= 0, 2, 0) + jnp.where(table[NEAR_Z, slot] >= 0, 1, 0)
    return parity, place


def lane_mask(scalars):
    lane = lax.broadcasted_iota(jnp.int32, (8, PLANE), 1)
    high_y = lane >= 128
    high_z = (lane & 8) != 0
    s = [jnp.full((8, PLANE), v, F32) for v in scalars]
    return jnp.where(high_y, jnp.where(high_z, s[3], s[2]), jnp.where(high_z, s[1], s[0]))


def plane_product(weight_ref, taps):
    blocks, channels = weight_ref.shape[0], weight_ref.shape[1]
    left = weight_ref[...].reshape(blocks * channels, KDIM)
    return jnp.dot(left, taps, preferred_element_type=F32)


def add_planes(acc, at, product, fresh=()):
    channels = acc.shape[1]
    for a in range(3):
        k = at + 1 - a
        if not 0 <= k < acc.shape[0]:
            continue
        part = product[a * channels : (a + 1) * channels]
        acc[k] = part if k in fresh else acc[k] + part


def weight_products(total, grads, taps):
    blank = jnp.zeros((total.shape[0] // 3, PLANE), BF16)

    def left(p):
        inside = [grads(p + 1 - a) if 0 <= p + 1 - a < EDGE else blank for a in range(3)]
        return jnp.concatenate(inside, axis=0)

    for p in range(-1, EDGE + 1, 2):
        both_left = jnp.concatenate([left(p), left(p + 1)], axis=1)
        both_right = jnp.concatenate([taps(p), taps(p + 1)], axis=1)
        part = lax.dot_general(
            both_left, both_right, (((1,), (1,)), ((), ())), preferred_element_type=F32
        )
        total[...] = part if p == -1 else total[...] + part


def write_tiles(flat, total, channels, even):
    lane = lax.broadcasted_iota(jnp.int32, (channels, 128), 1)
    blank = jnp.zeros((channels, 128), F32)
    low = total[pl.ds(pl.multiple_of(jnp.where(even, 0, 2 * channels), channels), channels), :]
    high = total[pl.ds(pl.multiple_of(jnp.where(even, 2 * channels, 0), channels), channels), :]
    second = jnp.concatenate([total[channels : 2 * channels, :], blank], axis=1)
    third = jnp.concatenate([high, blank], axis=1)
    second = pltpu.roll(second, 96, 1)
    third = pltpu.roll(third, 64, 1)

    def cut(value, k):
        return value[:, k * 128 : (k + 1) * 128]

    tiles = [cut(low, k) for k in range(6)]
    tiles.append(jnp.where(lane < 96, cut(low, 6), cut(second, 0)))
    tiles += [cut(second, k) for k in range(1, 7)]
    tiles.append(jnp.where(lane < 64, cut(second, 7), cut(third, 0)))
    tiles += [cut(third, k) for k in range(1, 8)]
    for k in range(TILES):
        flat[k * channels : (k + 1) * channels, :] = tiles[k]
    flat[TILES * channels :, :] = jnp.zeros((ROWS - TILES * channels, 128), F32)


def split_tiles(keep_ref, send_ref, flat, me):
    chips, rows = keep_ref.shape[0], keep_ref.shape[1]
    core, chip = me & 1, me >> 1
    for r in range(chips):
        at = jnp.clip(chip ^ r, 0, chips - 1) * rows
        here = at + jnp.where(core == 1, chips * rows, 0)
        there = at + jnp.where(core == 1, 0, chips * rows)
        keep_ref[r] = flat[pl.ds(pl.multiple_of(here, rows), rows), :]
        send_ref[r] = flat[pl.ds(pl.multiple_of(there, rows), rows), :]


def layout_kernel(
    table, own_ref, pair_ref, cot_own_ref, cot_pair_ref, move_ref,
    x_ref, cot_ref, edge_ref, mask_ref, bricks, cots,
):
    slots, channels = pair_ref.shape[0], pair_ref.shape[1]
    all_slots = table.shape[1]
    me = jnp.clip(table[DEVICE, 0], 0, all_slots // slots - 1)
    core = me & 1
    even = core == 0

    live = [[jnp.float32(0)] * 4 for _ in range(2)]
    beyond = [jnp.float32(0)] * 4
    for device, source, cot_source in (
        (me, own_ref, cot_own_ref), (me ^ 1, pair_ref, cot_pair_ref),
    ):
        for s in range(slots):
            slot = jnp.clip(device * slots + s, 0, all_slots - 1)
            parity, place = slot_place(table, slot, 2 * slots)
            alive = table[LIVE, slot].astype(F32)
            if source is own_ref:
                bricks[parity, place] = source[s]
                cots[parity, place] = cot_source[s]
            else:
                scale = jnp.full((channels, CELLS), alive, F32).astype(BF16)
                bricks[parity, place] = source[s] * scale
                cots[parity, place] = cot_source[s] * scale
            outer = jnp.where(even, table[DOWN, slot], table[UP, slot])
            alive_outer = table[LIVE, jnp.clip(outer, 0, all_slots - 1)].astype(F32)
            alive_outer = jnp.where(outer >= 0, alive_outer, 0.0)
            for k in range(4):
                for p in range(2):
                    here = jnp.logical_and(parity == p, place == k)
                    live[p][k] = jnp.where(here, alive, live[p][k])
                here = jnp.logical_and(parity == core, place == k)
                beyond[k] = jnp.where(here, alive_outer, beyond[k])
    mask_ref[0] = lane_mask(beyond)
    mask_ref[1] = lane_mask([jnp.where(even, live[0][k], live[1][k]) for k in range(4)])
    mask_ref[2] = lane_mask([jnp.where(even, live[1][k], live[0][k]) for k in range(4)])

    move = move_ref[...]
    mine = jnp.where(even, 0, 1)

    def spread(left, right):
        two = jnp.concatenate([left, right], axis=1)
        return jnp.dot(two, move, preferred_element_type=F32).astype(BF16)

    for y in range(2):
        row = slice(y * 128, (y + 1) * 128)
        for j in range(4):
            pair = slice(j * 128, (j + 1) * 128)
            first = jnp.where(even, 2 * j, 7 - 2 * j)
            second = jnp.where(even, 2 * j + 1, 6 - 2 * j)
            both = spread(bricks[mine, 2 * y, :, pair], bricks[mine, 2 * y + 1, :, pair])
            x_ref[first, :, row] = both[:, :128]
            x_ref[second, :, row] = both[:, 128:]
            both = spread(cots[mine, 2 * y, :, pair], cots[mine, 2 * y + 1, :, pair])
            cot_ref[first, :, row] = both[:, :128]
            cot_ref[second, :, row] = both[:, 128:]
        for j in range(2):
            start = pl.multiple_of(jnp.where(even, j * 128, 256 + j * 128), 128)
            pair = pl.ds(start, 128)
            both = spread(
                bricks[1 - mine, 2 * y, :, pair], bricks[1 - mine, 2 * y + 1, :, pair]
            )
            x_ref[jnp.where(even, 8 + 2 * j, 11 - 2 * j), :, row] = both[:, :128]
            x_ref[jnp.where(even, 9 + 2 * j, 10 - 2 * j), :, row] = both[:, 128:]
        pair = pl.ds(pl.multiple_of(jnp.where(even, 0, 384), 128), 128)
        both = spread(cots[1 - mine, 2 * y, :, pair], cots[1 - mine, 2 * y + 1, :, pair])
        side = jnp.full((channels, 128), jnp.where(even, 1.0, 0.0), F32).astype(BF16)
        cot_ref[8, :, row] = both[:, :128] * side + both[:, 128:] * (1 - side)
    edge_ref[:3] = x_ref[:3]
    edge_ref[3] = cot_ref[0]


def tap_weights(out_ref, weight_ref, wide, even):
    channels, width = weight_ref.shape
    wide[:, :width] = weight_ref[...]
    lane = lax.broadcasted_iota(jnp.int32, (channels, 128), 1)
    for a, (tile, moved) in enumerate(((0, 0), (6, 96), (13, 64))):
        span = wide[:, tile * 128 : (tile + 8) * 128].astype(F32)
        if moved:
            span = pltpu.roll(span, 1024 - moved, 1)
        last = jnp.where(lane < 96, span[:, 768:KDIM], 0.0)
        span = jnp.concatenate([span[:, :768], last], axis=1)
        at = a if a == 1 else jnp.where(even, a, 2 - a)
        out_ref[at] = span.astype(BF16)


def back_weights(out_ref, taps_ref):
    channels = taps_ref.shape[1]
    lane = lax.broadcasted_iota(jnp.int32, (channels, 128), 1)
    more = jnp.zeros((128 - channels, KDIM), F32)
    for a in range(3):
        block = jnp.concatenate([taps_ref[2 - a].astype(F32), more], axis=0)
        turned = block.T
        tiles = [jnp.zeros((channels, 128), F32)] * 7
        for k in range(9):
            piece = turned[(8 - k) * channels : (9 - k) * channels, :]
            tile, moved = divmod(k * channels, 128)
            if moved:
                piece = pltpu.roll(piece, moved, 1)
            tiles[tile] = tiles[tile] + jnp.where(lane >= moved, piece, 0.0)
            if moved + channels > 128:
                tiles[tile + 1] = tiles[tile + 1] + jnp.where(lane < moved, piece, 0.0)
        out_ref[a] = jnp.concatenate(tiles, axis=1).astype(BF16)


def column(row):
    return jnp.broadcast_to(row, (8, row.shape[1])).T[:, :1]


def layer_of(q):
    return 0 if q < 0 else 1 if q < EDGE else 2


def hidden_plane(pre, mask):
    sigma = jax.nn.sigmoid(pre)
    return (pre * sigma * mask).astype(BF16), sigma * (1.0 + pre * (1.0 - sigma)) * mask


def out_plane(pre, mask, cot):
    sigma = jax.nn.sigmoid(pre)
    grad = cot.astype(F32) * (sigma * (1.0 + pre * (1.0 - sigma)))
    return (pre * sigma * mask).astype(BF16), grad.astype(BF16)


def inner_kernel(
    table, x_ref, cot_ref, layer_mask, w1_ref, w2_ref, bias_ref, masks_ref,
    taps_ref, one_ref, two_ref, slope_ref, g_ref, out_ref, w1_taps, w2_taps, w2_back,
    wide, xc, acc_one, acc_two,
):
    channels = x_ref.shape[1]
    even = (table[DEVICE, 0] & 1) == 0
    tap_weights(w1_taps, w1_ref, wide, even)
    bias_one, bias_two = column(bias_ref[0:1]), column(bias_ref[1:2])
    ones = jnp.ones((KDIM - 9 * channels, PLANE), BF16)
    for k in range(2):
        xc[k, 9 * channels :, :] = ones
    for k in range(9):
        taps_ref[k, 9 * channels :, :] = ones
    write_taps(xc.at[0], x_ref[0], masks_ref)

    for p in range(15):
        if p <= 10:
            product = plane_product(w1_taps, xc[p & 1])
            if p < 10:
                write_taps(xc.at[1 - (p & 1)], x_ref[p + 1], masks_ref)
            add_planes(acc_one, p + 1, product, fresh=(0, 1, 2) if p == 0 else (p + 2,))
        if p == 1:
            tap_weights(w2_taps, w2_ref, wide, even)
        if p == 3:
            back_weights(w2_back, w2_taps)
        q = p - 2
        if 1 <= q <= 9:
            hidden, slope = hidden_plane(acc_one[q + 1] + bias_one, layer_mask[layer_of(q)][:1])
            write_taps(taps_ref.at[q - 1], hidden, masks_ref)
            if q < EDGE:
                slope_ref[q - 1] = slope
        q = p - 4
        if 1 <= q <= 9:
            product = plane_product(w2_taps, taps_ref[q - 1])
            add_planes(acc_two, q, product, fresh=(0, 1, 2) if q == 1 else (q + 1,))
        q = p - 6
        if 2 <= q <= 8:
            mask = layer_mask[layer_of(q)][:1]
            out, grad = out_plane(acc_two[q] + bias_two, mask, cot_ref[q])
            g_ref[q - 2] = grad
            if q < EDGE:
                out_ref[q - 2] = out
    one_ref[...] = acc_one[:2]
    two_ref[...] = acc_two[:2]


def outer_kernel(
    table, edge_ref, cot_ref, layer_mask, w1_taps, w2_taps, bias_ref, masks_ref,
    taps_ref, one_ref, two_ref, g_in_ref,
    keep_ref, send_ref, slope_ref, g_ref, out_ref,
    xc, hc, acc_one, acc_two, total, flat,
):
    channels = cot_ref.shape[1]
    me = jnp.clip(table[DEVICE, 0], 0, 2**15)
    bias_one, bias_two = column(bias_ref[0:1]), column(bias_ref[1:2])
    ones = jnp.ones((KDIM - 9 * channels, PLANE), BF16)
    for k in range(3):
        xc[k, 9 * channels :, :] = ones
        hc[k, 9 * channels :, :] = ones
        write_taps(xc.at[k], edge_ref[2 - k], masks_ref)
    acc_one[1:] = one_ref[...]
    acc_two[1:] = two_ref[...]
    for p in range(-3, 0):
        add_planes(acc_one, p + 2, plane_product(w1_taps, xc[p + 3]), fresh=(0,) if p == -3 else ())
    for q in range(-2, 1):
        hidden, slope = hidden_plane(acc_one[q + 2] + bias_one, layer_mask[layer_of(q)][:1])
        write_taps(hc.at[q + 2], hidden, masks_ref)
        if q == 0:
            slope_ref[0] = slope
    for q in range(-2, 1):
        add_planes(acc_two, q + 1, plane_product(w2_taps, hc[q + 2]), fresh=(0,) if q == -2 else ())
    for q in range(-1, 2):
        cot = edge_ref[3] if q < 0 else cot_ref[q]
        out, grad = out_plane(acc_two[q + 1] + bias_two, layer_mask[layer_of(q)][:1], cot)
        g_ref[q + 1] = grad
        if q >= 0:
            out_ref[q] = out

    def grads(q):
        return g_ref[q + 1] if q < 2 else g_in_ref[q - 2]

    def taps(q):
        return hc[q + 2] if q < 1 else taps_ref[q - 1]

    weight_products(total, grads, taps)
    write_tiles(flat, total, channels, (me & 1) == 0)
    split_tiles(keep_ref, send_ref, flat, me)


def output_kernel(table, first_ref, second_ref, back_ref, keep_ref, send_ref, outs, bricks):
    slots, channels = keep_ref.shape[0], keep_ref.shape[1]
    me = jnp.clip(table[DEVICE, 0], 0, table.shape[1] // slots - 1)
    core = me & 1
    even = core == 0
    outs[:2] = first_ref[...]
    outs[2:] = second_ref[...]
    back = back_ref[...]
    for y in range(2):
        row = slice(y * 128, (y + 1) * 128)
        for j in range(4):
            first = jnp.where(even, 2 * j, 7 - 2 * j)
            second = jnp.where(even, 2 * j + 1, 6 - 2 * j)
            two = jnp.concatenate([outs[first, :, row], outs[second, :, row]], axis=1)
            both = jnp.dot(two, back, preferred_element_type=F32).astype(BF16)
            pair = slice(j * 128, (j + 1) * 128)
            bricks[2 * y, :, pair] = both[:, :128]
            bricks[2 * y + 1, :, pair] = both[:, 128:]
    for target, device in ((keep_ref, me), (send_ref, me ^ 1)):
        for s in range(slots):
            slot = jnp.clip(device * slots + s, 0, table.shape[1] - 1)
            parity, place = slot_place(table, slot, 2 * slots)
            scale = jnp.where(parity == core, 1.0, 0.0)
            target[s] = bricks[place] * jnp.full((channels, CELLS), scale, F32).astype(BF16)


def backward_kernel(
    table, g_out_ref, g_in_ref, slope_out_ref, slope_in_ref, x_ref, edge_ref, w2_back, masks_ref,
    keep_ref, send_ref, gc, xc, acc, grad, total, flat,
):
    channels = x_ref.shape[1]
    me = jnp.clip(table[DEVICE, 0], 0, 2**15)
    ones = jnp.ones((KDIM - 9 * channels, PLANE), BF16)
    for k in range(2):
        gc[k, 9 * channels :, :] = ones
    for k in range(10):
        xc[k, 9 * channels :, :] = ones

    def g_plane(q):
        return g_out_ref[q + 1] if q < 2 else g_in_ref[q - 2]

    write_taps(gc.at[0], g_plane(-1), masks_ref)
    for p in range(-1, 10):
        if p <= 8:
            now = (p + 1) & 1
            product = plane_product(w2_back, gc[now])
            if p < 8:
                write_taps(gc.at[1 - now], g_plane(p + 1), masks_ref)
            write_taps(xc.at[p + 1], edge_ref[0] if p < 0 else x_ref[p], masks_ref)
            add_planes(acc, p + 2, product, fresh=(0, 1, 2) if p == -1 else (p + 3,))
        q = p - 2
        if 0 <= q < EDGE:
            slope = slope_out_ref[0] if q == 0 else slope_in_ref[q - 1]
            grad[q] = (acc[q + 2] * slope).astype(BF16)
    weight_products(total, lambda q: grad[q], lambda q: xc[q + 1])
    write_tiles(flat, total, channels, (me & 1) == 0)
    split_tiles(keep_ref, send_ref, flat, me)


def gather_kernel(table, *refs):
    chips = (len(refs) - 5) // 2
    w_one_ref, w_two_ref, b_one_ref, b_two_ref, flat = refs[2 * chips :]
    rows = refs[0].shape[1]
    channels = w_one_ref.shape[0]
    me = jnp.clip(table[DEVICE, 0], 0, 2 * chips - 1)
    core, chip = me & 1, me >> 1
    for half in range(2):
        base = jnp.where(core == half, 0, chips * rows)
        for r in range(chips):
            at = base + jnp.clip(chip ^ r, 0, chips - 1) * rows
            flat[:, pl.ds(pl.multiple_of(at, rows), rows), :] = refs[half * chips + r][...]
    for n, (weight, bias) in enumerate(((w_one_ref, b_one_ref), (w_two_ref, b_two_ref))):
        for k in range(TILES - 1):
            tile = flat[n, k * channels : (k + 1) * channels, :]
            weight[:, k * 128 : (k + 1) * 128] = tile.astype(F32)
        last = flat[n, (TILES - 1) * channels : TILES * channels, :].astype(F32)
        weight[:, 2560:2592] = last[:, :32]
        bias[...] = last.T[32:33, :]


VMEM = pl.BlockSpec(memory_space=pltpu.VMEM)
SMEM = pl.BlockSpec(memory_space=pltpu.SMEM)


def vmem(mebibytes):
    return pltpu.CompilerParams(vmem_limit_bytes=mebibytes * 2**20)


def shared_sum(keeps, sends, send_two_done):
    chips = keeps[0].shape[0]
    count = 2 * chips
    volumes = lax.axis_size("dp")
    swap = [(d, d ^ 1) for d in range(count)]
    halves = [keeps[0] + lax.ppermute(sends[0], "space", swap)]
    halves.append(keeps[1] + send_two_done)
    total = jnp.stack([half[0] for half in halves])
    for r in range(chips - 1, 0, -1):
        part = jnp.stack([half[r] for half in halves]).astype(BF16)
        hop = [(d, d ^ (2 * r)) for d in range(count)]
        total = total + lax.ppermute(part, "space", hop).astype(F32)
    total = total.astype(BF16)
    step = 1
    while step < volumes:
        hop = [(d, d ^ step) for d in range(volumes)]
        moved = lax.ppermute(total, "dp", hop)
        total = (total.astype(F32) + moved.astype(F32)).astype(BF16)
        step *= 2
    parts = [total]
    for r in range(chips - 1, 0, -1):
        parts.insert(1, lax.ppermute(total, "space", [(d, d ^ (2 * r)) for d in range(count)]))
    return parts + [lax.ppermute(part, "space", swap) for part in parts]


def local(volume, neighbours, active, cotangent, weight_one, weight_two, bias_one, bias_two):
    volume, cotangent = volume[0], cotangent[0]
    slots, channels = volume.shape[0], volume.shape[1]
    count = lax.axis_size("space")
    chips = count // 2
    me = lax.axis_index("space").astype(jnp.int32)

    swap = [(d, d ^ 1) for d in range(count)]
    hop = [(d, d + 1) for d in range(1, count - 1, 2)] + [(d, d - 1) for d in range(2, count, 2)]
    pair_volume = lax.ppermute(volume, "space", swap)
    pair_cot = lax.ppermute(cotangent, "space", swap)
    move = spread_matrix()
    masks = jnp.asarray(tap_masks(), BF16)
    biases = jnp.stack([bias_one, bias_two])
    near = neighbours[0].T
    table = [near[k : k + 1] for k in OFFSETS]
    table = jnp.concatenate([*table, active, jnp.full_like(active, me)], axis=0)
    alive = lax.dynamic_slice_in_dim(active[0], me * slots, slots, 0)
    alive = alive.astype(BF16)[:, None, None]

    def planes(number, dtype=BF16):
        return jax.ShapeDtypeStruct((number, channels, PLANE), dtype)

    def plane_space(number, dtype=BF16):
        return pltpu.VMEM((number, channels, PLANE), dtype)

    def tap_space(number):
        return pltpu.VMEM((number, KDIM, PLANE), BF16)

    bricks = (slots, channels, CELLS)
    x_planes, cot_planes, edge, layer_mask = pl.pallas_call(
        layout_kernel,
        out_shape=(planes(12), planes(9), planes(4), jax.ShapeDtypeStruct((3, 8, PLANE), F32)),
        in_specs=[SMEM] + [VMEM] * 5,
        out_specs=(VMEM,) * 4,
        scratch_shapes=[
            pltpu.VMEM((2, *bricks), BF16),
            pltpu.VMEM((2, *bricks), BF16),
        ],
        compiler_params=vmem(8),
        name="layout",
    )(table, volume * alive, pair_volume, cotangent * alive, pair_cot, jnp.asarray(move, BF16))
    outer = lax.ppermute(edge, "space", hop)

    weights = jax.ShapeDtypeStruct((3, channels, KDIM), BF16)
    taps, one, two, slope_in, g_in, out_in, w1, w2, w2_back = pl.pallas_call(
        inner_kernel,
        out_shape=(
            jax.ShapeDtypeStruct((9, KDIM, PLANE), BF16),
            planes(2, F32),
            planes(2, F32),
            planes(7, F32),
            planes(7),
            planes(6),
            weights,
            weights,
            weights,
        ),
        in_specs=[SMEM] + [VMEM] * 7,
        out_specs=(VMEM,) * 9,
        scratch_shapes=[
            pltpu.VMEM((channels, 21 * 128), BF16),
            tap_space(2),
            plane_space(13, F32),
            plane_space(11, F32),
        ],
        compiler_params=vmem(20),
        cost_estimate=pl.CostEstimate(flops=2**33, bytes_accessed=2**23, transcendentals=2**20),
        name="inner",
    )(table, x_planes, cot_planes, layer_mask, weight_one, weight_two, biases, masks)

    half = jax.ShapeDtypeStruct((chips, ROWS // count, 128), F32)
    keep_two, send_two, slope_out, g_out, out_out = pl.pallas_call(
        outer_kernel,
        out_shape=(half, half, planes(1, F32), planes(3), planes(2)),
        in_specs=[SMEM] + [VMEM] * 11,
        out_specs=(VMEM,) * 5,
        scratch_shapes=[
            tap_space(3),
            tap_space(3),
            plane_space(3, F32),
            plane_space(3, F32),
            pltpu.VMEM((3 * channels, KDIM), F32),
            pltpu.VMEM((ROWS, 128), F32),
        ],
        compiler_params=vmem(16),
        cost_estimate=pl.CostEstimate(flops=2**32, bytes_accessed=2**23, transcendentals=2**18),
        name="outer",
    )(
        table, outer, cot_planes, layer_mask, w1, w2, biases, masks, taps, one, two, g_in,
    )
    got_two = lax.ppermute(send_two, "space", swap)
    keep_one, send_one = pl.pallas_call(
        backward_kernel,
        out_shape=(half, half),
        in_specs=[SMEM] + [VMEM] * 8,
        out_specs=(VMEM,) * 2,
        scratch_shapes=[
            tap_space(2),
            tap_space(10),
            plane_space(12, F32),
            plane_space(8),
            pltpu.VMEM((3 * channels, KDIM), F32),
            pltpu.VMEM((ROWS, 128), F32),
        ],
        compiler_params=vmem(20),
        cost_estimate=pl.CostEstimate(flops=2**32, bytes_accessed=2**22, transcendentals=0),
        name="backward",
    )(table, g_out, g_in, slope_out, slope_in, x_planes, outer, w2_back, masks)
    keep, send = pl.pallas_call(
        output_kernel,
        out_shape=(jax.ShapeDtypeStruct(bricks, BF16),) * 2,
        in_specs=[SMEM] + [VMEM] * 3,
        out_specs=(VMEM,) * 2,
        scratch_shapes=[plane_space(8), pltpu.VMEM(bricks, BF16)],
        compiler_params=vmem(8),
        cost_estimate=pl.CostEstimate(flops=2**28, bytes_accessed=2**21, transcendentals=0),
        name="output",
    )(table, out_out, out_in, jnp.asarray(move.T, BF16))
    output = (keep + lax.ppermute(send, "space", swap))[None]
    parts = shared_sum([keep_one, keep_two], [send_one, send_two], got_two)
    weight_shape = jax.ShapeDtypeStruct((channels, 27 * channels), F32)
    bias_shape = jax.ShapeDtypeStruct((1, channels), F32)
    total_w_one, total_w_two, total_b_one, total_b_two = pl.pallas_call(
        gather_kernel,
        out_shape=(weight_shape, weight_shape, bias_shape, bias_shape),
        in_specs=[SMEM] + [VMEM] * len(parts),
        out_specs=(VMEM,) * 4,
        scratch_shapes=[pltpu.VMEM((2, ROWS, 128), BF16)],
        compiler_params=vmem(8),
        name="gather",
    )(table, *parts)
    return (output, total_w_one, total_w_two, total_b_one[0], total_b_two[0])


def solution(mesh):
    in_specs = (
        P("dp", "space", None, None),
        P("dp", None, None),
        P("dp", None),
        P("dp", "space", None, None),
        P(),
        P(),
        P(),
        P(),
    )
    out_specs = (P("dp", "space", None, None), P(), P(), P(), P())
    return jax.shard_map(local, mesh=mesh, in_specs=in_specs, out_specs=out_specs, check_vma=False)
```

```python
import jax
import jax.numpy as jnp
from jax import lax
from jax.experimental import pallas as pl
from jax.experimental.pallas import tpu as pltpu
from jax.sharding import PartitionSpec as P

EDGE = 8
PLANE = 256
CELLS = 512
KDIM = 896
TILES = 21
ROWS = 2048
OFFSETS = (4, 10, 12, 21)
DOWN, NEAR_Y, NEAR_Z, UP, LIVE, DEVICE = range(6)
F32 = jnp.float32
BF16 = jnp.bfloat16


def spread_matrix(back=False):
    near = lax.broadcasted_iota(jnp.int32, (256, 256), 1 if back else 0)
    far = lax.broadcasted_iota(jnp.int32, (256, 256), 0 if back else 1)
    source = ((far >> 3) & 1) * 128 + (far >> 7) * 64 + ((far >> 4) & 7) * 8 + (far & 7)
    return jnp.where(near == source, 1.0, 0.0).astype(BF16)


def fill_masks(masks):
    lane = lax.broadcasted_iota(jnp.int32, (16, PLANE), 1)
    for k in range(9):
        q, r = (lane >> 4) + (k // 3 - 1), (lane & 15) + (k % 3 - 1)
        inside = (q >= 0) & (q < 16) & (r >= 0) & (r < 16)
        masks[k] = jnp.where(inside, 1.0, 0.0).astype(BF16)


def write_taps(dst, plane, masks_ref):
    channels = plane.shape[0]
    wide = plane.astype(F32)
    for k in range(9):
        step = (k // 3 - 1) * 16 + (k % 3 - 1)
        if step == 0:
            moved = plane
        else:
            moved = pltpu.roll(wide, (-step) % PLANE, 1).astype(BF16)
            moved = moved * jnp.concatenate([masks_ref[k]] * (channels // 16), axis=0)
        dst[k * channels : (k + 1) * channels, :] = moved


def space_index(table, count):
    return jnp.clip(table[DEVICE, 0] & 255, 0, count - 1)


def slot_place(table, slot, pair_slots):
    shift = pair_slots.bit_length() - 1
    up = table[UP, slot]
    inside = jnp.logical_and(up >= 0, up >> shift == slot >> shift)
    parity = jnp.where(inside, 0, 1)
    place = jnp.where(table[NEAR_Y, slot] >= 0, 2, 0) + jnp.where(table[NEAR_Z, slot] >= 0, 1, 0)
    return parity, place


def lane_mask(scalars):
    lane = lax.broadcasted_iota(jnp.int32, (8, PLANE), 1)
    high_y = lane >= 128
    high_z = (lane & 8) != 0
    s = [jnp.full((8, PLANE), v, F32) for v in scalars]
    return jnp.where(high_y, jnp.where(high_z, s[3], s[2]), jnp.where(high_z, s[1], s[0]))


def plane_product(weight_ref, taps):
    blocks, channels = weight_ref.shape[0], weight_ref.shape[1]
    left = weight_ref[...].reshape(blocks * channels, KDIM)
    return jnp.dot(left, taps, preferred_element_type=F32)


def add_planes(acc, at, product, fresh=()):
    channels = acc.shape[1]
    for a in range(3):
        k = at + 1 - a
        if not 0 <= k < acc.shape[0]:
            continue
        part = product[a * channels : (a + 1) * channels]
        acc[k] = part if k in fresh else acc[k] + part


def weight_products(total, grads, taps):
    blank = jnp.zeros((total.shape[0] // 3, PLANE), BF16)

    def left(p):
        inside = [grads(p + 1 - a) if 0 <= p + 1 - a < EDGE else blank for a in range(3)]
        return jnp.concatenate(inside, axis=0)

    for p in range(-1, EDGE + 1, 2):
        both_left = jnp.concatenate([left(p), left(p + 1)], axis=1)
        both_right = jnp.concatenate([taps(p), taps(p + 1)], axis=1)
        part = lax.dot_general(
            both_left, both_right, (((1,), (1,)), ((), ())), preferred_element_type=F32
        )
        total[...] = part if p == -1 else total[...] + part


def write_tiles(flat, total, channels, even):
    lane = lax.broadcasted_iota(jnp.int32, (channels, 128), 1)
    blank = jnp.zeros((channels, 128), F32)
    low = total[pl.ds(pl.multiple_of(jnp.where(even, 0, 2 * channels), channels), channels), :]
    high = total[pl.ds(pl.multiple_of(jnp.where(even, 2 * channels, 0), channels), channels), :]
    second = jnp.concatenate([total[channels : 2 * channels, :], blank], axis=1)
    third = jnp.concatenate([high, blank], axis=1)
    second = pltpu.roll(second, 96, 1)
    third = pltpu.roll(third, 64, 1)

    def cut(value, k):
        return value[:, k * 128 : (k + 1) * 128]

    tiles = [cut(low, k) for k in range(6)]
    tiles.append(jnp.where(lane < 96, cut(low, 6), cut(second, 0)))
    tiles += [cut(second, k) for k in range(1, 7)]
    tiles.append(jnp.where(lane < 64, cut(second, 7), cut(third, 0)))
    tiles += [cut(third, k) for k in range(1, 8)]
    for k in range(TILES):
        flat[k * channels : (k + 1) * channels, :] = tiles[k]
    flat[TILES * channels :, :] = jnp.zeros((ROWS - TILES * channels, 128), F32)


def chunk_place(table, r, chunks):
    value = table[DEVICE, 0]
    chips = chunks // 2
    at = (((value >> 8) & 1) ^ (r // chips)) * chips + (((value & 255) >> 1) ^ (r % chips))
    return jnp.clip(at, 0, chunks - 1)


def split_tiles(keep_ref, send_ref, flat, table):
    chunks, rows = keep_ref.shape[0], keep_ref.shape[1]
    even = (table[DEVICE, 0] & 1) == 0
    for r in range(chunks):
        at = chunk_place(table, r, chunks) * rows
        here = at + jnp.where(even, 0, chunks * rows)
        there = at + jnp.where(even, chunks * rows, 0)
        keep_ref[r] = flat[pl.ds(pl.multiple_of(here, rows), rows), :]
        send_ref[r] = flat[pl.ds(pl.multiple_of(there, rows), rows), :].astype(BF16)


def layout_kernel(
    table, own_ref, pair_ref, cot_pair_ref,
    x_ref, cot_ref, edge_ref, mask_ref, bricks, cots,
):
    slots, channels = pair_ref.shape[0], pair_ref.shape[1]
    all_slots = table.shape[1]
    me = space_index(table, all_slots // slots)
    core = me & 1
    even = core == 0

    live = [[jnp.float32(0)] * 4 for _ in range(2)]
    beyond = [jnp.float32(0)] * 4
    for device in (me, me ^ 1):
        for s in range(slots):
            slot = jnp.clip(device * slots + s, 0, all_slots - 1)
            parity, place = slot_place(table, slot, 2 * slots)
            alive = table[LIVE, slot].astype(F32)
            scale = jnp.full((channels, CELLS), alive, F32).astype(BF16)
            own = device is me
            bricks[parity, place] = (own_ref[s] if own else pair_ref[s]) * scale
            cots[parity, place] = (own_ref[slots + s] if own else cot_pair_ref[s]) * scale
            outer = jnp.where(even, table[DOWN, slot], table[UP, slot])
            alive_outer = table[LIVE, jnp.clip(outer, 0, all_slots - 1)].astype(F32)
            alive_outer = jnp.where(outer >= 0, alive_outer, 0.0)
            for k in range(4):
                for p in range(2):
                    here = jnp.logical_and(parity == p, place == k)
                    live[p][k] = jnp.where(here, alive, live[p][k])
                here = jnp.logical_and(parity == core, place == k)
                beyond[k] = jnp.where(here, alive_outer, beyond[k])
    mask_ref[0] = lane_mask(beyond)
    mask_ref[1] = lane_mask([jnp.where(even, live[0][k], live[1][k]) for k in range(4)])
    mask_ref[2] = lane_mask([jnp.where(even, live[1][k], live[0][k]) for k in range(4)])

    move = spread_matrix()
    mine = jnp.where(even, 0, 1)

    def spread(left, right):
        two = jnp.concatenate([left, right], axis=1)
        return jnp.dot(two, move, preferred_element_type=F32).astype(BF16)

    for y in range(2):
        row = slice(y * 128, (y + 1) * 128)
        for j in range(4):
            pair = slice(j * 128, (j + 1) * 128)
            first = jnp.where(even, 2 * j, 7 - 2 * j)
            second = jnp.where(even, 2 * j + 1, 6 - 2 * j)
            both = spread(bricks[mine, 2 * y, :, pair], bricks[mine, 2 * y + 1, :, pair])
            x_ref[first, :, row] = both[:, :128]
            x_ref[second, :, row] = both[:, 128:]
            both = spread(cots[mine, 2 * y, :, pair], cots[mine, 2 * y + 1, :, pair])
            cot_ref[first, :, row] = both[:, :128]
            cot_ref[second, :, row] = both[:, 128:]
        for j in range(2):
            start = pl.multiple_of(jnp.where(even, j * 128, 256 + j * 128), 128)
            pair = pl.ds(start, 128)
            both = spread(
                bricks[1 - mine, 2 * y, :, pair], bricks[1 - mine, 2 * y + 1, :, pair]
            )
            x_ref[jnp.where(even, 8 + 2 * j, 11 - 2 * j), :, row] = both[:, :128]
            x_ref[jnp.where(even, 9 + 2 * j, 10 - 2 * j), :, row] = both[:, 128:]
        pair = pl.ds(pl.multiple_of(jnp.where(even, 0, 384), 128), 128)
        both = spread(cots[1 - mine, 2 * y, :, pair], cots[1 - mine, 2 * y + 1, :, pair])
        side = jnp.full((channels, 128), jnp.where(even, 1.0, 0.0), F32).astype(BF16)
        cot_ref[8, :, row] = both[:, :128] * side + both[:, 128:] * (1 - side)
    edge_ref[:3] = x_ref[:3]
    edge_ref[3] = cot_ref[0]


def tap_weights(out_ref, weight, wide, even):
    channels, width = weight.shape
    wide[:, :width] = weight
    lane = lax.broadcasted_iota(jnp.int32, (channels, 128), 1)
    for a, (tile, moved) in enumerate(((0, 0), (6, 96), (13, 64))):
        span = wide[:, tile * 128 : (tile + 8) * 128].astype(F32)
        if moved:
            span = pltpu.roll(span, 1024 - moved, 1)
        last = jnp.where(lane < 96, span[:, 768:KDIM], 0.0)
        span = jnp.concatenate([span[:, :768], last], axis=1)
        at = a if a == 1 else jnp.where(even, a, 2 - a)
        out_ref[at] = span.astype(BF16)


def back_weights(out_ref, taps_ref):
    channels = taps_ref.shape[1]
    lane = lax.broadcasted_iota(jnp.int32, (channels, 128), 1)
    more = jnp.zeros((128 - channels, KDIM), F32)
    for a in range(3):
        block = jnp.concatenate([taps_ref[2 - a].astype(F32), more], axis=0)
        turned = block.T
        tiles = [jnp.zeros((channels, 128), F32)] * 7
        for k in range(9):
            piece = turned[(8 - k) * channels : (9 - k) * channels, :]
            tile, moved = divmod(k * channels, 128)
            if moved:
                piece = pltpu.roll(piece, moved, 1)
            tiles[tile] = tiles[tile] + jnp.where(lane >= moved, piece, 0.0)
            if moved + channels > 128:
                tiles[tile + 1] = tiles[tile + 1] + jnp.where(lane < moved, piece, 0.0)
        out_ref[a] = jnp.concatenate(tiles, axis=1).astype(BF16)


def column(row):
    return jnp.broadcast_to(row, (8, row.shape[1])).T[:, :1]


def layer_of(q):
    return 0 if q < 0 else 1 if q < EDGE else 2


def hidden_plane(pre, mask):
    sigma = jax.nn.sigmoid(pre)
    return (pre * sigma * mask).astype(BF16), sigma * (1.0 + pre * (1.0 - sigma)) * mask


def out_plane(pre, mask, cot):
    sigma = jax.nn.sigmoid(pre)
    grad = cot.astype(F32) * (sigma * (1.0 + pre * (1.0 - sigma)))
    return (pre * sigma * mask).astype(BF16), grad.astype(BF16)


def inner_kernel(
    table, x_ref, cot_ref, layer_mask, weight_ref, bias_ref,
    taps_ref, one_ref, two_ref, slope_ref, g_ref, out_ref, w1_taps, w2_taps, w2_back,
    wide, xc, acc_one, acc_two, masks_ref,
):
    channels = x_ref.shape[1]
    even = (table[DEVICE, 0] & 1) == 0
    fill_masks(masks_ref)
    tap_weights(w1_taps, weight_ref[:channels, :], wide, even)
    bias_one, bias_two = column(bias_ref[0:1]), column(bias_ref[1:2])
    ones = jnp.ones((KDIM - 9 * channels, PLANE), BF16)
    for k in range(2):
        xc[k, 9 * channels :, :] = ones
    for k in range(9):
        taps_ref[k, 9 * channels :, :] = ones
    write_taps(xc.at[0], x_ref[0], masks_ref)

    for p in range(15):
        if p <= 10:
            product = plane_product(w1_taps, xc[p & 1])
            if p < 10:
                write_taps(xc.at[1 - (p & 1)], x_ref[p + 1], masks_ref)
            add_planes(acc_one, p + 1, product, fresh=(0, 1, 2) if p == 0 else (p + 2,))
        if p == 1:
            tap_weights(w2_taps, weight_ref[channels:, :], wide, even)
        if p == 3:
            back_weights(w2_back, w2_taps)
        q = p - 2
        if 1 <= q <= 9:
            hidden, slope = hidden_plane(acc_one[q + 1] + bias_one, layer_mask[layer_of(q)][:1])
            write_taps(taps_ref.at[q - 1], hidden, masks_ref)
            if q < EDGE:
                slope_ref[q - 1] = slope
        q = p - 4
        if 1 <= q <= 9:
            product = plane_product(w2_taps, taps_ref[q - 1])
            add_planes(acc_two, q, product, fresh=(0, 1, 2) if q == 1 else (q + 1,))
        q = p - 6
        if 2 <= q <= 8:
            mask = layer_mask[layer_of(q)][:1]
            out, grad = out_plane(acc_two[q] + bias_two, mask, cot_ref[q])
            g_ref[q - 2] = grad
            if q < EDGE:
                out_ref[q - 2] = out
    one_ref[...] = acc_one[:2]
    two_ref[...] = acc_two[:2]


def outer_kernel(
    table, edge_ref, cot_ref, layer_mask, w1_taps, w2_taps, bias_ref,
    taps_ref, one_ref, two_ref, g_in_ref,
    keep_ref, send_ref, slope_ref, g_ref, out_ref,
    xc, hc, acc_one, acc_two, total, flat, masks_ref,
):
    channels = cot_ref.shape[1]
    even = (table[DEVICE, 0] & 1) == 0
    fill_masks(masks_ref)
    bias_one, bias_two = column(bias_ref[0:1]), column(bias_ref[1:2])
    ones = jnp.ones((KDIM - 9 * channels, PLANE), BF16)
    for k in range(3):
        xc[k, 9 * channels :, :] = ones
        hc[k, 9 * channels :, :] = ones
        write_taps(xc.at[k], edge_ref[2 - k], masks_ref)
    acc_one[1:] = one_ref[...]
    acc_two[1:] = two_ref[...]
    for p in range(-3, 0):
        add_planes(acc_one, p + 2, plane_product(w1_taps, xc[p + 3]), fresh=(0,) if p == -3 else ())
    for q in range(-2, 1):
        hidden, slope = hidden_plane(acc_one[q + 2] + bias_one, layer_mask[layer_of(q)][:1])
        write_taps(hc.at[q + 2], hidden, masks_ref)
        if q == 0:
            slope_ref[0] = slope
    for q in range(-2, 1):
        add_planes(acc_two, q + 1, plane_product(w2_taps, hc[q + 2]), fresh=(0,) if q == -2 else ())
    for q in range(-1, 2):
        cot = edge_ref[3] if q < 0 else cot_ref[q]
        out, grad = out_plane(acc_two[q + 1] + bias_two, layer_mask[layer_of(q)][:1], cot)
        g_ref[q + 1] = grad
        if q >= 0:
            out_ref[q] = out

    def grads(q):
        return g_ref[q + 1] if q < 2 else g_in_ref[q - 2]

    def taps(q):
        return hc[q + 2] if q < 1 else taps_ref[q - 1]

    weight_products(total, grads, taps)
    write_tiles(flat, total, channels, even)
    split_tiles(keep_ref, send_ref, flat, table)


def output_kernel(table, first_ref, second_ref, keep_ref, send_ref, outs, bricks):
    slots, channels = keep_ref.shape[0], keep_ref.shape[1]
    me = space_index(table, table.shape[1] // slots)
    core = me & 1
    even = core == 0
    outs[:2] = first_ref[...]
    outs[2:] = second_ref[...]
    back = spread_matrix(True)
    for y in range(2):
        row = slice(y * 128, (y + 1) * 128)
        for j in range(4):
            first = jnp.where(even, 2 * j, 7 - 2 * j)
            second = jnp.where(even, 2 * j + 1, 6 - 2 * j)
            two = jnp.concatenate([outs[first, :, row], outs[second, :, row]], axis=1)
            both = jnp.dot(two, back, preferred_element_type=F32).astype(BF16)
            pair = slice(j * 128, (j + 1) * 128)
            bricks[2 * y, :, pair] = both[:, :128]
            bricks[2 * y + 1, :, pair] = both[:, 128:]
    for target, device in ((keep_ref, me), (send_ref, me ^ 1)):
        for s in range(slots):
            slot = jnp.clip(device * slots + s, 0, table.shape[1] - 1)
            parity, place = slot_place(table, slot, 2 * slots)
            scale = jnp.where(parity == core, 1.0, 0.0)
            target[s] = bricks[place] * jnp.full((channels, CELLS), scale, F32).astype(BF16)


def backward_kernel(
    table, g_out_ref, g_in_ref, slope_out_ref, slope_in_ref, x_ref, edge_ref, w2_back,
    keep_ref, send_ref, gc, xc, acc, grad, total, flat, masks_ref,
):
    channels = x_ref.shape[1]
    even = (table[DEVICE, 0] & 1) == 0
    fill_masks(masks_ref)
    ones = jnp.ones((KDIM - 9 * channels, PLANE), BF16)
    for k in range(2):
        gc[k, 9 * channels :, :] = ones
    for k in range(10):
        xc[k, 9 * channels :, :] = ones

    def g_plane(q):
        return g_out_ref[q + 1] if q < 2 else g_in_ref[q - 2]

    write_taps(gc.at[0], g_plane(-1), masks_ref)
    for p in range(-1, 10):
        if p <= 8:
            now = (p + 1) & 1
            product = plane_product(w2_back, gc[now])
            if p < 8:
                write_taps(gc.at[1 - now], g_plane(p + 1), masks_ref)
            write_taps(xc.at[p + 1], edge_ref[0] if p < 0 else x_ref[p], masks_ref)
            add_planes(acc, p + 2, product, fresh=(0, 1, 2) if p == -1 else (p + 3,))
        q = p - 2
        if 0 <= q < EDGE:
            slope = slope_out_ref[0] if q == 0 else slope_in_ref[q - 1]
            grad[q] = (acc[q + 2] * slope).astype(BF16)
    weight_products(total, lambda q: grad[q], lambda q: xc[q + 1])
    write_tiles(flat, total, channels, even)
    split_tiles(keep_ref, send_ref, flat, table)


def gather_kernel(table, *refs):
    chunks = (len(refs) - 5) // 2
    w_one_ref, w_two_ref, b_one_ref, b_two_ref, flat = refs[2 * chunks :]
    rows = refs[0].shape[1]
    channels = w_one_ref.shape[0]
    core = table[DEVICE, 0] & 1
    for half in range(2):
        base = jnp.where(core == half, 0, chunks * rows)
        for r in range(chunks):
            at = base + chunk_place(table, r, chunks) * rows
            flat[:, pl.ds(pl.multiple_of(at, rows), rows), :] = refs[half * chunks + r][...]
    for n, (weight, bias) in enumerate(((w_one_ref, b_one_ref), (w_two_ref, b_two_ref))):
        for k in range(TILES - 1):
            tile = flat[n, k * channels : (k + 1) * channels, :]
            weight[:, k * 128 : (k + 1) * 128] = tile.astype(F32)
        last = flat[n, (TILES - 1) * channels : TILES * channels, :].astype(F32)
        weight[:, 2560:2592] = last[:, :32]
        bias[...] = last.T[32:33, :]


VMEM = pl.BlockSpec(memory_space=pltpu.VMEM)
SMEM = pl.BlockSpec(memory_space=pltpu.SMEM)


def vmem(mebibytes):
    return pltpu.CompilerParams(vmem_limit_bytes=mebibytes * 2**20)


def shared_sum(keeps, sends):
    chunks = keeps[0].shape[0]
    chips = chunks // 2
    count = lax.axis_size("space")
    volumes = lax.axis_size("dp")
    swap = [(d, d ^ 1) for d in range(count)]

    def hop(r):
        space, volume = 2 * (r % chips), r // chips
        return [
            (d * volumes + v, (d ^ space) * volumes + (v ^ volume))
            for d in range(count)
            for v in range(volumes)
        ]

    order = sorted(range(1, chunks), key=lambda r: -bin(r).count("1"))
    halves = [
        keep + lax.ppermute(send, "space", swap).astype(F32) for keep, send in zip(keeps, sends)
    ]
    total = jnp.stack([half[0] for half in halves])
    for r in order:
        part = jnp.stack([half[r] for half in halves]).astype(BF16)
        total = total + lax.ppermute(part, ("space", "dp"), hop(r)).astype(F32)
    total = total.astype(BF16)
    step = 2
    while step < volumes:
        moved = lax.ppermute(total, "dp", [(v, v ^ step) for v in range(volumes)])
        total = (total.astype(F32) + moved.astype(F32)).astype(BF16)
        step *= 2
    parts = {0: total}
    for r in order:
        parts[r] = lax.ppermute(total, ("space", "dp"), hop(r))
    parts = [parts[r] for r in range(chunks)]
    return parts + [lax.ppermute(part, "space", swap) for part in parts]


def local(volume, neighbours, active, cotangent, weight_one, weight_two, bias_one, bias_two):
    volume, cotangent = volume[0], cotangent[0]
    slots, channels = volume.shape[0], volume.shape[1]
    count = lax.axis_size("space")
    chips = count // 2
    me = lax.axis_index("space").astype(jnp.int32)

    swap = [(d, d ^ 1) for d in range(count)]
    hop = [(d, d + 1) for d in range(1, count - 1, 2)] + [(d, d - 1) for d in range(2, count, 2)]
    pair_volume = lax.ppermute(volume, "space", swap)
    pair_cot = lax.ppermute(cotangent, "space", swap)
    biases = jnp.stack([bias_one, bias_two])
    weights = jnp.concatenate([weight_one, weight_two], axis=0)
    own = jnp.concatenate([volume, cotangent], axis=0)
    device = me + 256 * lax.axis_index("dp").astype(jnp.int32)
    table = [neighbours[:, :, k] for k in OFFSETS]
    table = jnp.concatenate([*table, active, jnp.full_like(active, device)], axis=0)

    def planes(number, dtype=BF16):
        return jax.ShapeDtypeStruct((number, channels, PLANE), dtype)

    def plane_space(number, dtype=BF16):
        return pltpu.VMEM((number, channels, PLANE), dtype)

    def tap_space(number):
        return pltpu.VMEM((number, KDIM, PLANE), BF16)

    bricks = (slots, channels, CELLS)
    x_planes, cot_planes, edge, layer_mask = pl.pallas_call(
        layout_kernel,
        out_shape=(planes(12), planes(9), planes(4), jax.ShapeDtypeStruct((3, 8, PLANE), F32)),
        in_specs=[SMEM] + [VMEM] * 3,
        out_specs=(VMEM,) * 4,
        scratch_shapes=[
            pltpu.VMEM((2, *bricks), BF16),
            pltpu.VMEM((2, *bricks), BF16),
        ],
        compiler_params=vmem(8),
        name="layout",
    )(table, own, pair_volume, pair_cot)
    outer = lax.ppermute(edge, "space", hop)

    rearranged = jax.ShapeDtypeStruct((3, channels, KDIM), BF16)
    taps, one, two, slope_in, g_in, out_in, w1, w2, w2_back = pl.pallas_call(
        inner_kernel,
        out_shape=(
            jax.ShapeDtypeStruct((9, KDIM, PLANE), BF16),
            planes(2, F32),
            planes(2, F32),
            planes(7, F32),
            planes(7),
            planes(6),
            rearranged,
            rearranged,
            rearranged,
        ),
        in_specs=[SMEM] + [VMEM] * 5,
        out_specs=(VMEM,) * 9,
        scratch_shapes=[
            pltpu.VMEM((channels, 21 * 128), BF16),
            tap_space(2),
            plane_space(13, F32),
            plane_space(11, F32),
            pltpu.VMEM((9, 16, PLANE), BF16),
        ],
        compiler_params=vmem(20),
        cost_estimate=pl.CostEstimate(flops=2**33, bytes_accessed=2**23, transcendentals=2**20),
        name="inner",
    )(table, x_planes, cot_planes, layer_mask, weights, biases)

    chunks = (2 * chips, ROWS // (4 * chips), 128)
    kept, sent = jax.ShapeDtypeStruct(chunks, F32), jax.ShapeDtypeStruct(chunks, BF16)
    keep_two, send_two, slope_out, g_out, out_out = pl.pallas_call(
        outer_kernel,
        out_shape=(kept, sent, planes(1, F32), planes(3), planes(2)),
        in_specs=[SMEM] + [VMEM] * 10,
        out_specs=(VMEM,) * 5,
        scratch_shapes=[
            tap_space(3),
            tap_space(3),
            plane_space(3, F32),
            plane_space(3, F32),
            pltpu.VMEM((3 * channels, KDIM), F32),
            pltpu.VMEM((ROWS, 128), F32),
            pltpu.VMEM((9, 16, PLANE), BF16),
        ],
        compiler_params=vmem(16),
        cost_estimate=pl.CostEstimate(flops=2**32, bytes_accessed=2**23, transcendentals=2**18),
        name="outer",
    )(
        table, outer, cot_planes, layer_mask, w1, w2, biases, taps, one, two, g_in,
    )
    keep_one, send_one = pl.pallas_call(
        backward_kernel,
        out_shape=(kept, sent),
        in_specs=[SMEM] + [VMEM] * 7,
        out_specs=(VMEM,) * 2,
        scratch_shapes=[
            tap_space(2),
            tap_space(10),
            plane_space(12, F32),
            plane_space(8),
            pltpu.VMEM((3 * channels, KDIM), F32),
            pltpu.VMEM((ROWS, 128), F32),
            pltpu.VMEM((9, 16, PLANE), BF16),
        ],
        compiler_params=vmem(20),
        cost_estimate=pl.CostEstimate(flops=2**32, bytes_accessed=2**22, transcendentals=0),
        name="backward",
    )(table, g_out, g_in, slope_out, slope_in, x_planes, outer, w2_back)
    keep, send = pl.pallas_call(
        output_kernel,
        out_shape=(jax.ShapeDtypeStruct(bricks, BF16),) * 2,
        in_specs=[SMEM] + [VMEM] * 2,
        out_specs=(VMEM,) * 2,
        scratch_shapes=[plane_space(8), pltpu.VMEM(bricks, BF16)],
        compiler_params=vmem(8),
        cost_estimate=pl.CostEstimate(flops=2**28, bytes_accessed=2**21, transcendentals=0),
        name="output",
    )(table, out_out, out_in)
    output = (keep + lax.ppermute(send, "space", swap))[None]
    parts = shared_sum([keep_one, keep_two], [send_one, send_two])
    weight_shape = jax.ShapeDtypeStruct((channels, 27 * channels), F32)
    bias_shape = jax.ShapeDtypeStruct((1, channels), F32)
    total_w_one, total_w_two, total_b_one, total_b_two = pl.pallas_call(
        gather_kernel,
        out_shape=(weight_shape, weight_shape, bias_shape, bias_shape),
        in_specs=[SMEM] + [VMEM] * len(parts),
        out_specs=(VMEM,) * 4,
        scratch_shapes=[pltpu.VMEM((2, ROWS, 128), BF16)],
        compiler_params=vmem(8),
        name="gather",
    )(table, *parts)
    return (output, total_w_one, total_w_two, total_b_one[0], total_b_two[0])


def solution(mesh):
    in_specs = (
        P("dp", "space", None, None),
        P("dp", None, None),
        P("dp", None),
        P("dp", "space", None, None),
        P(),
        P(),
        P(),
        P(),
    )
    out_specs = (P("dp", "space", None, None), P(), P(), P(), P())
    return jax.shard_map(local, mesh=mesh, in_specs=in_specs, out_specs=out_specs, check_vma=False)
```

```python
import jax
import jax.numpy as jnp
from jax import lax
from jax.experimental import pallas as pl
from jax.experimental.pallas import tpu as pltpu
from jax.sharding import PartitionSpec as P

EDGE = 8
PLANE = 256
CELLS = 512
KDIM = 896
TILES = 21
ROWS = 2048
OFFSETS = (4, 10, 12, 21)
DOWN, NEAR_Y, NEAR_Z, UP, LIVE, DEVICE = range(6)
F32 = jnp.float32
BF16 = jnp.bfloat16


def spread_matrix(back=False):
    near = lax.broadcasted_iota(jnp.int32, (256, 256), 1 if back else 0)
    far = lax.broadcasted_iota(jnp.int32, (256, 256), 0 if back else 1)
    source = ((far >> 3) & 1) * 128 + (far >> 7) * 64 + ((far >> 4) & 7) * 8 + (far & 7)
    return jnp.where(near == source, 1.0, 0.0).astype(BF16)


def fill_masks(masks):
    lane = lax.broadcasted_iota(jnp.int32, (16, PLANE), 1)
    for k in range(9):
        q, r = (lane >> 4) + (k // 3 - 1), (lane & 15) + (k % 3 - 1)
        inside = (q >= 0) & (q < 16) & (r >= 0) & (r < 16)
        masks[k] = jnp.where(inside, 1.0, 0.0).astype(BF16)


def write_taps(dst, plane, masks_ref):
    channels = plane.shape[0]
    wide = plane.astype(F32)
    for k in range(9):
        step = (k // 3 - 1) * 16 + (k % 3 - 1)
        if step == 0:
            moved = plane
        else:
            moved = pltpu.roll(wide, (-step) % PLANE, 1).astype(BF16)
            moved = moved * jnp.concatenate([masks_ref[k]] * (channels // 16), axis=0)
        dst[k * channels : (k + 1) * channels, :] = moved


def space_index(table, count):
    return jnp.clip(table[DEVICE, 0] & 255, 0, count - 1)


def slot_place(table, slot, pair_slots):
    shift = pair_slots.bit_length() - 1
    up = table[UP, slot]
    inside = jnp.logical_and(up >= 0, up >> shift == slot >> shift)
    parity = jnp.where(inside, 0, 1)
    place = jnp.where(table[NEAR_Y, slot] >= 0, 2, 0) + jnp.where(table[NEAR_Z, slot] >= 0, 1, 0)
    return parity, place


def lane_mask(scalars):
    lane = lax.broadcasted_iota(jnp.int32, (8, PLANE), 1)
    high_y = lane >= 128
    high_z = (lane & 8) != 0
    s = [jnp.full((8, PLANE), v, F32) for v in scalars]
    return jnp.where(high_y, jnp.where(high_z, s[3], s[2]), jnp.where(high_z, s[1], s[0]))


def plane_product(weight_ref, taps):
    blocks, channels = weight_ref.shape[0], weight_ref.shape[1]
    left = weight_ref[...].reshape(blocks * channels, KDIM)
    return jnp.dot(left, taps, preferred_element_type=F32)


def add_planes(acc, at, product, fresh=()):
    channels = acc.shape[1]
    for a in range(3):
        k = at + 1 - a
        if not 0 <= k < acc.shape[0]:
            continue
        part = product[a * channels : (a + 1) * channels]
        acc[k] = part if k in fresh else acc[k] + part


def weight_products(total, grads, taps):
    blank = jnp.zeros((total.shape[0] // 3, PLANE), BF16)

    def left(p):
        inside = [grads(p + 1 - a) if 0 <= p + 1 - a < EDGE else blank for a in range(3)]
        return jnp.concatenate(inside, axis=0)

    for p in range(-1, EDGE + 1, 2):
        both_left = jnp.concatenate([left(p), left(p + 1)], axis=1)
        both_right = jnp.concatenate([taps(p), taps(p + 1)], axis=1)
        part = lax.dot_general(
            both_left, both_right, (((1,), (1,)), ((), ())), preferred_element_type=F32
        )
        total[...] = part if p == -1 else total[...] + part


def write_tiles(flat, total, channels, even):
    lane = lax.broadcasted_iota(jnp.int32, (channels, 128), 1)
    blank = jnp.zeros((channels, 128), F32)
    low = total[pl.ds(pl.multiple_of(jnp.where(even, 0, 2 * channels), channels), channels), :]
    high = total[pl.ds(pl.multiple_of(jnp.where(even, 2 * channels, 0), channels), channels), :]
    second = jnp.concatenate([total[channels : 2 * channels, :], blank], axis=1)
    third = jnp.concatenate([high, blank], axis=1)
    second = pltpu.roll(second, 96, 1)
    third = pltpu.roll(third, 64, 1)

    def cut(value, k):
        return value[:, k * 128 : (k + 1) * 128]

    tiles = [cut(low, k) for k in range(6)]
    tiles.append(jnp.where(lane < 96, cut(low, 6), cut(second, 0)))
    tiles += [cut(second, k) for k in range(1, 7)]
    tiles.append(jnp.where(lane < 64, cut(second, 7), cut(third, 0)))
    tiles += [cut(third, k) for k in range(1, 8)]
    for k in range(TILES):
        flat[k * channels : (k + 1) * channels, :] = tiles[k]
    flat[TILES * channels :, :] = jnp.zeros((ROWS - TILES * channels, 128), F32)


def split_tiles(keep_ref, send_ref, flat, table):
    rows = keep_ref.shape[0]
    even = (table[DEVICE, 0] & 1) == 0
    here = pl.multiple_of(jnp.where(even, 0, rows), rows)
    there = pl.multiple_of(jnp.where(even, rows, 0), rows)
    keep_ref[...] = flat[pl.ds(here, rows), :]
    send_ref[...] = flat[pl.ds(there, rows), :].astype(BF16)


def layout_kernel(
    table, own_ref, pair_ref, cot_pair_ref,
    x_ref, cot_ref, edge_ref, mask_ref, bricks, cots,
):
    slots, channels = pair_ref.shape[0], pair_ref.shape[1]
    all_slots = table.shape[1]
    me = space_index(table, all_slots // slots)
    core = me & 1
    even = core == 0

    live = [[jnp.float32(0)] * 4 for _ in range(2)]
    beyond = [jnp.float32(0)] * 4
    for device in (me, me ^ 1):
        for s in range(slots):
            slot = jnp.clip(device * slots + s, 0, all_slots - 1)
            parity, place = slot_place(table, slot, 2 * slots)
            alive = table[LIVE, slot].astype(F32)
            scale = jnp.full((channels, CELLS), alive, F32).astype(BF16)
            own = device is me
            bricks[parity, place] = (own_ref[s] if own else pair_ref[s]) * scale
            cots[parity, place] = (own_ref[slots + s] if own else cot_pair_ref[s]) * scale
            outer = jnp.where(even, table[DOWN, slot], table[UP, slot])
            alive_outer = table[LIVE, jnp.clip(outer, 0, all_slots - 1)].astype(F32)
            alive_outer = jnp.where(outer >= 0, alive_outer, 0.0)
            for k in range(4):
                for p in range(2):
                    here = jnp.logical_and(parity == p, place == k)
                    live[p][k] = jnp.where(here, alive, live[p][k])
                here = jnp.logical_and(parity == core, place == k)
                beyond[k] = jnp.where(here, alive_outer, beyond[k])
    mask_ref[0] = lane_mask(beyond)
    mask_ref[1] = lane_mask([jnp.where(even, live[0][k], live[1][k]) for k in range(4)])
    mask_ref[2] = lane_mask([jnp.where(even, live[1][k], live[0][k]) for k in range(4)])

    move = spread_matrix()
    mine = jnp.where(even, 0, 1)

    def spread(left, right):
        two = jnp.concatenate([left, right], axis=1)
        return jnp.dot(two, move, preferred_element_type=F32).astype(BF16)

    for y in range(2):
        row = slice(y * 128, (y + 1) * 128)
        for j in range(4):
            pair = slice(j * 128, (j + 1) * 128)
            first = jnp.where(even, 2 * j, 7 - 2 * j)
            second = jnp.where(even, 2 * j + 1, 6 - 2 * j)
            both = spread(bricks[mine, 2 * y, :, pair], bricks[mine, 2 * y + 1, :, pair])
            x_ref[first, :, row] = both[:, :128]
            x_ref[second, :, row] = both[:, 128:]
            both = spread(cots[mine, 2 * y, :, pair], cots[mine, 2 * y + 1, :, pair])
            cot_ref[first, :, row] = both[:, :128]
            cot_ref[second, :, row] = both[:, 128:]
        for j in range(2):
            start = pl.multiple_of(jnp.where(even, j * 128, 256 + j * 128), 128)
            pair = pl.ds(start, 128)
            both = spread(
                bricks[1 - mine, 2 * y, :, pair], bricks[1 - mine, 2 * y + 1, :, pair]
            )
            x_ref[jnp.where(even, 8 + 2 * j, 11 - 2 * j), :, row] = both[:, :128]
            x_ref[jnp.where(even, 9 + 2 * j, 10 - 2 * j), :, row] = both[:, 128:]
        pair = pl.ds(pl.multiple_of(jnp.where(even, 0, 384), 128), 128)
        both = spread(cots[1 - mine, 2 * y, :, pair], cots[1 - mine, 2 * y + 1, :, pair])
        side = jnp.full((channels, 128), jnp.where(even, 1.0, 0.0), F32).astype(BF16)
        cot_ref[8, :, row] = both[:, :128] * side + both[:, 128:] * (1 - side)
    edge_ref[:3] = x_ref[:3]
    edge_ref[3] = cot_ref[0]


def tap_weights(out_ref, weight, wide, even):
    channels, width = weight.shape
    wide[:, :width] = weight
    lane = lax.broadcasted_iota(jnp.int32, (channels, 128), 1)
    for a, (tile, moved) in enumerate(((0, 0), (6, 96), (13, 64))):
        span = wide[:, tile * 128 : (tile + 8) * 128].astype(F32)
        if moved:
            span = pltpu.roll(span, 1024 - moved, 1)
        last = jnp.where(lane < 96, span[:, 768:KDIM], 0.0)
        span = jnp.concatenate([span[:, :768], last], axis=1)
        at = a if a == 1 else jnp.where(even, a, 2 - a)
        out_ref[at] = span.astype(BF16)


def back_weights(out_ref, taps_ref):
    channels = taps_ref.shape[1]
    lane = lax.broadcasted_iota(jnp.int32, (channels, 128), 1)
    more = jnp.zeros((128 - channels, KDIM), F32)
    for a in range(3):
        block = jnp.concatenate([taps_ref[2 - a].astype(F32), more], axis=0)
        turned = block.T
        tiles = [jnp.zeros((channels, 128), F32)] * 7
        for k in range(9):
            piece = turned[(8 - k) * channels : (9 - k) * channels, :]
            tile, moved = divmod(k * channels, 128)
            if moved:
                piece = pltpu.roll(piece, moved, 1)
            tiles[tile] = tiles[tile] + jnp.where(lane >= moved, piece, 0.0)
            if moved + channels > 128:
                tiles[tile + 1] = tiles[tile + 1] + jnp.where(lane < moved, piece, 0.0)
        out_ref[a] = jnp.concatenate(tiles, axis=1).astype(BF16)


def column(row):
    return jnp.broadcast_to(row, (8, row.shape[1])).T[:, :1]


def layer_of(q):
    return 0 if q < 0 else 1 if q < EDGE else 2


def hidden_plane(pre, mask):
    sigma = jax.nn.sigmoid(pre)
    return (pre * sigma * mask).astype(BF16), sigma * (1.0 + pre * (1.0 - sigma)) * mask


def out_plane(pre, mask, cot):
    sigma = jax.nn.sigmoid(pre)
    grad = cot.astype(F32) * (sigma * (1.0 + pre * (1.0 - sigma)))
    return (pre * sigma * mask).astype(BF16), grad.astype(BF16)


def inner_kernel(
    table, x_ref, cot_ref, layer_mask, weight_ref, bias_ref,
    taps_ref, one_ref, two_ref, slope_ref, g_ref, out_ref, w1_taps, w2_taps, w2_back,
    wide, xc, acc_one, acc_two, masks_ref,
):
    channels = x_ref.shape[1]
    even = (table[DEVICE, 0] & 1) == 0
    fill_masks(masks_ref)
    tap_weights(w1_taps, weight_ref[:channels, :], wide, even)
    bias_one, bias_two = column(bias_ref[0:1]), column(bias_ref[1:2])
    ones = jnp.ones((KDIM - 9 * channels, PLANE), BF16)
    for k in range(2):
        xc[k, 9 * channels :, :] = ones
    for k in range(9):
        taps_ref[k, 9 * channels :, :] = ones
    write_taps(xc.at[0], x_ref[0], masks_ref)

    for p in range(15):
        if p <= 10:
            product = plane_product(w1_taps, xc[p & 1])
            if p < 10:
                write_taps(xc.at[1 - (p & 1)], x_ref[p + 1], masks_ref)
            add_planes(acc_one, p + 1, product, fresh=(0, 1, 2) if p == 0 else (p + 2,))
        if p == 1:
            tap_weights(w2_taps, weight_ref[channels:, :], wide, even)
        if p == 3:
            back_weights(w2_back, w2_taps)
        q = p - 2
        if 1 <= q <= 9:
            hidden, slope = hidden_plane(acc_one[q + 1] + bias_one, layer_mask[layer_of(q)][:1])
            write_taps(taps_ref.at[q - 1], hidden, masks_ref)
            if q < EDGE:
                slope_ref[q - 1] = slope
        q = p - 4
        if 1 <= q <= 9:
            product = plane_product(w2_taps, taps_ref[q - 1])
            add_planes(acc_two, q, product, fresh=(0, 1, 2) if q == 1 else (q + 1,))
        q = p - 6
        if 2 <= q <= 8:
            mask = layer_mask[layer_of(q)][:1]
            out, grad = out_plane(acc_two[q] + bias_two, mask, cot_ref[q])
            g_ref[q - 2] = grad
            if q < EDGE:
                out_ref[q - 2] = out
    one_ref[...] = acc_one[:2]
    two_ref[...] = acc_two[:2]


def outer_kernel(
    table, edge_ref, cot_ref, layer_mask, w1_taps, w2_taps, bias_ref,
    taps_ref, one_ref, two_ref, g_in_ref,
    keep_ref, send_ref, slope_ref, g_ref, out_ref,
    xc, hc, acc_one, acc_two, total, flat, masks_ref,
):
    channels = cot_ref.shape[1]
    even = (table[DEVICE, 0] & 1) == 0
    fill_masks(masks_ref)
    bias_one, bias_two = column(bias_ref[0:1]), column(bias_ref[1:2])
    ones = jnp.ones((KDIM - 9 * channels, PLANE), BF16)
    for k in range(3):
        xc[k, 9 * channels :, :] = ones
        hc[k, 9 * channels :, :] = ones
        write_taps(xc.at[k], edge_ref[2 - k], masks_ref)
    acc_one[1:] = one_ref[...]
    acc_two[1:] = two_ref[...]
    for p in range(-3, 0):
        add_planes(acc_one, p + 2, plane_product(w1_taps, xc[p + 3]), fresh=(0,) if p == -3 else ())
    for q in range(-2, 1):
        hidden, slope = hidden_plane(acc_one[q + 2] + bias_one, layer_mask[layer_of(q)][:1])
        write_taps(hc.at[q + 2], hidden, masks_ref)
        if q == 0:
            slope_ref[0] = slope
    for q in range(-2, 1):
        add_planes(acc_two, q + 1, plane_product(w2_taps, hc[q + 2]), fresh=(0,) if q == -2 else ())
    for q in range(-1, 2):
        cot = edge_ref[3] if q < 0 else cot_ref[q]
        out, grad = out_plane(acc_two[q + 1] + bias_two, layer_mask[layer_of(q)][:1], cot)
        g_ref[q + 1] = grad
        if q >= 0:
            out_ref[q] = out

    def grads(q):
        return g_ref[q + 1] if q < 2 else g_in_ref[q - 2]

    def taps(q):
        return hc[q + 2] if q < 1 else taps_ref[q - 1]

    weight_products(total, grads, taps)
    write_tiles(flat, total, channels, even)
    split_tiles(keep_ref, send_ref, flat, table)


def output_kernel(table, first_ref, second_ref, keep_ref, send_ref, outs, bricks):
    slots, channels = keep_ref.shape[0], keep_ref.shape[1]
    me = space_index(table, table.shape[1] // slots)
    core = me & 1
    even = core == 0
    outs[:2] = first_ref[...]
    outs[2:] = second_ref[...]
    back = spread_matrix(True)
    for y in range(2):
        row = slice(y * 128, (y + 1) * 128)
        for j in range(4):
            first = jnp.where(even, 2 * j, 7 - 2 * j)
            second = jnp.where(even, 2 * j + 1, 6 - 2 * j)
            two = jnp.concatenate([outs[first, :, row], outs[second, :, row]], axis=1)
            both = jnp.dot(two, back, preferred_element_type=F32).astype(BF16)
            pair = slice(j * 128, (j + 1) * 128)
            bricks[2 * y, :, pair] = both[:, :128]
            bricks[2 * y + 1, :, pair] = both[:, 128:]
    for target, device in ((keep_ref, me), (send_ref, me ^ 1)):
        for s in range(slots):
            slot = jnp.clip(device * slots + s, 0, table.shape[1] - 1)
            parity, place = slot_place(table, slot, 2 * slots)
            scale = jnp.where(parity == core, 1.0, 0.0)
            target[s] = bricks[place] * jnp.full((channels, CELLS), scale, F32).astype(BF16)


def backward_kernel(
    table, g_out_ref, g_in_ref, slope_out_ref, slope_in_ref, x_ref, edge_ref, w2_back,
    keep_ref, send_ref, gc, xc, acc, grad, total, flat, masks_ref,
):
    channels = x_ref.shape[1]
    even = (table[DEVICE, 0] & 1) == 0
    fill_masks(masks_ref)
    ones = jnp.ones((KDIM - 9 * channels, PLANE), BF16)
    for k in range(2):
        gc[k, 9 * channels :, :] = ones
    for k in range(10):
        xc[k, 9 * channels :, :] = ones

    def g_plane(q):
        return g_out_ref[q + 1] if q < 2 else g_in_ref[q - 2]

    write_taps(gc.at[0], g_plane(-1), masks_ref)
    for p in range(-1, 10):
        if p <= 8:
            now = (p + 1) & 1
            product = plane_product(w2_back, gc[now])
            if p < 8:
                write_taps(gc.at[1 - now], g_plane(p + 1), masks_ref)
            write_taps(xc.at[p + 1], edge_ref[0] if p < 0 else x_ref[p], masks_ref)
            add_planes(acc, p + 2, product, fresh=(0, 1, 2) if p == -1 else (p + 3,))
        q = p - 2
        if 0 <= q < EDGE:
            slope = slope_out_ref[0] if q == 0 else slope_in_ref[q - 1]
            grad[q] = (acc[q + 2] * slope).astype(BF16)
    weight_products(total, lambda q: grad[q], lambda q: xc[q + 1])
    write_tiles(flat, total, channels, even)
    split_tiles(keep_ref, send_ref, flat, table)


def gather_kernel(
    table, own_ref, other_ref, w_one_ref, w_two_ref, b_one_ref, b_two_ref, flat
):
    chunks, _, rows, _ = own_ref.shape
    channels = w_one_ref.shape[0]
    core = table[DEVICE, 0] & 1
    for half, source in enumerate((own_ref, other_ref)):
        base = jnp.where(core == half, 0, chunks * rows)
        for k in range(chunks):
            at = pl.multiple_of(base + k * rows, rows)
            flat[:, pl.ds(at, rows), :] = source[k]
    for n, (weight, bias) in enumerate(((w_one_ref, b_one_ref), (w_two_ref, b_two_ref))):
        for k in range(TILES - 1):
            tile = flat[n, k * channels : (k + 1) * channels, :]
            weight[:, k * 128 : (k + 1) * 128] = tile.astype(F32)
        last = flat[n, (TILES - 1) * channels : TILES * channels, :].astype(F32)
        weight[:, 2560:2592] = last[:, :32]
        bias[...] = last.T[32:33, :]


VMEM = pl.BlockSpec(memory_space=pltpu.VMEM)
SMEM = pl.BlockSpec(memory_space=pltpu.SMEM)


def vmem(mebibytes):
    return pltpu.CompilerParams(vmem_limit_bytes=mebibytes * 2**20)


def shared_sum(keeps, sends):
    count = lax.axis_size("space")
    volumes = lax.axis_size("dp")
    swap = [(d, d ^ 1) for d in range(count)]
    both = ("space", "dp")
    groups = [
        [(chip * 2 + core) * volumes + first + v for v in range(2) for chip in range(count // 2)]
        for core in range(2)
        for first in range(0, volumes, 2)
    ]
    halves = [
        keep + lax.ppermute(send, "space", swap).astype(F32) for keep, send in zip(keeps, sends)
    ]
    halves = [half.astype(BF16).reshape(count, -1, 128) for half in halves]
    parts = jnp.stack(halves, axis=1)
    parts = lax.all_to_all(parts, both, 0, 0, axis_index_groups=groups)
    total = jnp.sum(parts.astype(F32), axis=0).astype(BF16)
    step = 2
    while step < volumes:
        moved = lax.ppermute(total, "dp", [(v, v ^ step) for v in range(volumes)])
        total = (total.astype(F32) + moved.astype(F32)).astype(BF16)
        step *= 2
    copies = jnp.broadcast_to(total[None], parts.shape)
    copies = lax.all_to_all(copies, both, 0, 0, axis_index_groups=groups)
    return [copies, lax.ppermute(copies, "space", swap)]


def local(volume, neighbours, active, cotangent, weight_one, weight_two, bias_one, bias_two):
    volume, cotangent = volume[0], cotangent[0]
    slots, channels = volume.shape[0], volume.shape[1]
    count = lax.axis_size("space")
    me = lax.axis_index("space").astype(jnp.int32)

    swap = [(d, d ^ 1) for d in range(count)]
    hop = [(d, d + 1) for d in range(1, count - 1, 2)] + [(d, d - 1) for d in range(2, count, 2)]
    pair_volume = lax.ppermute(volume, "space", swap)
    pair_cot = lax.ppermute(cotangent, "space", swap)
    biases = jnp.stack([bias_one, bias_two])
    weights = jnp.concatenate([weight_one, weight_two], axis=0)
    own = jnp.concatenate([volume, cotangent], axis=0)
    device = me + 256 * lax.axis_index("dp").astype(jnp.int32)
    table = [neighbours[:, :, k] for k in OFFSETS]
    table = jnp.concatenate([*table, active, jnp.full_like(active, device)], axis=0)

    def planes(number, dtype=BF16):
        return jax.ShapeDtypeStruct((number, channels, PLANE), dtype)

    def plane_space(number, dtype=BF16):
        return pltpu.VMEM((number, channels, PLANE), dtype)

    def tap_space(number):
        return pltpu.VMEM((number, KDIM, PLANE), BF16)

    bricks = (slots, channels, CELLS)
    x_planes, cot_planes, edge, layer_mask = pl.pallas_call(
        layout_kernel,
        out_shape=(planes(12), planes(9), planes(4), jax.ShapeDtypeStruct((3, 8, PLANE), F32)),
        in_specs=[SMEM] + [VMEM] * 3,
        out_specs=(VMEM,) * 4,
        scratch_shapes=[
            pltpu.VMEM((2, *bricks), BF16),
            pltpu.VMEM((2, *bricks), BF16),
        ],
        compiler_params=vmem(8),
        name="layout",
    )(table, own, pair_volume, pair_cot)
    outer = lax.ppermute(edge, "space", hop)

    rearranged = jax.ShapeDtypeStruct((3, channels, KDIM), BF16)
    taps, one, two, slope_in, g_in, out_in, w1, w2, w2_back = pl.pallas_call(
        inner_kernel,
        out_shape=(
            jax.ShapeDtypeStruct((9, KDIM, PLANE), BF16),
            planes(2, F32),
            planes(2, F32),
            planes(7, F32),
            planes(7),
            planes(6),
            rearranged,
            rearranged,
            rearranged,
        ),
        in_specs=[SMEM] + [VMEM] * 5,
        out_specs=(VMEM,) * 9,
        scratch_shapes=[
            pltpu.VMEM((channels, 21 * 128), BF16),
            tap_space(2),
            plane_space(13, F32),
            plane_space(11, F32),
            pltpu.VMEM((9, 16, PLANE), BF16),
        ],
        compiler_params=vmem(20),
        cost_estimate=pl.CostEstimate(flops=2**33, bytes_accessed=2**23, transcendentals=2**20),
        name="inner",
    )(table, x_planes, cot_planes, layer_mask, weights, biases)

    half = (ROWS // 2, 128)
    kept, sent = jax.ShapeDtypeStruct(half, F32), jax.ShapeDtypeStruct(half, BF16)
    keep_two, send_two, slope_out, g_out, out_out = pl.pallas_call(
        outer_kernel,
        out_shape=(kept, sent, planes(1, F32), planes(3), planes(2)),
        in_specs=[SMEM] + [VMEM] * 10,
        out_specs=(VMEM,) * 5,
        scratch_shapes=[
            tap_space(3),
            tap_space(3),
            plane_space(3, F32),
            plane_space(3, F32),
            pltpu.VMEM((3 * channels, KDIM), F32),
            pltpu.VMEM((ROWS, 128), F32),
            pltpu.VMEM((9, 16, PLANE), BF16),
        ],
        compiler_params=vmem(16),
        cost_estimate=pl.CostEstimate(flops=2**32, bytes_accessed=2**23, transcendentals=2**18),
        name="outer",
    )(
        table, outer, cot_planes, layer_mask, w1, w2, biases, taps, one, two, g_in,
    )
    keep_one, send_one = pl.pallas_call(
        backward_kernel,
        out_shape=(kept, sent),
        in_specs=[SMEM] + [VMEM] * 7,
        out_specs=(VMEM,) * 2,
        scratch_shapes=[
            tap_space(2),
            tap_space(10),
            plane_space(12, F32),
            plane_space(8),
            pltpu.VMEM((3 * channels, KDIM), F32),
            pltpu.VMEM((ROWS, 128), F32),
            pltpu.VMEM((9, 16, PLANE), BF16),
        ],
        compiler_params=vmem(20),
        cost_estimate=pl.CostEstimate(flops=2**32, bytes_accessed=2**22, transcendentals=0),
        name="backward",
    )(table, g_out, g_in, slope_out, slope_in, x_planes, outer, w2_back)
    keep, send = pl.pallas_call(
        output_kernel,
        out_shape=(jax.ShapeDtypeStruct(bricks, BF16),) * 2,
        in_specs=[SMEM] + [VMEM] * 2,
        out_specs=(VMEM,) * 2,
        scratch_shapes=[plane_space(8), pltpu.VMEM(bricks, BF16)],
        compiler_params=vmem(8),
        cost_estimate=pl.CostEstimate(flops=2**28, bytes_accessed=2**21, transcendentals=0),
        name="output",
    )(table, out_out, out_in)
    output = (keep + lax.ppermute(send, "space", swap))[None]
    parts = shared_sum([keep_one, keep_two], [send_one, send_two])
    weight_shape = jax.ShapeDtypeStruct((channels, 27 * channels), F32)
    bias_shape = jax.ShapeDtypeStruct((1, channels), F32)
    total_w_one, total_w_two, total_b_one, total_b_two = pl.pallas_call(
        gather_kernel,
        out_shape=(weight_shape, weight_shape, bias_shape, bias_shape),
        in_specs=[SMEM] + [VMEM] * len(parts),
        out_specs=(VMEM,) * 4,
        scratch_shapes=[pltpu.VMEM((2, ROWS, 128), BF16)],
        compiler_params=vmem(8),
        name="gather",
    )(table, *parts)
    return (output, total_w_one, total_w_two, total_b_one[0], total_b_two[0])


def solution(mesh):
    in_specs = (
        P("dp", "space", None, None),
        P("dp", None, None),
        P("dp", None),
        P("dp", "space", None, None),
        P(),
        P(),
        P(),
        P(),
    )
    out_specs = (P("dp", "space", None, None), P(), P(), P(), P())
    return jax.shard_map(local, mesh=mesh, in_specs=in_specs, out_specs=out_specs, check_vma=False)
```

```python
import jax
import jax.numpy as jnp
from jax import lax
from jax.experimental import pallas as pl
from jax.experimental.pallas import tpu as pltpu
from jax.sharding import PartitionSpec as P

EDGE = 8
PLANE = 256
CELLS = 512
KDIM = 896
TILES = 21
ROWS = 2048
OFFSETS = (4, 10, 12, 21)
DOWN, NEAR_Y, NEAR_Z, UP, LIVE, DEVICE = range(6)
F32 = jnp.float32
BF16 = jnp.bfloat16


def spread_matrix(back=False):
    near = lax.broadcasted_iota(jnp.int32, (256, 256), 1 if back else 0)
    far = lax.broadcasted_iota(jnp.int32, (256, 256), 0 if back else 1)
    source = ((far >> 3) & 1) * 128 + (far >> 7) * 64 + ((far >> 4) & 7) * 8 + (far & 7)
    return jnp.where(near == source, 1.0, 0.0).astype(BF16)


def fill_masks(masks):
    lane = lax.broadcasted_iota(jnp.int32, (16, PLANE), 1)
    for k in range(9):
        q, r = (lane >> 4) + (k // 3 - 1), (lane & 15) + (k % 3 - 1)
        inside = (q >= 0) & (q < 16) & (r >= 0) & (r < 16)
        masks[k] = jnp.where(inside, 1.0, 0.0).astype(BF16)


def write_taps(dst, plane, masks_ref):
    channels = plane.shape[0]
    for k in range(9):
        step = (k // 3 - 1) * 16 + (k % 3 - 1)
        if step == 0:
            moved = plane
        else:
            moved = pltpu.roll(plane, (-step) % PLANE, 1)
            moved = moved * jnp.concatenate([masks_ref[k]] * (channels // 16), axis=0)
        dst[k * channels : (k + 1) * channels, :] = moved


def space_index(table, count):
    return jnp.clip(table[DEVICE, 0] & 255, 0, count - 1)


def slot_place(table, slot, pair_slots):
    shift = pair_slots.bit_length() - 1
    up = table[UP, slot]
    inside = jnp.logical_and(up >= 0, up >> shift == slot >> shift)
    parity = jnp.where(inside, 0, 1)
    place = jnp.where(table[NEAR_Y, slot] >= 0, 2, 0) + jnp.where(table[NEAR_Z, slot] >= 0, 1, 0)
    return parity, place


def lane_mask(scalars):
    lane = lax.broadcasted_iota(jnp.int32, (8, PLANE), 1)
    high_y = lane >= 128
    high_z = (lane & 8) != 0
    s = [jnp.full((8, PLANE), v, F32) for v in scalars]
    return jnp.where(high_y, jnp.where(high_z, s[3], s[2]), jnp.where(high_z, s[1], s[0]))


def plane_product(weight_ref, taps):
    blocks, channels = weight_ref.shape[0], weight_ref.shape[1]
    left = weight_ref[...].reshape(blocks * channels, KDIM)
    return jnp.dot(left, taps, preferred_element_type=F32)


def add_planes(acc, at, product, fresh=()):
    channels = acc.shape[1]
    for a in range(3):
        k = at + 1 - a
        if not 0 <= k < acc.shape[0]:
            continue
        part = product[a * channels : (a + 1) * channels]
        acc[k] = part if k in fresh else acc[k] + part


def weight_products(total, grads, taps):
    blank = jnp.zeros((total.shape[0] // 3, PLANE), BF16)

    def left(p):
        inside = [grads(p + 1 - a) if 0 <= p + 1 - a < EDGE else blank for a in range(3)]
        return jnp.concatenate(inside, axis=0)

    for p in range(-1, EDGE + 1, 2):
        both_left = jnp.concatenate([left(p), left(p + 1)], axis=1)
        both_right = jnp.concatenate([taps(p), taps(p + 1)], axis=1)
        part = lax.dot_general(
            both_left, both_right, (((1,), (1,)), ((), ())), preferred_element_type=F32
        )
        total[...] = part if p == -1 else total[...] + part


def write_tiles(flat, total, channels, even):
    lane = lax.broadcasted_iota(jnp.int32, (channels, 128), 1)
    blank = jnp.zeros((channels, 128), F32)
    low = total[pl.ds(pl.multiple_of(jnp.where(even, 0, 2 * channels), channels), channels), :]
    high = total[pl.ds(pl.multiple_of(jnp.where(even, 2 * channels, 0), channels), channels), :]
    second = jnp.concatenate([total[channels : 2 * channels, :], blank], axis=1)
    third = jnp.concatenate([high, blank], axis=1)
    second = pltpu.roll(second, 96, 1)
    third = pltpu.roll(third, 64, 1)

    def cut(value, k):
        return value[:, k * 128 : (k + 1) * 128]

    tiles = [cut(low, k) for k in range(6)]
    tiles.append(jnp.where(lane < 96, cut(low, 6), cut(second, 0)))
    tiles += [cut(second, k) for k in range(1, 7)]
    tiles.append(jnp.where(lane < 64, cut(second, 7), cut(third, 0)))
    tiles += [cut(third, k) for k in range(1, 8)]
    for k in range(TILES):
        flat[k * channels : (k + 1) * channels, :] = tiles[k]
    flat[TILES * channels :, :] = jnp.zeros((ROWS - TILES * channels, 128), F32)


def split_tiles(keep_ref, send_ref, flat, table):
    rows = keep_ref.shape[0]
    even = (table[DEVICE, 0] & 1) == 0
    here = pl.multiple_of(jnp.where(even, 0, rows), rows)
    there = pl.multiple_of(jnp.where(even, rows, 0), rows)
    keep_ref[...] = flat[pl.ds(here, rows), :]
    send_ref[...] = flat[pl.ds(there, rows), :].astype(BF16)


def layout_kernel(
    table, own_ref, pair_ref, cot_pair_ref,
    x_ref, cot_ref, edge_ref, mask_ref, bricks, cots,
):
    slots, channels = pair_ref.shape[0], pair_ref.shape[1]
    all_slots = table.shape[1]
    me = space_index(table, all_slots // slots)
    layer = table[DEVICE, 0] >> 16
    even = layer == 0

    live = [[jnp.float32(0)] * 4 for _ in range(2)]
    beyond = [jnp.float32(0)] * 4
    for device in (me, me ^ 1):
        for s in range(slots):
            slot = jnp.clip(device * slots + s, 0, all_slots - 1)
            parity, place = slot_place(table, slot, 2 * slots)
            alive = table[LIVE, slot].astype(F32)
            scale = jnp.full((channels, CELLS), alive, F32).astype(BF16)
            own = device is me
            bricks[parity, place] = (own_ref[s] if own else pair_ref[s]) * scale
            cots[parity, place] = (own_ref[slots + s] if own else cot_pair_ref[s]) * scale
            outer = jnp.where(even, table[DOWN, slot], table[UP, slot])
            alive_outer = table[LIVE, jnp.clip(outer, 0, all_slots - 1)].astype(F32)
            alive_outer = jnp.where(outer >= 0, alive_outer, 0.0)
            for k in range(4):
                for p in range(2):
                    here = jnp.logical_and(parity == p, place == k)
                    live[p][k] = jnp.where(here, alive, live[p][k])
                here = jnp.logical_and(parity == layer, place == k)
                beyond[k] = jnp.where(here, alive_outer, beyond[k])
    mask_ref[0] = lane_mask(beyond)
    mask_ref[1] = lane_mask([jnp.where(even, live[0][k], live[1][k]) for k in range(4)])
    mask_ref[2] = lane_mask([jnp.where(even, live[1][k], live[0][k]) for k in range(4)])

    move = spread_matrix()
    mine = jnp.where(even, 0, 1)

    def spread(left, right):
        two = jnp.concatenate([left, right], axis=1)
        return jnp.dot(two, move, preferred_element_type=F32).astype(BF16)

    for y in range(2):
        row = slice(y * 128, (y + 1) * 128)
        for j in range(4):
            pair = slice(j * 128, (j + 1) * 128)
            first = jnp.where(even, 2 * j, 7 - 2 * j)
            second = jnp.where(even, 2 * j + 1, 6 - 2 * j)
            both = spread(bricks[mine, 2 * y, :, pair], bricks[mine, 2 * y + 1, :, pair])
            x_ref[first, :, row] = both[:, :128]
            x_ref[second, :, row] = both[:, 128:]
            both = spread(cots[mine, 2 * y, :, pair], cots[mine, 2 * y + 1, :, pair])
            cot_ref[first, :, row] = both[:, :128]
            cot_ref[second, :, row] = both[:, 128:]
        for j in range(2):
            start = pl.multiple_of(jnp.where(even, j * 128, 256 + j * 128), 128)
            pair = pl.ds(start, 128)
            both = spread(
                bricks[1 - mine, 2 * y, :, pair], bricks[1 - mine, 2 * y + 1, :, pair]
            )
            x_ref[jnp.where(even, 8 + 2 * j, 11 - 2 * j), :, row] = both[:, :128]
            x_ref[jnp.where(even, 9 + 2 * j, 10 - 2 * j), :, row] = both[:, 128:]
        pair = pl.ds(pl.multiple_of(jnp.where(even, 0, 384), 128), 128)
        both = spread(cots[1 - mine, 2 * y, :, pair], cots[1 - mine, 2 * y + 1, :, pair])
        side = jnp.full((channels, 128), jnp.where(even, 1.0, 0.0), F32).astype(BF16)
        cot_ref[8, :, row] = both[:, :128] * side + both[:, 128:] * (1 - side)
    edge_ref[:3] = x_ref[:3]
    edge_ref[3] = cot_ref[0]


def tap_weights(out_ref, weight, wide, even):
    channels, width = weight.shape
    wide[:, :width] = weight
    lane = lax.broadcasted_iota(jnp.int32, (channels, 128), 1)
    for a, (tile, moved) in enumerate(((0, 0), (6, 96), (13, 64))):
        span = wide[:, tile * 128 : (tile + 8) * 128].astype(F32)
        if moved:
            span = pltpu.roll(span, 1024 - moved, 1)
        last = jnp.where(lane < 96, span[:, 768:KDIM], 0.0)
        span = jnp.concatenate([span[:, :768], last], axis=1)
        at = a if a == 1 else jnp.where(even, a, 2 - a)
        out_ref[at] = span.astype(BF16)


def back_weights(out_ref, taps_ref):
    channels = taps_ref.shape[1]
    lane = lax.broadcasted_iota(jnp.int32, (channels, 128), 1)
    more = jnp.zeros((128 - channels, KDIM), F32)
    for a in range(3):
        block = jnp.concatenate([taps_ref[2 - a].astype(F32), more], axis=0)
        turned = block.T
        tiles = [jnp.zeros((channels, 128), F32)] * 7
        for k in range(9):
            piece = turned[(8 - k) * channels : (9 - k) * channels, :]
            tile, moved = divmod(k * channels, 128)
            if moved:
                piece = pltpu.roll(piece, moved, 1)
            tiles[tile] = tiles[tile] + jnp.where(lane >= moved, piece, 0.0)
            if moved + channels > 128:
                tiles[tile + 1] = tiles[tile + 1] + jnp.where(lane < moved, piece, 0.0)
        out_ref[a] = jnp.concatenate(tiles, axis=1).astype(BF16)


def column(row):
    return jnp.broadcast_to(row, (8, row.shape[1])).T[:, :1]


def layer_of(q):
    return 0 if q < 0 else 1 if q < EDGE else 2


def hidden_plane(pre, mask):
    sigma = jax.nn.sigmoid(pre)
    return (pre * sigma * mask).astype(BF16), sigma * (1.0 + pre * (1.0 - sigma)) * mask


def out_plane(pre, mask, cot):
    sigma = jax.nn.sigmoid(pre)
    grad = cot.astype(F32) * (sigma * (1.0 + pre * (1.0 - sigma)))
    return (pre * sigma * mask).astype(BF16), grad.astype(BF16)


def inner_kernel(
    table, x_ref, cot_ref, layer_mask, weight_ref, bias_ref,
    taps_ref, one_ref, two_ref, slope_ref, g_ref, out_ref, w1_taps, w2_taps, w2_back,
    wide, xc, acc_one, acc_two, masks_ref,
):
    channels = x_ref.shape[1]
    even = (table[DEVICE, 0] >> 16) == 0
    fill_masks(masks_ref)
    tap_weights(w1_taps, weight_ref[:channels, :], wide, even)
    bias_one, bias_two = column(bias_ref[0:1]), column(bias_ref[1:2])
    ones = jnp.ones((KDIM - 9 * channels, PLANE), BF16)
    for k in range(2):
        xc[k, 9 * channels :, :] = ones
    for k in range(9):
        taps_ref[k, 9 * channels :, :] = ones
    write_taps(xc.at[0], x_ref[0], masks_ref)

    for p in range(15):
        if p <= 10:
            product = plane_product(w1_taps, xc[p & 1])
            if p < 10:
                write_taps(xc.at[1 - (p & 1)], x_ref[p + 1], masks_ref)
            add_planes(acc_one, p + 1, product, fresh=(0, 1, 2) if p == 0 else (p + 2,))
        if p == 1:
            tap_weights(w2_taps, weight_ref[channels:, :], wide, even)
        if p == 3:
            back_weights(w2_back, w2_taps)
        q = p - 2
        if 1 <= q <= 9:
            hidden, slope = hidden_plane(acc_one[q + 1] + bias_one, layer_mask[layer_of(q)][:1])
            write_taps(taps_ref.at[q - 1], hidden, masks_ref)
            if q < EDGE:
                slope_ref[q - 1] = slope
        q = p - 4
        if 1 <= q <= 9:
            product = plane_product(w2_taps, taps_ref[q - 1])
            add_planes(acc_two, q, product, fresh=(0, 1, 2) if q == 1 else (q + 1,))
        q = p - 6
        if 2 <= q <= 8:
            mask = layer_mask[layer_of(q)][:1]
            out, grad = out_plane(acc_two[q] + bias_two, mask, cot_ref[q])
            g_ref[q - 2] = grad
            if q < EDGE:
                out_ref[q - 2] = out
    one_ref[...] = acc_one[:2]
    two_ref[...] = acc_two[:2]


def outer_kernel(
    table, edge_ref, cot_ref, layer_mask, w1_taps, w2_taps, bias_ref,
    taps_ref, one_ref, two_ref, g_in_ref,
    keep_ref, send_ref, slope_ref, g_ref, out_ref,
    xc, hc, acc_one, acc_two, total, flat, masks_ref,
):
    channels = cot_ref.shape[1]
    even = (table[DEVICE, 0] >> 16) == 0
    fill_masks(masks_ref)
    bias_one, bias_two = column(bias_ref[0:1]), column(bias_ref[1:2])
    ones = jnp.ones((KDIM - 9 * channels, PLANE), BF16)
    for k in range(3):
        xc[k, 9 * channels :, :] = ones
        hc[k, 9 * channels :, :] = ones
        write_taps(xc.at[k], edge_ref[2 - k], masks_ref)
    acc_one[1:] = one_ref[...]
    acc_two[1:] = two_ref[...]
    for p in range(-3, 0):
        add_planes(acc_one, p + 2, plane_product(w1_taps, xc[p + 3]), fresh=(0,) if p == -3 else ())
    for q in range(-2, 1):
        hidden, slope = hidden_plane(acc_one[q + 2] + bias_one, layer_mask[layer_of(q)][:1])
        write_taps(hc.at[q + 2], hidden, masks_ref)
        if q == 0:
            slope_ref[0] = slope
    for q in range(-2, 1):
        add_planes(acc_two, q + 1, plane_product(w2_taps, hc[q + 2]), fresh=(0,) if q == -2 else ())
    for q in range(-1, 2):
        cot = edge_ref[3] if q < 0 else cot_ref[q]
        out, grad = out_plane(acc_two[q + 1] + bias_two, layer_mask[layer_of(q)][:1], cot)
        g_ref[q + 1] = grad
        if q >= 0:
            out_ref[q] = out

    def grads(q):
        return g_ref[q + 1] if q < 2 else g_in_ref[q - 2]

    def taps(q):
        return hc[q + 2] if q < 1 else taps_ref[q - 1]

    weight_products(total, grads, taps)
    write_tiles(flat, total, channels, even)
    split_tiles(keep_ref, send_ref, flat, table)


def output_kernel(table, first_ref, second_ref, keep_ref, send_ref, outs, bricks):
    slots, channels = keep_ref.shape[0], keep_ref.shape[1]
    me = space_index(table, table.shape[1] // slots)
    layer = table[DEVICE, 0] >> 16
    even = layer == 0
    outs[:2] = first_ref[...]
    outs[2:] = second_ref[...]
    back = spread_matrix(True)
    for y in range(2):
        row = slice(y * 128, (y + 1) * 128)
        for j in range(4):
            first = jnp.where(even, 2 * j, 7 - 2 * j)
            second = jnp.where(even, 2 * j + 1, 6 - 2 * j)
            two = jnp.concatenate([outs[first, :, row], outs[second, :, row]], axis=1)
            both = jnp.dot(two, back, preferred_element_type=F32).astype(BF16)
            pair = slice(j * 128, (j + 1) * 128)
            bricks[2 * y, :, pair] = both[:, :128]
            bricks[2 * y + 1, :, pair] = both[:, 128:]
    for target, device in ((keep_ref, me), (send_ref, me ^ 1)):
        for s in range(slots):
            slot = jnp.clip(device * slots + s, 0, table.shape[1] - 1)
            parity, place = slot_place(table, slot, 2 * slots)
            scale = jnp.where(parity == layer, 1.0, 0.0)
            target[s] = bricks[place] * jnp.full((channels, CELLS), scale, F32).astype(BF16)


def backward_kernel(
    table, g_out_ref, g_in_ref, slope_out_ref, slope_in_ref, x_ref, edge_ref, w2_back,
    keep_ref, send_ref, gc, xc, acc, grad, total, flat, masks_ref,
):
    channels = x_ref.shape[1]
    even = (table[DEVICE, 0] >> 16) == 0
    fill_masks(masks_ref)
    ones = jnp.ones((KDIM - 9 * channels, PLANE), BF16)
    for k in range(2):
        gc[k, 9 * channels :, :] = ones
    for k in range(10):
        xc[k, 9 * channels :, :] = ones

    def g_plane(q):
        return g_out_ref[q + 1] if q < 2 else g_in_ref[q - 2]

    write_taps(gc.at[0], g_plane(-1), masks_ref)
    for p in range(-1, 10):
        if p <= 8:
            now = (p + 1) & 1
            product = plane_product(w2_back, gc[now])
            if p < 8:
                write_taps(gc.at[1 - now], g_plane(p + 1), masks_ref)
            write_taps(xc.at[p + 1], edge_ref[0] if p < 0 else x_ref[p], masks_ref)
            add_planes(acc, p + 2, product, fresh=(0, 1, 2) if p == -1 else (p + 3,))
        q = p - 2
        if 0 <= q < EDGE:
            slope = slope_out_ref[0] if q == 0 else slope_in_ref[q - 1]
            grad[q] = (acc[q + 2] * slope).astype(BF16)
    weight_products(total, lambda q: grad[q], lambda q: xc[q + 1])
    write_tiles(flat, total, channels, even)
    split_tiles(keep_ref, send_ref, flat, table)


def copies_kernel(first_ref, second_ref, out_ref):
    total = (first_ref[...].astype(F32) + second_ref[...].astype(F32)).astype(BF16)
    for k in range(out_ref.shape[0]):
        out_ref[k] = total


def gather_kernel(
    table, own_ref, other_ref, w_one_ref, w_two_ref, b_one_ref, b_two_ref, flat, wide, sems
):
    chunks, _, rows, _ = own_ref.shape
    channels = w_one_ref.shape[0]
    core = table[DEVICE, 0] & 1
    for half, source in enumerate((own_ref, other_ref)):
        base = jnp.where(core == half, 0, chunks * rows)
        for k in range(chunks):
            at = pl.multiple_of(base + k * rows, rows)
            flat[:, pl.ds(at, rows), :] = source[k]
    copies = []
    for n, (weight, bias) in enumerate(((w_one_ref, b_one_ref), (w_two_ref, b_two_ref))):
        for k in range(TILES - 1):
            tile = flat[n, k * channels : (k + 1) * channels, :]
            wide[n, :, k * 128 : (k + 1) * 128] = tile.astype(F32)
        last = flat[n, (TILES - 1) * channels : TILES * channels, :].astype(F32)
        wide[n, :, 2560:2592] = last[:, :32]
        copies.append(pltpu.make_async_copy(wide.at[n], weight, sems.at[n]))
        copies[n].start()
        bias[...] = last.T[32:33, :]
    for copy in copies:
        copy.wait()


VMEM = pl.BlockSpec(memory_space=pltpu.VMEM)
SMEM = pl.BlockSpec(memory_space=pltpu.SMEM)
ANY = pl.BlockSpec(memory_space=pl.ANY)


def vmem(mebibytes):
    return pltpu.CompilerParams(vmem_limit_bytes=mebibytes * 2**20)


def shared_sum(keeps, sends):
    count = lax.axis_size("space")
    volumes = lax.axis_size("dp")
    swap = [(d, d ^ 1) for d in range(count)]
    both = ("space", "dp")
    groups = [
        [(chip * 2 + core) * volumes + first + v for v in range(2) for chip in range(count // 2)]
        for core in range(2)
        for first in range(0, volumes, 2)
    ]
    halves = [
        keep + lax.ppermute(send, "space", swap).astype(F32) for keep, send in zip(keeps, sends)
    ]
    halves = [half.astype(BF16).reshape(count, -1, 128) for half in halves]
    parts = jnp.stack(halves, axis=1)
    parts = lax.all_to_all(parts, both, 0, 0, axis_index_groups=groups)
    total = jnp.sum(parts.astype(F32), axis=0).astype(BF16)
    moved, step = jnp.zeros_like(total), 2
    while step < volumes:
        moved = lax.ppermute(total, "dp", [(v, v ^ step) for v in range(volumes)])
        if step * 2 < volumes:
            total = (total.astype(F32) + moved.astype(F32)).astype(BF16)
        step *= 2
    copies = pl.pallas_call(
        copies_kernel,
        out_shape=jax.ShapeDtypeStruct(parts.shape, BF16),
        in_specs=[VMEM] * 2,
        out_specs=VMEM,
        compiler_params=vmem(8),
        name="copies",
    )(total, moved)
    copies = lax.all_to_all(copies, both, 0, 0, axis_index_groups=groups)
    return [copies, lax.ppermute(copies, "space", swap)]


def local(volume, neighbours, active, cotangent, weight_one, weight_two, bias_one, bias_two):
    volume, cotangent = volume[0], cotangent[0]
    slots, channels = volume.shape[0], volume.shape[1]
    count = lax.axis_size("space")
    me = lax.axis_index("space").astype(jnp.int32)

    swap = [(d, d ^ 1) for d in range(count)]
    at = [2 * (n // 2) + (n & 1 ^ n // 2 & 1) for n in range(count)]
    hop = [(at[n], at[n + 1]) for n in range(1, count - 1, 2)]
    hop += [(there, here) for here, there in hop]
    pair_volume = lax.ppermute(volume, "space", swap)
    pair_cot = lax.ppermute(cotangent, "space", swap)
    biases = jnp.stack([bias_one, bias_two])
    weights = jnp.concatenate([weight_one, weight_two], axis=0)
    own = jnp.concatenate([volume, cotangent], axis=0)
    device = me + 256 * lax.axis_index("dp").astype(jnp.int32)
    device = device + 65536 * ((me ^ (me >> 1)) & 1)
    table = [neighbours[:, :, k] for k in OFFSETS]
    table = jnp.concatenate([*table, active, jnp.full_like(active, device)], axis=0)

    def planes(number, dtype=BF16):
        return jax.ShapeDtypeStruct((number, channels, PLANE), dtype)

    def plane_space(number, dtype=BF16):
        return pltpu.VMEM((number, channels, PLANE), dtype)

    def tap_space(number):
        return pltpu.VMEM((number, KDIM, PLANE), BF16)

    bricks = (slots, channels, CELLS)
    x_planes, cot_planes, edge, layer_mask = pl.pallas_call(
        layout_kernel,
        out_shape=(planes(12), planes(9), planes(4), jax.ShapeDtypeStruct((3, 8, PLANE), F32)),
        in_specs=[SMEM] + [VMEM] * 3,
        out_specs=(VMEM,) * 4,
        scratch_shapes=[
            pltpu.VMEM((2, *bricks), BF16),
            pltpu.VMEM((2, *bricks), BF16),
        ],
        compiler_params=vmem(8),
        name="layout",
    )(table, own, pair_volume, pair_cot)
    outer = lax.ppermute(edge, "space", hop)

    rearranged = jax.ShapeDtypeStruct((3, channels, KDIM), BF16)
    taps, one, two, slope_in, g_in, out_in, w1, w2, w2_back = pl.pallas_call(
        inner_kernel,
        out_shape=(
            jax.ShapeDtypeStruct((9, KDIM, PLANE), BF16),
            planes(2, F32),
            planes(2, F32),
            planes(7, F32),
            planes(7),
            planes(6),
            rearranged,
            rearranged,
            rearranged,
        ),
        in_specs=[SMEM] + [VMEM] * 5,
        out_specs=(VMEM,) * 9,
        scratch_shapes=[
            pltpu.VMEM((channels, 21 * 128), BF16),
            tap_space(2),
            plane_space(13, F32),
            plane_space(11, F32),
            pltpu.VMEM((9, 16, PLANE), BF16),
        ],
        compiler_params=vmem(20),
        cost_estimate=pl.CostEstimate(flops=2**33, bytes_accessed=2**23, transcendentals=2**20),
        name="inner",
    )(table, x_planes, cot_planes, layer_mask, weights, biases)

    half = (ROWS // 2, 128)
    kept, sent = jax.ShapeDtypeStruct(half, F32), jax.ShapeDtypeStruct(half, BF16)
    keep_two, send_two, slope_out, g_out, out_out = pl.pallas_call(
        outer_kernel,
        out_shape=(kept, sent, planes(1, F32), planes(3), planes(2)),
        in_specs=[SMEM] + [VMEM] * 10,
        out_specs=(VMEM,) * 5,
        scratch_shapes=[
            tap_space(3),
            tap_space(3),
            plane_space(3, F32),
            plane_space(3, F32),
            pltpu.VMEM((3 * channels, KDIM), F32),
            pltpu.VMEM((ROWS, 128), F32),
            pltpu.VMEM((9, 16, PLANE), BF16),
        ],
        compiler_params=vmem(16),
        cost_estimate=pl.CostEstimate(flops=2**32, bytes_accessed=2**23, transcendentals=2**18),
        name="outer",
    )(
        table, outer, cot_planes, layer_mask, w1, w2, biases, taps, one, two, g_in,
    )
    keep_one, send_one = pl.pallas_call(
        backward_kernel,
        out_shape=(kept, sent),
        in_specs=[SMEM] + [VMEM] * 7,
        out_specs=(VMEM,) * 2,
        scratch_shapes=[
            tap_space(2),
            tap_space(10),
            plane_space(12, F32),
            plane_space(8),
            pltpu.VMEM((3 * channels, KDIM), F32),
            pltpu.VMEM((ROWS, 128), F32),
            pltpu.VMEM((9, 16, PLANE), BF16),
        ],
        compiler_params=vmem(20),
        cost_estimate=pl.CostEstimate(flops=2**32, bytes_accessed=2**22, transcendentals=0),
        name="backward",
    )(table, g_out, g_in, slope_out, slope_in, x_planes, outer, w2_back)
    keep, send = pl.pallas_call(
        output_kernel,
        out_shape=(jax.ShapeDtypeStruct(bricks, BF16),) * 2,
        in_specs=[SMEM] + [VMEM] * 2,
        out_specs=(VMEM,) * 2,
        scratch_shapes=[plane_space(8), pltpu.VMEM(bricks, BF16)],
        compiler_params=vmem(8),
        cost_estimate=pl.CostEstimate(flops=2**28, bytes_accessed=2**21, transcendentals=0),
        name="output",
    )(table, out_out, out_in)
    output = (keep + lax.ppermute(send, "space", swap))[None]
    parts = shared_sum([keep_one, keep_two], [send_one, send_two])
    weight_shape = jax.ShapeDtypeStruct((channels, 27 * channels), F32)
    bias_shape = jax.ShapeDtypeStruct((1, channels), F32)
    total_w_one, total_w_two, total_b_one, total_b_two = pl.pallas_call(
        gather_kernel,
        out_shape=(weight_shape, weight_shape, bias_shape, bias_shape),
        in_specs=[SMEM] + [VMEM] * len(parts),
        out_specs=(ANY, ANY, VMEM, VMEM),
        scratch_shapes=[
            pltpu.VMEM((2, ROWS, 128), BF16),
            pltpu.VMEM((2, channels, 27 * channels), F32),
            pltpu.SemaphoreType.DMA((2,)),
        ],
        compiler_params=vmem(8),
        name="gather",
    )(table, *parts)
    return (output, total_w_one, total_w_two, total_b_one[0], total_b_two[0])


def solution(mesh):
    in_specs = (
        P("dp", "space", None, None),
        P("dp", None, None),
        P("dp", None),
        P("dp", "space", None, None),
        P(),
        P(),
        P(),
        P(),
    )
    out_specs = (P("dp", "space", None, None), P(), P(), P(), P())
    return jax.shard_map(local, mesh=mesh, in_specs=in_specs, out_specs=out_specs, check_vma=False)
```

```python
import jax
import jax.numpy as jnp
from jax import lax
from jax.experimental import pallas as pl
from jax.experimental.pallas import tpu as pltpu
from jax.sharding import PartitionSpec as P

EDGE = 8
PLANE = 256
CELLS = 512
KDIM = 896
TILES = 21
ROWS = 2048
OFFSETS = (4, 10, 12, 21)
DOWN, NEAR_Y, NEAR_Z, UP, LIVE, DEVICE = range(6)
F32 = jnp.float32
BF16 = jnp.bfloat16


def spread_matrix(back=False):
    near = lax.broadcasted_iota(jnp.int32, (256, 256), 1 if back else 0)
    far = lax.broadcasted_iota(jnp.int32, (256, 256), 0 if back else 1)
    source = ((far >> 3) & 1) * 128 + (far >> 7) * 64 + ((far >> 4) & 7) * 8 + (far & 7)
    return jnp.where(near == source, 1.0, 0.0).astype(BF16)


def fill_masks(masks):
    lane = lax.broadcasted_iota(jnp.int32, (16, PLANE), 1)
    for k in range(9):
        q, r = (lane >> 4) + (k // 3 - 1), (lane & 15) + (k % 3 - 1)
        inside = (q >= 0) & (q < 16) & (r >= 0) & (r < 16)
        masks[k] = jnp.where(inside, 1.0, 0.0).astype(BF16)


def write_taps(dst, plane, masks_ref):
    channels = plane.shape[0]
    for k in range(9):
        step = (k // 3 - 1) * 16 + (k % 3 - 1)
        if step == 0:
            moved = plane
        else:
            moved = pltpu.roll(plane, (-step) % PLANE, 1)
            moved = moved * jnp.concatenate([masks_ref[k]] * (channels // 16), axis=0)
        dst[k * channels : (k + 1) * channels, :] = moved


def space_index(table, count):
    return jnp.clip(table[DEVICE, 0] & 255, 0, count - 1)


def slot_place(table, slot, pair_slots):
    shift = pair_slots.bit_length() - 1
    up = table[UP, slot]
    inside = jnp.logical_and(up >= 0, up >> shift == slot >> shift)
    parity = jnp.where(inside, 0, 1)
    place = jnp.where(table[NEAR_Y, slot] >= 0, 2, 0) + jnp.where(table[NEAR_Z, slot] >= 0, 1, 0)
    return parity, place


def lane_mask(scalars):
    lane = lax.broadcasted_iota(jnp.int32, (8, PLANE), 1)
    high_y = lane >= 128
    high_z = (lane & 8) != 0
    s = [jnp.full((8, PLANE), v, F32) for v in scalars]
    return jnp.where(high_y, jnp.where(high_z, s[3], s[2]), jnp.where(high_z, s[1], s[0]))


def product(weight_ref, taps, plane_taps=slice(0, 3)):
    left = weight_ref[plane_taps]
    left = left.reshape(left.shape[0] * left.shape[1], KDIM)
    return jnp.dot(left, taps, preferred_element_type=F32)


def pair_sums(full, low, weight_ref, taps, first):
    channels = low.shape[1]
    both = product(weight_ref, taps)
    left, right = both[:, :PLANE], both[:, PLANE:]

    def part(value, a):
        return value[a * channels : (a + 1) * channels]

    before = part(left, 2)
    here = part(left, 1) + part(right, 2)
    full[0] = before if first else low[0] + before
    full[1] = here if first else low[1] + here
    low[0] = part(left, 0) + part(right, 1)
    low[1] = part(right, 0)


def half(k):
    return pl.ds((k & 1) * PLANE, PLANE)


def weight_products(total, grads, taps):
    blank = jnp.zeros((total.shape[0] // 3, PLANE), BF16)

    def left(p):
        inside = [grads(p + 1 - a) if 0 <= p + 1 - a < EDGE else blank for a in range(3)]
        return jnp.concatenate(inside, axis=0)

    for p in range(-1, EDGE + 1, 2):
        both_left = jnp.concatenate([left(p), left(p + 1)], axis=1)
        part = lax.dot_general(
            both_left, taps(p), (((1,), (1,)), ((), ())), preferred_element_type=F32
        )
        total[...] = part if p == -1 else total[...] + part


def write_tiles(flat, total, channels, even):
    lane = lax.broadcasted_iota(jnp.int32, (channels, 128), 1)
    blank = jnp.zeros((channels, 128), F32)
    low = total[pl.ds(pl.multiple_of(jnp.where(even, 0, 2 * channels), channels), channels), :]
    high = total[pl.ds(pl.multiple_of(jnp.where(even, 2 * channels, 0), channels), channels), :]
    second = jnp.concatenate([total[channels : 2 * channels, :], blank], axis=1)
    third = jnp.concatenate([high, blank], axis=1)
    second = pltpu.roll(second, 96, 1)
    third = pltpu.roll(third, 64, 1)

    def cut(value, k):
        return value[:, k * 128 : (k + 1) * 128]

    tiles = [cut(low, k) for k in range(6)]
    tiles.append(jnp.where(lane < 96, cut(low, 6), cut(second, 0)))
    tiles += [cut(second, k) for k in range(1, 7)]
    tiles.append(jnp.where(lane < 64, cut(second, 7), cut(third, 0)))
    tiles += [cut(third, k) for k in range(1, 8)]
    for k in range(TILES):
        flat[k * channels : (k + 1) * channels, :] = tiles[k]
    flat[TILES * channels :, :] = jnp.zeros((ROWS - TILES * channels, 128), F32)


def split_tiles(keep_ref, send_ref, flat, table):
    rows = keep_ref.shape[0]
    even = (table[DEVICE, 0] & 1) == 0
    here = pl.multiple_of(jnp.where(even, 0, rows), rows)
    there = pl.multiple_of(jnp.where(even, rows, 0), rows)
    keep_ref[...] = flat[pl.ds(here, rows), :]
    send_ref[...] = flat[pl.ds(there, rows), :].astype(BF16)


def layout_kernel(
    table, own_ref, pair_ref, cot_pair_ref,
    x_ref, cot_ref, edge_ref, mask_ref, bricks, cots,
):
    slots, channels = pair_ref.shape[0], pair_ref.shape[1]
    all_slots = table.shape[1]
    me = space_index(table, all_slots // slots)
    layer = table[DEVICE, 0] >> 16
    even = layer == 0

    live = [[jnp.float32(0)] * 4 for _ in range(2)]
    beyond = [jnp.float32(0)] * 4
    for device in (me, me ^ 1):
        for s in range(slots):
            slot = jnp.clip(device * slots + s, 0, all_slots - 1)
            parity, place = slot_place(table, slot, 2 * slots)
            alive = table[LIVE, slot].astype(F32)
            scale = jnp.full((channels, CELLS), alive, F32).astype(BF16)
            own = device is me
            bricks[parity, place] = (own_ref[s] if own else pair_ref[s]) * scale
            cots[parity, place] = (own_ref[slots + s] if own else cot_pair_ref[s]) * scale
            outer = jnp.where(even, table[DOWN, slot], table[UP, slot])
            alive_outer = table[LIVE, jnp.clip(outer, 0, all_slots - 1)].astype(F32)
            alive_outer = jnp.where(outer >= 0, alive_outer, 0.0)
            for k in range(4):
                for p in range(2):
                    here = jnp.logical_and(parity == p, place == k)
                    live[p][k] = jnp.where(here, alive, live[p][k])
                here = jnp.logical_and(parity == layer, place == k)
                beyond[k] = jnp.where(here, alive_outer, beyond[k])
    mask_ref[0] = lane_mask(beyond)
    mask_ref[1] = lane_mask([jnp.where(even, live[0][k], live[1][k]) for k in range(4)])
    mask_ref[2] = lane_mask([jnp.where(even, live[1][k], live[0][k]) for k in range(4)])

    move = spread_matrix()
    mine = jnp.where(even, 0, 1)

    def spread(left, right):
        two = jnp.concatenate([left, right], axis=1)
        return jnp.dot(two, move, preferred_element_type=F32).astype(BF16)

    for y in range(2):
        row = slice(y * 128, (y + 1) * 128)
        for j in range(4):
            pair = slice(j * 128, (j + 1) * 128)
            first = jnp.where(even, 2 * j, 7 - 2 * j)
            second = jnp.where(even, 2 * j + 1, 6 - 2 * j)
            both = spread(bricks[mine, 2 * y, :, pair], bricks[mine, 2 * y + 1, :, pair])
            x_ref[first, :, row] = both[:, :128]
            x_ref[second, :, row] = both[:, 128:]
            both = spread(cots[mine, 2 * y, :, pair], cots[mine, 2 * y + 1, :, pair])
            cot_ref[first, :, row] = both[:, :128]
            cot_ref[second, :, row] = both[:, 128:]
        for j in range(2):
            start = pl.multiple_of(jnp.where(even, j * 128, 256 + j * 128), 128)
            pair = pl.ds(start, 128)
            both = spread(
                bricks[1 - mine, 2 * y, :, pair], bricks[1 - mine, 2 * y + 1, :, pair]
            )
            x_ref[jnp.where(even, 8 + 2 * j, 11 - 2 * j), :, row] = both[:, :128]
            x_ref[jnp.where(even, 9 + 2 * j, 10 - 2 * j), :, row] = both[:, 128:]
        pair = pl.ds(pl.multiple_of(jnp.where(even, 0, 384), 128), 128)
        both = spread(cots[1 - mine, 2 * y, :, pair], cots[1 - mine, 2 * y + 1, :, pair])
        side = jnp.full((channels, 128), jnp.where(even, 1.0, 0.0), F32).astype(BF16)
        cot_ref[8, :, row] = both[:, :128] * side + both[:, 128:] * (1 - side)
    edge_ref[:3] = x_ref[:3]
    edge_ref[3] = cot_ref[0]


def tap_weights(out_ref, weight, wide, even):
    channels, width = weight.shape
    wide[:, :width] = weight
    lane = lax.broadcasted_iota(jnp.int32, (channels, 128), 1)
    for a, (tile, moved) in enumerate(((0, 0), (6, 96), (13, 64))):
        span = wide[:, tile * 128 : (tile + 8) * 128].astype(F32)
        if moved:
            span = pltpu.roll(span, 1024 - moved, 1)
        last = jnp.where(lane < 96, span[:, 768:KDIM], 0.0)
        span = jnp.concatenate([span[:, :768], last], axis=1)
        at = a if a == 1 else jnp.where(even, a, 2 - a)
        out_ref[at] = span.astype(BF16)


def back_weights(out_ref, taps_ref):
    channels = taps_ref.shape[1]
    lane = lax.broadcasted_iota(jnp.int32, (channels, 128), 1)
    more = jnp.zeros((128 - channels, KDIM), F32)
    for a in range(3):
        block = jnp.concatenate([taps_ref[2 - a].astype(F32), more], axis=0)
        turned = block.T
        tiles = [jnp.zeros((channels, 128), F32)] * 7
        for k in range(9):
            piece = turned[(8 - k) * channels : (9 - k) * channels, :]
            tile, moved = divmod(k * channels, 128)
            if moved:
                piece = pltpu.roll(piece, moved, 1)
            tiles[tile] = tiles[tile] + jnp.where(lane >= moved, piece, 0.0)
            if moved + channels > 128:
                tiles[tile + 1] = tiles[tile + 1] + jnp.where(lane < moved, piece, 0.0)
        out_ref[a] = jnp.concatenate(tiles, axis=1).astype(BF16)


def column(row):
    return jnp.broadcast_to(row, (8, row.shape[1])).T[:, :1]


def layer_of(q):
    return 0 if q < 0 else 1 if q < EDGE else 2


def hidden_plane(pre, mask):
    sigma = jax.nn.sigmoid(pre)
    return (pre * sigma * mask).astype(BF16), sigma * (1.0 + pre * (1.0 - sigma)) * mask


def out_plane(pre, mask, cot):
    sigma = jax.nn.sigmoid(pre)
    grad = cot.astype(F32) * (sigma * (1.0 + pre * (1.0 - sigma)))
    return (pre * sigma * mask).astype(BF16), grad.astype(BF16)


def inner_kernel(
    table, x_ref, cot_ref, layer_mask, weight_ref, bias_ref,
    taps_ref, one_ref, two_ref, slope_ref, g_ref, out_ref, w1_taps, w2_taps, w2_back,
    wide, xc, hc, full_one, low_one, full_two, low_two, masks_ref,
):
    channels = x_ref.shape[1]
    even = (table[DEVICE, 0] >> 16) == 0
    fill_masks(masks_ref)
    tap_weights(w1_taps, weight_ref[:channels, :], wide, even)
    bias_one, bias_two = column(bias_ref[0:1]), column(bias_ref[1:2])
    ones = jnp.ones((KDIM - 9 * channels, 2 * PLANE), BF16)
    for k in range(2):
        xc[k, 9 * channels :, :] = ones
    for k in range(4):
        taps_ref[k, 9 * channels :, :] = ones
    hc[9 * channels :, :] = ones[:, :PLANE]

    def write_x(p):
        write_taps(xc.at[(p >> 1) & 1, :, half(p)], x_ref[p], masks_ref)

    def finish_one(q, pre):
        hidden, slope = hidden_plane(pre + bias_one, layer_mask[layer_of(q)][:1])
        dst = taps_ref.at[(q - 1) // 2, :, half(q - 1)] if q < 9 else hc
        write_taps(dst, hidden, masks_ref)
        if q < EDGE:
            slope_ref[q - 1] = slope

    def finish_two(q, pre):
        out, grad = out_plane(pre + bias_two, layer_mask[layer_of(q)][:1], cot_ref[q])
        g_ref[q - 2] = grad
        if q < EDGE:
            out_ref[q - 2] = out

    write_x(0)
    write_x(1)
    for j in range(8):
        now, last = j & 1, (j + 1) & 1
        if j < 5:
            pair_sums(full_one.at[now], low_one, w1_taps, xc[now], j == 0)
            for p in (2 * j + 2, 2 * j + 3):
                if p <= 10:
                    write_x(p)
        if j == 5:
            third = product(w1_taps, xc[1, :, :PLANE], slice(2, 3))
            full_one[now, 0] = low_one[0] + third
        if j == 0:
            tap_weights(w2_taps, weight_ref[channels:, :], wide, even)
        if j == 1:
            one_ref[...] = full_one[0]
            back_weights(w2_back, w2_taps)
        if 2 <= j <= 5:
            finish_one(2 * j - 3, full_one[last, 0])
            finish_one(2 * j - 2, full_one[last, 1])
        if j == 6:
            finish_one(9, full_one[last, 0])
        if 3 <= j <= 6:
            pair_sums(full_two.at[now], low_two, w2_taps, taps_ref[j - 3], j == 3)
        if j == 7:
            third = product(w2_taps, hc[...], slice(2, 3))
            finish_two(8, low_two[0] + third)
        if j == 4:
            two_ref[...] = full_two[last]
        if 5 <= j:
            finish_two(2 * j - 8, full_two[last, 0])
            finish_two(2 * j - 7, full_two[last, 1])


def outer_kernel(
    table, edge_ref, cot_ref, layer_mask, w1_taps, w2_taps, bias_ref,
    taps_ref, one_ref, two_ref, g_in_ref,
    keep_ref, send_ref, slope_ref, g_ref, out_ref,
    xc, hc, x_pair, h_pair, total, flat, masks_ref,
):
    channels = cot_ref.shape[1]
    even = (table[DEVICE, 0] >> 16) == 0
    fill_masks(masks_ref)
    bias_one, bias_two = column(bias_ref[0:1]), column(bias_ref[1:2])
    ones = jnp.ones((KDIM - 9 * channels, 2 * PLANE), BF16)
    for single in (xc, hc):
        single[9 * channels :, :] = ones[:, :PLANE]
    for pair in (x_pair, h_pair):
        pair[9 * channels :, :] = ones
    write_taps(xc, edge_ref[2], masks_ref)
    write_taps(x_pair.at[:, half(0)], edge_ref[1], masks_ref)
    write_taps(x_pair.at[:, half(1)], edge_ref[0], masks_ref)

    def three_planes(weights, single, pair, parts):
        first = product(weights, single[...], slice(0, 1))
        both = product(weights, pair[...])
        left, right = both[:, :PLANE], both[:, PLANE:]
        one, two = slice(channels, 2 * channels), slice(2 * channels, 3 * channels)
        return (
            first + left[one] + right[two],
            left[:channels] + right[one] + parts[0],
            right[:channels] + parts[1],
        )

    for q, pre in zip(range(-2, 1), three_planes(w1_taps, xc, x_pair, one_ref)):
        hidden, slope = hidden_plane(pre + bias_one, layer_mask[layer_of(q)][:1])
        write_taps(hc if q == -2 else h_pair.at[:, half(q + 1)], hidden, masks_ref)
        if q == 0:
            slope_ref[0] = slope
    for q, pre in zip(range(-1, 2), three_planes(w2_taps, hc, h_pair, two_ref)):
        cot = edge_ref[3] if q < 0 else cot_ref[q]
        out, grad = out_plane(pre + bias_two, layer_mask[layer_of(q)][:1], cot)
        g_ref[q + 1] = grad
        if q >= 0:
            out_ref[q] = out

    def grads(q):
        return g_ref[q + 1] if q < 2 else g_in_ref[q - 2]

    def taps(p):
        return h_pair[...] if p < 0 else taps_ref[p // 2]

    weight_products(total, grads, taps)
    write_tiles(flat, total, channels, even)
    split_tiles(keep_ref, send_ref, flat, table)


def output_kernel(table, first_ref, second_ref, keep_ref, send_ref, outs, bricks):
    slots, channels = keep_ref.shape[0], keep_ref.shape[1]
    me = space_index(table, table.shape[1] // slots)
    layer = table[DEVICE, 0] >> 16
    even = layer == 0
    outs[:2] = first_ref[...]
    outs[2:] = second_ref[...]
    back = spread_matrix(True)
    for y in range(2):
        row = slice(y * 128, (y + 1) * 128)
        for j in range(4):
            first = jnp.where(even, 2 * j, 7 - 2 * j)
            second = jnp.where(even, 2 * j + 1, 6 - 2 * j)
            two = jnp.concatenate([outs[first, :, row], outs[second, :, row]], axis=1)
            both = jnp.dot(two, back, preferred_element_type=F32).astype(BF16)
            pair = slice(j * 128, (j + 1) * 128)
            bricks[2 * y, :, pair] = both[:, :128]
            bricks[2 * y + 1, :, pair] = both[:, 128:]
    for target, device in ((keep_ref, me), (send_ref, me ^ 1)):
        for s in range(slots):
            slot = jnp.clip(device * slots + s, 0, table.shape[1] - 1)
            parity, place = slot_place(table, slot, 2 * slots)
            scale = jnp.where(parity == layer, 1.0, 0.0)
            target[s] = bricks[place] * jnp.full((channels, CELLS), scale, F32).astype(BF16)


def backward_kernel(
    table, g_out_ref, g_in_ref, slope_out_ref, slope_in_ref, x_ref, edge_ref, w2_back,
    keep_ref, send_ref, gc, xc, full, low, grad, total, flat, masks_ref,
):
    channels = x_ref.shape[1]
    even = (table[DEVICE, 0] >> 16) == 0
    fill_masks(masks_ref)
    ones = jnp.ones((KDIM - 9 * channels, 2 * PLANE), BF16)
    for k in range(2):
        gc[k, 9 * channels :, :] = ones
    for k in range(5):
        xc[k, 9 * channels :, :] = ones

    def write_g(q):
        plane = g_out_ref[q + 1] if q < 2 else g_in_ref[q - 2]
        write_taps(gc.at[((q + 1) >> 1) & 1, :, half(q + 1)], plane, masks_ref)

    write_g(-1)
    write_g(0)
    for j in range(6):
        now, last = j & 1, (j + 1) & 1
        if j < 5:
            pair_sums(full.at[now], low, w2_back, gc[now], j == 0)
            for q in (2 * j + 1, 2 * j + 2):
                if q <= 8:
                    write_g(q)
            for q in (2 * j - 1, 2 * j):
                plane = edge_ref[0] if q < 0 else x_ref[q]
                write_taps(xc.at[j, :, half(q + 1)], plane, masks_ref)
        if j >= 2:
            for k, q in enumerate((2 * j - 4, 2 * j - 3)):
                slope = slope_out_ref[0] if q == 0 else slope_in_ref[q - 1]
                grad[q] = (full[last, k] * slope).astype(BF16)
    weight_products(total, lambda q: grad[q], lambda p: xc[(p + 1) // 2])
    write_tiles(flat, total, channels, even)
    split_tiles(keep_ref, send_ref, flat, table)


def copies_kernel(first_ref, second_ref, out_ref):
    total = (first_ref[...].astype(F32) + second_ref[...].astype(F32)).astype(BF16)
    for k in range(out_ref.shape[0]):
        out_ref[k] = total


def gather_kernel(
    table, own_ref, other_ref, w_one_ref, w_two_ref, b_one_ref, b_two_ref, flat
):
    chunks, _, rows, _ = own_ref.shape
    channels = w_one_ref.shape[0]
    core = table[DEVICE, 0] & 1
    for half, source in enumerate((own_ref, other_ref)):
        base = jnp.where(core == half, 0, chunks * rows)
        for k in range(chunks):
            at = pl.multiple_of(base + k * rows, rows)
            flat[:, pl.ds(at, rows), :] = source[k]
    for n, (weight, bias) in enumerate(((w_one_ref, b_one_ref), (w_two_ref, b_two_ref))):
        for k in range(TILES - 1):
            tile = flat[n, k * channels : (k + 1) * channels, :]
            weight[:, k * 128 : (k + 1) * 128] = tile.astype(F32)
        last = flat[n, (TILES - 1) * channels : TILES * channels, :].astype(F32)
        weight[:, 2560:2592] = last[:, :32]
        bias[...] = last.T[32:33, :]


VMEM = pl.BlockSpec(memory_space=pltpu.VMEM)
SMEM = pl.BlockSpec(memory_space=pltpu.SMEM)


def vmem(mebibytes):
    return pltpu.CompilerParams(vmem_limit_bytes=mebibytes * 2**20)


def shared_sum(keeps, sends):
    count = lax.axis_size("space")
    volumes = lax.axis_size("dp")
    swap = [(d, d ^ 1) for d in range(count)]
    both = ("space", "dp")
    groups = [
        [(chip * 2 + core) * volumes + first + v for v in range(2) for chip in range(count // 2)]
        for core in range(2)
        for first in range(0, volumes, 2)
    ]
    halves = [
        keep + lax.ppermute(send, "space", swap).astype(F32) for keep, send in zip(keeps, sends)
    ]
    halves = [half.astype(BF16).reshape(count, -1, 128) for half in halves]
    parts = jnp.stack(halves, axis=1)
    parts = lax.all_to_all(parts, both, 0, 0, axis_index_groups=groups)
    total = jnp.sum(parts.astype(F32), axis=0).astype(BF16)
    moved, step = jnp.zeros_like(total), 2
    while step < volumes:
        moved = lax.ppermute(total, "dp", [(v, v ^ step) for v in range(volumes)])
        if step * 2 < volumes:
            total = (total.astype(F32) + moved.astype(F32)).astype(BF16)
        step *= 2
    copies = pl.pallas_call(
        copies_kernel,
        out_shape=jax.ShapeDtypeStruct(parts.shape, BF16),
        in_specs=[VMEM] * 2,
        out_specs=VMEM,
        compiler_params=vmem(8),
        name="copies",
    )(total, moved)
    copies = lax.all_to_all(copies, both, 0, 0, axis_index_groups=groups)
    return [copies, lax.ppermute(copies, "space", swap)]


def local(volume, neighbours, active, cotangent, weight_one, weight_two, bias_one, bias_two):
    volume, cotangent = volume[0], cotangent[0]
    slots, channels = volume.shape[0], volume.shape[1]
    count = lax.axis_size("space")
    me = lax.axis_index("space").astype(jnp.int32)

    swap = [(d, d ^ 1) for d in range(count)]
    at = [2 * (n // 2) + (n & 1 ^ n // 2 & 1) for n in range(count)]
    hop = [(at[n], at[n + 1]) for n in range(1, count - 1, 2)]
    hop += [(there, here) for here, there in hop]
    pair_volume = lax.ppermute(volume, "space", swap)
    pair_cot = lax.ppermute(cotangent, "space", swap)
    biases = jnp.stack([bias_one, bias_two])
    weights = jnp.concatenate([weight_one, weight_two], axis=0)
    own = jnp.concatenate([volume, cotangent], axis=0)
    device = me + 256 * lax.axis_index("dp").astype(jnp.int32)
    device = device + 65536 * ((me ^ (me >> 1)) & 1)
    table = [neighbours[:, :, k] for k in OFFSETS]
    table = jnp.concatenate([*table, active, jnp.full_like(active, device)], axis=0)

    def planes(number, dtype=BF16):
        return jax.ShapeDtypeStruct((number, channels, PLANE), dtype)

    def plane_space(number):
        return pltpu.VMEM((number, channels, PLANE), BF16)

    def tap_space(*extent):
        return pltpu.VMEM(extent, BF16)

    def sum_space(*extent):
        return pltpu.VMEM((*extent, channels, PLANE), F32)

    bricks = (slots, channels, CELLS)
    x_planes, cot_planes, edge, layer_mask = pl.pallas_call(
        layout_kernel,
        out_shape=(planes(12), planes(9), planes(4), jax.ShapeDtypeStruct((3, 8, PLANE), F32)),
        in_specs=[SMEM] + [VMEM] * 3,
        out_specs=(VMEM,) * 4,
        scratch_shapes=[
            pltpu.VMEM((2, *bricks), BF16),
            pltpu.VMEM((2, *bricks), BF16),
        ],
        compiler_params=vmem(8),
        name="layout",
    )(table, own, pair_volume, pair_cot)
    outer = lax.ppermute(edge, "space", hop)

    rearranged = jax.ShapeDtypeStruct((3, channels, KDIM), BF16)
    taps, one, two, slope_in, g_in, out_in, w1, w2, w2_back = pl.pallas_call(
        inner_kernel,
        out_shape=(
            jax.ShapeDtypeStruct((4, KDIM, 2 * PLANE), BF16),
            planes(2, F32),
            planes(2, F32),
            planes(7, F32),
            planes(7),
            planes(6),
            rearranged,
            rearranged,
            rearranged,
        ),
        in_specs=[SMEM] + [VMEM] * 5,
        out_specs=(VMEM,) * 9,
        scratch_shapes=[
            pltpu.VMEM((channels, 21 * 128), BF16),
            tap_space(2, KDIM, 2 * PLANE),
            tap_space(KDIM, PLANE),
            sum_space(2, 2),
            sum_space(2),
            sum_space(2, 2),
            sum_space(2),
            pltpu.VMEM((9, 16, PLANE), BF16),
        ],
        compiler_params=vmem(20),
        cost_estimate=pl.CostEstimate(flops=2**33, bytes_accessed=2**23, transcendentals=2**20),
        name="inner",
    )(table, x_planes, cot_planes, layer_mask, weights, biases)

    rows = (ROWS // 2, 128)
    kept, sent = jax.ShapeDtypeStruct(rows, F32), jax.ShapeDtypeStruct(rows, BF16)
    keep_two, send_two, slope_out, g_out, out_out = pl.pallas_call(
        outer_kernel,
        out_shape=(kept, sent, planes(1, F32), planes(3), planes(2)),
        in_specs=[SMEM] + [VMEM] * 10,
        out_specs=(VMEM,) * 5,
        scratch_shapes=[
            tap_space(KDIM, PLANE),
            tap_space(KDIM, PLANE),
            tap_space(KDIM, 2 * PLANE),
            tap_space(KDIM, 2 * PLANE),
            pltpu.VMEM((3 * channels, KDIM), F32),
            pltpu.VMEM((ROWS, 128), F32),
            pltpu.VMEM((9, 16, PLANE), BF16),
        ],
        compiler_params=vmem(16),
        cost_estimate=pl.CostEstimate(flops=2**32, bytes_accessed=2**23, transcendentals=2**18),
        name="outer",
    )(
        table, outer, cot_planes, layer_mask, w1, w2, biases, taps, one, two, g_in,
    )
    keep_one, send_one = pl.pallas_call(
        backward_kernel,
        out_shape=(kept, sent),
        in_specs=[SMEM] + [VMEM] * 7,
        out_specs=(VMEM,) * 2,
        scratch_shapes=[
            tap_space(2, KDIM, 2 * PLANE),
            tap_space(5, KDIM, 2 * PLANE),
            sum_space(2, 2),
            sum_space(2),
            plane_space(8),
            pltpu.VMEM((3 * channels, KDIM), F32),
            pltpu.VMEM((ROWS, 128), F32),
            pltpu.VMEM((9, 16, PLANE), BF16),
        ],
        compiler_params=vmem(20),
        cost_estimate=pl.CostEstimate(flops=2**32, bytes_accessed=2**22, transcendentals=0),
        name="backward",
    )(table, g_out, g_in, slope_out, slope_in, x_planes, outer, w2_back)
    keep, send = pl.pallas_call(
        output_kernel,
        out_shape=(jax.ShapeDtypeStruct(bricks, BF16),) * 2,
        in_specs=[SMEM] + [VMEM] * 2,
        out_specs=(VMEM,) * 2,
        scratch_shapes=[plane_space(8), pltpu.VMEM(bricks, BF16)],
        compiler_params=vmem(8),
        cost_estimate=pl.CostEstimate(flops=2**28, bytes_accessed=2**21, transcendentals=0),
        name="output",
    )(table, out_out, out_in)
    output = (keep + lax.ppermute(send, "space", swap))[None]
    parts = shared_sum([keep_one, keep_two], [send_one, send_two])
    weight_shape = jax.ShapeDtypeStruct((channels, 27 * channels), F32)
    bias_shape = jax.ShapeDtypeStruct((1, channels), F32)
    total_w_one, total_w_two, total_b_one, total_b_two = pl.pallas_call(
        gather_kernel,
        out_shape=(weight_shape, weight_shape, bias_shape, bias_shape),
        in_specs=[SMEM] + [VMEM] * len(parts),
        out_specs=(VMEM,) * 4,
        scratch_shapes=[pltpu.VMEM((2, ROWS, 128), BF16)],
        compiler_params=vmem(8),
        name="gather",
    )(table, *parts)
    return (output, total_w_one, total_w_two, total_b_one[0], total_b_two[0])


def solution(mesh):
    in_specs = (
        P("dp", "space", None, None),
        P("dp", None, None),
        P("dp", None),
        P("dp", "space", None, None),
        P(),
        P(),
        P(),
        P(),
    )
    out_specs = (P("dp", "space", None, None), P(), P(), P(), P())
    return jax.shard_map(local, mesh=mesh, in_specs=in_specs, out_specs=out_specs, check_vma=False)
```

```python
import jax
import jax.numpy as jnp
from jax import lax
from jax.experimental import pallas as pl
from jax.experimental.pallas import tpu as pltpu
from jax.sharding import PartitionSpec as P

EDGE = 8
PLANE = 256
CELLS = 512
KDIM = 896
TILES = 21
ROWS = 2048
DOWN, NEAR_Y, NEAR_Z, UP, LIVE, DEVICE = 4, 10, 12, 21, 26, 27
F32 = jnp.float32
BF16 = jnp.bfloat16


def spread_matrix(back=False):
    near = lax.broadcasted_iota(jnp.int32, (256, 256), 1 if back else 0)
    far = lax.broadcasted_iota(jnp.int32, (256, 256), 0 if back else 1)
    source = ((far >> 3) & 1) * 128 + (far >> 7) * 64 + ((far >> 4) & 7) * 8 + (far & 7)
    return jnp.where(near == source, 1.0, 0.0).astype(BF16)


def fill_masks(masks):
    lane = lax.broadcasted_iota(jnp.int32, (16, PLANE), 1)
    for k in range(9):
        q, r = (lane >> 4) + (k // 3 - 1), (lane & 15) + (k % 3 - 1)
        inside = (q >= 0) & (q < 16) & (r >= 0) & (r < 16)
        masks[k] = jnp.where(inside, 1.0, 0.0).astype(BF16)


def write_taps(dst, plane, masks_ref):
    channels = plane.shape[0]
    for k in range(9):
        step = (k // 3 - 1) * 16 + (k % 3 - 1)
        if step == 0:
            moved = plane
        else:
            moved = pltpu.roll(plane, (-step) % PLANE, 1)
            moved = moved * jnp.concatenate([masks_ref[k]] * (channels // 16), axis=0)
        dst[k * channels : (k + 1) * channels, :] = moved


def space_index(table, count):
    return jnp.clip(table[DEVICE, 0, 0] & 255, 0, count - 1)


def slot_place(table, slot, pair_slots):
    shift = pair_slots.bit_length() - 1
    up = table[UP, 0, slot]
    inside = jnp.logical_and(up >= 0, up >> shift == slot >> shift)
    parity = jnp.where(inside, 0, 1)
    place = jnp.where(table[NEAR_Y, 0, slot] >= 0, 2, 0) + jnp.where(table[NEAR_Z, 0, slot] >= 0, 1, 0)
    return parity, place


def lane_mask(scalars):
    lane = lax.broadcasted_iota(jnp.int32, (8, PLANE), 1)
    high_y = lane >= 128
    high_z = (lane & 8) != 0
    s = [jnp.full((8, PLANE), v, F32) for v in scalars]
    return jnp.where(high_y, jnp.where(high_z, s[3], s[2]), jnp.where(high_z, s[1], s[0]))


def product(weight_ref, taps, plane_taps=slice(0, 3)):
    left = weight_ref[plane_taps]
    left = left.reshape(left.shape[0] * left.shape[1], KDIM)
    return jnp.dot(left, taps, preferred_element_type=F32)


def pair_sums(full, low, weight_ref, taps, first):
    channels = low.shape[1]
    both = product(weight_ref, taps)
    left, right = both[:, :PLANE], both[:, PLANE:]

    def part(value, a):
        return value[a * channels : (a + 1) * channels]

    before = part(left, 2)
    here = part(left, 1) + part(right, 2)
    full[0] = before if first else low[0] + before
    full[1] = here if first else low[1] + here
    low[0] = part(left, 0) + part(right, 1)
    low[1] = part(right, 0)


def place(k):
    return pl.ds(k * PLANE, PLANE)


def weight_products(grads, planes, taps):
    blank = jnp.zeros_like(grads(3))

    def left(p):
        inside = [grads(p + 1 - a) if 0 <= p + 1 - a < EDGE else blank for a in range(3)]
        return jnp.concatenate(inside, axis=0)

    lefts = jnp.concatenate([left(p) for p in planes], axis=1)
    return lax.dot_general(lefts, taps, (((1,), (1,)), ((), ())), preferred_element_type=F32)


def write_tiles(flat, total, channels, even):
    lane = lax.broadcasted_iota(jnp.int32, (channels, 128), 1)
    blank = jnp.zeros((channels, 128), F32)
    first, last = total[:channels, :], total[2 * channels :, :]
    low, high = jnp.where(even, first, last), jnp.where(even, last, first)
    second = jnp.concatenate([total[channels : 2 * channels, :], blank], axis=1)
    third = jnp.concatenate([high, blank], axis=1)
    second = pltpu.roll(second, 96, 1)
    third = pltpu.roll(third, 64, 1)

    def cut(value, k):
        return value[:, k * 128 : (k + 1) * 128]

    tiles = [cut(low, k) for k in range(6)]
    tiles.append(jnp.where(lane < 96, cut(low, 6), cut(second, 0)))
    tiles += [cut(second, k) for k in range(1, 7)]
    tiles.append(jnp.where(lane < 64, cut(second, 7), cut(third, 0)))
    tiles += [cut(third, k) for k in range(1, 8)]
    for k in range(TILES):
        flat[k * channels : (k + 1) * channels, :] = tiles[k]
    flat[TILES * channels :, :] = jnp.zeros((ROWS - TILES * channels, 128), F32)


def split_tiles(keep_ref, send_ref, flat, table):
    rows = keep_ref.shape[0]
    even = (table[DEVICE, 0, 0] & 1) == 0
    here = pl.multiple_of(jnp.where(even, 0, rows), rows)
    there = pl.multiple_of(jnp.where(even, rows, 0), rows)
    keep_ref[...] = flat[pl.ds(here, rows), :]
    send_ref[...] = flat[pl.ds(there, rows), :].astype(BF16)


def layout_kernel(
    table, own_ref, pair_ref, cot_pair_ref,
    x_ref, cot_ref, edge_ref, mask_ref, bricks, cots,
):
    slots, channels = pair_ref.shape[0], pair_ref.shape[1]
    all_slots = table.shape[2]
    me = space_index(table, all_slots // slots)
    layer = table[DEVICE, 0, 0] >> 16
    even = layer == 0

    live = [[jnp.float32(0)] * 4 for _ in range(2)]
    beyond = [jnp.float32(0)] * 4
    for device in (me, me ^ 1):
        for s in range(slots):
            slot = jnp.clip(device * slots + s, 0, all_slots - 1)
            parity, spot = slot_place(table, slot, 2 * slots)
            alive = table[LIVE, 0, slot].astype(F32)
            scale = jnp.full((channels, CELLS), alive, F32).astype(BF16)
            own = device is me
            bricks[parity, spot] = (own_ref[s] if own else pair_ref[s]) * scale
            cots[parity, spot] = (own_ref[slots + s] if own else cot_pair_ref[s]) * scale
            outer = jnp.where(even, table[DOWN, 0, slot], table[UP, 0, slot])
            alive_outer = table[LIVE, 0, jnp.clip(outer, 0, all_slots - 1)].astype(F32)
            alive_outer = jnp.where(outer >= 0, alive_outer, 0.0)
            for k in range(4):
                for p in range(2):
                    here = jnp.logical_and(parity == p, spot == k)
                    live[p][k] = jnp.where(here, alive, live[p][k])
                here = jnp.logical_and(parity == layer, spot == k)
                beyond[k] = jnp.where(here, alive_outer, beyond[k])
    mask_ref[0] = lane_mask(beyond)
    mask_ref[1] = lane_mask([jnp.where(even, live[0][k], live[1][k]) for k in range(4)])
    mask_ref[2] = lane_mask([jnp.where(even, live[1][k], live[0][k]) for k in range(4)])

    move = spread_matrix()
    mine = jnp.where(even, 0, 1)

    def spread(left, right):
        two = jnp.concatenate([left, right], axis=1)
        return jnp.dot(two, move, preferred_element_type=F32).astype(BF16)

    for y in range(2):
        row = slice(y * 128, (y + 1) * 128)
        for j in range(4):
            pair = slice(j * 128, (j + 1) * 128)
            first = jnp.where(even, 2 * j, 7 - 2 * j)
            second = jnp.where(even, 2 * j + 1, 6 - 2 * j)
            both = spread(bricks[mine, 2 * y, :, pair], bricks[mine, 2 * y + 1, :, pair])
            x_ref[first, :, row] = both[:, :128]
            x_ref[second, :, row] = both[:, 128:]
            both = spread(cots[mine, 2 * y, :, pair], cots[mine, 2 * y + 1, :, pair])
            cot_ref[first, :, row] = both[:, :128]
            cot_ref[second, :, row] = both[:, 128:]
        for j in range(2):
            start = pl.multiple_of(jnp.where(even, j * 128, 256 + j * 128), 128)
            pair = pl.ds(start, 128)
            both = spread(
                bricks[1 - mine, 2 * y, :, pair], bricks[1 - mine, 2 * y + 1, :, pair]
            )
            x_ref[jnp.where(even, 8 + 2 * j, 11 - 2 * j), :, row] = both[:, :128]
            x_ref[jnp.where(even, 9 + 2 * j, 10 - 2 * j), :, row] = both[:, 128:]
        pair = pl.ds(pl.multiple_of(jnp.where(even, 0, 384), 128), 128)
        both = spread(cots[1 - mine, 2 * y, :, pair], cots[1 - mine, 2 * y + 1, :, pair])
        side = jnp.full((channels, 128), jnp.where(even, 1.0, 0.0), F32).astype(BF16)
        cot_ref[8, :, row] = both[:, :128] * side + both[:, 128:] * (1 - side)
    edge_ref[:3] = x_ref[:3]
    edge_ref[3] = cot_ref[0]


def tap_weights(out_ref, weight, wide, even):
    channels, width = weight.shape
    wide[:, :width] = weight
    lane = lax.broadcasted_iota(jnp.int32, (channels, 128), 1)
    for a, (tile, moved) in enumerate(((0, 0), (6, 96), (13, 64))):
        span = wide[:, tile * 128 : (tile + 8) * 128].astype(F32)
        if moved:
            span = pltpu.roll(span, 1024 - moved, 1)
        last = jnp.where(lane < 96, span[:, 768:KDIM], 0.0)
        span = jnp.concatenate([span[:, :768], last], axis=1)
        at = a if a == 1 else jnp.where(even, a, 2 - a)
        out_ref[at] = span.astype(BF16)


def back_weights(out_ref, taps_ref):
    channels = taps_ref.shape[1]
    lane = lax.broadcasted_iota(jnp.int32, (channels, 128), 1)
    more = jnp.zeros((128 - channels, KDIM), F32)
    for a in range(3):
        block = jnp.concatenate([taps_ref[2 - a].astype(F32), more], axis=0)
        turned = block.T
        tiles = [jnp.zeros((channels, 128), F32)] * 7
        for k in range(9):
            piece = turned[(8 - k) * channels : (9 - k) * channels, :]
            tile, moved = divmod(k * channels, 128)
            if moved:
                piece = pltpu.roll(piece, moved, 1)
            tiles[tile] = tiles[tile] + jnp.where(lane >= moved, piece, 0.0)
            if moved + channels > 128:
                tiles[tile + 1] = tiles[tile + 1] + jnp.where(lane < moved, piece, 0.0)
        out_ref[a] = jnp.concatenate(tiles, axis=1).astype(BF16)


def column(row):
    return jnp.broadcast_to(row, (8, row.shape[1])).T[:, :1]


def layer_of(q):
    return 0 if q < 0 else 1 if q < EDGE else 2


def hidden_plane(pre, mask):
    sigma = jax.nn.sigmoid(pre)
    return (pre * sigma * mask).astype(BF16), sigma * (1.0 + pre * (1.0 - sigma)) * mask


def out_plane(pre, mask, cot):
    sigma = jax.nn.sigmoid(pre)
    grad = cot.astype(F32) * (sigma * (1.0 + pre * (1.0 - sigma)))
    return (pre * sigma * mask).astype(BF16), grad.astype(BF16)


def inner_kernel(
    table, x_ref, cot_ref, layer_mask, weight_ref, bias_ref,
    taps_ref, one_ref, two_ref, slope_ref, g_ref, out_ref, total_ref, w1_taps, w2_taps, w2_back,
    wide, xc, hc, full_one, low_one, full_two, low_two, masks_ref,
):
    channels = x_ref.shape[1]
    even = (table[DEVICE, 0, 0] >> 16) == 0
    fill_masks(masks_ref)
    tap_weights(w1_taps, weight_ref[:channels, :], wide, even)
    bias_one, bias_two = column(bias_ref[0:1]), column(bias_ref[1:2])
    ones = jnp.ones((KDIM - 9 * channels, 2 * PLANE), BF16)
    for k in range(2):
        xc[k, 9 * channels :, :] = ones
    for k in range(4):
        taps_ref[9 * channels :, 2 * k * PLANE : (2 * k + 2) * PLANE] = ones
    hc[9 * channels :, :] = ones[:, :PLANE]

    def write_x(p):
        write_taps(xc.at[(p >> 1) & 1, :, place(p & 1)], x_ref[p], masks_ref)

    def finish_one(q, pre):
        hidden, slope = hidden_plane(pre + bias_one, layer_mask[layer_of(q)][:1])
        dst = taps_ref.at[:, place(q - 1)] if q < 9 else hc
        write_taps(dst, hidden, masks_ref)
        if q < EDGE:
            slope_ref[q - 1] = slope

    def finish_two(q, pre):
        out, grad = out_plane(pre + bias_two, layer_mask[layer_of(q)][:1], cot_ref[q])
        g_ref[q - 2] = grad
        if q < EDGE:
            out_ref[q - 2] = out

    write_x(0)
    write_x(1)
    for j in range(8):
        now, last = j & 1, (j + 1) & 1
        if j < 5:
            pair_sums(full_one.at[now], low_one, w1_taps, xc[now], j == 0)
            for p in (2 * j + 2, 2 * j + 3):
                if p <= 10:
                    write_x(p)
        if j == 5:
            third = product(w1_taps, xc[1, :, :PLANE], slice(2, 3))
            full_one[now, 0] = low_one[0] + third
        if j == 0:
            tap_weights(w2_taps, weight_ref[channels:, :], wide, even)
        if j == 1:
            one_ref[...] = full_one[0]
            back_weights(w2_back, w2_taps)
        if 2 <= j <= 5:
            finish_one(2 * j - 3, full_one[last, 0])
            finish_one(2 * j - 2, full_one[last, 1])
        if j == 6:
            finish_one(9, full_one[last, 0])
        if 3 <= j <= 6:
            hidden = taps_ref[:, (2 * j - 6) * PLANE : (2 * j - 4) * PLANE]
            pair_sums(full_two.at[now], low_two, w2_taps, hidden, j == 3)
        if j == 7:
            third = product(w2_taps, hc[...], slice(2, 3))
            finish_two(8, low_two[0] + third)
        if j == 4:
            two_ref[...] = full_two[last]
        if 5 <= j:
            finish_two(2 * j - 8, full_two[last, 0])
            finish_two(2 * j - 7, full_two[last, 1])
    hidden = taps_ref[:, 2 * PLANE : 6 * PLANE]
    total_ref[...] = weight_products(lambda q: g_ref[q - 2], range(3, 7), hidden)


def outer_kernel(
    table, edge_ref, cot_ref, layer_mask, w1_taps, w2_taps, bias_ref,
    taps_ref, one_ref, two_ref, g_in_ref, total_ref,
    keep_ref, send_ref, slope_ref, g_ref, out_ref,
    xc, hc, x_pair, h_pair, flat, masks_ref,
):
    channels = cot_ref.shape[1]
    even = (table[DEVICE, 0, 0] >> 16) == 0
    fill_masks(masks_ref)
    bias_one, bias_two = column(bias_ref[0:1]), column(bias_ref[1:2])
    ones = jnp.ones((KDIM - 9 * channels, 2 * PLANE), BF16)
    for single in (xc, hc):
        single[9 * channels :, :] = ones[:, :PLANE]
    for pair in (x_pair, h_pair):
        pair[9 * channels :, :] = ones
    write_taps(xc, edge_ref[2], masks_ref)
    write_taps(x_pair.at[:, place(0)], edge_ref[1], masks_ref)
    write_taps(x_pair.at[:, place(1)], edge_ref[0], masks_ref)

    def three_planes(weights, single, pair, parts):
        first = product(weights, single[...], slice(0, 1))
        both = product(weights, pair[...])
        left, right = both[:, :PLANE], both[:, PLANE:]
        one, two = slice(channels, 2 * channels), slice(2 * channels, 3 * channels)
        return (
            first + left[one] + right[two],
            left[:channels] + right[one] + parts[0],
            right[:channels] + parts[1],
        )

    for q, pre in zip(range(-2, 1), three_planes(w1_taps, xc, x_pair, one_ref)):
        hidden, slope = hidden_plane(pre + bias_one, layer_mask[layer_of(q)][:1])
        write_taps(hc if q == -2 else h_pair.at[:, place(q + 1)], hidden, masks_ref)
        if q == 0:
            slope_ref[0] = slope
    for q, pre in zip(range(-1, 2), three_planes(w2_taps, hc, h_pair, two_ref)):
        cot = edge_ref[3] if q < 0 else cot_ref[q]
        out, grad = out_plane(pre + bias_two, layer_mask[layer_of(q)][:1], cot)
        g_ref[q + 1] = grad
        if q >= 0:
            out_ref[q] = out

    def grads(q):
        return g_ref[q + 1] if q < 2 else g_in_ref[q - 2]

    planes = (-1, 0, 1, 2, 7, 8)
    taps = [h_pair[...], taps_ref[:, : 2 * PLANE], taps_ref[:, 6 * PLANE :]]
    total = total_ref[...] + weight_products(grads, planes, jnp.concatenate(taps, axis=1))
    write_tiles(flat, total, channels, even)
    split_tiles(keep_ref, send_ref, flat, table)


def output_kernel(table, first_ref, second_ref, keep_ref, send_ref, outs, bricks):
    slots, channels = keep_ref.shape[0], keep_ref.shape[1]
    me = space_index(table, table.shape[2] // slots)
    layer = table[DEVICE, 0, 0] >> 16
    even = layer == 0
    outs[:2] = first_ref[...]
    outs[2:] = second_ref[...]
    back = spread_matrix(True)
    for y in range(2):
        row = slice(y * 128, (y + 1) * 128)
        for j in range(4):
            first = jnp.where(even, 2 * j, 7 - 2 * j)
            second = jnp.where(even, 2 * j + 1, 6 - 2 * j)
            two = jnp.concatenate([outs[first, :, row], outs[second, :, row]], axis=1)
            both = jnp.dot(two, back, preferred_element_type=F32).astype(BF16)
            pair = slice(j * 128, (j + 1) * 128)
            bricks[2 * y, :, pair] = both[:, :128]
            bricks[2 * y + 1, :, pair] = both[:, 128:]
    for target, device in ((keep_ref, me), (send_ref, me ^ 1)):
        for s in range(slots):
            slot = jnp.clip(device * slots + s, 0, table.shape[2] - 1)
            parity, spot = slot_place(table, slot, 2 * slots)
            scale = jnp.where(parity == layer, 1.0, 0.0)
            target[s] = bricks[spot] * jnp.full((channels, CELLS), scale, F32).astype(BF16)


def backward_kernel(
    table, g_out_ref, g_in_ref, slope_out_ref, slope_in_ref, x_ref, edge_ref, w2_back,
    keep_ref, send_ref, gc, xc, full, low, grad, flat, masks_ref,
):
    channels = x_ref.shape[1]
    even = (table[DEVICE, 0, 0] >> 16) == 0
    fill_masks(masks_ref)
    ones = jnp.ones((KDIM - 9 * channels, 2 * PLANE), BF16)
    for k in range(2):
        gc[k, 9 * channels :, :] = ones
    for k in range(5):
        xc[9 * channels :, 2 * k * PLANE : (2 * k + 2) * PLANE] = ones

    def write_g(q):
        plane = g_out_ref[q + 1] if q < 2 else g_in_ref[q - 2]
        write_taps(gc.at[((q + 1) >> 1) & 1, :, place((q + 1) & 1)], plane, masks_ref)

    write_g(-1)
    write_g(0)
    for j in range(6):
        now, last = j & 1, (j + 1) & 1
        if j < 5:
            pair_sums(full.at[now], low, w2_back, gc[now], j == 0)
            for q in (2 * j + 1, 2 * j + 2):
                if q <= 8:
                    write_g(q)
            for q in (2 * j - 1, 2 * j):
                plane = edge_ref[0] if q < 0 else x_ref[q]
                write_taps(xc.at[:, place(q + 1)], plane, masks_ref)
        if j >= 2:
            for k, q in enumerate((2 * j - 4, 2 * j - 3)):
                slope = slope_out_ref[0] if q == 0 else slope_in_ref[q - 1]
                grad[q] = (full[last, k] * slope).astype(BF16)
    total = weight_products(lambda q: grad[q], range(-1, EDGE + 1), xc[...])
    write_tiles(flat, total, channels, even)
    split_tiles(keep_ref, send_ref, flat, table)


def copies_kernel(first_ref, second_ref, out_ref):
    total = (first_ref[...].astype(F32) + second_ref[...].astype(F32)).astype(BF16)
    for k in range(out_ref.shape[0]):
        out_ref[k] = total


def gather_kernel(
    table, own_ref, other_ref, w_one_ref, w_two_ref, b_one_ref, b_two_ref, flat
):
    chunks, _, rows, _ = own_ref.shape
    channels = w_one_ref.shape[0]
    core = table[DEVICE, 0, 0] & 1
    for half, source in enumerate((own_ref, other_ref)):
        base = jnp.where(core == half, 0, chunks * rows)
        for k in range(chunks):
            at = pl.multiple_of(base + k * rows, rows)
            flat[:, pl.ds(at, rows), :] = source[k]
    for n, (weight, bias) in enumerate(((w_one_ref, b_one_ref), (w_two_ref, b_two_ref))):
        for k in range(TILES - 1):
            tile = flat[n, k * channels : (k + 1) * channels, :]
            weight[:, k * 128 : (k + 1) * 128] = tile.astype(F32)
        last = flat[n, (TILES - 1) * channels : TILES * channels, :].astype(F32)
        weight[:, 2560:2592] = last[:, :32]
        bias[...] = last.T[32:33, :]


VMEM = pl.BlockSpec(memory_space=pltpu.VMEM)
SMEM = pl.BlockSpec(memory_space=pltpu.SMEM)


def vmem(mebibytes):
    return pltpu.CompilerParams(vmem_limit_bytes=mebibytes * 2**20)


def shared_sum(keeps, sends):
    count = lax.axis_size("space")
    volumes = lax.axis_size("dp")
    swap = [(d, d ^ 1) for d in range(count)]
    both = ("space", "dp")
    groups = [
        [(chip * 2 + core) * volumes + first + v for v in range(2) for chip in range(count // 2)]
        for core in range(2)
        for first in range(0, volumes, 2)
    ]
    halves = [
        keep + lax.ppermute(send, "space", swap).astype(F32) for keep, send in zip(keeps, sends)
    ]
    halves = [half.astype(BF16).reshape(count, -1, 128) for half in halves]
    parts = jnp.stack(halves, axis=1)
    parts = lax.all_to_all(parts, both, 0, 0, axis_index_groups=groups)
    total = jnp.sum(parts.astype(F32), axis=0).astype(BF16)
    moved, step = jnp.zeros_like(total), 2
    while step < volumes:
        moved = lax.ppermute(total, "dp", [(v, v ^ step) for v in range(volumes)])
        if step * 2 < volumes:
            total = (total.astype(F32) + moved.astype(F32)).astype(BF16)
        step *= 2
    copies = pl.pallas_call(
        copies_kernel,
        out_shape=jax.ShapeDtypeStruct(parts.shape, BF16),
        in_specs=[VMEM] * 2,
        out_specs=VMEM,
        compiler_params=vmem(8),
        name="copies",
    )(total, moved)
    copies = lax.all_to_all(copies, both, 0, 0, axis_index_groups=groups)
    return [copies, lax.ppermute(copies, "space", swap)]


def local(volume, neighbours, active, cotangent, weight_one, weight_two, bias_one, bias_two):
    volume, cotangent = volume[0], cotangent[0]
    slots, channels = volume.shape[0], volume.shape[1]
    count = lax.axis_size("space")
    me = lax.axis_index("space").astype(jnp.int32)

    swap = [(d, d ^ 1) for d in range(count)]
    at = [2 * (n // 2) + (n & 1 ^ n // 2 & 1) for n in range(count)]
    hop = [(at[n], at[n + 1]) for n in range(1, count - 1, 2)]
    hop += [(there, here) for here, there in hop]
    pair_volume = lax.ppermute(volume, "space", swap)
    pair_cot = lax.ppermute(cotangent, "space", swap)
    biases = jnp.stack([bias_one, bias_two])
    weights = jnp.concatenate([weight_one, weight_two], axis=0)
    own = jnp.concatenate([volume, cotangent], axis=0)
    device = me + 256 * lax.axis_index("dp").astype(jnp.int32)
    device = device + 65536 * ((me ^ (me >> 1)) & 1)
    rows = [neighbours.transpose(2, 0, 1), active[None], jnp.full_like(active, device)[None]]
    table = jnp.concatenate(rows, axis=0)

    def planes(number, dtype=BF16):
        return jax.ShapeDtypeStruct((number, channels, PLANE), dtype)

    def plane_space(number):
        return pltpu.VMEM((number, channels, PLANE), BF16)

    def tap_space(*extent):
        return pltpu.VMEM(extent, BF16)

    def sum_space(*extent):
        return pltpu.VMEM((*extent, channels, PLANE), F32)

    bricks = (slots, channels, CELLS)
    x_planes, cot_planes, edge, layer_mask = pl.pallas_call(
        layout_kernel,
        out_shape=(planes(12), planes(9), planes(4), jax.ShapeDtypeStruct((3, 8, PLANE), F32)),
        in_specs=[SMEM] + [VMEM] * 3,
        out_specs=(VMEM,) * 4,
        scratch_shapes=[
            pltpu.VMEM((2, *bricks), BF16),
            pltpu.VMEM((2, *bricks), BF16),
        ],
        compiler_params=vmem(8),
        name="layout",
    )(table, own, pair_volume, pair_cot)
    outer = lax.ppermute(edge, "space", hop)

    rearranged = jax.ShapeDtypeStruct((3, channels, KDIM), BF16)
    taps, one, two, slope_in, g_in, out_in, part_two, w1, w2, w2_back = pl.pallas_call(
        inner_kernel,
        out_shape=(
            jax.ShapeDtypeStruct((KDIM, EDGE * PLANE), BF16),
            planes(2, F32),
            planes(2, F32),
            planes(7, F32),
            planes(7),
            planes(6),
            jax.ShapeDtypeStruct((3 * channels, KDIM), F32),
            rearranged,
            rearranged,
            rearranged,
        ),
        in_specs=[SMEM] + [VMEM] * 5,
        out_specs=(VMEM,) * 10,
        scratch_shapes=[
            pltpu.VMEM((channels, 21 * 128), BF16),
            tap_space(2, KDIM, 2 * PLANE),
            tap_space(KDIM, PLANE),
            sum_space(2, 2),
            sum_space(2),
            sum_space(2, 2),
            sum_space(2),
            pltpu.VMEM((9, 16, PLANE), BF16),
        ],
        compiler_params=vmem(20),
        cost_estimate=pl.CostEstimate(flops=2**33, bytes_accessed=2**23, transcendentals=2**20),
        name="inner",
    )(table, x_planes, cot_planes, layer_mask, weights, biases)

    rows = (ROWS // 2, 128)
    kept, sent = jax.ShapeDtypeStruct(rows, F32), jax.ShapeDtypeStruct(rows, BF16)
    keep_two, send_two, slope_out, g_out, out_out = pl.pallas_call(
        outer_kernel,
        out_shape=(kept, sent, planes(1, F32), planes(3), planes(2)),
        in_specs=[SMEM] + [VMEM] * 11,
        out_specs=(VMEM,) * 5,
        scratch_shapes=[
            tap_space(KDIM, PLANE),
            tap_space(KDIM, PLANE),
            tap_space(KDIM, 2 * PLANE),
            tap_space(KDIM, 2 * PLANE),
            pltpu.VMEM((ROWS, 128), F32),
            pltpu.VMEM((9, 16, PLANE), BF16),
        ],
        compiler_params=vmem(16),
        cost_estimate=pl.CostEstimate(flops=2**32, bytes_accessed=2**23, transcendentals=2**18),
        name="outer",
    )(
        table, outer, cot_planes, layer_mask, w1, w2, biases, taps, one, two, g_in,
        part_two,
    )
    keep_one, send_one = pl.pallas_call(
        backward_kernel,
        out_shape=(kept, sent),
        in_specs=[SMEM] + [VMEM] * 7,
        out_specs=(VMEM,) * 2,
        scratch_shapes=[
            tap_space(2, KDIM, 2 * PLANE),
            tap_space(KDIM, (EDGE + 2) * PLANE),
            sum_space(2, 2),
            sum_space(2),
            plane_space(8),
            pltpu.VMEM((ROWS, 128), F32),
            pltpu.VMEM((9, 16, PLANE), BF16),
        ],
        compiler_params=vmem(20),
        cost_estimate=pl.CostEstimate(flops=2**32, bytes_accessed=2**22, transcendentals=0),
        name="backward",
    )(table, g_out, g_in, slope_out, slope_in, x_planes, outer, w2_back)
    keep, send = pl.pallas_call(
        output_kernel,
        out_shape=(jax.ShapeDtypeStruct(bricks, BF16),) * 2,
        in_specs=[SMEM] + [VMEM] * 2,
        out_specs=(VMEM,) * 2,
        scratch_shapes=[plane_space(8), pltpu.VMEM(bricks, BF16)],
        compiler_params=vmem(8),
        cost_estimate=pl.CostEstimate(flops=2**28, bytes_accessed=2**21, transcendentals=0),
        name="output",
    )(table, out_out, out_in)
    output = (keep + lax.ppermute(send, "space", swap))[None]
    parts = shared_sum([keep_one, keep_two], [send_one, send_two])
    weight_shape = jax.ShapeDtypeStruct((channels, 27 * channels), F32)
    bias_shape = jax.ShapeDtypeStruct((1, channels), F32)
    total_w_one, total_w_two, total_b_one, total_b_two = pl.pallas_call(
        gather_kernel,
        out_shape=(weight_shape, weight_shape, bias_shape, bias_shape),
        in_specs=[SMEM] + [VMEM] * len(parts),
        out_specs=(VMEM,) * 4,
        scratch_shapes=[pltpu.VMEM((2, ROWS, 128), BF16)],
        compiler_params=vmem(8),
        name="gather",
    )(table, *parts)
    return (output, total_w_one, total_w_two, total_b_one[0], total_b_two[0])


def solution(mesh):
    in_specs = (
        P("dp", "space", None, None),
        P("dp", None, None),
        P("dp", None),
        P("dp", "space", None, None),
        P(),
        P(),
        P(),
        P(),
    )
    out_specs = (P("dp", "space", None, None), P(), P(), P(), P())
    return jax.shard_map(local, mesh=mesh, in_specs=in_specs, out_specs=out_specs, check_vma=False)
```

```python
import jax
import jax.numpy as jnp
from jax import lax
from jax.experimental import pallas as pl
from jax.experimental.pallas import tpu as pltpu
from jax.sharding import PartitionSpec as P

EDGE = 8
PLANE = 256
CELLS = 512
KDIM = 896
TILES = 21
ROWS = 2048
DOWN, NEAR_Y, NEAR_Z, UP, LIVE, DEVICE = 4, 10, 12, 21, 26, 27
F32 = jnp.float32
BF16 = jnp.bfloat16


def spread_matrix(back=False):
    near = lax.broadcasted_iota(jnp.int32, (256, 256), 1 if back else 0)
    far = lax.broadcasted_iota(jnp.int32, (256, 256), 0 if back else 1)
    source = ((far >> 3) & 1) * 128 + (far >> 7) * 64 + ((far >> 4) & 7) * 8 + (far & 7)
    return jnp.where(near == source, 1.0, 0.0).astype(BF16)


def fill_masks(masks):
    lane = lax.broadcasted_iota(jnp.int32, (16, PLANE), 1)
    for k in range(9):
        q, r = (lane >> 4) + (k // 3 - 1), (lane & 15) + (k % 3 - 1)
        inside = (q >= 0) & (q < 16) & (r >= 0) & (r < 16)
        masks[k] = jnp.where(inside, 1.0, 0.0).astype(BF16)


def write_taps(dst, plane, masks_ref):
    channels = plane.shape[0]
    for k in range(9):
        step = (k // 3 - 1) * 16 + (k % 3 - 1)
        if step == 0:
            moved = plane
        else:
            moved = pltpu.roll(plane, (-step) % PLANE, 1)
            moved = moved * jnp.concatenate([masks_ref[k]] * (channels // 16), axis=0)
        dst[k * channels : (k + 1) * channels, :] = moved


def space_index(table, count):
    return jnp.clip(table[DEVICE, 0, 0] & 255, 0, count - 1)


def slot_place(table, slot, pair_slots):
    shift = pair_slots.bit_length() - 1
    up = table[UP, 0, slot]
    inside = jnp.logical_and(up >= 0, up >> shift == slot >> shift)
    parity = jnp.where(inside, 0, 1)
    place = jnp.where(table[NEAR_Y, 0, slot] >= 0, 2, 0) + jnp.where(table[NEAR_Z, 0, slot] >= 0, 1, 0)
    return parity, place


def lane_mask(scalars):
    lane = lax.broadcasted_iota(jnp.int32, (8, PLANE), 1)
    high_y = lane >= 128
    high_z = (lane & 8) != 0
    s = [jnp.full((8, PLANE), v, F32) for v in scalars]
    return jnp.where(high_y, jnp.where(high_z, s[3], s[2]), jnp.where(high_z, s[1], s[0]))


def product(weight_ref, taps, plane_taps=slice(0, 3)):
    left = weight_ref[plane_taps]
    left = left.reshape(left.shape[0] * left.shape[1], KDIM)
    return jnp.dot(left, taps, preferred_element_type=F32)


def pair_sums(full, low, weight_ref, taps, first):
    channels = low.shape[1]
    both = product(weight_ref, taps)
    left, right = both[:, :PLANE], both[:, PLANE:]

    def part(value, a):
        return value[a * channels : (a + 1) * channels]

    before = part(left, 2)
    here = part(left, 1) + part(right, 2)
    full[0] = before if first else low[0] + before
    full[1] = here if first else low[1] + here
    low[0] = part(left, 0) + part(right, 1)
    low[1] = part(right, 0)


def place(k):
    return pl.ds(k * PLANE, PLANE)


def weight_products(total, grads, planes, taps, start=None):
    blank = jnp.zeros_like(grads(3))

    def left(p):
        inside = [grads(p + 1 - a) if 0 <= p + 1 - a < EDGE else blank for a in range(3)]
        return jnp.concatenate(inside, axis=0)

    for first in range(0, KDIM, 256):
        rows = slice(first, min(first + 256, KDIM))
        block = None if start is None else start[:, rows]
        for p in planes:
            both = jnp.concatenate([left(p), left(p + 1)], axis=1)
            part = lax.dot_general(
                both, taps(p, rows), (((1,), (1,)), ((), ())), preferred_element_type=F32
            )
            block = part if block is None else block + part
        total[:, rows] = block


def write_tiles(flat, total, channels, even):
    lane = lax.broadcasted_iota(jnp.int32, (channels, 128), 1)
    blank = jnp.zeros((channels, 128), F32)
    first, last = total[:channels, :], total[2 * channels :, :]
    low, high = jnp.where(even, first, last), jnp.where(even, last, first)
    second = jnp.concatenate([total[channels : 2 * channels, :], blank], axis=1)
    third = jnp.concatenate([high, blank], axis=1)
    second = pltpu.roll(second, 96, 1)
    third = pltpu.roll(third, 64, 1)

    def cut(value, k):
        return value[:, k * 128 : (k + 1) * 128]

    tiles = [cut(low, k) for k in range(6)]
    tiles.append(jnp.where(lane < 96, cut(low, 6), cut(second, 0)))
    tiles += [cut(second, k) for k in range(1, 7)]
    tiles.append(jnp.where(lane < 64, cut(second, 7), cut(third, 0)))
    tiles += [cut(third, k) for k in range(1, 8)]
    for k in range(TILES):
        flat[k * channels : (k + 1) * channels, :] = tiles[k]
    flat[TILES * channels :, :] = jnp.zeros((ROWS - TILES * channels, 128), F32)


def split_tiles(keep_ref, send_ref, flat, table):
    rows = keep_ref.shape[0]
    even = (table[DEVICE, 0, 0] & 1) == 0
    here = pl.multiple_of(jnp.where(even, 0, rows), rows)
    there = pl.multiple_of(jnp.where(even, rows, 0), rows)
    keep_ref[...] = flat[pl.ds(here, rows), :]
    send_ref[...] = flat[pl.ds(there, rows), :].astype(BF16)


def layout_kernel(
    table, own_ref, pair_ref, cot_pair_ref,
    x_ref, cot_ref, edge_ref, mask_ref, bricks, cots,
):
    slots, channels = pair_ref.shape[0], pair_ref.shape[1]
    all_slots = table.shape[2]
    me = space_index(table, all_slots // slots)
    layer = table[DEVICE, 0, 0] >> 16
    even = layer == 0

    live = [[jnp.float32(0)] * 4 for _ in range(2)]
    beyond = [jnp.float32(0)] * 4
    for device in (me, me ^ 1):
        for s in range(slots):
            slot = jnp.clip(device * slots + s, 0, all_slots - 1)
            parity, spot = slot_place(table, slot, 2 * slots)
            alive = table[LIVE, 0, slot].astype(F32)
            scale = jnp.full((channels, CELLS), alive, F32).astype(BF16)
            own = device is me
            bricks[parity, spot] = (own_ref[s] if own else pair_ref[s]) * scale
            cots[parity, spot] = (own_ref[slots + s] if own else cot_pair_ref[s]) * scale
            outer = jnp.where(even, table[DOWN, 0, slot], table[UP, 0, slot])
            alive_outer = table[LIVE, 0, jnp.clip(outer, 0, all_slots - 1)].astype(F32)
            alive_outer = jnp.where(outer >= 0, alive_outer, 0.0)
            for k in range(4):
                for p in range(2):
                    here = jnp.logical_and(parity == p, spot == k)
                    live[p][k] = jnp.where(here, alive, live[p][k])
                here = jnp.logical_and(parity == layer, spot == k)
                beyond[k] = jnp.where(here, alive_outer, beyond[k])
    mask_ref[0] = lane_mask(beyond)
    mask_ref[1] = lane_mask([jnp.where(even, live[0][k], live[1][k]) for k in range(4)])
    mask_ref[2] = lane_mask([jnp.where(even, live[1][k], live[0][k]) for k in range(4)])

    move = spread_matrix()
    mine = jnp.where(even, 0, 1)

    def spread(left, right):
        two = jnp.concatenate([left, right], axis=1)
        return jnp.dot(two, move, preferred_element_type=F32).astype(BF16)

    for y in range(2):
        row = slice(y * 128, (y + 1) * 128)
        for j in range(4):
            pair = slice(j * 128, (j + 1) * 128)
            first = jnp.where(even, 2 * j, 7 - 2 * j)
            second = jnp.where(even, 2 * j + 1, 6 - 2 * j)
            both = spread(bricks[mine, 2 * y, :, pair], bricks[mine, 2 * y + 1, :, pair])
            x_ref[first, :, row] = both[:, :128]
            x_ref[second, :, row] = both[:, 128:]
            both = spread(cots[mine, 2 * y, :, pair], cots[mine, 2 * y + 1, :, pair])
            cot_ref[first, :, row] = both[:, :128]
            cot_ref[second, :, row] = both[:, 128:]
        for j in range(2):
            start = pl.multiple_of(jnp.where(even, j * 128, 256 + j * 128), 128)
            pair = pl.ds(start, 128)
            both = spread(
                bricks[1 - mine, 2 * y, :, pair], bricks[1 - mine, 2 * y + 1, :, pair]
            )
            x_ref[jnp.where(even, 8 + 2 * j, 11 - 2 * j), :, row] = both[:, :128]
            x_ref[jnp.where(even, 9 + 2 * j, 10 - 2 * j), :, row] = both[:, 128:]
        pair = pl.ds(pl.multiple_of(jnp.where(even, 0, 384), 128), 128)
        both = spread(cots[1 - mine, 2 * y, :, pair], cots[1 - mine, 2 * y + 1, :, pair])
        side = jnp.full((channels, 128), jnp.where(even, 1.0, 0.0), F32).astype(BF16)
        cot_ref[8, :, row] = both[:, :128] * side + both[:, 128:] * (1 - side)
    edge_ref[:3] = x_ref[:3]
    edge_ref[3] = cot_ref[0]


def tap_weights(out_ref, weight, wide, even):
    channels, width = weight.shape
    wide[:, :width] = weight
    lane = lax.broadcasted_iota(jnp.int32, (channels, 128), 1)
    for a, (tile, moved) in enumerate(((0, 0), (6, 96), (13, 64))):
        span = wide[:, tile * 128 : (tile + 8) * 128].astype(F32)
        if moved:
            span = pltpu.roll(span, 1024 - moved, 1)
        last = jnp.where(lane < 96, span[:, 768:KDIM], 0.0)
        span = jnp.concatenate([span[:, :768], last], axis=1)
        at = a if a == 1 else jnp.where(even, a, 2 - a)
        out_ref[at] = span.astype(BF16)


def back_weights(out_ref, taps_ref):
    channels = taps_ref.shape[1]
    lane = lax.broadcasted_iota(jnp.int32, (channels, 128), 1)
    more = jnp.zeros((128 - channels, KDIM), F32)
    for a in range(3):
        block = jnp.concatenate([taps_ref[2 - a].astype(F32), more], axis=0)
        turned = block.T
        tiles = [jnp.zeros((channels, 128), F32)] * 7
        for k in range(9):
            piece = turned[(8 - k) * channels : (9 - k) * channels, :]
            tile, moved = divmod(k * channels, 128)
            if moved:
                piece = pltpu.roll(piece, moved, 1)
            tiles[tile] = tiles[tile] + jnp.where(lane >= moved, piece, 0.0)
            if moved + channels > 128:
                tiles[tile + 1] = tiles[tile + 1] + jnp.where(lane < moved, piece, 0.0)
        out_ref[a] = jnp.concatenate(tiles, axis=1).astype(BF16)


def column(row):
    return jnp.broadcast_to(row, (8, row.shape[1])).T[:, :1]


def layer_of(q):
    return 0 if q < 0 else 1 if q < EDGE else 2


def hidden_plane(pre, mask):
    sigma = jax.nn.sigmoid(pre)
    return (pre * sigma * mask).astype(BF16), sigma * (1.0 + pre * (1.0 - sigma)) * mask


def out_plane(pre, mask, cot):
    sigma = jax.nn.sigmoid(pre)
    grad = cot.astype(F32) * (sigma * (1.0 + pre * (1.0 - sigma)))
    return (pre * sigma * mask).astype(BF16), grad.astype(BF16)


def inner_kernel(
    table, x_ref, cot_ref, layer_mask, weight_ref, bias_ref,
    taps_ref, one_ref, two_ref, slope_ref, g_ref, out_ref, total_ref, w1_taps, w2_taps, w2_back,
    wide, xc, hc, full_one, low_one, full_two, low_two, masks_ref,
):
    channels = x_ref.shape[1]
    even = (table[DEVICE, 0, 0] >> 16) == 0
    fill_masks(masks_ref)
    tap_weights(w1_taps, weight_ref[:channels, :], wide, even)
    bias_one, bias_two = column(bias_ref[0:1]), column(bias_ref[1:2])
    ones = jnp.ones((KDIM - 9 * channels, 2 * PLANE), BF16)
    for k in range(2):
        xc[k, 9 * channels :, :] = ones
    for k in range(4):
        taps_ref[9 * channels :, 2 * k * PLANE : (2 * k + 2) * PLANE] = ones
    hc[9 * channels :, :] = ones[:, :PLANE]

    def write_x(p):
        write_taps(xc.at[(p >> 1) & 1, :, place(p & 1)], x_ref[p], masks_ref)

    def finish_one(q, pre):
        hidden, slope = hidden_plane(pre + bias_one, layer_mask[layer_of(q)][:1])
        dst = taps_ref.at[:, place(q - 1)] if q < 9 else hc
        write_taps(dst, hidden, masks_ref)
        if q < EDGE:
            slope_ref[q - 1] = slope

    def finish_two(q, pre):
        out, grad = out_plane(pre + bias_two, layer_mask[layer_of(q)][:1], cot_ref[q])
        g_ref[q - 2] = grad
        if q < EDGE:
            out_ref[q - 2] = out

    write_x(0)
    write_x(1)
    for j in range(8):
        now, last = j & 1, (j + 1) & 1
        if j < 5:
            pair_sums(full_one.at[now], low_one, w1_taps, xc[now], j == 0)
            for p in (2 * j + 2, 2 * j + 3):
                if p <= 10:
                    write_x(p)
        if j == 5:
            third = product(w1_taps, xc[1, :, :PLANE], slice(2, 3))
            full_one[now, 0] = low_one[0] + third
        if j == 0:
            tap_weights(w2_taps, weight_ref[channels:, :], wide, even)
        if j == 1:
            one_ref[...] = full_one[0]
            back_weights(w2_back, w2_taps)
        if 2 <= j <= 5:
            finish_one(2 * j - 3, full_one[last, 0])
            finish_one(2 * j - 2, full_one[last, 1])
        if j == 6:
            finish_one(9, full_one[last, 0])
        if 3 <= j <= 6:
            hidden = taps_ref[:, (2 * j - 6) * PLANE : (2 * j - 4) * PLANE]
            pair_sums(full_two.at[now], low_two, w2_taps, hidden, j == 3)
        if j == 7:
            third = product(w2_taps, hc[...], slice(2, 3))
            finish_two(8, low_two[0] + third)
        if j == 4:
            two_ref[...] = full_two[last]
        if 5 <= j:
            finish_two(2 * j - 8, full_two[last, 0])
            finish_two(2 * j - 7, full_two[last, 1])

    def taps(p, rows):
        return taps_ref[rows, (p - 1) * PLANE : (p + 1) * PLANE]

    weight_products(total_ref, lambda q: g_ref[q - 2], (3, 5), taps)


def outer_kernel(
    table, edge_ref, cot_ref, layer_mask, w1_taps, w2_taps, bias_ref,
    taps_ref, one_ref, two_ref, g_in_ref, total_ref,
    keep_ref, send_ref, slope_ref, g_ref, out_ref,
    xc, hc, x_pair, h_pair, total, flat, masks_ref,
):
    channels = cot_ref.shape[1]
    even = (table[DEVICE, 0, 0] >> 16) == 0
    fill_masks(masks_ref)
    bias_one, bias_two = column(bias_ref[0:1]), column(bias_ref[1:2])
    ones = jnp.ones((KDIM - 9 * channels, 2 * PLANE), BF16)
    for single in (xc, hc):
        single[9 * channels :, :] = ones[:, :PLANE]
    for pair in (x_pair, h_pair):
        pair[9 * channels :, :] = ones
    write_taps(xc, edge_ref[2], masks_ref)
    write_taps(x_pair.at[:, place(0)], edge_ref[1], masks_ref)
    write_taps(x_pair.at[:, place(1)], edge_ref[0], masks_ref)

    def three_planes(weights, single, pair, parts):
        first = product(weights, single[...], slice(0, 1))
        both = product(weights, pair[...])
        left, right = both[:, :PLANE], both[:, PLANE:]
        one, two = slice(channels, 2 * channels), slice(2 * channels, 3 * channels)
        return (
            first + left[one] + right[two],
            left[:channels] + right[one] + parts[0],
            right[:channels] + parts[1],
        )

    for q, pre in zip(range(-2, 1), three_planes(w1_taps, xc, x_pair, one_ref)):
        hidden, slope = hidden_plane(pre + bias_one, layer_mask[layer_of(q)][:1])
        write_taps(hc if q == -2 else h_pair.at[:, place(q + 1)], hidden, masks_ref)
        if q == 0:
            slope_ref[0] = slope
    for q, pre in zip(range(-1, 2), three_planes(w2_taps, hc, h_pair, two_ref)):
        cot = edge_ref[3] if q < 0 else cot_ref[q]
        out, grad = out_plane(pre + bias_two, layer_mask[layer_of(q)][:1], cot)
        g_ref[q + 1] = grad
        if q >= 0:
            out_ref[q] = out

    def grads(q):
        return g_ref[q + 1] if q < 2 else g_in_ref[q - 2]

    def taps(p, rows):
        return h_pair[rows] if p < 0 else taps_ref[rows, (p - 1) * PLANE : (p + 1) * PLANE]

    weight_products(total, grads, (-1, 1, 7), taps, total_ref)
    write_tiles(flat, total, channels, even)
    split_tiles(keep_ref, send_ref, flat, table)


def output_kernel(table, first_ref, second_ref, keep_ref, send_ref, outs, bricks):
    slots, channels = keep_ref.shape[0], keep_ref.shape[1]
    me = space_index(table, table.shape[2] // slots)
    layer = table[DEVICE, 0, 0] >> 16
    even = layer == 0
    outs[:2] = first_ref[...]
    outs[2:] = second_ref[...]
    back = spread_matrix(True)
    for y in range(2):
        row = slice(y * 128, (y + 1) * 128)
        for j in range(4):
            first = jnp.where(even, 2 * j, 7 - 2 * j)
            second = jnp.where(even, 2 * j + 1, 6 - 2 * j)
            two = jnp.concatenate([outs[first, :, row], outs[second, :, row]], axis=1)
            both = jnp.dot(two, back, preferred_element_type=F32).astype(BF16)
            pair = slice(j * 128, (j + 1) * 128)
            bricks[2 * y, :, pair] = both[:, :128]
            bricks[2 * y + 1, :, pair] = both[:, 128:]
    for target, device in ((keep_ref, me), (send_ref, me ^ 1)):
        for s in range(slots):
            slot = jnp.clip(device * slots + s, 0, table.shape[2] - 1)
            parity, spot = slot_place(table, slot, 2 * slots)
            scale = jnp.where(parity == layer, 1.0, 0.0)
            target[s] = bricks[spot] * jnp.full((channels, CELLS), scale, F32).astype(BF16)


def backward_kernel(
    table, g_out_ref, g_in_ref, slope_out_ref, slope_in_ref, x_ref, edge_ref, w2_back,
    keep_ref, send_ref, gc, xc, full, low, grad, total, flat, masks_ref,
):
    channels = x_ref.shape[1]
    even = (table[DEVICE, 0, 0] >> 16) == 0
    fill_masks(masks_ref)
    ones = jnp.ones((KDIM - 9 * channels, 2 * PLANE), BF16)
    for k in range(2):
        gc[k, 9 * channels :, :] = ones
    for k in range(5):
        xc[9 * channels :, 2 * k * PLANE : (2 * k + 2) * PLANE] = ones

    def write_g(q):
        plane = g_out_ref[q + 1] if q < 2 else g_in_ref[q - 2]
        write_taps(gc.at[((q + 1) >> 1) & 1, :, place((q + 1) & 1)], plane, masks_ref)

    write_g(-1)
    write_g(0)
    for j in range(6):
        now, last = j & 1, (j + 1) & 1
        if j < 5:
            pair_sums(full.at[now], low, w2_back, gc[now], j == 0)
            for q in (2 * j + 1, 2 * j + 2):
                if q <= 8:
                    write_g(q)
            for q in (2 * j - 1, 2 * j):
                plane = edge_ref[0] if q < 0 else x_ref[q]
                write_taps(xc.at[:, place(q + 1)], plane, masks_ref)
        if j >= 2:
            for k, q in enumerate((2 * j - 4, 2 * j - 3)):
                slope = slope_out_ref[0] if q == 0 else slope_in_ref[q - 1]
                grad[q] = (full[last, k] * slope).astype(BF16)

    def taps(p, rows):
        return xc[rows, (p + 1) * PLANE : (p + 3) * PLANE]

    weight_products(total, lambda q: grad[q], range(-1, EDGE, 2), taps)
    write_tiles(flat, total, channels, even)
    split_tiles(keep_ref, send_ref, flat, table)


def copies_kernel(first_ref, second_ref, out_ref):
    total = (first_ref[...].astype(F32) + second_ref[...].astype(F32)).astype(BF16)
    for k in range(out_ref.shape[0]):
        out_ref[k] = total


def gather_kernel(
    table, own_ref, other_ref, w_one_ref, w_two_ref, b_one_ref, b_two_ref, flat
):
    chunks, _, rows, _ = own_ref.shape
    channels = w_one_ref.shape[0]
    core = table[DEVICE, 0, 0] & 1
    for half, source in enumerate((own_ref, other_ref)):
        base = jnp.where(core == half, 0, chunks * rows)
        for k in range(chunks):
            at = pl.multiple_of(base + k * rows, rows)
            flat[:, pl.ds(at, rows), :] = source[k]
    for n, (weight, bias) in enumerate(((w_one_ref, b_one_ref), (w_two_ref, b_two_ref))):
        for k in range(TILES - 1):
            tile = flat[n, k * channels : (k + 1) * channels, :]
            weight[:, k * 128 : (k + 1) * 128] = tile.astype(F32)
        last = flat[n, (TILES - 1) * channels : TILES * channels, :].astype(F32)
        weight[:, 2560:2592] = last[:, :32]
        bias[...] = last.T[32:33, :]


VMEM = pl.BlockSpec(memory_space=pltpu.VMEM)
SMEM = pl.BlockSpec(memory_space=pltpu.SMEM)


def vmem(mebibytes):
    return pltpu.CompilerParams(vmem_limit_bytes=mebibytes * 2**20)


def shared_sum(keeps, sends):
    count = lax.axis_size("space")
    volumes = lax.axis_size("dp")
    swap = [(d, d ^ 1) for d in range(count)]
    both = ("space", "dp")
    groups = [
        [(chip * 2 + core) * volumes + first + v for v in range(2) for chip in range(count // 2)]
        for core in range(2)
        for first in range(0, volumes, 2)
    ]
    halves = [
        keep + lax.ppermute(send, "space", swap).astype(F32) for keep, send in zip(keeps, sends)
    ]
    halves = [half.astype(BF16).reshape(count, -1, 128) for half in halves]
    parts = jnp.stack(halves, axis=1)
    parts = lax.all_to_all(parts, both, 0, 0, axis_index_groups=groups)
    total = jnp.sum(parts.astype(F32), axis=0).astype(BF16)
    moved, step = jnp.zeros_like(total), 2
    while step < volumes:
        moved = lax.ppermute(total, "dp", [(v, v ^ step) for v in range(volumes)])
        if step * 2 < volumes:
            total = (total.astype(F32) + moved.astype(F32)).astype(BF16)
        step *= 2
    copies = pl.pallas_call(
        copies_kernel,
        out_shape=jax.ShapeDtypeStruct(parts.shape, BF16),
        in_specs=[VMEM] * 2,
        out_specs=VMEM,
        compiler_params=vmem(8),
        name="copies",
    )(total, moved)
    copies = lax.all_to_all(copies, both, 0, 0, axis_index_groups=groups)
    return [copies, lax.ppermute(copies, "space", swap)]


def local(volume, neighbours, active, cotangent, weight_one, weight_two, bias_one, bias_two):
    volume, cotangent = volume[0], cotangent[0]
    slots, channels = volume.shape[0], volume.shape[1]
    count = lax.axis_size("space")
    me = lax.axis_index("space").astype(jnp.int32)

    swap = [(d, d ^ 1) for d in range(count)]
    at = [2 * (n // 2) + (n & 1 ^ n // 2 & 1) for n in range(count)]
    hop = [(at[n], at[n + 1]) for n in range(1, count - 1, 2)]
    hop += [(there, here) for here, there in hop]
    pair_volume = lax.ppermute(volume, "space", swap)
    pair_cot = lax.ppermute(cotangent, "space", swap)
    biases = jnp.stack([bias_one, bias_two])
    weights = jnp.concatenate([weight_one, weight_two], axis=0)
    own = jnp.concatenate([volume, cotangent], axis=0)
    device = me + 256 * lax.axis_index("dp").astype(jnp.int32)
    device = device + 65536 * ((me ^ (me >> 1)) & 1)
    rows = [neighbours.transpose(2, 0, 1), active[None], jnp.full_like(active, device)[None]]
    table = jnp.concatenate(rows, axis=0)

    def planes(number, dtype=BF16):
        return jax.ShapeDtypeStruct((number, channels, PLANE), dtype)

    def plane_space(number):
        return pltpu.VMEM((number, channels, PLANE), BF16)

    def tap_space(*extent):
        return pltpu.VMEM(extent, BF16)

    def sum_space(*extent):
        return pltpu.VMEM((*extent, channels, PLANE), F32)

    bricks = (slots, channels, CELLS)
    x_planes, cot_planes, edge, layer_mask = pl.pallas_call(
        layout_kernel,
        out_shape=(planes(12), planes(9), planes(4), jax.ShapeDtypeStruct((3, 8, PLANE), F32)),
        in_specs=[SMEM] + [VMEM] * 3,
        out_specs=(VMEM,) * 4,
        scratch_shapes=[
            pltpu.VMEM((2, *bricks), BF16),
            pltpu.VMEM((2, *bricks), BF16),
        ],
        compiler_params=vmem(8),
        name="layout",
    )(table, own, pair_volume, pair_cot)
    outer = lax.ppermute(edge, "space", hop)

    rearranged = jax.ShapeDtypeStruct((3, channels, KDIM), BF16)
    taps, one, two, slope_in, g_in, out_in, part_two, w1, w2, w2_back = pl.pallas_call(
        inner_kernel,
        out_shape=(
            jax.ShapeDtypeStruct((KDIM, EDGE * PLANE), BF16),
            planes(2, F32),
            planes(2, F32),
            planes(7, F32),
            planes(7),
            planes(6),
            jax.ShapeDtypeStruct((3 * channels, KDIM), F32),
            rearranged,
            rearranged,
            rearranged,
        ),
        in_specs=[SMEM] + [VMEM] * 5,
        out_specs=(VMEM,) * 10,
        scratch_shapes=[
            pltpu.VMEM((channels, 21 * 128), BF16),
            tap_space(2, KDIM, 2 * PLANE),
            tap_space(KDIM, PLANE),
            sum_space(2, 2),
            sum_space(2),
            sum_space(2, 2),
            sum_space(2),
            pltpu.VMEM((9, 16, PLANE), BF16),
        ],
        compiler_params=vmem(20),
        cost_estimate=pl.CostEstimate(flops=2**33, bytes_accessed=2**23, transcendentals=2**20),
        name="inner",
    )(table, x_planes, cot_planes, layer_mask, weights, biases)

    rows = (ROWS // 2, 128)
    kept, sent = jax.ShapeDtypeStruct(rows, F32), jax.ShapeDtypeStruct(rows, BF16)
    keep_two, send_two, slope_out, g_out, out_out = pl.pallas_call(
        outer_kernel,
        out_shape=(kept, sent, planes(1, F32), planes(3), planes(2)),
        in_specs=[SMEM] + [VMEM] * 11,
        out_specs=(VMEM,) * 5,
        scratch_shapes=[
            tap_space(KDIM, PLANE),
            tap_space(KDIM, PLANE),
            tap_space(KDIM, 2 * PLANE),
            tap_space(KDIM, 2 * PLANE),
            pltpu.VMEM((3 * channels, KDIM), F32),
            pltpu.VMEM((ROWS, 128), F32),
            pltpu.VMEM((9, 16, PLANE), BF16),
        ],
        compiler_params=vmem(16),
        cost_estimate=pl.CostEstimate(flops=2**32, bytes_accessed=2**23, transcendentals=2**18),
        name="outer",
    )(
        table, outer, cot_planes, layer_mask, w1, w2, biases, taps, one, two, g_in,
        part_two,
    )
    keep_one, send_one = pl.pallas_call(
        backward_kernel,
        out_shape=(kept, sent),
        in_specs=[SMEM] + [VMEM] * 7,
        out_specs=(VMEM,) * 2,
        scratch_shapes=[
            tap_space(2, KDIM, 2 * PLANE),
            tap_space(KDIM, (EDGE + 2) * PLANE),
            sum_space(2, 2),
            sum_space(2),
            plane_space(8),
            pltpu.VMEM((3 * channels, KDIM), F32),
            pltpu.VMEM((ROWS, 128), F32),
            pltpu.VMEM((9, 16, PLANE), BF16),
        ],
        compiler_params=vmem(20),
        cost_estimate=pl.CostEstimate(flops=2**32, bytes_accessed=2**22, transcendentals=0),
        name="backward",
    )(table, g_out, g_in, slope_out, slope_in, x_planes, outer, w2_back)
    keep, send = pl.pallas_call(
        output_kernel,
        out_shape=(jax.ShapeDtypeStruct(bricks, BF16),) * 2,
        in_specs=[SMEM] + [VMEM] * 2,
        out_specs=(VMEM,) * 2,
        scratch_shapes=[plane_space(8), pltpu.VMEM(bricks, BF16)],
        compiler_params=vmem(8),
        cost_estimate=pl.CostEstimate(flops=2**28, bytes_accessed=2**21, transcendentals=0),
        name="output",
    )(table, out_out, out_in)
    output = (keep + lax.ppermute(send, "space", swap))[None]
    parts = shared_sum([keep_one, keep_two], [send_one, send_two])
    weight_shape = jax.ShapeDtypeStruct((channels, 27 * channels), F32)
    bias_shape = jax.ShapeDtypeStruct((1, channels), F32)
    total_w_one, total_w_two, total_b_one, total_b_two = pl.pallas_call(
        gather_kernel,
        out_shape=(weight_shape, weight_shape, bias_shape, bias_shape),
        in_specs=[SMEM] + [VMEM] * len(parts),
        out_specs=(VMEM,) * 4,
        scratch_shapes=[pltpu.VMEM((2, ROWS, 128), BF16)],
        compiler_params=vmem(8),
        name="gather",
    )(table, *parts)
    return (output, total_w_one, total_w_two, total_b_one[0], total_b_two[0])


def solution(mesh):
    in_specs = (
        P("dp", "space", None, None),
        P("dp", None, None),
        P("dp", None),
        P("dp", "space", None, None),
        P(),
        P(),
        P(),
        P(),
    )
    out_specs = (P("dp", "space", None, None), P(), P(), P(), P())
    return jax.shard_map(local, mesh=mesh, in_specs=in_specs, out_specs=out_specs, check_vma=False)
```

```python
import jax
import jax.numpy as jnp
from jax import lax
from jax.experimental import pallas as pl
from jax.experimental.pallas import tpu as pltpu
from jax.sharding import PartitionSpec as P

EDGE = 8
PLANE = 256
CELLS = 512
KDIM = 896
TILES = 21
ROWS = 2048
DOWN, NEAR_Y, NEAR_Z, UP, LIVE = 4, 10, 12, 21, 26
F32 = jnp.float32
BF16 = jnp.bfloat16


def spread_matrix(back=False):
    near = lax.broadcasted_iota(jnp.int32, (256, 256), 1 if back else 0)
    far = lax.broadcasted_iota(jnp.int32, (256, 256), 0 if back else 1)
    source = ((far >> 3) & 1) * 128 + (far >> 7) * 64 + ((far >> 4) & 7) * 8 + (far & 7)
    return jnp.where(near == source, 1.0, 0.0).astype(BF16)


def fill_masks(masks):
    lane = lax.broadcasted_iota(jnp.int32, (16, PLANE), 1)
    for k in range(9):
        q, r = (lane >> 4) + (k // 3 - 1), (lane & 15) + (k % 3 - 1)
        inside = (q >= 0) & (q < 16) & (r >= 0) & (r < 16)
        masks[k] = jnp.where(inside, 1.0, 0.0).astype(BF16)


def write_taps(dst, plane, masks_ref):
    channels = plane.shape[0]
    for k in range(9):
        step = (k // 3 - 1) * 16 + (k % 3 - 1)
        if step == 0:
            moved = plane
        else:
            moved = pltpu.roll(plane, (-step) % PLANE, 1)
            moved = moved * jnp.concatenate([masks_ref[k]] * (channels // 16), axis=0)
        dst[k * channels : (k + 1) * channels, :] = moved


def space_index(device, count):
    return jnp.clip(device[0] >> 1, 0, count - 1)


def layer_side(device):
    return device[0] & 1


def core_of(device):
    return (device[0] >> 1) & 1


def slot_place(table, slot, pair_slots):
    shift = pair_slots.bit_length() - 1
    up = table[UP, 0, slot]
    inside = jnp.logical_and(up >= 0, up >> shift == slot >> shift)
    parity = jnp.where(inside, 0, 1)
    place = jnp.where(table[NEAR_Y, 0, slot] >= 0, 2, 0) + jnp.where(table[NEAR_Z, 0, slot] >= 0, 1, 0)
    return parity, place


def lane_mask(scalars):
    lane = lax.broadcasted_iota(jnp.int32, (8, PLANE), 1)
    high_y = lane >= 128
    high_z = (lane & 8) != 0
    s = [jnp.full((8, PLANE), v, F32) for v in scalars]
    return jnp.where(high_y, jnp.where(high_z, s[3], s[2]), jnp.where(high_z, s[1], s[0]))


def product(weight_ref, taps, plane_taps=slice(0, 3)):
    left = weight_ref[plane_taps]
    left = left.reshape(left.shape[0] * left.shape[1], KDIM)
    return jnp.dot(left, taps, preferred_element_type=F32)


def pair_sums(full, low, weight_ref, taps, first):
    channels = low.shape[1]
    both = product(weight_ref, taps)
    left, right = both[:, :PLANE], both[:, PLANE:]

    def part(value, a):
        return value[a * channels : (a + 1) * channels]

    before = part(left, 2)
    here = part(left, 1) + part(right, 2)
    full[0] = before if first else low[0] + before
    full[1] = here if first else low[1] + here
    low[0] = part(left, 0) + part(right, 1)
    low[1] = part(right, 0)


def place(k):
    return pl.ds(k * PLANE, PLANE)


def weight_products(total, grads, planes, taps, start=None):
    blank = jnp.zeros_like(grads(3))

    def left(p):
        inside = [grads(p + 1 - a) if 0 <= p + 1 - a < EDGE else blank for a in range(3)]
        return jnp.concatenate(inside, axis=0)

    for first in range(0, KDIM, 256):
        rows = slice(first, min(first + 256, KDIM))
        block = None if start is None else start[:, rows]
        for p in planes:
            both = jnp.concatenate([left(p), left(p + 1)], axis=1)
            part = lax.dot_general(
                both, taps(p, rows), (((1,), (1,)), ((), ())), preferred_element_type=F32
            )
            block = part if block is None else block + part
        total[:, rows] = block


def write_tiles(flat, total, channels, even):
    lane = lax.broadcasted_iota(jnp.int32, (channels, 128), 1)
    blank = jnp.zeros((channels, 128), F32)
    first, last = total[:channels, :], total[2 * channels :, :]
    low, high = jnp.where(even, first, last), jnp.where(even, last, first)
    second = jnp.concatenate([total[channels : 2 * channels, :], blank], axis=1)
    third = jnp.concatenate([high, blank], axis=1)
    second = pltpu.roll(second, 96, 1)
    third = pltpu.roll(third, 64, 1)

    def cut(value, k):
        return value[:, k * 128 : (k + 1) * 128]

    tiles = [cut(low, k) for k in range(6)]
    tiles.append(jnp.where(lane < 96, cut(low, 6), cut(second, 0)))
    tiles += [cut(second, k) for k in range(1, 7)]
    tiles.append(jnp.where(lane < 64, cut(second, 7), cut(third, 0)))
    tiles += [cut(third, k) for k in range(1, 8)]
    for k in range(TILES):
        flat[k * channels : (k + 1) * channels, :] = tiles[k]
    flat[TILES * channels :, :] = jnp.zeros((ROWS - TILES * channels, 128), F32)


def split_tiles(keep_ref, send_ref, flat, device):
    rows = keep_ref.shape[0]
    even = core_of(device) == 0
    here = pl.multiple_of(jnp.where(even, 0, rows), rows)
    there = pl.multiple_of(jnp.where(even, rows, 0), rows)
    keep_ref[...] = flat[pl.ds(here, rows), :]
    send_ref[...] = flat[pl.ds(there, rows), :].astype(BF16)


def layout_kernel(
    device, table, own_ref, pair_ref, cot_pair_ref,
    x_ref, cot_ref, edge_ref, mask_ref, bricks, cots,
):
    slots, channels = pair_ref.shape[0], pair_ref.shape[1]
    all_slots = table.shape[2]
    me = space_index(device, all_slots // slots)
    layer = layer_side(device)
    even = layer == 0

    live = [[jnp.float32(0)] * 4 for _ in range(2)]
    beyond = [jnp.float32(0)] * 4
    for index in (me, me ^ 1):
        for s in range(slots):
            slot = jnp.clip(index * slots + s, 0, all_slots - 1)
            parity, spot = slot_place(table, slot, 2 * slots)
            alive = table[LIVE, 0, slot].astype(F32)
            scale = jnp.full((channels, CELLS), alive, F32).astype(BF16)
            own = index is me
            bricks[parity, spot] = (own_ref[s] if own else pair_ref[s]) * scale
            cots[parity, spot] = (own_ref[slots + s] if own else cot_pair_ref[s]) * scale
            outer = jnp.where(even, table[DOWN, 0, slot], table[UP, 0, slot])
            alive_outer = table[LIVE, 0, jnp.clip(outer, 0, all_slots - 1)].astype(F32)
            alive_outer = jnp.where(outer >= 0, alive_outer, 0.0)
            for k in range(4):
                for p in range(2):
                    here = jnp.logical_and(parity == p, spot == k)
                    live[p][k] = jnp.where(here, alive, live[p][k])
                here = jnp.logical_and(parity == layer, spot == k)
                beyond[k] = jnp.where(here, alive_outer, beyond[k])
    mask_ref[0] = lane_mask(beyond)
    mask_ref[1] = lane_mask([jnp.where(even, live[0][k], live[1][k]) for k in range(4)])
    mask_ref[2] = lane_mask([jnp.where(even, live[1][k], live[0][k]) for k in range(4)])

    move = spread_matrix()
    mine = jnp.where(even, 0, 1)

    def spread(left, right):
        two = jnp.concatenate([left, right], axis=1)
        return jnp.dot(two, move, preferred_element_type=F32).astype(BF16)

    for y in range(2):
        row = slice(y * 128, (y + 1) * 128)
        for j in range(4):
            pair = slice(j * 128, (j + 1) * 128)
            first = jnp.where(even, 2 * j, 7 - 2 * j)
            second = jnp.where(even, 2 * j + 1, 6 - 2 * j)
            both = spread(bricks[mine, 2 * y, :, pair], bricks[mine, 2 * y + 1, :, pair])
            x_ref[first, :, row] = both[:, :128]
            x_ref[second, :, row] = both[:, 128:]
            both = spread(cots[mine, 2 * y, :, pair], cots[mine, 2 * y + 1, :, pair])
            cot_ref[first, :, row] = both[:, :128]
            cot_ref[second, :, row] = both[:, 128:]
        for j in range(2):
            start = pl.multiple_of(jnp.where(even, j * 128, 256 + j * 128), 128)
            pair = pl.ds(start, 128)
            both = spread(
                bricks[1 - mine, 2 * y, :, pair], bricks[1 - mine, 2 * y + 1, :, pair]
            )
            x_ref[jnp.where(even, 8 + 2 * j, 11 - 2 * j), :, row] = both[:, :128]
            x_ref[jnp.where(even, 9 + 2 * j, 10 - 2 * j), :, row] = both[:, 128:]
        pair = pl.ds(pl.multiple_of(jnp.where(even, 0, 384), 128), 128)
        both = spread(cots[1 - mine, 2 * y, :, pair], cots[1 - mine, 2 * y + 1, :, pair])
        side = jnp.full((channels, 128), jnp.where(even, 1.0, 0.0), F32).astype(BF16)
        cot_ref[8, :, row] = both[:, :128] * side + both[:, 128:] * (1 - side)
    edge_ref[:3] = x_ref[:3]
    edge_ref[3] = cot_ref[0]


def tap_weights(out_ref, weight, wide, even):
    channels, width = weight.shape
    wide[:, :width] = weight
    lane = lax.broadcasted_iota(jnp.int32, (channels, 128), 1)
    for a, (tile, moved) in enumerate(((0, 0), (6, 96), (13, 64))):
        span = wide[:, tile * 128 : (tile + 8) * 128].astype(F32)
        if moved:
            span = pltpu.roll(span, 1024 - moved, 1)
        last = jnp.where(lane < 96, span[:, 768:KDIM], 0.0)
        span = jnp.concatenate([span[:, :768], last], axis=1)
        at = a if a == 1 else jnp.where(even, a, 2 - a)
        out_ref[at] = span.astype(BF16)


def back_weights(out_ref, taps_ref):
    channels = taps_ref.shape[1]
    lane = lax.broadcasted_iota(jnp.int32, (channels, 128), 1)
    more = jnp.zeros((128 - channels, KDIM), F32)
    for a in range(3):
        block = jnp.concatenate([taps_ref[2 - a].astype(F32), more], axis=0)
        turned = block.T
        tiles = [jnp.zeros((channels, 128), F32)] * 7
        for k in range(9):
            piece = turned[(8 - k) * channels : (9 - k) * channels, :]
            tile, moved = divmod(k * channels, 128)
            if moved:
                piece = pltpu.roll(piece, moved, 1)
            tiles[tile] = tiles[tile] + jnp.where(lane >= moved, piece, 0.0)
            if moved + channels > 128:
                tiles[tile + 1] = tiles[tile + 1] + jnp.where(lane < moved, piece, 0.0)
        out_ref[a] = jnp.concatenate(tiles, axis=1).astype(BF16)


def column(row):
    return jnp.broadcast_to(row, (8, row.shape[1])).T[:, :1]


def layer_of(q):
    return 0 if q < 0 else 1 if q < EDGE else 2


def hidden_plane(pre, mask):
    sigma = jax.nn.sigmoid(pre)
    return (pre * sigma * mask).astype(BF16), sigma * (1.0 + pre * (1.0 - sigma)) * mask


def out_plane(pre, mask, cot):
    sigma = jax.nn.sigmoid(pre)
    grad = cot.astype(F32) * (sigma * (1.0 + pre * (1.0 - sigma)))
    return (pre * sigma * mask).astype(BF16), grad.astype(BF16)


def inner_kernel(
    device, x_ref, cot_ref, layer_mask, weight_ref, bias_ref,
    taps_ref, one_ref, two_ref, slope_ref, g_ref, out_ref, total_ref, w1_taps, w2_taps, w2_back,
    wide, xc, hc, full_one, low_one, full_two, low_two, masks_ref,
):
    channels = x_ref.shape[1]
    even = layer_side(device) == 0
    fill_masks(masks_ref)
    tap_weights(w1_taps, weight_ref[:channels, :], wide, even)
    bias_one, bias_two = column(bias_ref[0:1]), column(bias_ref[1:2])
    ones = jnp.ones((KDIM - 9 * channels, 2 * PLANE), BF16)
    for k in range(2):
        xc[k, 9 * channels :, :] = ones
    for k in range(4):
        taps_ref[k, 9 * channels :, :] = ones
    hc[9 * channels :, :] = ones[:, :PLANE]

    def write_x(p):
        write_taps(xc.at[(p >> 1) & 1, :, place(p & 1)], x_ref[p], masks_ref)

    def finish_one(q, pre):
        hidden, slope = hidden_plane(pre + bias_one, layer_mask[layer_of(q)][:1])
        dst = taps_ref.at[(q - 1) // 2, :, place((q - 1) & 1)] if q < 9 else hc
        write_taps(dst, hidden, masks_ref)
        if q < EDGE:
            slope_ref[q - 1] = slope

    def finish_two(q, pre):
        out, grad = out_plane(pre + bias_two, layer_mask[layer_of(q)][:1], cot_ref[q])
        g_ref[q - 2] = grad
        if q < EDGE:
            out_ref[q - 2] = out

    write_x(0)
    write_x(1)
    for j in range(8):
        now, last = j & 1, (j + 1) & 1
        if j < 5:
            pair_sums(full_one.at[now], low_one, w1_taps, xc[now], j == 0)
            for p in (2 * j + 2, 2 * j + 3):
                if p <= 10:
                    write_x(p)
        if j == 5:
            third = product(w1_taps, xc[1, :, :PLANE], slice(2, 3))
            full_one[now, 0] = low_one[0] + third
        if j == 0:
            tap_weights(w2_taps, weight_ref[channels:, :], wide, even)
        if j == 1:
            one_ref[...] = full_one[0]
            back_weights(w2_back, w2_taps)
        if 2 <= j <= 5:
            finish_one(2 * j - 3, full_one[last, 0])
            finish_one(2 * j - 2, full_one[last, 1])
        if j == 6:
            finish_one(9, full_one[last, 0])
        if 3 <= j <= 6:
            pair_sums(full_two.at[now], low_two, w2_taps, taps_ref[j - 3], j == 3)
        if j == 7:
            third = product(w2_taps, hc[...], slice(2, 3))
            finish_two(8, low_two[0] + third)
        if j == 4:
            two_ref[...] = full_two[last]
        if 5 <= j:
            finish_two(2 * j - 8, full_two[last, 0])
            finish_two(2 * j - 7, full_two[last, 1])

    def taps(p, rows):
        return taps_ref[p // 2, rows]

    weight_products(total_ref, lambda q: g_ref[q - 2], (3, 5), taps)


def outer_kernel(
    device, edge_ref, cot_ref, layer_mask, w1_taps, w2_taps, bias_ref,
    taps_ref, one_ref, two_ref, g_in_ref, total_ref,
    keep_ref, send_ref, slope_ref, g_ref, out_ref,
    xc, hc, x_pair, h_pair, total, flat, masks_ref,
):
    channels = cot_ref.shape[1]
    even = layer_side(device) == 0
    fill_masks(masks_ref)
    bias_one, bias_two = column(bias_ref[0:1]), column(bias_ref[1:2])
    ones = jnp.ones((KDIM - 9 * channels, 2 * PLANE), BF16)
    for single in (xc, hc):
        single[9 * channels :, :] = ones[:, :PLANE]
    for pair in (x_pair, h_pair):
        pair[9 * channels :, :] = ones
    write_taps(xc, edge_ref[2], masks_ref)
    write_taps(x_pair.at[:, place(0)], edge_ref[1], masks_ref)
    write_taps(x_pair.at[:, place(1)], edge_ref[0], masks_ref)

    def three_planes(weights, single, pair, parts):
        first = product(weights, single[...], slice(0, 1))
        both = product(weights, pair[...])
        left, right = both[:, :PLANE], both[:, PLANE:]
        one, two = slice(channels, 2 * channels), slice(2 * channels, 3 * channels)
        return (
            first + left[one] + right[two],
            left[:channels] + right[one] + parts[0],
            right[:channels] + parts[1],
        )

    for q, pre in zip(range(-2, 1), three_planes(w1_taps, xc, x_pair, one_ref)):
        hidden, slope = hidden_plane(pre + bias_one, layer_mask[layer_of(q)][:1])
        write_taps(hc if q == -2 else h_pair.at[:, place(q + 1)], hidden, masks_ref)
        if q == 0:
            slope_ref[0] = slope
    for q, pre in zip(range(-1, 2), three_planes(w2_taps, hc, h_pair, two_ref)):
        cot = edge_ref[3] if q < 0 else cot_ref[q]
        out, grad = out_plane(pre + bias_two, layer_mask[layer_of(q)][:1], cot)
        g_ref[q + 1] = grad
        if q >= 0:
            out_ref[q] = out

    def grads(q):
        return g_ref[q + 1] if q < 2 else g_in_ref[q - 2]

    def taps(p, rows):
        return h_pair[rows] if p < 0 else taps_ref[p // 2, rows]

    weight_products(total, grads, (-1, 1, 7), taps, total_ref)
    write_tiles(flat, total, channels, even)
    split_tiles(keep_ref, send_ref, flat, device)


def output_kernel(device, table, first_ref, second_ref, keep_ref, send_ref, outs, bricks):
    slots, channels = keep_ref.shape[0], keep_ref.shape[1]
    me = space_index(device, table.shape[2] // slots)
    layer = layer_side(device)
    even = layer == 0
    outs[:2] = first_ref[...]
    outs[2:] = second_ref[...]
    back = spread_matrix(True)
    for y in range(2):
        row = slice(y * 128, (y + 1) * 128)
        for j in range(4):
            first = jnp.where(even, 2 * j, 7 - 2 * j)
            second = jnp.where(even, 2 * j + 1, 6 - 2 * j)
            two = jnp.concatenate([outs[first, :, row], outs[second, :, row]], axis=1)
            both = jnp.dot(two, back, preferred_element_type=F32).astype(BF16)
            pair = slice(j * 128, (j + 1) * 128)
            bricks[2 * y, :, pair] = both[:, :128]
            bricks[2 * y + 1, :, pair] = both[:, 128:]
    for target, index in ((keep_ref, me), (send_ref, me ^ 1)):
        for s in range(slots):
            slot = jnp.clip(index * slots + s, 0, table.shape[2] - 1)
            parity, spot = slot_place(table, slot, 2 * slots)
            scale = jnp.where(parity == layer, 1.0, 0.0)
            target[s] = bricks[spot] * jnp.full((channels, CELLS), scale, F32).astype(BF16)


def backward_kernel(
    device, g_out_ref, g_in_ref, slope_out_ref, slope_in_ref, x_ref, edge_ref, w2_back,
    keep_ref, send_ref, gc, xc, full, low, grad, total, flat, masks_ref,
):
    channels = x_ref.shape[1]
    even = layer_side(device) == 0
    fill_masks(masks_ref)
    ones = jnp.ones((KDIM - 9 * channels, 2 * PLANE), BF16)
    for k in range(2):
        gc[k, 9 * channels :, :] = ones
    for k in range(5):
        xc[k, 9 * channels :, :] = ones

    def write_g(q):
        plane = g_out_ref[q + 1] if q < 2 else g_in_ref[q - 2]
        write_taps(gc.at[((q + 1) >> 1) & 1, :, place((q + 1) & 1)], plane, masks_ref)

    write_g(-1)
    write_g(0)
    for j in range(6):
        now, last = j & 1, (j + 1) & 1
        if j < 5:
            pair_sums(full.at[now], low, w2_back, gc[now], j == 0)
            for q in (2 * j + 1, 2 * j + 2):
                if q <= 8:
                    write_g(q)
            for q in (2 * j - 1, 2 * j):
                plane = edge_ref[0] if q < 0 else x_ref[q]
                write_taps(xc.at[j, :, place((q + 1) & 1)], plane, masks_ref)
        if j >= 2:
            for k, q in enumerate((2 * j - 4, 2 * j - 3)):
                slope = slope_out_ref[0] if q == 0 else slope_in_ref[q - 1]
                grad[q] = (full[last, k] * slope).astype(BF16)

    def taps(p, rows):
        return xc[(p + 1) // 2, rows]

    weight_products(total, lambda q: grad[q], range(-1, EDGE, 2), taps)
    write_tiles(flat, total, channels, even)
    split_tiles(keep_ref, send_ref, flat, device)


def copies_kernel(first_ref, second_ref, out_ref):
    total = (first_ref[...].astype(F32) + second_ref[...].astype(F32)).astype(BF16)
    for k in range(out_ref.shape[0]):
        out_ref[k] = total


def gather_kernel(
    device, own_ref, other_ref, w_one_ref, w_two_ref, b_one_ref, b_two_ref, flat
):
    chunks, _, rows, _ = own_ref.shape
    channels = w_one_ref.shape[0]
    core = core_of(device)
    for half, source in enumerate((own_ref, other_ref)):
        base = jnp.where(core == half, 0, chunks * rows)
        for k in range(chunks):
            at = pl.multiple_of(base + k * rows, rows)
            flat[:, pl.ds(at, rows), :] = source[k]
    for n, (weight, bias) in enumerate(((w_one_ref, b_one_ref), (w_two_ref, b_two_ref))):
        for k in range(TILES - 1):
            tile = flat[n, k * channels : (k + 1) * channels, :]
            weight[:, k * 128 : (k + 1) * 128] = tile.astype(F32)
        last = flat[n, (TILES - 1) * channels : TILES * channels, :].astype(F32)
        weight[:, 2560:2592] = last[:, :32]
        bias[...] = last.T[32:33, :]


VMEM = pl.BlockSpec(memory_space=pltpu.VMEM)
SMEM = pl.BlockSpec(memory_space=pltpu.SMEM)


def vmem(mebibytes):
    return pltpu.CompilerParams(vmem_limit_bytes=mebibytes * 2**20)


def shared_sum(keeps, sends):
    count = lax.axis_size("space")
    volumes = lax.axis_size("dp")
    swap = [(d, d ^ 1) for d in range(count)]
    both = ("space", "dp")
    groups = [
        [(chip * 2 + core) * volumes + first + v for v in range(2) for chip in range(count // 2)]
        for core in range(2)
        for first in range(0, volumes, 2)
    ]
    halves = [
        keep + lax.ppermute(send, "space", swap).astype(F32) for keep, send in zip(keeps, sends)
    ]
    halves = [half.astype(BF16).reshape(count, -1, 128) for half in halves]
    parts = jnp.stack(halves, axis=1)
    parts = lax.all_to_all(parts, both, 0, 0, axis_index_groups=groups)
    total = jnp.sum(parts.astype(F32), axis=0).astype(BF16)
    moved, step = jnp.zeros_like(total), 2
    while step < volumes:
        moved = lax.ppermute(total, "dp", [(v, v ^ step) for v in range(volumes)])
        if step * 2 < volumes:
            total = (total.astype(F32) + moved.astype(F32)).astype(BF16)
        step *= 2
    copies = pl.pallas_call(
        copies_kernel,
        out_shape=jax.ShapeDtypeStruct(parts.shape, BF16),
        in_specs=[VMEM] * 2,
        out_specs=VMEM,
        compiler_params=vmem(8),
        name="copies",
    )(total, moved)
    copies = lax.all_to_all(copies, both, 0, 0, axis_index_groups=groups)
    return [copies, lax.ppermute(copies, "space", swap)]


def local(volume, neighbours, active, cotangent, weight_one, weight_two, bias_one, bias_two):
    volume, cotangent = volume[0], cotangent[0]
    slots, channels = volume.shape[0], volume.shape[1]
    count = lax.axis_size("space")
    me = lax.axis_index("space").astype(jnp.int32)

    swap = [(d, d ^ 1) for d in range(count)]
    at = [2 * (n // 2) + (n & 1 ^ n // 2 & 1) for n in range(count)]
    hop = [(at[n], at[n + 1]) for n in range(1, count - 1, 2)]
    hop += [(there, here) for here, there in hop]
    pair_volume = lax.ppermute(volume, "space", swap)
    pair_cot = lax.ppermute(cotangent, "space", swap)
    biases = jnp.stack([bias_one, bias_two])
    weights = jnp.concatenate([weight_one, weight_two], axis=0)
    own = jnp.concatenate([volume, cotangent], axis=0)
    device = (2 * me + ((me ^ (me >> 1)) & 1))[None]
    table = jnp.concatenate([neighbours.transpose(2, 0, 1), active[None]], axis=0)

    def planes(number, dtype=BF16):
        return jax.ShapeDtypeStruct((number, channels, PLANE), dtype)

    def plane_space(number):
        return pltpu.VMEM((number, channels, PLANE), BF16)

    def tap_space(*extent):
        return pltpu.VMEM(extent, BF16)

    def sum_space(*extent):
        return pltpu.VMEM((*extent, channels, PLANE), F32)

    bricks = (slots, channels, CELLS)
    x_planes, cot_planes, edge, layer_mask = pl.pallas_call(
        layout_kernel,
        out_shape=(planes(12), planes(9), planes(4), jax.ShapeDtypeStruct((3, 8, PLANE), F32)),
        in_specs=[SMEM] * 2 + [VMEM] * 3,
        out_specs=(VMEM,) * 4,
        scratch_shapes=[
            pltpu.VMEM((2, *bricks), BF16),
            pltpu.VMEM((2, *bricks), BF16),
        ],
        compiler_params=vmem(8),
        name="layout",
    )(device, table, own, pair_volume, pair_cot)
    outer = lax.ppermute(edge, "space", hop)

    rearranged = jax.ShapeDtypeStruct((3, channels, KDIM), BF16)
    taps, one, two, slope_in, g_in, out_in, part_two, w1, w2, w2_back = pl.pallas_call(
        inner_kernel,
        out_shape=(
            jax.ShapeDtypeStruct((4, KDIM, 2 * PLANE), BF16),
            planes(2, F32),
            planes(2, F32),
            planes(7, F32),
            planes(7),
            planes(6),
            jax.ShapeDtypeStruct((3 * channels, KDIM), F32),
            rearranged,
            rearranged,
            rearranged,
        ),
        in_specs=[SMEM] + [VMEM] * 5,
        out_specs=(VMEM,) * 10,
        scratch_shapes=[
            pltpu.VMEM((channels, 21 * 128), BF16),
            tap_space(2, KDIM, 2 * PLANE),
            tap_space(KDIM, PLANE),
            sum_space(2, 2),
            sum_space(2),
            sum_space(2, 2),
            sum_space(2),
            pltpu.VMEM((9, 16, PLANE), BF16),
        ],
        compiler_params=vmem(20),
        cost_estimate=pl.CostEstimate(flops=2**33, bytes_accessed=2**23, transcendentals=2**20),
        name="inner",
    )(device, x_planes, cot_planes, layer_mask, weights, biases)

    rows = (ROWS // 2, 128)
    kept, sent = jax.ShapeDtypeStruct(rows, F32), jax.ShapeDtypeStruct(rows, BF16)
    keep_two, send_two, slope_out, g_out, out_out = pl.pallas_call(
        outer_kernel,
        out_shape=(kept, sent, planes(1, F32), planes(3), planes(2)),
        in_specs=[SMEM] + [VMEM] * 11,
        out_specs=(VMEM,) * 5,
        scratch_shapes=[
            tap_space(KDIM, PLANE),
            tap_space(KDIM, PLANE),
            tap_space(KDIM, 2 * PLANE),
            tap_space(KDIM, 2 * PLANE),
            pltpu.VMEM((3 * channels, KDIM), F32),
            pltpu.VMEM((ROWS, 128), F32),
            pltpu.VMEM((9, 16, PLANE), BF16),
        ],
        compiler_params=vmem(16),
        cost_estimate=pl.CostEstimate(flops=2**32, bytes_accessed=2**23, transcendentals=2**18),
        name="outer",
    )(
        device, outer, cot_planes, layer_mask, w1, w2, biases, taps, one, two, g_in,
        part_two,
    )
    keep_one, send_one = pl.pallas_call(
        backward_kernel,
        out_shape=(kept, sent),
        in_specs=[SMEM] + [VMEM] * 7,
        out_specs=(VMEM,) * 2,
        scratch_shapes=[
            tap_space(2, KDIM, 2 * PLANE),
            tap_space(5, KDIM, 2 * PLANE),
            sum_space(2, 2),
            sum_space(2),
            plane_space(8),
            pltpu.VMEM((3 * channels, KDIM), F32),
            pltpu.VMEM((ROWS, 128), F32),
            pltpu.VMEM((9, 16, PLANE), BF16),
        ],
        compiler_params=vmem(20),
        cost_estimate=pl.CostEstimate(flops=2**32, bytes_accessed=2**22, transcendentals=0),
        name="backward",
    )(device, g_out, g_in, slope_out, slope_in, x_planes, outer, w2_back)
    keep, send = pl.pallas_call(
        output_kernel,
        out_shape=(jax.ShapeDtypeStruct(bricks, BF16),) * 2,
        in_specs=[SMEM] * 2 + [VMEM] * 2,
        out_specs=(VMEM,) * 2,
        scratch_shapes=[plane_space(8), pltpu.VMEM(bricks, BF16)],
        compiler_params=vmem(8),
        cost_estimate=pl.CostEstimate(flops=2**28, bytes_accessed=2**21, transcendentals=0),
        name="output",
    )(device, table, out_out, out_in)
    output = (keep + lax.ppermute(send, "space", swap))[None]
    parts = shared_sum([keep_one, keep_two], [send_one, send_two])
    weight_shape = jax.ShapeDtypeStruct((channels, 27 * channels), F32)
    bias_shape = jax.ShapeDtypeStruct((1, channels), F32)
    total_w_one, total_w_two, total_b_one, total_b_two = pl.pallas_call(
        gather_kernel,
        out_shape=(weight_shape, weight_shape, bias_shape, bias_shape),
        in_specs=[SMEM] + [VMEM] * len(parts),
        out_specs=(VMEM,) * 4,
        scratch_shapes=[pltpu.VMEM((2, ROWS, 128), BF16)],
        compiler_params=vmem(8),
        name="gather",
    )(device, *parts)
    return (output, total_w_one, total_w_two, total_b_one[0], total_b_two[0])


def solution(mesh):
    in_specs = (
        P("dp", "space", None, None),
        P("dp", None, None),
        P("dp", None),
        P("dp", "space", None, None),
        P(),
        P(),
        P(),
        P(),
    )
    out_specs = (P("dp", "space", None, None), P(), P(), P(), P())
    return jax.shard_map(local, mesh=mesh, in_specs=in_specs, out_specs=out_specs, check_vma=False)
```

```python
import jax
import jax.numpy as jnp
from jax import lax
from jax.experimental import pallas as pl
from jax.experimental.pallas import tpu as pltpu
from jax.sharding import PartitionSpec as P

EDGE = 8
PLANE = 256
CELLS = 512
KDIM = 896
TILES = 21
ROWS = 2048
DOWN, NEAR_Y, NEAR_Z, UP, LIVE = 4, 10, 12, 21, 26
F32 = jnp.float32
BF16 = jnp.bfloat16


def spread_matrix(back=False):
    near = lax.broadcasted_iota(jnp.int32, (256, 256), 1 if back else 0)
    far = lax.broadcasted_iota(jnp.int32, (256, 256), 0 if back else 1)
    source = ((far >> 3) & 1) * 128 + (far >> 7) * 64 + ((far >> 4) & 7) * 8 + (far & 7)
    return jnp.where(near == source, 1.0, 0.0).astype(BF16)


def fill_masks(masks):
    lane = lax.broadcasted_iota(jnp.int32, (16, PLANE), 1)
    for k in range(9):
        q, r = (lane >> 4) + (k // 3 - 1), (lane & 15) + (k % 3 - 1)
        inside = (q >= 0) & (q < 16) & (r >= 0) & (r < 16)
        masks[k] = jnp.where(inside, 1.0, 0.0).astype(BF16)


def write_taps(dst, plane, masks_ref):
    channels = plane.shape[0]
    for k in range(9):
        step = (k // 3 - 1) * 16 + (k % 3 - 1)
        if step == 0:
            moved = plane
        else:
            moved = pltpu.roll(plane, (-step) % PLANE, 1)
            moved = moved * jnp.concatenate([masks_ref[k]] * (channels // 16), axis=0)
        dst[k * channels : (k + 1) * channels, :] = moved


def space_index(device, count):
    return jnp.clip(device[0] >> 1, 0, count - 1)


def layer_side(device):
    return device[0] & 1


def core_of(device):
    return (device[0] >> 1) & 1


def slot_place(table, slot, pair_slots):
    shift = pair_slots.bit_length() - 1
    up = table[UP, 0, slot]
    inside = jnp.logical_and(up >= 0, up >> shift == slot >> shift)
    parity = jnp.where(inside, 0, 1)
    place = jnp.where(table[NEAR_Y, 0, slot] >= 0, 2, 0) + jnp.where(table[NEAR_Z, 0, slot] >= 0, 1, 0)
    return parity, place


def lane_mask(scalars):
    lane = lax.broadcasted_iota(jnp.int32, (8, PLANE), 1)
    high_y = lane >= 128
    high_z = (lane & 8) != 0
    s = [jnp.full((8, PLANE), v, F32) for v in scalars]
    return jnp.where(high_y, jnp.where(high_z, s[3], s[2]), jnp.where(high_z, s[1], s[0]))


def product(weight_ref, taps, plane_taps=slice(0, 3)):
    left = weight_ref[plane_taps]
    left = left.reshape(left.shape[0] * left.shape[1], KDIM)
    return jnp.dot(left, taps, preferred_element_type=F32)


def pair_sums(full, low, weight_ref, taps, first):
    channels = low.shape[1]
    both = product(weight_ref, taps)
    left, right = both[:, :PLANE], both[:, PLANE:]

    def part(value, a):
        return value[a * channels : (a + 1) * channels]

    before = part(left, 2)
    here = part(left, 1) + part(right, 2)
    full[0] = before if first else low[0] + before
    full[1] = here if first else low[1] + here
    low[0] = part(left, 0) + part(right, 1)
    low[1] = part(right, 0)


def place(k):
    return pl.ds(k * PLANE, PLANE)


def pair_grads(grads, p):
    blank = jnp.zeros_like(grads(3))

    def left(p):
        inside = [grads(p + 1 - a) if 0 <= p + 1 - a < EDGE else blank for a in range(3)]
        return jnp.concatenate(inside, axis=0)

    return jnp.concatenate([left(p), left(p + 1)], axis=1)


def weight_part(left, taps):
    return lax.dot_general(left, taps, (((1,), (1,)), ((), ())), preferred_element_type=F32)


def weight_products(total, grads, planes, taps, start=None):
    for first in range(0, KDIM, 256):
        rows = slice(first, min(first + 256, KDIM))
        block = None if start is None else start[:, rows]
        for p in planes:
            part = weight_part(pair_grads(grads, p), taps(p, rows))
            block = part if block is None else block + part
        total[:, rows] = block


def write_tiles(flat, total, channels, even):
    lane = lax.broadcasted_iota(jnp.int32, (channels, 128), 1)
    blank = jnp.zeros((channels, 128), F32)
    first, last = total[:channels, :], total[2 * channels :, :]
    low, high = jnp.where(even, first, last), jnp.where(even, last, first)
    second = jnp.concatenate([total[channels : 2 * channels, :], blank], axis=1)
    third = jnp.concatenate([high, blank], axis=1)
    second = pltpu.roll(second, 96, 1)
    third = pltpu.roll(third, 64, 1)

    def cut(value, k):
        return value[:, k * 128 : (k + 1) * 128]

    tiles = [cut(low, k) for k in range(6)]
    tiles.append(jnp.where(lane < 96, cut(low, 6), cut(second, 0)))
    tiles += [cut(second, k) for k in range(1, 7)]
    tiles.append(jnp.where(lane < 64, cut(second, 7), cut(third, 0)))
    tiles += [cut(third, k) for k in range(1, 8)]
    for k in range(TILES):
        flat[k * channels : (k + 1) * channels, :] = tiles[k]
    flat[TILES * channels :, :] = jnp.zeros((ROWS - TILES * channels, 128), F32)


def split_tiles(keep_ref, send_ref, flat, device):
    rows = keep_ref.shape[0]
    even = core_of(device) == 0
    here = pl.multiple_of(jnp.where(even, 0, rows), rows)
    there = pl.multiple_of(jnp.where(even, rows, 0), rows)
    keep_ref[...] = flat[pl.ds(here, rows), :]
    send_ref[...] = flat[pl.ds(there, rows), :].astype(BF16)


def layout_kernel(
    device, table, own_ref, pair_ref, cot_pair_ref,
    x_ref, cot_ref, edge_ref, mask_ref, bricks, cots,
):
    slots, channels = pair_ref.shape[0], pair_ref.shape[1]
    all_slots = table.shape[2]
    me = space_index(device, all_slots // slots)
    layer = layer_side(device)
    even = layer == 0

    live = [[jnp.float32(0)] * 4 for _ in range(2)]
    beyond = [jnp.float32(0)] * 4
    for index in (me, me ^ 1):
        for s in range(slots):
            slot = jnp.clip(index * slots + s, 0, all_slots - 1)
            parity, spot = slot_place(table, slot, 2 * slots)
            alive = table[LIVE, 0, slot].astype(F32)
            scale = jnp.full((channels, CELLS), alive, F32).astype(BF16)
            own = index is me
            bricks[parity, spot] = (own_ref[s] if own else pair_ref[s]) * scale
            cots[parity, spot] = (own_ref[slots + s] if own else cot_pair_ref[s]) * scale
            outer = jnp.where(even, table[DOWN, 0, slot], table[UP, 0, slot])
            alive_outer = table[LIVE, 0, jnp.clip(outer, 0, all_slots - 1)].astype(F32)
            alive_outer = jnp.where(outer >= 0, alive_outer, 0.0)
            for k in range(4):
                for p in range(2):
                    here = jnp.logical_and(parity == p, spot == k)
                    live[p][k] = jnp.where(here, alive, live[p][k])
                here = jnp.logical_and(parity == layer, spot == k)
                beyond[k] = jnp.where(here, alive_outer, beyond[k])
    mask_ref[0] = lane_mask(beyond)
    mask_ref[1] = lane_mask([jnp.where(even, live[0][k], live[1][k]) for k in range(4)])
    mask_ref[2] = lane_mask([jnp.where(even, live[1][k], live[0][k]) for k in range(4)])

    move = spread_matrix()
    mine = jnp.where(even, 0, 1)

    def spread(left, right):
        two = jnp.concatenate([left, right], axis=1)
        return jnp.dot(two, move, preferred_element_type=F32).astype(BF16)

    for y in range(2):
        row = slice(y * 128, (y + 1) * 128)
        for j in range(4):
            pair = slice(j * 128, (j + 1) * 128)
            first = jnp.where(even, 2 * j, 7 - 2 * j)
            second = jnp.where(even, 2 * j + 1, 6 - 2 * j)
            both = spread(bricks[mine, 2 * y, :, pair], bricks[mine, 2 * y + 1, :, pair])
            x_ref[first, :, row] = both[:, :128]
            x_ref[second, :, row] = both[:, 128:]
            both = spread(cots[mine, 2 * y, :, pair], cots[mine, 2 * y + 1, :, pair])
            cot_ref[first, :, row] = both[:, :128]
            cot_ref[second, :, row] = both[:, 128:]
        for j in range(2):
            start = pl.multiple_of(jnp.where(even, j * 128, 256 + j * 128), 128)
            pair = pl.ds(start, 128)
            both = spread(
                bricks[1 - mine, 2 * y, :, pair], bricks[1 - mine, 2 * y + 1, :, pair]
            )
            x_ref[jnp.where(even, 8 + 2 * j, 11 - 2 * j), :, row] = both[:, :128]
            x_ref[jnp.where(even, 9 + 2 * j, 10 - 2 * j), :, row] = both[:, 128:]
        pair = pl.ds(pl.multiple_of(jnp.where(even, 0, 384), 128), 128)
        both = spread(cots[1 - mine, 2 * y, :, pair], cots[1 - mine, 2 * y + 1, :, pair])
        side = jnp.full((channels, 128), jnp.where(even, 1.0, 0.0), F32).astype(BF16)
        cot_ref[8, :, row] = both[:, :128] * side + both[:, 128:] * (1 - side)
    edge_ref[:3] = x_ref[:3]
    edge_ref[3] = cot_ref[0]


def tap_weights(out_ref, weight, wide, even):
    channels, width = weight.shape
    wide[:, :width] = weight
    lane = lax.broadcasted_iota(jnp.int32, (channels, 128), 1)
    for a, (tile, moved) in enumerate(((0, 0), (6, 96), (13, 64))):
        span = wide[:, tile * 128 : (tile + 8) * 128].astype(F32)
        if moved:
            span = pltpu.roll(span, 1024 - moved, 1)
        last = jnp.where(lane < 96, span[:, 768:KDIM], 0.0)
        span = jnp.concatenate([span[:, :768], last], axis=1)
        at = a if a == 1 else jnp.where(even, a, 2 - a)
        out_ref[at] = span.astype(BF16)


def back_weights(out_ref, taps_ref):
    channels = taps_ref.shape[1]
    lane = lax.broadcasted_iota(jnp.int32, (channels, 128), 1)
    more = jnp.zeros((128 - channels, KDIM), F32)
    for a in range(3):
        block = jnp.concatenate([taps_ref[2 - a].astype(F32), more], axis=0)
        turned = block.T
        tiles = [jnp.zeros((channels, 128), F32)] * 7
        for k in range(9):
            piece = turned[(8 - k) * channels : (9 - k) * channels, :]
            tile, moved = divmod(k * channels, 128)
            if moved:
                piece = pltpu.roll(piece, moved, 1)
            tiles[tile] = tiles[tile] + jnp.where(lane >= moved, piece, 0.0)
            if moved + channels > 128:
                tiles[tile + 1] = tiles[tile + 1] + jnp.where(lane < moved, piece, 0.0)
        out_ref[a] = jnp.concatenate(tiles, axis=1).astype(BF16)


def column(row):
    return jnp.broadcast_to(row, (8, row.shape[1])).T[:, :1]


def layer_of(q):
    return 0 if q < 0 else 1 if q < EDGE else 2


def hidden_plane(pre, mask):
    sigma = jax.nn.sigmoid(pre)
    return (pre * sigma * mask).astype(BF16), sigma * (1.0 + pre * (1.0 - sigma)) * mask


def out_plane(pre, mask, cot):
    sigma = jax.nn.sigmoid(pre)
    grad = cot.astype(F32) * (sigma * (1.0 + pre * (1.0 - sigma)))
    return (pre * sigma * mask).astype(BF16), grad.astype(BF16)


def inner_kernel(
    device, x_ref, cot_ref, layer_mask, weight_ref, bias_ref,
    taps_ref, x_taps, one_ref, two_ref, slope_ref, g_ref, out_ref, total_ref, w1_taps, w2_taps, w2_back,
    wide, xc, hc, full_one, low_one, full_two, low_two, masks_ref,
):
    channels = x_ref.shape[1]
    even = layer_side(device) == 0
    fill_masks(masks_ref)
    tap_weights(w1_taps, weight_ref[:channels, :], wide, even)
    bias_one, bias_two = column(bias_ref[0:1]), column(bias_ref[1:2])
    ones = jnp.ones((KDIM - 9 * channels, 2 * PLANE), BF16)
    for k in range(5):
        x_taps[k, 9 * channels :, :] = ones
    for k in range(4):
        taps_ref[k, 9 * channels :, :] = ones
    for single in (xc, hc):
        single[9 * channels :, :] = ones[:, :PLANE]

    def write_x(p):
        write_taps(x_taps.at[p // 2, :, place(p & 1)] if p < 10 else xc, x_ref[p], masks_ref)

    def finish_one(q, pre):
        hidden, slope = hidden_plane(pre + bias_one, layer_mask[layer_of(q)][:1])
        dst = taps_ref.at[(q - 1) // 2, :, place((q - 1) & 1)] if q < 9 else hc
        write_taps(dst, hidden, masks_ref)
        if q < EDGE:
            slope_ref[q - 1] = slope

    def finish_two(q, pre):
        out, grad = out_plane(pre + bias_two, layer_mask[layer_of(q)][:1], cot_ref[q])
        g_ref[q - 2] = grad
        if q < EDGE:
            out_ref[q - 2] = out

    write_x(0)
    write_x(1)
    for j in range(8):
        now, last = j & 1, (j + 1) & 1
        if j < 5:
            pair_sums(full_one.at[now], low_one, w1_taps, x_taps[j], j == 0)
            for p in (2 * j + 2, 2 * j + 3):
                if p <= 10:
                    write_x(p)
        if j == 5:
            third = product(w1_taps, xc[...], slice(2, 3))
            full_one[now, 0] = low_one[0] + third
        if j == 0:
            tap_weights(w2_taps, weight_ref[channels:, :], wide, even)
        if j == 1:
            one_ref[...] = full_one[0]
            back_weights(w2_back, w2_taps)
        if 2 <= j <= 5:
            finish_one(2 * j - 3, full_one[last, 0])
            finish_one(2 * j - 2, full_one[last, 1])
        if j == 6:
            finish_one(9, full_one[last, 0])
        if 3 <= j <= 6:
            pair_sums(full_two.at[now], low_two, w2_taps, taps_ref[j - 3], j == 3)
        if j == 7:
            third = product(w2_taps, hc[...], slice(2, 3))
            finish_two(8, low_two[0] + third)
        if j == 4:
            two_ref[...] = full_two[last]
        if 5 <= j:
            finish_two(2 * j - 8, full_two[last, 0])
            finish_two(2 * j - 7, full_two[last, 1])

    def taps(p, rows):
        return taps_ref[p // 2, rows]

    weight_products(total_ref, lambda q: g_ref[q - 2], (3, 5, 7), taps)


def outer_kernel(
    device, edge_ref, cot_ref, layer_mask, w1_taps, w2_taps, bias_ref,
    taps_ref, one_ref, two_ref, g_in_ref, total_ref,
    keep_ref, send_ref, slope_ref, g_ref, out_ref, x_pair,
    xc, hc, h_pair, total, flat, masks_ref,
):
    channels = cot_ref.shape[1]
    even = layer_side(device) == 0
    fill_masks(masks_ref)
    bias_one, bias_two = column(bias_ref[0:1]), column(bias_ref[1:2])
    ones = jnp.ones((KDIM - 9 * channels, 2 * PLANE), BF16)
    for single in (xc, hc):
        single[9 * channels :, :] = ones[:, :PLANE]
    for pair in (x_pair, h_pair):
        pair[9 * channels :, :] = ones
    write_taps(xc, edge_ref[2], masks_ref)
    write_taps(x_pair.at[:, place(0)], edge_ref[1], masks_ref)
    write_taps(x_pair.at[:, place(1)], edge_ref[0], masks_ref)

    def three_planes(weights, single, pair, parts):
        first = product(weights, single[...], slice(0, 1))
        both = product(weights, pair[...])
        left, right = both[:, :PLANE], both[:, PLANE:]
        one, two = slice(channels, 2 * channels), slice(2 * channels, 3 * channels)
        return (
            first + left[one] + right[two],
            left[:channels] + right[one] + parts[0],
            right[:channels] + parts[1],
        )

    for q, pre in zip(range(-2, 1), three_planes(w1_taps, xc, x_pair, one_ref)):
        hidden, slope = hidden_plane(pre + bias_one, layer_mask[layer_of(q)][:1])
        write_taps(hc if q == -2 else h_pair.at[:, place(q + 1)], hidden, masks_ref)
        if q == 0:
            slope_ref[0] = slope
    for q, pre in zip(range(-1, 2), three_planes(w2_taps, hc, h_pair, two_ref)):
        cot = edge_ref[3] if q < 0 else cot_ref[q]
        out, grad = out_plane(pre + bias_two, layer_mask[layer_of(q)][:1], cot)
        g_ref[q + 1] = grad
        if q >= 0:
            out_ref[q] = out

    def grads(q):
        return g_ref[q + 1] if q < 2 else g_in_ref[q - 2]

    def taps(p, rows):
        return h_pair[rows] if p < 0 else taps_ref[p // 2, rows]

    weight_products(total, grads, (-1, 1), taps, total_ref)
    write_tiles(flat, total, channels, even)
    split_tiles(keep_ref, send_ref, flat, device)


def output_kernel(device, table, first_ref, second_ref, keep_ref, send_ref, outs, bricks):
    slots, channels = keep_ref.shape[0], keep_ref.shape[1]
    me = space_index(device, table.shape[2] // slots)
    layer = layer_side(device)
    even = layer == 0
    outs[:2] = first_ref[...]
    outs[2:] = second_ref[...]
    back = spread_matrix(True)
    for y in range(2):
        row = slice(y * 128, (y + 1) * 128)
        for j in range(4):
            first = jnp.where(even, 2 * j, 7 - 2 * j)
            second = jnp.where(even, 2 * j + 1, 6 - 2 * j)
            two = jnp.concatenate([outs[first, :, row], outs[second, :, row]], axis=1)
            both = jnp.dot(two, back, preferred_element_type=F32).astype(BF16)
            pair = slice(j * 128, (j + 1) * 128)
            bricks[2 * y, :, pair] = both[:, :128]
            bricks[2 * y + 1, :, pair] = both[:, 128:]
    for target, index in ((keep_ref, me), (send_ref, me ^ 1)):
        for s in range(slots):
            slot = jnp.clip(index * slots + s, 0, table.shape[2] - 1)
            parity, spot = slot_place(table, slot, 2 * slots)
            scale = jnp.where(parity == layer, 1.0, 0.0)
            target[s] = bricks[spot] * jnp.full((channels, CELLS), scale, F32).astype(BF16)


def backward_kernel(
    device, g_out_ref, g_in_ref, slope_out_ref, slope_in_ref, x_taps, x_pair, w2_back,
    keep_ref, send_ref, gc, full, low, grad, total, flat, masks_ref,
):
    channels = g_in_ref.shape[1]
    even = layer_side(device) == 0
    fill_masks(masks_ref)
    ones = jnp.ones((KDIM - 9 * channels, 2 * PLANE), BF16)
    for k in range(2):
        gc[k, 9 * channels :, :] = ones

    def write_g(q):
        plane = g_out_ref[q + 1] if q < 2 else g_in_ref[q - 2]
        write_taps(gc.at[((q + 1) >> 1) & 1, :, place((q + 1) & 1)], plane, masks_ref)

    write_g(-1)
    write_g(0)
    for j in range(6):
        now, last = j & 1, (j + 1) & 1
        if j < 5:
            pair_sums(full.at[now], low, w2_back, gc[now], j == 0)
            for q in (2 * j + 1, 2 * j + 2):
                if q <= 8:
                    write_g(q)
        if j >= 2:
            for k, q in enumerate((2 * j - 4, 2 * j - 3)):
                slope = slope_out_ref[0] if q == 0 else slope_in_ref[q - 1]
                grad[q] = (full[last, k] * slope).astype(BF16)
        if j >= 3:
            for p in (2 * j - 6,) if j < 5 else (4, 6):
                part = weight_part(pair_grads(lambda q: grad[q], p), x_taps[p // 2])
                total[...] = part if p == 0 else total[...] + part
    low_rows, high_rows = slice(0, channels), slice(2 * channels, 3 * channels)
    total[low_rows] = total[low_rows] + weight_part(grad[0], x_pair[:, PLANE:])
    total[high_rows] = total[high_rows] + weight_part(grad[EDGE - 1], x_taps[4, :, :PLANE])
    write_tiles(flat, total, channels, even)
    split_tiles(keep_ref, send_ref, flat, device)


def copies_kernel(first_ref, second_ref, out_ref):
    total = (first_ref[...].astype(F32) + second_ref[...].astype(F32)).astype(BF16)
    for k in range(out_ref.shape[0]):
        out_ref[k] = total


def gather_kernel(
    device, own_ref, other_ref, w_one_ref, w_two_ref, b_one_ref, b_two_ref, flat
):
    chunks, _, rows, _ = own_ref.shape
    channels = w_one_ref.shape[0]
    core = core_of(device)
    for half, source in enumerate((own_ref, other_ref)):
        base = jnp.where(core == half, 0, chunks * rows)
        for k in range(chunks):
            at = pl.multiple_of(base + k * rows, rows)
            flat[:, pl.ds(at, rows), :] = source[k]
    for n, (weight, bias) in enumerate(((w_one_ref, b_one_ref), (w_two_ref, b_two_ref))):
        for k in range(TILES - 1):
            tile = flat[n, k * channels : (k + 1) * channels, :]
            weight[:, k * 128 : (k + 1) * 128] = tile.astype(F32)
        last = flat[n, (TILES - 1) * channels : TILES * channels, :].astype(F32)
        weight[:, 2560:2592] = last[:, :32]
        bias[...] = last.T[32:33, :]


VMEM = pl.BlockSpec(memory_space=pltpu.VMEM)
SMEM = pl.BlockSpec(memory_space=pltpu.SMEM)


def vmem(mebibytes):
    return pltpu.CompilerParams(vmem_limit_bytes=mebibytes * 2**20)


def shared_sum(keeps, sends):
    count = lax.axis_size("space")
    volumes = lax.axis_size("dp")
    swap = [(d, d ^ 1) for d in range(count)]
    both = ("space", "dp")
    groups = [
        [(chip * 2 + core) * volumes + first + v for v in range(2) for chip in range(count // 2)]
        for core in range(2)
        for first in range(0, volumes, 2)
    ]
    halves = [
        keep + lax.ppermute(send, "space", swap).astype(F32) for keep, send in zip(keeps, sends)
    ]
    halves = [half.astype(BF16).reshape(count, -1, 128) for half in halves]
    parts = jnp.stack(halves, axis=1)
    parts = lax.all_to_all(parts, both, 0, 0, axis_index_groups=groups)
    total = jnp.sum(parts.astype(F32), axis=0).astype(BF16)
    moved, step = jnp.zeros_like(total), 2
    while step < volumes:
        moved = lax.ppermute(total, "dp", [(v, v ^ step) for v in range(volumes)])
        if step * 2 < volumes:
            total = (total.astype(F32) + moved.astype(F32)).astype(BF16)
        step *= 2
    copies = pl.pallas_call(
        copies_kernel,
        out_shape=jax.ShapeDtypeStruct(parts.shape, BF16),
        in_specs=[VMEM] * 2,
        out_specs=VMEM,
        compiler_params=vmem(8),
        name="copies",
    )(total, moved)
    copies = lax.all_to_all(copies, both, 0, 0, axis_index_groups=groups)
    return [copies, lax.ppermute(copies, "space", swap)]


def local(volume, neighbours, active, cotangent, weight_one, weight_two, bias_one, bias_two):
    volume, cotangent = volume[0], cotangent[0]
    slots, channels = volume.shape[0], volume.shape[1]
    count = lax.axis_size("space")
    me = lax.axis_index("space").astype(jnp.int32)

    swap = [(d, d ^ 1) for d in range(count)]
    at = [2 * (n // 2) + (n & 1 ^ n // 2 & 1) for n in range(count)]
    hop = [(at[n], at[n + 1]) for n in range(1, count - 1, 2)]
    hop += [(there, here) for here, there in hop]
    pair_volume = lax.ppermute(volume, "space", swap)
    pair_cot = lax.ppermute(cotangent, "space", swap)
    biases = jnp.stack([bias_one, bias_two])
    weights = jnp.concatenate([weight_one, weight_two], axis=0)
    own = jnp.concatenate([volume, cotangent], axis=0)
    device = (2 * me + ((me ^ (me >> 1)) & 1))[None]
    table = jnp.concatenate([neighbours.transpose(2, 0, 1), active[None]], axis=0)

    def planes(number, dtype=BF16):
        return jax.ShapeDtypeStruct((number, channels, PLANE), dtype)

    def plane_space(number):
        return pltpu.VMEM((number, channels, PLANE), BF16)

    def tap_space(*extent):
        return pltpu.VMEM(extent, BF16)

    def sum_space(*extent):
        return pltpu.VMEM((*extent, channels, PLANE), F32)

    bricks = (slots, channels, CELLS)
    x_planes, cot_planes, edge, layer_mask = pl.pallas_call(
        layout_kernel,
        out_shape=(planes(12), planes(9), planes(4), jax.ShapeDtypeStruct((3, 8, PLANE), F32)),
        in_specs=[SMEM] * 2 + [VMEM] * 3,
        out_specs=(VMEM,) * 4,
        scratch_shapes=[
            pltpu.VMEM((2, *bricks), BF16),
            pltpu.VMEM((2, *bricks), BF16),
        ],
        compiler_params=vmem(8),
        name="layout",
    )(device, table, own, pair_volume, pair_cot)
    outer = lax.ppermute(edge, "space", hop)

    rearranged = jax.ShapeDtypeStruct((3, channels, KDIM), BF16)
    taps, x_taps, one, two, slope_in, g_in, out_in, part_two, w1, w2, w2_back = pl.pallas_call(
        inner_kernel,
        out_shape=(
            jax.ShapeDtypeStruct((4, KDIM, 2 * PLANE), BF16),
            jax.ShapeDtypeStruct((5, KDIM, 2 * PLANE), BF16),
            planes(2, F32),
            planes(2, F32),
            planes(7, F32),
            planes(7),
            planes(6),
            jax.ShapeDtypeStruct((3 * channels, KDIM), F32),
            rearranged,
            rearranged,
            rearranged,
        ),
        in_specs=[SMEM] + [VMEM] * 5,
        out_specs=(VMEM,) * 11,
        scratch_shapes=[
            pltpu.VMEM((channels, 21 * 128), BF16),
            tap_space(KDIM, PLANE),
            tap_space(KDIM, PLANE),
            sum_space(2, 2),
            sum_space(2),
            sum_space(2, 2),
            sum_space(2),
            pltpu.VMEM((9, 16, PLANE), BF16),
        ],
        compiler_params=vmem(20),
        cost_estimate=pl.CostEstimate(flops=2**33, bytes_accessed=2**23, transcendentals=2**20),
        name="inner",
    )(device, x_planes, cot_planes, layer_mask, weights, biases)

    rows = (ROWS // 2, 128)
    kept, sent = jax.ShapeDtypeStruct(rows, F32), jax.ShapeDtypeStruct(rows, BF16)
    keep_two, send_two, slope_out, g_out, out_out, x_pair = pl.pallas_call(
        outer_kernel,
        out_shape=(
            kept,
            sent,
            planes(1, F32),
            planes(3),
            planes(2),
            jax.ShapeDtypeStruct((KDIM, 2 * PLANE), BF16),
        ),
        in_specs=[SMEM] + [VMEM] * 11,
        out_specs=(VMEM,) * 6,
        scratch_shapes=[
            tap_space(KDIM, PLANE),
            tap_space(KDIM, PLANE),
            tap_space(KDIM, 2 * PLANE),
            pltpu.VMEM((3 * channels, KDIM), F32),
            pltpu.VMEM((ROWS, 128), F32),
            pltpu.VMEM((9, 16, PLANE), BF16),
        ],
        compiler_params=vmem(16),
        cost_estimate=pl.CostEstimate(flops=2**32, bytes_accessed=2**23, transcendentals=2**18),
        name="outer",
    )(
        device, outer, cot_planes, layer_mask, w1, w2, biases, taps, one, two, g_in,
        part_two,
    )
    keep_one, send_one = pl.pallas_call(
        backward_kernel,
        out_shape=(kept, sent),
        in_specs=[SMEM] + [VMEM] * 7,
        out_specs=(VMEM,) * 2,
        scratch_shapes=[
            tap_space(2, KDIM, 2 * PLANE),
            sum_space(2, 2),
            sum_space(2),
            plane_space(8),
            pltpu.VMEM((3 * channels, KDIM), F32),
            pltpu.VMEM((ROWS, 128), F32),
            pltpu.VMEM((9, 16, PLANE), BF16),
        ],
        compiler_params=vmem(20),
        cost_estimate=pl.CostEstimate(flops=2**32, bytes_accessed=2**22, transcendentals=0),
        name="backward",
    )(device, g_out, g_in, slope_out, slope_in, x_taps, x_pair, w2_back)
    keep, send = pl.pallas_call(
        output_kernel,
        out_shape=(jax.ShapeDtypeStruct(bricks, BF16),) * 2,
        in_specs=[SMEM] * 2 + [VMEM] * 2,
        out_specs=(VMEM,) * 2,
        scratch_shapes=[plane_space(8), pltpu.VMEM(bricks, BF16)],
        compiler_params=vmem(8),
        cost_estimate=pl.CostEstimate(flops=2**28, bytes_accessed=2**21, transcendentals=0),
        name="output",
    )(device, table, out_out, out_in)
    output = (keep + lax.ppermute(send, "space", swap))[None]
    parts = shared_sum([keep_one, keep_two], [send_one, send_two])
    weight_shape = jax.ShapeDtypeStruct((channels, 27 * channels), F32)
    bias_shape = jax.ShapeDtypeStruct((1, channels), F32)
    total_w_one, total_w_two, total_b_one, total_b_two = pl.pallas_call(
        gather_kernel,
        out_shape=(weight_shape, weight_shape, bias_shape, bias_shape),
        in_specs=[SMEM] + [VMEM] * len(parts),
        out_specs=(VMEM,) * 4,
        scratch_shapes=[pltpu.VMEM((2, ROWS, 128), BF16)],
        compiler_params=vmem(8),
        name="gather",
    )(device, *parts)
    return (output, total_w_one, total_w_two, total_b_one[0], total_b_two[0])


def solution(mesh):
    in_specs = (
        P("dp", "space", None, None),
        P("dp", None, None),
        P("dp", None),
        P("dp", "space", None, None),
        P(),
        P(),
        P(),
        P(),
    )
    out_specs = (P("dp", "space", None, None), P(), P(), P(), P())
    return jax.shard_map(local, mesh=mesh, in_specs=in_specs, out_specs=out_specs, check_vma=False)
```

```python
import jax
import jax.numpy as jnp
from jax import lax
from jax.experimental import pallas as pl
from jax.experimental.pallas import tpu as pltpu
from jax.sharding import PartitionSpec as P

EDGE = 8
PLANE = 256
CELLS = 512
KDIM = 896
TILES = 21
ROWS = 2048
DOWN, NEAR_Y, NEAR_Z, UP, LIVE = 4, 10, 12, 21, 26
F32 = jnp.float32
BF16 = jnp.bfloat16


def spread_matrix(back=False):
    near = lax.broadcasted_iota(jnp.int32, (256, 256), 1 if back else 0)
    far = lax.broadcasted_iota(jnp.int32, (256, 256), 0 if back else 1)
    source = ((far >> 3) & 1) * 128 + (far >> 7) * 64 + ((far >> 4) & 7) * 8 + (far & 7)
    return jnp.where(near == source, 1.0, 0.0).astype(BF16)


def fill_masks(masks):
    lane = lax.broadcasted_iota(jnp.int32, (16, PLANE), 1)
    for k in range(9):
        q, r = (lane >> 4) + (k // 3 - 1), (lane & 15) + (k % 3 - 1)
        inside = (q >= 0) & (q < 16) & (r >= 0) & (r < 16)
        masks[k] = jnp.where(inside, 1.0, 0.0).astype(BF16)


def write_taps(dst, plane, masks_ref):
    channels = plane.shape[0]
    for k in range(9):
        step = (k // 3 - 1) * 16 + (k % 3 - 1)
        if step == 0:
            moved = plane
        else:
            moved = pltpu.roll(plane, (-step) % PLANE, 1)
            moved = moved * jnp.concatenate([masks_ref[k]] * (channels // 16), axis=0)
        dst[k * channels : (k + 1) * channels, :] = moved


def space_index(device, count):
    return jnp.clip(device[0] >> 1, 0, count - 1)


def layer_side(device):
    return device[0] & 1


def core_of(device):
    return (device[0] >> 1) & 1


def slot_place(table, slot, pair_slots):
    shift = pair_slots.bit_length() - 1
    up = table[UP, 0, slot]
    inside = jnp.logical_and(up >= 0, up >> shift == slot >> shift)
    parity = jnp.where(inside, 0, 1)
    place = jnp.where(table[NEAR_Y, 0, slot] >= 0, 2, 0) + jnp.where(table[NEAR_Z, 0, slot] >= 0, 1, 0)
    return parity, place


def lane_mask(scalars):
    lane = lax.broadcasted_iota(jnp.int32, (8, PLANE), 1)
    high_y = lane >= 128
    high_z = (lane & 8) != 0
    s = [jnp.full((8, PLANE), v, F32) for v in scalars]
    return jnp.where(high_y, jnp.where(high_z, s[3], s[2]), jnp.where(high_z, s[1], s[0]))


def product(weight_ref, taps, plane_taps=slice(0, 3)):
    left = weight_ref[plane_taps]
    left = left.reshape(left.shape[0] * left.shape[1], KDIM)
    return jnp.dot(left, taps, preferred_element_type=F32)


def pair_sums(full, low, weight_ref, taps, first):
    channels = low.shape[1]
    both = product(weight_ref, taps)
    left, right = both[:, :PLANE], both[:, PLANE:]

    def part(value, a):
        return value[a * channels : (a + 1) * channels]

    before = part(left, 2)
    here = part(left, 1) + part(right, 2)
    full[0] = before if first else low[0] + before
    full[1] = here if first else low[1] + here
    low[0] = part(left, 0) + part(right, 1)
    low[1] = part(right, 0)


def place(k):
    return pl.ds(k * PLANE, PLANE)


def pair_grads(grads, p):
    blank = jnp.zeros_like(grads(3))

    def left(p):
        inside = [grads(p + 1 - a) if 0 <= p + 1 - a < EDGE else blank for a in range(3)]
        return jnp.concatenate(inside, axis=0)

    return jnp.concatenate([left(p), left(p + 1)], axis=1)


def weight_part(left, taps):
    return lax.dot_general(left, taps, (((1,), (1,)), ((), ())), preferred_element_type=F32)


def weight_products(total, grads, planes, taps, start=None):
    for first in range(0, KDIM, 256):
        rows = slice(first, min(first + 256, KDIM))
        block = None if start is None else start[:, rows]
        for p in planes:
            part = weight_part(pair_grads(grads, p), taps(p, rows))
            block = part if block is None else block + part
        total[:, rows] = block


def write_tiles(flat, total, channels, even):
    lane = lax.broadcasted_iota(jnp.int32, (channels, 128), 1)
    blank = jnp.zeros((channels, 128), F32)
    first, last = total[:channels, :], total[2 * channels :, :]
    low, high = jnp.where(even, first, last), jnp.where(even, last, first)
    second = jnp.concatenate([total[channels : 2 * channels, :], blank], axis=1)
    third = jnp.concatenate([high, blank], axis=1)
    second = pltpu.roll(second, 96, 1)
    third = pltpu.roll(third, 64, 1)

    def cut(value, k):
        return value[:, k * 128 : (k + 1) * 128]

    tiles = [cut(low, k) for k in range(6)]
    tiles.append(jnp.where(lane < 96, cut(low, 6), cut(second, 0)))
    tiles += [cut(second, k) for k in range(1, 7)]
    tiles.append(jnp.where(lane < 64, cut(second, 7), cut(third, 0)))
    tiles += [cut(third, k) for k in range(1, 8)]
    for k in range(TILES):
        flat[k * channels : (k + 1) * channels, :] = tiles[k]
    flat[TILES * channels :, :] = jnp.zeros((ROWS - TILES * channels, 128), F32)


def split_tiles(keep_ref, send_ref, flat, device):
    chunks, rows = keep_ref.shape[0], keep_ref.shape[1]
    even = core_of(device) == 0
    here = jnp.where(even, 0, chunks * rows)
    there = jnp.where(even, chunks * rows, 0)
    for k in range(chunks):
        at = pl.multiple_of(here + k * rows, rows)
        keep_ref[k] = flat[pl.ds(at, rows), :]
        at = pl.multiple_of(there + k * rows, rows)
        send_ref[k] = flat[pl.ds(at, rows), :].astype(BF16)


def layout_kernel(
    device, table, own_ref, pair_ref, cot_pair_ref,
    x_ref, cot_ref, edge_ref, mask_ref, bricks, cots,
):
    slots, channels = pair_ref.shape[0], pair_ref.shape[1]
    all_slots = table.shape[2]
    me = space_index(device, all_slots // slots)
    layer = layer_side(device)
    even = layer == 0

    live = [[jnp.float32(0)] * 4 for _ in range(2)]
    beyond = [jnp.float32(0)] * 4
    for index in (me, me ^ 1):
        for s in range(slots):
            slot = jnp.clip(index * slots + s, 0, all_slots - 1)
            parity, spot = slot_place(table, slot, 2 * slots)
            alive = table[LIVE, 0, slot].astype(F32)
            scale = jnp.full((channels, CELLS), alive, F32).astype(BF16)
            own = index is me
            bricks[parity, spot] = (own_ref[s] if own else pair_ref[s]) * scale
            cots[parity, spot] = (own_ref[slots + s] if own else cot_pair_ref[s]) * scale
            outer = jnp.where(even, table[DOWN, 0, slot], table[UP, 0, slot])
            alive_outer = table[LIVE, 0, jnp.clip(outer, 0, all_slots - 1)].astype(F32)
            alive_outer = jnp.where(outer >= 0, alive_outer, 0.0)
            for k in range(4):
                for p in range(2):
                    here = jnp.logical_and(parity == p, spot == k)
                    live[p][k] = jnp.where(here, alive, live[p][k])
                here = jnp.logical_and(parity == layer, spot == k)
                beyond[k] = jnp.where(here, alive_outer, beyond[k])
    mask_ref[0] = lane_mask(beyond)
    mask_ref[1] = lane_mask([jnp.where(even, live[0][k], live[1][k]) for k in range(4)])
    mask_ref[2] = lane_mask([jnp.where(even, live[1][k], live[0][k]) for k in range(4)])

    move = spread_matrix()
    mine = jnp.where(even, 0, 1)

    def spread(left, right):
        two = jnp.concatenate([left, right], axis=1)
        return jnp.dot(two, move, preferred_element_type=F32).astype(BF16)

    for y in range(2):
        row = slice(y * 128, (y + 1) * 128)
        for j in range(4):
            pair = slice(j * 128, (j + 1) * 128)
            first = jnp.where(even, 2 * j, 7 - 2 * j)
            second = jnp.where(even, 2 * j + 1, 6 - 2 * j)
            both = spread(bricks[mine, 2 * y, :, pair], bricks[mine, 2 * y + 1, :, pair])
            x_ref[first, :, row] = both[:, :128]
            x_ref[second, :, row] = both[:, 128:]
            both = spread(cots[mine, 2 * y, :, pair], cots[mine, 2 * y + 1, :, pair])
            cot_ref[first, :, row] = both[:, :128]
            cot_ref[second, :, row] = both[:, 128:]
        for j in range(2):
            start = pl.multiple_of(jnp.where(even, j * 128, 256 + j * 128), 128)
            pair = pl.ds(start, 128)
            both = spread(
                bricks[1 - mine, 2 * y, :, pair], bricks[1 - mine, 2 * y + 1, :, pair]
            )
            x_ref[jnp.where(even, 8 + 2 * j, 11 - 2 * j), :, row] = both[:, :128]
            x_ref[jnp.where(even, 9 + 2 * j, 10 - 2 * j), :, row] = both[:, 128:]
        pair = pl.ds(pl.multiple_of(jnp.where(even, 0, 384), 128), 128)
        both = spread(cots[1 - mine, 2 * y, :, pair], cots[1 - mine, 2 * y + 1, :, pair])
        side = jnp.full((channels, 128), jnp.where(even, 1.0, 0.0), F32).astype(BF16)
        cot_ref[8, :, row] = both[:, :128] * side + both[:, 128:] * (1 - side)
    edge_ref[:3] = x_ref[:3]
    edge_ref[3] = cot_ref[0]


def tap_weights(out_ref, weight, wide, even):
    channels, width = weight.shape
    wide[:, :width] = weight
    lane = lax.broadcasted_iota(jnp.int32, (channels, 128), 1)
    for a, (tile, moved) in enumerate(((0, 0), (6, 96), (13, 64))):
        span = wide[:, tile * 128 : (tile + 8) * 128].astype(F32)
        if moved:
            span = pltpu.roll(span, 1024 - moved, 1)
        last = jnp.where(lane < 96, span[:, 768:KDIM], 0.0)
        span = jnp.concatenate([span[:, :768], last], axis=1)
        at = a if a == 1 else jnp.where(even, a, 2 - a)
        out_ref[at] = span.astype(BF16)


def back_weights(out_ref, taps_ref):
    channels = taps_ref.shape[1]
    lane = lax.broadcasted_iota(jnp.int32, (channels, 128), 1)
    more = jnp.zeros((128 - channels, KDIM), F32)
    for a in range(3):
        block = jnp.concatenate([taps_ref[2 - a].astype(F32), more], axis=0)
        turned = block.T
        tiles = [jnp.zeros((channels, 128), F32)] * 7
        for k in range(9):
            piece = turned[(8 - k) * channels : (9 - k) * channels, :]
            tile, moved = divmod(k * channels, 128)
            if moved:
                piece = pltpu.roll(piece, moved, 1)
            tiles[tile] = tiles[tile] + jnp.where(lane >= moved, piece, 0.0)
            if moved + channels > 128:
                tiles[tile + 1] = tiles[tile + 1] + jnp.where(lane < moved, piece, 0.0)
        out_ref[a] = jnp.concatenate(tiles, axis=1).astype(BF16)


def column(row):
    return jnp.broadcast_to(row, (8, row.shape[1])).T[:, :1]


def layer_of(q):
    return 0 if q < 0 else 1 if q < EDGE else 2


def hidden_plane(pre, mask):
    sigma = jax.nn.sigmoid(pre)
    return (pre * sigma * mask).astype(BF16), sigma * (1.0 + pre * (1.0 - sigma)) * mask


def out_plane(pre, mask, cot):
    sigma = jax.nn.sigmoid(pre)
    grad = cot.astype(F32) * (sigma * (1.0 + pre * (1.0 - sigma)))
    return (pre * sigma * mask).astype(BF16), grad.astype(BF16)


def inner_kernel(
    device, x_ref, cot_ref, layer_mask, weight_ref, b1_ref, b2_ref,
    taps_ref, x_taps, one_ref, two_ref, slope_ref, g_ref, out_ref, total_ref, w1_taps, w2_taps, w2_back,
    wide, xc, hc, full_one, low_one, full_two, low_two, masks_ref,
):
    channels = x_ref.shape[1]
    even = layer_side(device) == 0
    fill_masks(masks_ref)
    tap_weights(w1_taps, weight_ref[:channels, :], wide, even)
    bias_one, bias_two = column(b1_ref[...]), column(b2_ref[...])
    ones = jnp.ones((KDIM - 9 * channels, 2 * PLANE), BF16)
    for k in range(5):
        x_taps[k, 9 * channels :, :] = ones
    for k in range(4):
        taps_ref[k, 9 * channels :, :] = ones
    for single in (xc, hc):
        single[9 * channels :, :] = ones[:, :PLANE]

    def write_x(p):
        write_taps(x_taps.at[p // 2, :, place(p & 1)] if p < 10 else xc, x_ref[p], masks_ref)

    def finish_one(q, pre):
        hidden, slope = hidden_plane(pre + bias_one, layer_mask[layer_of(q)][:1])
        dst = taps_ref.at[(q - 1) // 2, :, place((q - 1) & 1)] if q < 9 else hc
        write_taps(dst, hidden, masks_ref)
        if q < EDGE:
            slope_ref[q - 1] = slope

    def finish_two(q, pre):
        out, grad = out_plane(pre + bias_two, layer_mask[layer_of(q)][:1], cot_ref[q])
        g_ref[q - 2] = grad
        if q < EDGE:
            out_ref[q - 2] = out

    write_x(0)
    write_x(1)
    for j in range(8):
        now, last = j & 1, (j + 1) & 1
        if j < 5:
            pair_sums(full_one.at[now], low_one, w1_taps, x_taps[j], j == 0)
            for p in (2 * j + 2, 2 * j + 3):
                if p <= 10:
                    write_x(p)
        if j == 5:
            third = product(w1_taps, xc[...], slice(2, 3))
            full_one[now, 0] = low_one[0] + third
        if j == 0:
            tap_weights(w2_taps, weight_ref[channels:, :], wide, even)
        if j == 1:
            one_ref[...] = full_one[0]
            back_weights(w2_back, w2_taps)
        if 2 <= j <= 5:
            finish_one(2 * j - 3, full_one[last, 0])
            finish_one(2 * j - 2, full_one[last, 1])
        if j == 6:
            finish_one(9, full_one[last, 0])
        if 3 <= j <= 6:
            pair_sums(full_two.at[now], low_two, w2_taps, taps_ref[j - 3], j == 3)
        if j == 7:
            third = product(w2_taps, hc[...], slice(2, 3))
            finish_two(8, low_two[0] + third)
        if j == 4:
            two_ref[...] = full_two[last]
        if 5 <= j:
            finish_two(2 * j - 8, full_two[last, 0])
            finish_two(2 * j - 7, full_two[last, 1])

    def taps(p, rows):
        return taps_ref[p // 2, rows]

    weight_products(total_ref, lambda q: g_ref[q - 2], (3, 5, 7), taps)


def outer_kernel(
    device, edge_ref, cot_ref, layer_mask, w1_taps, w2_taps, b1_ref, b2_ref,
    taps_ref, one_ref, two_ref, g_in_ref, total_ref,
    keep_ref, send_ref, slope_ref, g_ref, out_ref, x_pair,
    xc, hc, h_pair, total, flat, masks_ref,
):
    channels = cot_ref.shape[1]
    even = layer_side(device) == 0
    fill_masks(masks_ref)
    bias_one, bias_two = column(b1_ref[...]), column(b2_ref[...])
    ones = jnp.ones((KDIM - 9 * channels, 2 * PLANE), BF16)
    for single in (xc, hc):
        single[9 * channels :, :] = ones[:, :PLANE]
    for pair in (x_pair, h_pair):
        pair[9 * channels :, :] = ones
    write_taps(xc, edge_ref[2], masks_ref)
    write_taps(x_pair.at[:, place(0)], edge_ref[1], masks_ref)
    write_taps(x_pair.at[:, place(1)], edge_ref[0], masks_ref)

    def three_planes(weights, single, pair, parts):
        first = product(weights, single[...], slice(0, 1))
        both = product(weights, pair[...])
        left, right = both[:, :PLANE], both[:, PLANE:]
        one, two = slice(channels, 2 * channels), slice(2 * channels, 3 * channels)
        return (
            first + left[one] + right[two],
            left[:channels] + right[one] + parts[0],
            right[:channels] + parts[1],
        )

    for q, pre in zip(range(-2, 1), three_planes(w1_taps, xc, x_pair, one_ref)):
        hidden, slope = hidden_plane(pre + bias_one, layer_mask[layer_of(q)][:1])
        write_taps(hc if q == -2 else h_pair.at[:, place(q + 1)], hidden, masks_ref)
        if q == 0:
            slope_ref[0] = slope
    for q, pre in zip(range(-1, 2), three_planes(w2_taps, hc, h_pair, two_ref)):
        cot = edge_ref[3] if q < 0 else cot_ref[q]
        out, grad = out_plane(pre + bias_two, layer_mask[layer_of(q)][:1], cot)
        g_ref[q + 1] = grad
        if q >= 0:
            out_ref[q] = out

    def grads(q):
        return g_ref[q + 1] if q < 2 else g_in_ref[q - 2]

    def taps(p, rows):
        return h_pair[rows] if p < 0 else taps_ref[p // 2, rows]

    weight_products(total, grads, (-1, 1), taps, total_ref)
    write_tiles(flat, total, channels, even)
    split_tiles(keep_ref, send_ref, flat, device)


def output_kernel(device, table, first_ref, second_ref, keep_ref, send_ref, outs, bricks):
    slots, channels = keep_ref.shape[0], keep_ref.shape[1]
    me = space_index(device, table.shape[2] // slots)
    layer = layer_side(device)
    even = layer == 0
    outs[:2] = first_ref[...]
    outs[2:] = second_ref[...]
    back = spread_matrix(True)
    for y in range(2):
        row = slice(y * 128, (y + 1) * 128)
        for j in range(4):
            first = jnp.where(even, 2 * j, 7 - 2 * j)
            second = jnp.where(even, 2 * j + 1, 6 - 2 * j)
            two = jnp.concatenate([outs[first, :, row], outs[second, :, row]], axis=1)
            both = jnp.dot(two, back, preferred_element_type=F32).astype(BF16)
            pair = slice(j * 128, (j + 1) * 128)
            bricks[2 * y, :, pair] = both[:, :128]
            bricks[2 * y + 1, :, pair] = both[:, 128:]
    for target, index in ((keep_ref, me), (send_ref, me ^ 1)):
        for s in range(slots):
            slot = jnp.clip(index * slots + s, 0, table.shape[2] - 1)
            parity, spot = slot_place(table, slot, 2 * slots)
            scale = jnp.where(parity == layer, 1.0, 0.0)
            target[s] = bricks[spot] * jnp.full((channels, CELLS), scale, F32).astype(BF16)


def backward_kernel(
    device, g_out_ref, g_in_ref, slope_out_ref, slope_in_ref, x_taps, x_pair, w2_back, keep_two,
    send_two, keep_ref, send_ref, gc, full, low, grad, total, flat, masks_ref,
):
    channels = g_in_ref.shape[1]
    even = layer_side(device) == 0
    fill_masks(masks_ref)
    ones = jnp.ones((KDIM - 9 * channels, 2 * PLANE), BF16)
    for k in range(2):
        gc[k, 9 * channels :, :] = ones

    def write_g(q):
        plane = g_out_ref[q + 1] if q < 2 else g_in_ref[q - 2]
        write_taps(gc.at[((q + 1) >> 1) & 1, :, place((q + 1) & 1)], plane, masks_ref)

    write_g(-1)
    write_g(0)
    for j in range(6):
        now, last = j & 1, (j + 1) & 1
        if j < 5:
            pair_sums(full.at[now], low, w2_back, gc[now], j == 0)
            for q in (2 * j + 1, 2 * j + 2):
                if q <= 8:
                    write_g(q)
        if j >= 2:
            for k, q in enumerate((2 * j - 4, 2 * j - 3)):
                slope = slope_out_ref[0] if q == 0 else slope_in_ref[q - 1]
                grad[q] = (full[last, k] * slope).astype(BF16)
        if j >= 3:
            for p in (2 * j - 6,) if j < 5 else (4, 6):
                part = weight_part(pair_grads(lambda q: grad[q], p), x_taps[p // 2])
                total[...] = part if p == 0 else total[...] + part
    low_rows, high_rows = slice(0, channels), slice(2 * channels, 3 * channels)
    total[low_rows] = total[low_rows] + weight_part(grad[0], x_pair[:, PLANE:])
    total[high_rows] = total[high_rows] + weight_part(grad[EDGE - 1], x_taps[4, :, :PLANE])
    write_tiles(flat, total, channels, even)
    split_tiles(keep_ref.at[:, 0], send_ref.at[:, 0], flat, device)
    keep_ref[:, 1] = keep_two[...]
    send_ref[:, 1] = send_two[...]


def copies_kernel(first_ref, second_ref, out_ref):
    total = (first_ref[...].astype(F32) + second_ref[...].astype(F32)).astype(BF16)
    for k in range(out_ref.shape[0]):
        out_ref[k] = total


def gather_kernel(
    device, own_ref, other_ref, w_one_ref, w_two_ref, b_one_ref, b_two_ref, flat
):
    chunks, _, rows, _ = own_ref.shape
    channels = w_one_ref.shape[0]
    core = core_of(device)
    for half, source in enumerate((own_ref, other_ref)):
        base = jnp.where(core == half, 0, chunks * rows)
        for k in range(chunks):
            at = pl.multiple_of(base + k * rows, rows)
            flat[:, pl.ds(at, rows), :] = source[k]
    for n, (weight, bias) in enumerate(((w_one_ref, b_one_ref), (w_two_ref, b_two_ref))):
        for k in range(TILES - 1):
            tile = flat[n, k * channels : (k + 1) * channels, :]
            weight[:, k * 128 : (k + 1) * 128] = tile.astype(F32)
        last = flat[n, (TILES - 1) * channels : TILES * channels, :].astype(F32)
        weight[:, 2560:2592] = last[:, :32]
        bias[...] = last.T[32:33, :]


VMEM = pl.BlockSpec(memory_space=pltpu.VMEM)
SMEM = pl.BlockSpec(memory_space=pltpu.SMEM)


def vmem(mebibytes):
    return pltpu.CompilerParams(vmem_limit_bytes=mebibytes * 2**20)


def shared_sum(keep, send):
    count = lax.axis_size("space")
    volumes = lax.axis_size("dp")
    swap = [(d, d ^ 1) for d in range(count)]
    both = ("space", "dp")
    groups = [
        [(chip * 2 + core) * volumes + first + v for v in range(2) for chip in range(count // 2)]
        for core in range(2)
        for first in range(0, volumes, 2)
    ]
    parts = (keep + lax.ppermute(send, "space", swap).astype(F32)).astype(BF16)
    parts = lax.all_to_all(parts, both, 0, 0, axis_index_groups=groups)
    total = jnp.sum(parts.astype(F32), axis=0).astype(BF16)
    moved, step = jnp.zeros_like(total), 2
    while step < volumes:
        moved = lax.ppermute(total, "dp", [(v, v ^ step) for v in range(volumes)])
        if step * 2 < volumes:
            total = (total.astype(F32) + moved.astype(F32)).astype(BF16)
        step *= 2
    copies = pl.pallas_call(
        copies_kernel,
        out_shape=jax.ShapeDtypeStruct(parts.shape, BF16),
        in_specs=[VMEM] * 2,
        out_specs=VMEM,
        compiler_params=vmem(8),
        name="copies",
    )(total, moved)
    copies = lax.all_to_all(copies, both, 0, 0, axis_index_groups=groups)
    return [copies, lax.ppermute(copies, "space", swap)]


def local(volume, neighbours, active, cotangent, weight_one, weight_two, bias_one, bias_two):
    volume, cotangent = volume[0], cotangent[0]
    slots, channels = volume.shape[0], volume.shape[1]
    count = lax.axis_size("space")
    me = lax.axis_index("space").astype(jnp.int32)

    swap = [(d, d ^ 1) for d in range(count)]
    at = [2 * (n // 2) + (n & 1 ^ n // 2 & 1) for n in range(count)]
    hop = [(at[n], at[n + 1]) for n in range(1, count - 1, 2)]
    hop += [(there, here) for here, there in hop]
    pair_volume = lax.ppermute(volume, "space", swap)
    pair_cot = lax.ppermute(cotangent, "space", swap)
    biases = (bias_one[None], bias_two[None])
    weights = jnp.concatenate([weight_one, weight_two], axis=0)
    own = jnp.concatenate([volume, cotangent], axis=0)
    device = (2 * me + ((me ^ (me >> 1)) & 1))[None]
    table = jnp.concatenate([neighbours.transpose(2, 0, 1), active[None]], axis=0)

    def planes(number, dtype=BF16):
        return jax.ShapeDtypeStruct((number, channels, PLANE), dtype)

    def plane_space(number):
        return pltpu.VMEM((number, channels, PLANE), BF16)

    def tap_space(*extent):
        return pltpu.VMEM(extent, BF16)

    def sum_space(*extent):
        return pltpu.VMEM((*extent, channels, PLANE), F32)

    bricks = (slots, channels, CELLS)
    x_planes, cot_planes, edge, layer_mask = pl.pallas_call(
        layout_kernel,
        out_shape=(planes(12), planes(9), planes(4), jax.ShapeDtypeStruct((3, 8, PLANE), F32)),
        in_specs=[SMEM] * 2 + [VMEM] * 3,
        out_specs=(VMEM,) * 4,
        scratch_shapes=[
            pltpu.VMEM((2, *bricks), BF16),
            pltpu.VMEM((2, *bricks), BF16),
        ],
        compiler_params=vmem(8),
        name="layout",
    )(device, table, own, pair_volume, pair_cot)
    outer = lax.ppermute(edge, "space", hop)

    rearranged = jax.ShapeDtypeStruct((3, channels, KDIM), BF16)
    taps, x_taps, one, two, slope_in, g_in, out_in, part_two, w1, w2, w2_back = pl.pallas_call(
        inner_kernel,
        out_shape=(
            jax.ShapeDtypeStruct((4, KDIM, 2 * PLANE), BF16),
            jax.ShapeDtypeStruct((5, KDIM, 2 * PLANE), BF16),
            planes(2, F32),
            planes(2, F32),
            planes(7, F32),
            planes(7),
            planes(6),
            jax.ShapeDtypeStruct((3 * channels, KDIM), F32),
            rearranged,
            rearranged,
            rearranged,
        ),
        in_specs=[SMEM] + [VMEM] * 6,
        out_specs=(VMEM,) * 11,
        scratch_shapes=[
            pltpu.VMEM((channels, 21 * 128), BF16),
            tap_space(KDIM, PLANE),
            tap_space(KDIM, PLANE),
            sum_space(2, 2),
            sum_space(2),
            sum_space(2, 2),
            sum_space(2),
            pltpu.VMEM((9, 16, PLANE), BF16),
        ],
        compiler_params=vmem(20),
        cost_estimate=pl.CostEstimate(flops=2**33, bytes_accessed=2**23, transcendentals=2**20),
        name="inner",
    )(device, x_planes, cot_planes, layer_mask, weights, *biases)

    chunks = (count, ROWS // (2 * count), 128)
    kept, sent = jax.ShapeDtypeStruct(chunks, F32), jax.ShapeDtypeStruct(chunks, BF16)
    keep_two, send_two, slope_out, g_out, out_out, x_pair = pl.pallas_call(
        outer_kernel,
        out_shape=(
            kept,
            sent,
            planes(1, F32),
            planes(3),
            planes(2),
            jax.ShapeDtypeStruct((KDIM, 2 * PLANE), BF16),
        ),
        in_specs=[SMEM] + [VMEM] * 12,
        out_specs=(VMEM,) * 6,
        scratch_shapes=[
            tap_space(KDIM, PLANE),
            tap_space(KDIM, PLANE),
            tap_space(KDIM, 2 * PLANE),
            pltpu.VMEM((3 * channels, KDIM), F32),
            pltpu.VMEM((ROWS, 128), F32),
            pltpu.VMEM((9, 16, PLANE), BF16),
        ],
        compiler_params=vmem(16),
        cost_estimate=pl.CostEstimate(flops=2**32, bytes_accessed=2**23, transcendentals=2**18),
        name="outer",
    )(
        device, outer, cot_planes, layer_mask, w1, w2, *biases, taps, one, two, g_in,
        part_two,
    )
    gradient_keep, gradient_send = pl.pallas_call(
        backward_kernel,
        out_shape=(
            jax.ShapeDtypeStruct((count, 2, *chunks[1:]), F32),
            jax.ShapeDtypeStruct((count, 2, *chunks[1:]), BF16),
        ),
        in_specs=[SMEM] + [VMEM] * 9,
        out_specs=(VMEM,) * 2,
        scratch_shapes=[
            tap_space(2, KDIM, 2 * PLANE),
            sum_space(2, 2),
            sum_space(2),
            plane_space(8),
            pltpu.VMEM((3 * channels, KDIM), F32),
            pltpu.VMEM((ROWS, 128), F32),
            pltpu.VMEM((9, 16, PLANE), BF16),
        ],
        compiler_params=vmem(20),
        cost_estimate=pl.CostEstimate(flops=2**32, bytes_accessed=2**22, transcendentals=0),
        name="backward",
    )(
        device, g_out, g_in, slope_out, slope_in, x_taps, x_pair, w2_back, keep_two, send_two,
    )
    keep, send = pl.pallas_call(
        output_kernel,
        out_shape=(jax.ShapeDtypeStruct(bricks, BF16),) * 2,
        in_specs=[SMEM] * 2 + [VMEM] * 2,
        out_specs=(VMEM,) * 2,
        scratch_shapes=[plane_space(8), pltpu.VMEM(bricks, BF16)],
        compiler_params=vmem(8),
        cost_estimate=pl.CostEstimate(flops=2**28, bytes_accessed=2**21, transcendentals=0),
        name="output",
    )(device, table, out_out, out_in)
    output = (keep + lax.ppermute(send, "space", swap))[None]
    parts = shared_sum(gradient_keep, gradient_send)
    weight_shape = jax.ShapeDtypeStruct((channels, 27 * channels), F32)
    bias_shape = jax.ShapeDtypeStruct((1, channels), F32)
    total_w_one, total_w_two, total_b_one, total_b_two = pl.pallas_call(
        gather_kernel,
        out_shape=(weight_shape, weight_shape, bias_shape, bias_shape),
        in_specs=[SMEM] + [VMEM] * len(parts),
        out_specs=(VMEM,) * 4,
        scratch_shapes=[pltpu.VMEM((2, ROWS, 128), BF16)],
        compiler_params=vmem(8),
        name="gather",
    )(device, *parts)
    return (output, total_w_one, total_w_two, total_b_one[0], total_b_two[0])


def solution(mesh):
    in_specs = (
        P("dp", "space", None, None),
        P("dp", None, None),
        P("dp", None),
        P("dp", "space", None, None),
        P(),
        P(),
        P(),
        P(),
    )
    out_specs = (P("dp", "space", None, None), P(), P(), P(), P())
    return jax.shard_map(local, mesh=mesh, in_specs=in_specs, out_specs=out_specs, check_vma=False)
```

```python
import jax
import jax.numpy as jnp
from jax import lax
from jax.experimental import pallas as pl
from jax.experimental.pallas import tpu as pltpu
from jax.sharding import PartitionSpec as P

EDGE = 8
PLANE = 256
CELLS = 512
KDIM = 896
TILES = 21
ROWS = 2048
DOWN, NEAR_Y, NEAR_Z, UP, LIVE = 4, 10, 12, 21, 26
F32 = jnp.float32
BF16 = jnp.bfloat16


def spread_matrix(back=False):
    near = lax.broadcasted_iota(jnp.int32, (256, 256), 1 if back else 0)
    far = lax.broadcasted_iota(jnp.int32, (256, 256), 0 if back else 1)
    source = ((far >> 3) & 1) * 128 + (far >> 7) * 64 + ((far >> 4) & 7) * 8 + (far & 7)
    return jnp.where(near == source, 1.0, 0.0).astype(BF16)


def fill_masks(masks):
    lane = lax.broadcasted_iota(jnp.int32, (16, PLANE), 1)
    for k in range(9):
        q, r = (lane >> 4) + (k // 3 - 1), (lane & 15) + (k % 3 - 1)
        inside = (q >= 0) & (q < 16) & (r >= 0) & (r < 16)
        masks[k] = jnp.where(inside, 1.0, 0.0).astype(BF16)


def write_taps(dst, plane, masks_ref):
    channels = plane.shape[0]
    for k in range(9):
        step = (k // 3 - 1) * 16 + (k % 3 - 1)
        if step == 0:
            moved = plane
        else:
            moved = pltpu.roll(plane, (-step) % PLANE, 1)
            moved = moved * jnp.concatenate([masks_ref[k]] * (channels // 16), axis=0)
        dst[k * channels : (k + 1) * channels, :] = moved


def space_index(device, count):
    return jnp.clip(device[0] >> 1, 0, count - 1)


def layer_side(device):
    return device[0] & 1


def core_of(device):
    return (device[0] >> 1) & 1


def slot_place(table, slot, pair_slots):
    shift = pair_slots.bit_length() - 1
    up = table[UP, 0, slot]
    inside = jnp.logical_and(up >= 0, up >> shift == slot >> shift)
    parity = jnp.where(inside, 0, 1)
    place = jnp.where(table[NEAR_Y, 0, slot] >= 0, 2, 0) + jnp.where(table[NEAR_Z, 0, slot] >= 0, 1, 0)
    return parity, place


def lane_mask(scalars):
    lane = lax.broadcasted_iota(jnp.int32, (8, PLANE), 1)
    high_y = lane >= 128
    high_z = (lane & 8) != 0
    s = [jnp.full((8, PLANE), v, F32) for v in scalars]
    return jnp.where(high_y, jnp.where(high_z, s[3], s[2]), jnp.where(high_z, s[1], s[0]))


def product(weight_ref, taps, plane_taps=slice(0, 3)):
    left = weight_ref[plane_taps]
    left = left.reshape(left.shape[0] * left.shape[1], KDIM)
    return jnp.dot(left, taps, preferred_element_type=F32)


def pair_sums(full, low, weight_ref, taps, first):
    channels = low.shape[1]
    both = product(weight_ref, taps)
    left, right = both[:, :PLANE], both[:, PLANE:]

    def part(value, a):
        return value[a * channels : (a + 1) * channels]

    before = part(left, 2)
    here = part(left, 1) + part(right, 2)
    full[0] = before if first else low[0] + before
    full[1] = here if first else low[1] + here
    low[0] = part(left, 0) + part(right, 1)
    low[1] = part(right, 0)


def place(k):
    return pl.ds(k * PLANE, PLANE)


def pair_grads(grads, p):
    blank = jnp.zeros_like(grads(3))

    def left(p):
        inside = [grads(p + 1 - a) if 0 <= p + 1 - a < EDGE else blank for a in range(3)]
        return jnp.concatenate(inside, axis=0)

    return jnp.concatenate([left(p), left(p + 1)], axis=1)


def weight_part(left, taps):
    return lax.dot_general(left, taps, (((1,), (1,)), ((), ())), preferred_element_type=F32)


def weight_products(total, grads, planes, taps, start=None):
    for first in range(0, KDIM, 256):
        rows = slice(first, min(first + 256, KDIM))
        block = None if start is None else start[:, rows]
        for p in planes:
            part = weight_part(pair_grads(grads, p), taps(p, rows))
            block = part if block is None else block + part
        total[:, rows] = block


def write_tiles(flat, total, channels, even):
    lane = lax.broadcasted_iota(jnp.int32, (channels, 128), 1)
    blank = jnp.zeros((channels, 128), F32)
    first, last = total[:channels, :], total[2 * channels :, :]
    low, high = jnp.where(even, first, last), jnp.where(even, last, first)
    second = jnp.concatenate([total[channels : 2 * channels, :], blank], axis=1)
    third = jnp.concatenate([high, blank], axis=1)
    second = pltpu.roll(second, 96, 1)
    third = pltpu.roll(third, 64, 1)

    def cut(value, k):
        return value[:, k * 128 : (k + 1) * 128]

    tiles = [cut(low, k) for k in range(6)]
    tiles.append(jnp.where(lane < 96, cut(low, 6), cut(second, 0)))
    tiles += [cut(second, k) for k in range(1, 7)]
    tiles.append(jnp.where(lane < 64, cut(second, 7), cut(third, 0)))
    tiles += [cut(third, k) for k in range(1, 8)]
    for k in range(TILES):
        flat[k * channels : (k + 1) * channels, :] = tiles[k]
    flat[TILES * channels :, :] = jnp.zeros((ROWS - TILES * channels, 128), F32)


def split_tiles(keep_ref, send_ref, flat, device):
    chunks, rows = keep_ref.shape[0], keep_ref.shape[1]
    even = core_of(device) == 0
    here = jnp.where(even, 0, chunks * rows)
    there = jnp.where(even, chunks * rows, 0)
    for k in range(chunks):
        at = pl.multiple_of(here + k * rows, rows)
        keep_ref[k] = flat[pl.ds(at, rows), :]
        at = pl.multiple_of(there + k * rows, rows)
        send_ref[k] = flat[pl.ds(at, rows), :].astype(BF16)


def layout_kernel(
    device, table, own_ref, pair_ref, cot_pair_ref,
    x_ref, cot_ref, edge_ref, mask_ref, bricks, cots,
):
    slots, channels = pair_ref.shape[0], pair_ref.shape[1]
    all_slots = table.shape[2]
    me = space_index(device, all_slots // slots)
    layer = layer_side(device)
    even = layer == 0

    live = [[jnp.float32(0)] * 4 for _ in range(2)]
    beyond = [jnp.float32(0)] * 4
    for index in (me, me ^ 1):
        for s in range(slots):
            slot = jnp.clip(index * slots + s, 0, all_slots - 1)
            parity, spot = slot_place(table, slot, 2 * slots)
            alive = table[LIVE, 0, slot].astype(F32)
            scale = jnp.full((channels, CELLS), alive, F32).astype(BF16)
            own = index is me
            bricks[parity, spot] = (own_ref[s] if own else pair_ref[s]) * scale
            cots[parity, spot] = (own_ref[slots + s] if own else cot_pair_ref[s]) * scale
            outer = jnp.where(even, table[DOWN, 0, slot], table[UP, 0, slot])
            alive_outer = table[LIVE, 0, jnp.clip(outer, 0, all_slots - 1)].astype(F32)
            alive_outer = jnp.where(outer >= 0, alive_outer, 0.0)
            for k in range(4):
                for p in range(2):
                    here = jnp.logical_and(parity == p, spot == k)
                    live[p][k] = jnp.where(here, alive, live[p][k])
                here = jnp.logical_and(parity == layer, spot == k)
                beyond[k] = jnp.where(here, alive_outer, beyond[k])
    mask_ref[0] = lane_mask(beyond)
    mask_ref[1] = lane_mask([jnp.where(even, live[0][k], live[1][k]) for k in range(4)])
    mask_ref[2] = lane_mask([jnp.where(even, live[1][k], live[0][k]) for k in range(4)])

    move = spread_matrix()
    mine = jnp.where(even, 0, 1)

    def spread(left, right):
        two = jnp.concatenate([left, right], axis=1)
        return jnp.dot(two, move, preferred_element_type=F32).astype(BF16)

    for y in range(2):
        row = slice(y * 128, (y + 1) * 128)
        for j in range(4):
            pair = slice(j * 128, (j + 1) * 128)
            first = jnp.where(even, 2 * j, 7 - 2 * j)
            second = jnp.where(even, 2 * j + 1, 6 - 2 * j)
            both = spread(bricks[mine, 2 * y, :, pair], bricks[mine, 2 * y + 1, :, pair])
            x_ref[first, :, row] = both[:, :128]
            x_ref[second, :, row] = both[:, 128:]
            both = spread(cots[mine, 2 * y, :, pair], cots[mine, 2 * y + 1, :, pair])
            cot_ref[first, :, row] = both[:, :128]
            cot_ref[second, :, row] = both[:, 128:]
        for j in range(2):
            start = pl.multiple_of(jnp.where(even, j * 128, 256 + j * 128), 128)
            pair = pl.ds(start, 128)
            both = spread(
                bricks[1 - mine, 2 * y, :, pair], bricks[1 - mine, 2 * y + 1, :, pair]
            )
            x_ref[jnp.where(even, 8 + 2 * j, 11 - 2 * j), :, row] = both[:, :128]
            x_ref[jnp.where(even, 9 + 2 * j, 10 - 2 * j), :, row] = both[:, 128:]
        pair = pl.ds(pl.multiple_of(jnp.where(even, 0, 384), 128), 128)
        both = spread(cots[1 - mine, 2 * y, :, pair], cots[1 - mine, 2 * y + 1, :, pair])
        side = jnp.full((channels, 128), jnp.where(even, 1.0, 0.0), F32).astype(BF16)
        cot_ref[8, :, row] = both[:, :128] * side + both[:, 128:] * (1 - side)
    edge_ref[:3] = x_ref[:3]
    edge_ref[3] = cot_ref[0]


def tap_weights(out_ref, weight, wide, even):
    channels, width = weight.shape
    wide[:, :width] = weight
    lane = lax.broadcasted_iota(jnp.int32, (channels, 128), 1)
    for a, (tile, moved) in enumerate(((0, 0), (6, 96), (13, 64))):
        span = wide[:, tile * 128 : (tile + 8) * 128].astype(F32)
        if moved:
            span = pltpu.roll(span, 1024 - moved, 1)
        last = jnp.where(lane < 96, span[:, 768:KDIM], 0.0)
        span = jnp.concatenate([span[:, :768], last], axis=1)
        at = a if a == 1 else jnp.where(even, a, 2 - a)
        out_ref[at] = span.astype(BF16)


def back_weights(out_ref, taps_ref):
    channels = taps_ref.shape[1]
    lane = lax.broadcasted_iota(jnp.int32, (channels, 128), 1)
    more = jnp.zeros((128 - channels, KDIM), F32)
    for a in range(3):
        block = jnp.concatenate([taps_ref[2 - a].astype(F32), more], axis=0)
        turned = block.T
        tiles = [jnp.zeros((channels, 128), F32)] * 7
        for k in range(9):
            piece = turned[(8 - k) * channels : (9 - k) * channels, :]
            tile, moved = divmod(k * channels, 128)
            if moved:
                piece = pltpu.roll(piece, moved, 1)
            tiles[tile] = tiles[tile] + jnp.where(lane >= moved, piece, 0.0)
            if moved + channels > 128:
                tiles[tile + 1] = tiles[tile + 1] + jnp.where(lane < moved, piece, 0.0)
        out_ref[a] = jnp.concatenate(tiles, axis=1).astype(BF16)


def column(row):
    return jnp.broadcast_to(row, (8, row.shape[1])).T[:, :1]


def layer_of(q):
    return 0 if q < 0 else 1 if q < EDGE else 2


def hidden_plane(pre, mask):
    sigma = jax.nn.sigmoid(pre)
    return (pre * sigma * mask).astype(BF16), sigma * (1.0 + pre * (1.0 - sigma)) * mask


def out_plane(pre, mask, cot):
    sigma = jax.nn.sigmoid(pre)
    grad = cot.astype(F32) * (sigma * (1.0 + pre * (1.0 - sigma)))
    return (pre * sigma * mask).astype(BF16), grad.astype(BF16)


def inner_kernel(
    device, x_ref, cot_ref, layer_mask, weight_ref, b1_ref, b2_ref,
    taps_ref, x_taps, one_ref, two_ref, slope_ref, g_ref, out_ref, total_ref, w1_taps, w2_taps, w2_back,
    wide, xc, hc, full_one, low_one, full_two, low_two, masks_ref,
):
    channels = x_ref.shape[1]
    even = layer_side(device) == 0
    fill_masks(masks_ref)
    tap_weights(w1_taps, weight_ref[:channels, :], wide, even)
    bias_one, bias_two = column(b1_ref[...]), column(b2_ref[...])
    ones = jnp.ones((KDIM - 9 * channels, 2 * PLANE), BF16)
    for k in range(5):
        x_taps[k, 9 * channels :, :] = ones
    for k in range(4):
        taps_ref[k, 9 * channels :, :] = ones
    for single in (xc, hc):
        single[9 * channels :, :] = ones[:, :PLANE]

    def write_x(p):
        write_taps(x_taps.at[p // 2, :, place(p & 1)] if p < 10 else xc, x_ref[p], masks_ref)

    def finish_one(q, pre):
        hidden, slope = hidden_plane(pre + bias_one, layer_mask[layer_of(q)][:1])
        dst = taps_ref.at[(q - 1) // 2, :, place((q - 1) & 1)] if q < 9 else hc
        write_taps(dst, hidden, masks_ref)
        if q < EDGE:
            slope_ref[q - 1] = slope

    def finish_two(q, pre):
        out, grad = out_plane(pre + bias_two, layer_mask[layer_of(q)][:1], cot_ref[q])
        g_ref[q - 2] = grad
        if q < EDGE:
            out_ref[q - 2] = out

    write_x(0)
    write_x(1)
    for j in range(8):
        now, last = j & 1, (j + 1) & 1
        if j < 5:
            pair_sums(full_one.at[now], low_one, w1_taps, x_taps[j], j == 0)
            for p in (2 * j + 2, 2 * j + 3):
                if p <= 10:
                    write_x(p)
        if j == 5:
            third = product(w1_taps, xc[...], slice(2, 3))
            full_one[now, 0] = low_one[0] + third
        if j == 0:
            tap_weights(w2_taps, weight_ref[channels:, :], wide, even)
        if j == 1:
            one_ref[...] = full_one[0]
            back_weights(w2_back, w2_taps)
        if 2 <= j <= 5:
            finish_one(2 * j - 3, full_one[last, 0])
            finish_one(2 * j - 2, full_one[last, 1])
        if j == 6:
            finish_one(9, full_one[last, 0])
        if 3 <= j <= 6:
            pair_sums(full_two.at[now], low_two, w2_taps, taps_ref[j - 3], j == 3)
        if j == 7:
            third = product(w2_taps, hc[...], slice(2, 3))
            finish_two(8, low_two[0] + third)
        if j == 4:
            two_ref[...] = full_two[last]
        if 5 <= j:
            finish_two(2 * j - 8, full_two[last, 0])
            finish_two(2 * j - 7, full_two[last, 1])

    def taps(p, rows):
        return taps_ref[p // 2, rows]

    weight_products(total_ref, lambda q: g_ref[q - 2], (3, 5, 7), taps)


def outer_kernel(
    device, edge_ref, cot_ref, layer_mask, w1_taps, w2_taps, w2_back, b1_ref, b2_ref,
    taps_ref, x_taps, one_ref, two_ref, slope_in_ref, g_in_ref, total_ref,
    keep_ref, send_ref, out_ref,
    xc, hc, x_pair, h_pair, gc, slope_out_ref, g_out_ref, full, low, grad, total, flat, masks_ref,
):
    channels = cot_ref.shape[1]
    even = layer_side(device) == 0
    fill_masks(masks_ref)
    bias_one, bias_two = column(b1_ref[...]), column(b2_ref[...])
    ones = jnp.ones((KDIM - 9 * channels, 2 * PLANE), BF16)
    for single in (xc, hc):
        single[9 * channels :, :] = ones[:, :PLANE]
    for pair in (x_pair, h_pair):
        pair[9 * channels :, :] = ones
    write_taps(xc, edge_ref[2], masks_ref)
    write_taps(x_pair.at[:, place(0)], edge_ref[1], masks_ref)
    write_taps(x_pair.at[:, place(1)], edge_ref[0], masks_ref)

    def three_planes(weights, single, pair, parts):
        first = product(weights, single[...], slice(0, 1))
        both = product(weights, pair[...])
        left, right = both[:, :PLANE], both[:, PLANE:]
        one, two = slice(channels, 2 * channels), slice(2 * channels, 3 * channels)
        return (
            first + left[one] + right[two],
            left[:channels] + right[one] + parts[0],
            right[:channels] + parts[1],
        )

    for q, pre in zip(range(-2, 1), three_planes(w1_taps, xc, x_pair, one_ref)):
        hidden, slope = hidden_plane(pre + bias_one, layer_mask[layer_of(q)][:1])
        write_taps(hc if q == -2 else h_pair.at[:, place(q + 1)], hidden, masks_ref)
        if q == 0:
            slope_out_ref[0] = slope
    for q, pre in zip(range(-1, 2), three_planes(w2_taps, hc, h_pair, two_ref)):
        cot = edge_ref[3] if q < 0 else cot_ref[q]
        out, g_out_ref[q + 1] = out_plane(pre + bias_two, layer_mask[layer_of(q)][:1], cot)
        if q >= 0:
            out_ref[q] = out

    def grads(q):
        return g_out_ref[q + 1] if q < 2 else g_in_ref[q - 2]

    for k in range(2):
        gc[k, 9 * channels :, :] = ones

    def write_g(q):
        plane = g_out_ref[q + 1] if q < 2 else g_in_ref[q - 2]
        write_taps(gc.at[((q + 1) >> 1) & 1, :, place((q + 1) & 1)], plane, masks_ref)

    write_g(-1)
    write_g(0)
    for j in range(6):
        now, last = j & 1, (j + 1) & 1
        if j < 5:
            pair_sums(full.at[now], low, w2_back, gc[now], j == 0)
            for q in (2 * j + 1, 2 * j + 2):
                if q <= 8:
                    write_g(q)
        if j == 0:
            part = weight_part(pair_grads(grads, -1), h_pair[...])
            total[...] = total_ref[...] + part
        if j == 1:
            total[...] = total[...] + weight_part(pair_grads(grads, 1), taps_ref[0])
        if j == 2:
            write_tiles(flat, total, channels, even)
            split_tiles(keep_ref.at[:, 1], send_ref.at[:, 1], flat, device)
        if j >= 2:
            for k, q in enumerate((2 * j - 4, 2 * j - 3)):
                slope = slope_out_ref[0] if q == 0 else slope_in_ref[q - 1]
                grad[q] = (full[last, k] * slope).astype(BF16)
        if j >= 3:
            for p in (2 * j - 6,) if j < 5 else (4, 6):
                part = weight_part(pair_grads(lambda q: grad[q], p), x_taps[p // 2])
                total[...] = part if p == 0 else total[...] + part
    low_rows, high_rows = slice(0, channels), slice(2 * channels, 3 * channels)
    total[low_rows] = total[low_rows] + weight_part(grad[0], x_pair[:, PLANE:])
    total[high_rows] = total[high_rows] + weight_part(grad[EDGE - 1], x_taps[4, :, :PLANE])
    write_tiles(flat, total, channels, even)
    split_tiles(keep_ref.at[:, 0], send_ref.at[:, 0], flat, device)


def output_kernel(device, table, first_ref, second_ref, keep_ref, send_ref, outs, bricks):
    slots, channels = keep_ref.shape[0], keep_ref.shape[1]
    me = space_index(device, table.shape[2] // slots)
    layer = layer_side(device)
    even = layer == 0
    outs[:2] = first_ref[...]
    outs[2:] = second_ref[...]
    back = spread_matrix(True)
    for y in range(2):
        row = slice(y * 128, (y + 1) * 128)
        for j in range(4):
            first = jnp.where(even, 2 * j, 7 - 2 * j)
            second = jnp.where(even, 2 * j + 1, 6 - 2 * j)
            two = jnp.concatenate([outs[first, :, row], outs[second, :, row]], axis=1)
            both = jnp.dot(two, back, preferred_element_type=F32).astype(BF16)
            pair = slice(j * 128, (j + 1) * 128)
            bricks[2 * y, :, pair] = both[:, :128]
            bricks[2 * y + 1, :, pair] = both[:, 128:]
    for target, index in ((keep_ref, me), (send_ref, me ^ 1)):
        for s in range(slots):
            slot = jnp.clip(index * slots + s, 0, table.shape[2] - 1)
            parity, spot = slot_place(table, slot, 2 * slots)
            scale = jnp.where(parity == layer, 1.0, 0.0)
            target[s] = bricks[spot] * jnp.full((channels, CELLS), scale, F32).astype(BF16)


def copies_kernel(first_ref, second_ref, out_ref):
    total = (first_ref[...].astype(F32) + second_ref[...].astype(F32)).astype(BF16)
    for k in range(out_ref.shape[0]):
        out_ref[k] = total


def gather_kernel(
    device, own_ref, other_ref, w_one_ref, w_two_ref, b_one_ref, b_two_ref, flat
):
    chunks, _, rows, _ = own_ref.shape
    channels = w_one_ref.shape[0]
    core = core_of(device)
    for half, source in enumerate((own_ref, other_ref)):
        base = jnp.where(core == half, 0, chunks * rows)
        for k in range(chunks):
            at = pl.multiple_of(base + k * rows, rows)
            flat[:, pl.ds(at, rows), :] = source[k]
    for n, (weight, bias) in enumerate(((w_one_ref, b_one_ref), (w_two_ref, b_two_ref))):
        for k in range(TILES - 1):
            tile = flat[n, k * channels : (k + 1) * channels, :]
            weight[:, k * 128 : (k + 1) * 128] = tile.astype(F32)
        last = flat[n, (TILES - 1) * channels : TILES * channels, :].astype(F32)
        weight[:, 2560:2592] = last[:, :32]
        bias[...] = last.T[32:33, :]


VMEM = pl.BlockSpec(memory_space=pltpu.VMEM)
SMEM = pl.BlockSpec(memory_space=pltpu.SMEM)


def vmem(mebibytes):
    return pltpu.CompilerParams(vmem_limit_bytes=mebibytes * 2**20)


def shared_sum(keep, send):
    count = lax.axis_size("space")
    volumes = lax.axis_size("dp")
    swap = [(d, d ^ 1) for d in range(count)]
    both = ("space", "dp")
    groups = [
        [(chip * 2 + core) * volumes + first + v for v in range(2) for chip in range(count // 2)]
        for core in range(2)
        for first in range(0, volumes, 2)
    ]
    parts = (keep + lax.ppermute(send, "space", swap).astype(F32)).astype(BF16)
    parts = lax.all_to_all(parts, both, 0, 0, axis_index_groups=groups)
    total = jnp.sum(parts.astype(F32), axis=0).astype(BF16)
    moved, step = jnp.zeros_like(total), 2
    while step < volumes:
        moved = lax.ppermute(total, "dp", [(v, v ^ step) for v in range(volumes)])
        if step * 2 < volumes:
            total = (total.astype(F32) + moved.astype(F32)).astype(BF16)
        step *= 2
    copies = pl.pallas_call(
        copies_kernel,
        out_shape=jax.ShapeDtypeStruct(parts.shape, BF16),
        in_specs=[VMEM] * 2,
        out_specs=VMEM,
        compiler_params=vmem(8),
        name="copies",
    )(total, moved)
    copies = lax.all_to_all(copies, both, 0, 0, axis_index_groups=groups)
    return [copies, lax.ppermute(copies, "space", swap)]


def local(volume, neighbours, active, cotangent, weight_one, weight_two, bias_one, bias_two):
    volume, cotangent = volume[0], cotangent[0]
    slots, channels = volume.shape[0], volume.shape[1]
    count = lax.axis_size("space")
    me = lax.axis_index("space").astype(jnp.int32)

    swap = [(d, d ^ 1) for d in range(count)]
    at = [2 * (n // 2) + (n & 1 ^ n // 2 & 1) for n in range(count)]
    hop = [(at[n], at[n + 1]) for n in range(1, count - 1, 2)]
    hop += [(there, here) for here, there in hop]
    pair_volume = lax.ppermute(volume, "space", swap)
    pair_cot = lax.ppermute(cotangent, "space", swap)
    biases = (bias_one[None], bias_two[None])
    weights = jnp.concatenate([weight_one, weight_two], axis=0)
    own = jnp.concatenate([volume, cotangent], axis=0)
    device = (2 * me + ((me ^ (me >> 1)) & 1))[None]
    table = jnp.concatenate([neighbours.transpose(2, 0, 1), active[None]], axis=0)

    def planes(number, dtype=BF16):
        return jax.ShapeDtypeStruct((number, channels, PLANE), dtype)

    def plane_space(number):
        return pltpu.VMEM((number, channels, PLANE), BF16)

    def tap_space(*extent):
        return pltpu.VMEM(extent, BF16)

    def sum_space(*extent):
        return pltpu.VMEM((*extent, channels, PLANE), F32)

    bricks = (slots, channels, CELLS)
    x_planes, cot_planes, edge, layer_mask = pl.pallas_call(
        layout_kernel,
        out_shape=(planes(12), planes(9), planes(4), jax.ShapeDtypeStruct((3, 8, PLANE), F32)),
        in_specs=[SMEM] * 2 + [VMEM] * 3,
        out_specs=(VMEM,) * 4,
        scratch_shapes=[
            pltpu.VMEM((2, *bricks), BF16),
            pltpu.VMEM((2, *bricks), BF16),
        ],
        compiler_params=vmem(8),
        name="layout",
    )(device, table, own, pair_volume, pair_cot)
    outer = lax.ppermute(edge, "space", hop)

    rearranged = jax.ShapeDtypeStruct((3, channels, KDIM), BF16)
    taps, x_taps, one, two, slope_in, g_in, out_in, part_two, w1, w2, w2_back = pl.pallas_call(
        inner_kernel,
        out_shape=(
            jax.ShapeDtypeStruct((4, KDIM, 2 * PLANE), BF16),
            jax.ShapeDtypeStruct((5, KDIM, 2 * PLANE), BF16),
            planes(2, F32),
            planes(2, F32),
            planes(7, F32),
            planes(7),
            planes(6),
            jax.ShapeDtypeStruct((3 * channels, KDIM), F32),
            rearranged,
            rearranged,
            rearranged,
        ),
        in_specs=[SMEM] + [VMEM] * 6,
        out_specs=(VMEM,) * 11,
        scratch_shapes=[
            pltpu.VMEM((channels, 21 * 128), BF16),
            tap_space(KDIM, PLANE),
            tap_space(KDIM, PLANE),
            sum_space(2, 2),
            sum_space(2),
            sum_space(2, 2),
            sum_space(2),
            pltpu.VMEM((9, 16, PLANE), BF16),
        ],
        compiler_params=vmem(20),
        cost_estimate=pl.CostEstimate(flops=2**33, bytes_accessed=2**23, transcendentals=2**20),
        name="inner",
    )(device, x_planes, cot_planes, layer_mask, weights, *biases)

    halves = (count, 2, ROWS // (2 * count), 128)
    gradient_keep, gradient_send, out_out = pl.pallas_call(
        outer_kernel,
        out_shape=(
            jax.ShapeDtypeStruct(halves, F32),
            jax.ShapeDtypeStruct(halves, BF16),
            planes(2),
        ),
        in_specs=[SMEM] + [VMEM] * 15,
        out_specs=(VMEM,) * 3,
        scratch_shapes=[
            tap_space(KDIM, PLANE),
            tap_space(KDIM, PLANE),
            tap_space(KDIM, 2 * PLANE),
            tap_space(KDIM, 2 * PLANE),
            tap_space(2, KDIM, 2 * PLANE),
            sum_space(1),
            plane_space(3),
            sum_space(2, 2),
            sum_space(2),
            plane_space(8),
            pltpu.VMEM((3 * channels, KDIM), F32),
            pltpu.VMEM((ROWS, 128), F32),
            pltpu.VMEM((9, 16, PLANE), BF16),
        ],
        compiler_params=vmem(24),
        cost_estimate=pl.CostEstimate(flops=2**33, bytes_accessed=2**23, transcendentals=2**18),
        name="outer",
    )(
        device, outer, cot_planes, layer_mask, w1, w2, w2_back, *biases, taps, x_taps, one, two,
        slope_in, g_in, part_two,
    )
    keep, send = pl.pallas_call(
        output_kernel,
        out_shape=(jax.ShapeDtypeStruct(bricks, BF16),) * 2,
        in_specs=[SMEM] * 2 + [VMEM] * 2,
        out_specs=(VMEM,) * 2,
        scratch_shapes=[plane_space(8), pltpu.VMEM(bricks, BF16)],
        compiler_params=vmem(8),
        cost_estimate=pl.CostEstimate(flops=2**28, bytes_accessed=2**21, transcendentals=0),
        name="output",
    )(device, table, out_out, out_in)
    output = (keep + lax.ppermute(send, "space", swap))[None]
    parts = shared_sum(gradient_keep, gradient_send)
    weight_shape = jax.ShapeDtypeStruct((channels, 27 * channels), F32)
    bias_shape = jax.ShapeDtypeStruct((1, channels), F32)
    total_w_one, total_w_two, total_b_one, total_b_two = pl.pallas_call(
        gather_kernel,
        out_shape=(weight_shape, weight_shape, bias_shape, bias_shape),
        in_specs=[SMEM] + [VMEM] * len(parts),
        out_specs=(VMEM,) * 4,
        scratch_shapes=[pltpu.VMEM((2, ROWS, 128), BF16)],
        compiler_params=vmem(8),
        name="gather",
    )(device, *parts)
    return (output, total_w_one, total_w_two, total_b_one[0], total_b_two[0])


def solution(mesh):
    in_specs = (
        P("dp", "space", None, None),
        P("dp", None, None),
        P("dp", None),
        P("dp", "space", None, None),
        P(),
        P(),
        P(),
        P(),
    )
    out_specs = (P("dp", "space", None, None), P(), P(), P(), P())
    return jax.shard_map(local, mesh=mesh, in_specs=in_specs, out_specs=out_specs, check_vma=False)
```

```python
import jax
import jax.numpy as jnp
from jax import lax
from jax.experimental import pallas as pl
from jax.experimental.pallas import tpu as pltpu
from jax.sharding import PartitionSpec as P

EDGE = 8
PLANE = 256
CELLS = 512
KDIM = 896
TILES = 21
ROWS = 2048
DOWN, NEAR_Y, NEAR_Z, UP, LIVE = 4, 10, 12, 21, 26
F32 = jnp.float32
BF16 = jnp.bfloat16


def spread_matrix(back=False):
    near = lax.broadcasted_iota(jnp.int32, (256, 256), 1 if back else 0)
    far = lax.broadcasted_iota(jnp.int32, (256, 256), 0 if back else 1)
    source = ((far >> 3) & 1) * 128 + (far >> 7) * 64 + ((far >> 4) & 7) * 8 + (far & 7)
    return jnp.where(near == source, 1.0, 0.0).astype(BF16)


def fill_masks(masks):
    lane = lax.broadcasted_iota(jnp.int32, (16, PLANE), 1)
    for k in range(9):
        q, r = (lane >> 4) + (k // 3 - 1), (lane & 15) + (k % 3 - 1)
        inside = (q >= 0) & (q < 16) & (r >= 0) & (r < 16)
        masks[k] = jnp.where(inside, 1.0, 0.0).astype(BF16)


def write_taps(dst, plane, masks_ref):
    channels = plane.shape[0]
    for k in range(9):
        step = (k // 3 - 1) * 16 + (k % 3 - 1)
        if step == 0:
            moved = plane
        else:
            moved = pltpu.roll(plane, (-step) % PLANE, 1)
            moved = moved * jnp.concatenate([masks_ref[k]] * (channels // 16), axis=0)
        dst[k * channels : (k + 1) * channels, :] = moved


def space_index(device, count):
    return jnp.clip(device[0] >> 1, 0, count - 1)


def layer_side(device):
    return device[0] & 1


def core_of(device):
    return (device[0] >> 1) & 1


def slot_place(table, slot, pair_slots):
    shift = pair_slots.bit_length() - 1
    up = table[UP, 0, slot]
    inside = jnp.logical_and(up >= 0, up >> shift == slot >> shift)
    parity = jnp.where(inside, 0, 1)
    place = jnp.where(table[NEAR_Y, 0, slot] >= 0, 2, 0) + jnp.where(table[NEAR_Z, 0, slot] >= 0, 1, 0)
    return parity, place


def lane_mask(scalars):
    lane = lax.broadcasted_iota(jnp.int32, (8, PLANE), 1)
    high_y = lane >= 128
    high_z = (lane & 8) != 0
    s = [jnp.full((8, PLANE), v, F32) for v in scalars]
    return jnp.where(high_y, jnp.where(high_z, s[3], s[2]), jnp.where(high_z, s[1], s[0]))


def product(weight_ref, taps, plane_taps=slice(0, 3)):
    left = weight_ref[plane_taps]
    left = left.reshape(left.shape[0] * left.shape[1], KDIM)
    return jnp.dot(left, taps, preferred_element_type=F32)


def pair_sums(full, low, weight_ref, taps, first):
    channels = low.shape[1]
    both = product(weight_ref, taps)
    left, right = both[:, :PLANE], both[:, PLANE:]

    def part(value, a):
        return value[a * channels : (a + 1) * channels]

    before = part(left, 2)
    here = part(left, 1) + part(right, 2)
    full[0] = before if first else low[0] + before
    full[1] = here if first else low[1] + here
    low[0] = part(left, 0) + part(right, 1)
    low[1] = part(right, 0)


def place(k):
    return pl.ds(k * PLANE, PLANE)


def pair_grads(grads, p):
    blank = jnp.zeros_like(grads(3))

    def left(p):
        inside = [grads(p + 1 - a) if 0 <= p + 1 - a < EDGE else blank for a in range(3)]
        return jnp.concatenate(inside, axis=0)

    return jnp.concatenate([left(p), left(p + 1)], axis=1)


def weight_part(left, taps):
    return lax.dot_general(left, taps, (((1,), (1,)), ((), ())), preferred_element_type=F32)


def weight_products(total, grads, planes, taps, start=None):
    for first in range(0, KDIM, 256):
        rows = slice(first, min(first + 256, KDIM))
        block = None if start is None else start[:, rows]
        for p in planes:
            part = weight_part(pair_grads(grads, p), taps(p, rows))
            block = part if block is None else block + part
        total[:, rows] = block


def write_tiles(flat, total, channels, even):
    lane = lax.broadcasted_iota(jnp.int32, (channels, 128), 1)
    blank = jnp.zeros((channels, 128), F32)
    first, last = total[:channels, :], total[2 * channels :, :]
    low, high = jnp.where(even, first, last), jnp.where(even, last, first)
    second = jnp.concatenate([total[channels : 2 * channels, :], blank], axis=1)
    third = jnp.concatenate([high, blank], axis=1)
    second = pltpu.roll(second, 96, 1)
    third = pltpu.roll(third, 64, 1)

    def cut(value, k):
        return value[:, k * 128 : (k + 1) * 128]

    tiles = [cut(low, k) for k in range(6)]
    tiles.append(jnp.where(lane < 96, cut(low, 6), cut(second, 0)))
    tiles += [cut(second, k) for k in range(1, 7)]
    tiles.append(jnp.where(lane < 64, cut(second, 7), cut(third, 0)))
    tiles += [cut(third, k) for k in range(1, 8)]
    for k in range(TILES):
        flat[k * channels : (k + 1) * channels, :] = tiles[k]
    flat[TILES * channels :, :] = jnp.zeros((ROWS - TILES * channels, 128), F32)


def split_tiles(keep_ref, send_ref, flat, device):
    chunks, rows = keep_ref.shape[0], keep_ref.shape[1]
    even = core_of(device) == 0
    here = jnp.where(even, 0, chunks * rows)
    there = jnp.where(even, chunks * rows, 0)
    for k in range(chunks):
        at = pl.multiple_of(here + k * rows, rows)
        keep_ref[k] = flat[pl.ds(at, rows), :]
        at = pl.multiple_of(there + k * rows, rows)
        send_ref[k] = flat[pl.ds(at, rows), :].astype(BF16)


def layout_kernel(
    device, table, own_ref, pair_ref, cot_pair_ref,
    x_ref, cot_ref, edge_ref, mask_ref, bricks, cots,
):
    slots, channels = pair_ref.shape[0], pair_ref.shape[1]
    all_slots = table.shape[2]
    me = space_index(device, all_slots // slots)
    layer = layer_side(device)
    even = layer == 0

    live = [[jnp.float32(0)] * 4 for _ in range(2)]
    beyond = [jnp.float32(0)] * 4
    for index in (me, me ^ 1):
        for s in range(slots):
            slot = jnp.clip(index * slots + s, 0, all_slots - 1)
            parity, spot = slot_place(table, slot, 2 * slots)
            alive = table[LIVE, 0, slot].astype(F32)
            scale = jnp.full((channels, CELLS), alive, F32).astype(BF16)
            own = index is me
            bricks[parity, spot] = (own_ref[s] if own else pair_ref[s]) * scale
            cots[parity, spot] = (own_ref[slots + s] if own else cot_pair_ref[s]) * scale
            outer = jnp.where(even, table[DOWN, 0, slot], table[UP, 0, slot])
            alive_outer = table[LIVE, 0, jnp.clip(outer, 0, all_slots - 1)].astype(F32)
            alive_outer = jnp.where(outer >= 0, alive_outer, 0.0)
            for k in range(4):
                for p in range(2):
                    here = jnp.logical_and(parity == p, spot == k)
                    live[p][k] = jnp.where(here, alive, live[p][k])
                here = jnp.logical_and(parity == layer, spot == k)
                beyond[k] = jnp.where(here, alive_outer, beyond[k])
    mask_ref[0] = lane_mask(beyond)
    mask_ref[1] = lane_mask([jnp.where(even, live[0][k], live[1][k]) for k in range(4)])
    mask_ref[2] = lane_mask([jnp.where(even, live[1][k], live[0][k]) for k in range(4)])

    move = spread_matrix()
    mine = jnp.where(even, 0, 1)

    def spread(left, right):
        two = jnp.concatenate([left, right], axis=1)
        return jnp.dot(two, move, preferred_element_type=F32).astype(BF16)

    for y in range(2):
        row = slice(y * 128, (y + 1) * 128)
        for j in range(4):
            pair = slice(j * 128, (j + 1) * 128)
            first = jnp.where(even, 2 * j, 7 - 2 * j)
            second = jnp.where(even, 2 * j + 1, 6 - 2 * j)
            both = spread(bricks[mine, 2 * y, :, pair], bricks[mine, 2 * y + 1, :, pair])
            x_ref[first, :, row] = both[:, :128]
            x_ref[second, :, row] = both[:, 128:]
            both = spread(cots[mine, 2 * y, :, pair], cots[mine, 2 * y + 1, :, pair])
            cot_ref[first, :, row] = both[:, :128]
            cot_ref[second, :, row] = both[:, 128:]
        for j in range(2):
            start = pl.multiple_of(jnp.where(even, j * 128, 256 + j * 128), 128)
            pair = pl.ds(start, 128)
            both = spread(
                bricks[1 - mine, 2 * y, :, pair], bricks[1 - mine, 2 * y + 1, :, pair]
            )
            x_ref[jnp.where(even, 8 + 2 * j, 11 - 2 * j), :, row] = both[:, :128]
            x_ref[jnp.where(even, 9 + 2 * j, 10 - 2 * j), :, row] = both[:, 128:]
        pair = pl.ds(pl.multiple_of(jnp.where(even, 0, 384), 128), 128)
        both = spread(cots[1 - mine, 2 * y, :, pair], cots[1 - mine, 2 * y + 1, :, pair])
        side = jnp.full((channels, 128), jnp.where(even, 1.0, 0.0), F32).astype(BF16)
        cot_ref[8, :, row] = both[:, :128] * side + both[:, 128:] * (1 - side)
    edge_ref[:3] = x_ref[:3]
    edge_ref[3] = cot_ref[0]


def tap_weights(out_ref, weight, wide, even):
    channels, width = weight.shape
    wide[:, :width] = weight
    lane = lax.broadcasted_iota(jnp.int32, (channels, 128), 1)
    for a, (tile, moved) in enumerate(((0, 0), (6, 96), (13, 64))):
        span = wide[:, tile * 128 : (tile + 8) * 128].astype(F32)
        if moved:
            span = pltpu.roll(span, 1024 - moved, 1)
        last = jnp.where(lane < 96, span[:, 768:KDIM], 0.0)
        span = jnp.concatenate([span[:, :768], last], axis=1)
        at = a if a == 1 else jnp.where(even, a, 2 - a)
        out_ref[at] = span.astype(BF16)


def back_weights(out_ref, taps_ref):
    channels = taps_ref.shape[1]
    lane = lax.broadcasted_iota(jnp.int32, (channels, 128), 1)
    more = jnp.zeros((128 - channels, KDIM), F32)
    for a in range(3):
        block = jnp.concatenate([taps_ref[2 - a].astype(F32), more], axis=0)
        turned = block.T
        tiles = [jnp.zeros((channels, 128), F32)] * 7
        for k in range(9):
            piece = turned[(8 - k) * channels : (9 - k) * channels, :]
            tile, moved = divmod(k * channels, 128)
            if moved:
                piece = pltpu.roll(piece, moved, 1)
            tiles[tile] = tiles[tile] + jnp.where(lane >= moved, piece, 0.0)
            if moved + channels > 128:
                tiles[tile + 1] = tiles[tile + 1] + jnp.where(lane < moved, piece, 0.0)
        out_ref[a] = jnp.concatenate(tiles, axis=1).astype(BF16)


def column(row):
    return jnp.broadcast_to(row, (8, row.shape[1])).T[:, :1]


def layer_of(q):
    return 0 if q < 0 else 1 if q < EDGE else 2


def hidden_plane(pre, mask):
    sigma = jax.nn.sigmoid(pre)
    return (pre * sigma * mask).astype(BF16), sigma * (1.0 + pre * (1.0 - sigma)) * mask


def out_plane(pre, mask, cot):
    sigma = jax.nn.sigmoid(pre)
    grad = cot.astype(F32) * (sigma * (1.0 + pre * (1.0 - sigma)))
    return (pre * sigma * mask).astype(BF16), grad.astype(BF16)


def inner_kernel(
    device, x_ref, cot_ref, layer_mask, weight_ref, b1_ref, b2_ref,
    taps_ref, x_taps, one_ref, two_ref, slope_ref, g_ref, out_ref, total_ref, w1_taps, w2_taps, w2_back,
    wide, xc, hc, full_one, low_one, full_two, low_two, masks_ref,
):
    channels = x_ref.shape[1]
    even = layer_side(device) == 0
    fill_masks(masks_ref)
    tap_weights(w1_taps, weight_ref[:channels, :], wide, even)
    bias_one, bias_two = column(b1_ref[...]), column(b2_ref[...])
    ones = jnp.ones((KDIM - 9 * channels, 2 * PLANE), BF16)
    for k in range(5):
        x_taps[k, 9 * channels :, :] = ones
    for k in range(4):
        taps_ref[k, 9 * channels :, :] = ones
    for single in (xc, hc):
        single[9 * channels :, :] = ones[:, :PLANE]

    def write_x(p):
        write_taps(x_taps.at[p // 2, :, place(p & 1)] if p < 10 else xc, x_ref[p], masks_ref)

    def finish_one(q, pre):
        hidden, slope = hidden_plane(pre + bias_one, layer_mask[layer_of(q)][:1])
        dst = taps_ref.at[(q - 1) // 2, :, place((q - 1) & 1)] if q < 9 else hc
        write_taps(dst, hidden, masks_ref)
        if q < EDGE:
            slope_ref[q - 1] = slope

    def finish_two(q, pre):
        out, grad = out_plane(pre + bias_two, layer_mask[layer_of(q)][:1], cot_ref[q])
        g_ref[q - 2] = grad
        if q < EDGE:
            out_ref[q - 2] = out

    write_x(0)
    write_x(1)
    for j in range(8):
        now, last = j & 1, (j + 1) & 1
        if j < 5:
            pair_sums(full_one.at[now], low_one, w1_taps, x_taps[j], j == 0)
            for p in (2 * j + 2, 2 * j + 3):
                if p <= 10:
                    write_x(p)
        if j == 5:
            third = product(w1_taps, xc[...], slice(2, 3))
            full_one[now, 0] = low_one[0] + third
        if j == 0:
            tap_weights(w2_taps, weight_ref[channels:, :], wide, even)
        if j == 1:
            one_ref[...] = full_one[0]
            back_weights(w2_back, w2_taps)
        if 2 <= j <= 5:
            finish_one(2 * j - 3, full_one[last, 0])
            finish_one(2 * j - 2, full_one[last, 1])
        if j == 6:
            finish_one(9, full_one[last, 0])
        if 3 <= j <= 6:
            pair_sums(full_two.at[now], low_two, w2_taps, taps_ref[j - 3], j == 3)
        if j == 7:
            third = product(w2_taps, hc[...], slice(2, 3))
            finish_two(8, low_two[0] + third)
        if j == 4:
            two_ref[...] = full_two[last]
        if 5 <= j:
            finish_two(2 * j - 8, full_two[last, 0])
            finish_two(2 * j - 7, full_two[last, 1])

    def taps(p, rows):
        return taps_ref[p // 2, rows]

    weight_products(total_ref, lambda q: g_ref[q - 2], (5, 7), taps)


def outer_kernel(
    device, edge_ref, cot_ref, layer_mask, w1_taps, w2_taps, w2_back, b1_ref, b2_ref,
    taps_ref, x_taps, one_ref, two_ref, slope_in_ref, g_in_ref, total_ref,
    keep_ref, send_ref, out_ref,
    xc, hc, x_pair, h_pair, gc, slope_out_ref, g_out_ref, full, low, grad, total, flat, masks_ref,
):
    channels = cot_ref.shape[1]
    even = layer_side(device) == 0
    fill_masks(masks_ref)
    bias_one, bias_two = column(b1_ref[...]), column(b2_ref[...])
    ones = jnp.ones((KDIM - 9 * channels, 2 * PLANE), BF16)
    for single in (xc, hc):
        single[9 * channels :, :] = ones[:, :PLANE]
    for pair in (x_pair, h_pair):
        pair[9 * channels :, :] = ones
    write_taps(xc, edge_ref[2], masks_ref)
    write_taps(x_pair.at[:, place(0)], edge_ref[1], masks_ref)
    write_taps(x_pair.at[:, place(1)], edge_ref[0], masks_ref)

    def three_planes(weights, single, pair, parts):
        first = product(weights, single[...], slice(0, 1))
        both = product(weights, pair[...])
        left, right = both[:, :PLANE], both[:, PLANE:]
        one, two = slice(channels, 2 * channels), slice(2 * channels, 3 * channels)
        return (
            first + left[one] + right[two],
            left[:channels] + right[one] + parts[0],
            right[:channels] + parts[1],
        )

    for q, pre in zip(range(-2, 1), three_planes(w1_taps, xc, x_pair, one_ref)):
        hidden, slope = hidden_plane(pre + bias_one, layer_mask[layer_of(q)][:1])
        write_taps(hc if q == -2 else h_pair.at[:, place(q + 1)], hidden, masks_ref)
        if q == 0:
            slope_out_ref[0] = slope
    for q, pre in zip(range(-1, 2), three_planes(w2_taps, hc, h_pair, two_ref)):
        cot = edge_ref[3] if q < 0 else cot_ref[q]
        out, g_out_ref[q + 1] = out_plane(pre + bias_two, layer_mask[layer_of(q)][:1], cot)
        if q >= 0:
            out_ref[q] = out

    def grads(q):
        return g_out_ref[q + 1] if q < 2 else g_in_ref[q - 2]

    for k in range(2):
        gc[k, 9 * channels :, :] = ones

    def write_g(q):
        plane = g_out_ref[q + 1] if q < 2 else g_in_ref[q - 2]
        write_taps(gc.at[((q + 1) >> 1) & 1, :, place((q + 1) & 1)], plane, masks_ref)

    write_g(-1)
    write_g(0)
    for j in range(6):
        now, last = j & 1, (j + 1) & 1
        if j < 5:
            pair_sums(full.at[now], low, w2_back, gc[now], j == 0)
            for q in (2 * j + 1, 2 * j + 2):
                if q <= 8:
                    write_g(q)
        if j == 0:
            part = weight_part(pair_grads(grads, -1), h_pair[...])
            total[...] = total_ref[...] + part
        if j == 1:
            total[...] = total[...] + weight_part(pair_grads(grads, 1), taps_ref[0])
            total[...] = total[...] + weight_part(pair_grads(grads, 3), taps_ref[1])
        if j == 2:
            write_tiles(flat, total, channels, even)
            split_tiles(keep_ref.at[:, 1], send_ref.at[:, 1], flat, device)
        if j >= 2:
            for k, q in enumerate((2 * j - 4, 2 * j - 3)):
                slope = slope_out_ref[0] if q == 0 else slope_in_ref[q - 1]
                grad[q] = (full[last, k] * slope).astype(BF16)
        if j >= 3:
            for p in (2 * j - 6,) if j < 5 else (4, 6):
                part = weight_part(pair_grads(lambda q: grad[q], p), x_taps[p // 2])
                total[...] = part if p == 0 else total[...] + part
    low_rows, high_rows = slice(0, channels), slice(2 * channels, 3 * channels)
    total[low_rows] = total[low_rows] + weight_part(grad[0], x_pair[:, PLANE:])
    total[high_rows] = total[high_rows] + weight_part(grad[EDGE - 1], x_taps[4, :, :PLANE])
    write_tiles(flat, total, channels, even)
    split_tiles(keep_ref.at[:, 0], send_ref.at[:, 0], flat, device)


def output_kernel(device, table, first_ref, second_ref, keep_ref, send_ref, outs, bricks):
    slots, channels = keep_ref.shape[0], keep_ref.shape[1]
    me = space_index(device, table.shape[2] // slots)
    layer = layer_side(device)
    even = layer == 0
    outs[:2] = first_ref[...]
    outs[2:] = second_ref[...]
    back = spread_matrix(True)
    for y in range(2):
        row = slice(y * 128, (y + 1) * 128)
        for j in range(4):
            first = jnp.where(even, 2 * j, 7 - 2 * j)
            second = jnp.where(even, 2 * j + 1, 6 - 2 * j)
            two = jnp.concatenate([outs[first, :, row], outs[second, :, row]], axis=1)
            both = jnp.dot(two, back, preferred_element_type=F32).astype(BF16)
            pair = slice(j * 128, (j + 1) * 128)
            bricks[2 * y, :, pair] = both[:, :128]
            bricks[2 * y + 1, :, pair] = both[:, 128:]
    for target, index in ((keep_ref, me), (send_ref, me ^ 1)):
        for s in range(slots):
            slot = jnp.clip(index * slots + s, 0, table.shape[2] - 1)
            parity, spot = slot_place(table, slot, 2 * slots)
            scale = jnp.where(parity == layer, 1.0, 0.0)
            target[s] = bricks[spot] * jnp.full((channels, CELLS), scale, F32).astype(BF16)


def copies_kernel(first_ref, second_ref, out_ref):
    total = (first_ref[...].astype(F32) + second_ref[...].astype(F32)).astype(BF16)
    for k in range(out_ref.shape[0]):
        out_ref[k] = total


def gather_kernel(
    device, own_ref, other_ref, w_one_ref, w_two_ref, b_one_ref, b_two_ref, flat
):
    chunks, _, rows, _ = own_ref.shape
    channels = w_one_ref.shape[0]
    core = core_of(device)
    for half, source in enumerate((own_ref, other_ref)):
        base = jnp.where(core == half, 0, chunks * rows)
        for k in range(chunks):
            at = pl.multiple_of(base + k * rows, rows)
            flat[:, pl.ds(at, rows), :] = source[k]
    for n, (weight, bias) in enumerate(((w_one_ref, b_one_ref), (w_two_ref, b_two_ref))):
        for k in range(TILES - 1):
            tile = flat[n, k * channels : (k + 1) * channels, :]
            weight[:, k * 128 : (k + 1) * 128] = tile.astype(F32)
        last = flat[n, (TILES - 1) * channels : TILES * channels, :].astype(F32)
        weight[:, 2560:2592] = last[:, :32]
        bias[...] = last.T[32:33, :]


VMEM = pl.BlockSpec(memory_space=pltpu.VMEM)
SMEM = pl.BlockSpec(memory_space=pltpu.SMEM)


def vmem(mebibytes):
    return pltpu.CompilerParams(vmem_limit_bytes=mebibytes * 2**20)


def shared_sum(keep, send):
    count = lax.axis_size("space")
    volumes = lax.axis_size("dp")
    swap = [(d, d ^ 1) for d in range(count)]
    both = ("space", "dp")
    groups = [
        [(chip * 2 + core) * volumes + first + v for v in range(2) for chip in range(count // 2)]
        for core in range(2)
        for first in range(0, volumes, 2)
    ]
    parts = (keep + lax.ppermute(send, "space", swap).astype(F32)).astype(BF16)
    parts = lax.all_to_all(parts, both, 0, 0, axis_index_groups=groups)
    total = jnp.sum(parts.astype(F32), axis=0).astype(BF16)
    moved, step = jnp.zeros_like(total), 2
    while step < volumes:
        moved = lax.ppermute(total, "dp", [(v, v ^ step) for v in range(volumes)])
        if step * 2 < volumes:
            total = (total.astype(F32) + moved.astype(F32)).astype(BF16)
        step *= 2
    copies = pl.pallas_call(
        copies_kernel,
        out_shape=jax.ShapeDtypeStruct(parts.shape, BF16),
        in_specs=[VMEM] * 2,
        out_specs=VMEM,
        compiler_params=vmem(8),
        name="copies",
    )(total, moved)
    copies = lax.all_to_all(copies, both, 0, 0, axis_index_groups=groups)
    return [copies, lax.ppermute(copies, "space", swap)]


def local(volume, neighbours, active, cotangent, weight_one, weight_two, bias_one, bias_two):
    volume, cotangent = volume[0], cotangent[0]
    slots, channels = volume.shape[0], volume.shape[1]
    count = lax.axis_size("space")
    me = lax.axis_index("space").astype(jnp.int32)

    swap = [(d, d ^ 1) for d in range(count)]
    at = [2 * (n // 2) + (n & 1 ^ n // 2 & 1) for n in range(count)]
    hop = [(at[n], at[n + 1]) for n in range(1, count - 1, 2)]
    hop += [(there, here) for here, there in hop]
    pair_volume = lax.ppermute(volume, "space", swap)
    pair_cot = lax.ppermute(cotangent, "space", swap)
    biases = (bias_one[None], bias_two[None])
    own = jnp.concatenate([volume, cotangent], axis=0)
    device = (2 * me + ((me ^ (me >> 1)) & 1))[None]
    table = jnp.concatenate([neighbours.transpose(2, 0, 1), active[None]], axis=0)

    def planes(number, dtype=BF16):
        return jax.ShapeDtypeStruct((number, channels, PLANE), dtype)

    def plane_space(number):
        return pltpu.VMEM((number, channels, PLANE), BF16)

    def tap_space(*extent):
        return pltpu.VMEM(extent, BF16)

    def sum_space(*extent):
        return pltpu.VMEM((*extent, channels, PLANE), F32)

    bricks = (slots, channels, CELLS)
    x_planes, cot_planes, edge, layer_mask = pl.pallas_call(
        layout_kernel,
        out_shape=(planes(12), planes(9), planes(4), jax.ShapeDtypeStruct((3, 8, PLANE), F32)),
        in_specs=[SMEM] * 2 + [VMEM] * 3,
        out_specs=(VMEM,) * 4,
        scratch_shapes=[
            pltpu.VMEM((2, *bricks), BF16),
            pltpu.VMEM((2, *bricks), BF16),
        ],
        compiler_params=vmem(8),
        name="layout",
    )(device, table, own, pair_volume, pair_cot)
    edge, weight_one, weight_two = lax.optimization_barrier((edge, weight_one, weight_two))
    outer = lax.ppermute(edge, "space", hop)
    weights = jnp.concatenate([weight_one, weight_two], axis=0)

    rearranged = jax.ShapeDtypeStruct((3, channels, KDIM), BF16)
    taps, x_taps, one, two, slope_in, g_in, out_in, part_two, w1, w2, w2_back = pl.pallas_call(
        inner_kernel,
        out_shape=(
            jax.ShapeDtypeStruct((4, KDIM, 2 * PLANE), BF16),
            jax.ShapeDtypeStruct((5, KDIM, 2 * PLANE), BF16),
            planes(2, F32),
            planes(2, F32),
            planes(7, F32),
            planes(7),
            planes(6),
            jax.ShapeDtypeStruct((3 * channels, KDIM), F32),
            rearranged,
            rearranged,
            rearranged,
        ),
        in_specs=[SMEM] + [VMEM] * 6,
        out_specs=(VMEM,) * 11,
        scratch_shapes=[
            pltpu.VMEM((channels, 21 * 128), BF16),
            tap_space(KDIM, PLANE),
            tap_space(KDIM, PLANE),
            sum_space(2, 2),
            sum_space(2),
            sum_space(2, 2),
            sum_space(2),
            pltpu.VMEM((9, 16, PLANE), BF16),
        ],
        compiler_params=vmem(20),
        cost_estimate=pl.CostEstimate(flops=2**33, bytes_accessed=2**23, transcendentals=2**20),
        name="inner",
    )(device, x_planes, cot_planes, layer_mask, weights, *biases)

    halves = (count, 2, ROWS // (2 * count), 128)
    gradient_keep, gradient_send, out_out = pl.pallas_call(
        outer_kernel,
        out_shape=(
            jax.ShapeDtypeStruct(halves, F32),
            jax.ShapeDtypeStruct(halves, BF16),
            planes(2),
        ),
        in_specs=[SMEM] + [VMEM] * 15,
        out_specs=(VMEM,) * 3,
        scratch_shapes=[
            tap_space(KDIM, PLANE),
            tap_space(KDIM, PLANE),
            tap_space(KDIM, 2 * PLANE),
            tap_space(KDIM, 2 * PLANE),
            tap_space(2, KDIM, 2 * PLANE),
            sum_space(1),
            plane_space(3),
            sum_space(2, 2),
            sum_space(2),
            plane_space(8),
            pltpu.VMEM((3 * channels, KDIM), F32),
            pltpu.VMEM((ROWS, 128), F32),
            pltpu.VMEM((9, 16, PLANE), BF16),
        ],
        compiler_params=vmem(24),
        cost_estimate=pl.CostEstimate(flops=2**33, bytes_accessed=2**23, transcendentals=2**18),
        name="outer",
    )(
        device, outer, cot_planes, layer_mask, w1, w2, w2_back, *biases, taps, x_taps, one, two,
        slope_in, g_in, part_two,
    )
    keep, send = pl.pallas_call(
        output_kernel,
        out_shape=(jax.ShapeDtypeStruct(bricks, BF16),) * 2,
        in_specs=[SMEM] * 2 + [VMEM] * 2,
        out_specs=(VMEM,) * 2,
        scratch_shapes=[plane_space(8), pltpu.VMEM(bricks, BF16)],
        compiler_params=vmem(8),
        cost_estimate=pl.CostEstimate(flops=2**28, bytes_accessed=2**21, transcendentals=0),
        name="output",
    )(device, table, out_out, out_in)
    output = (keep + lax.ppermute(send, "space", swap))[None]
    parts = shared_sum(gradient_keep, gradient_send)
    weight_shape = jax.ShapeDtypeStruct((channels, 27 * channels), F32)
    bias_shape = jax.ShapeDtypeStruct((1, channels), F32)
    total_w_one, total_w_two, total_b_one, total_b_two = pl.pallas_call(
        gather_kernel,
        out_shape=(weight_shape, weight_shape, bias_shape, bias_shape),
        in_specs=[SMEM] + [VMEM] * len(parts),
        out_specs=(VMEM,) * 4,
        scratch_shapes=[pltpu.VMEM((2, ROWS, 128), BF16)],
        compiler_params=vmem(8),
        name="gather",
    )(device, *parts)
    return (output, total_w_one, total_w_two, total_b_one[0], total_b_two[0])


def solution(mesh):
    in_specs = (
        P("dp", "space", None, None),
        P("dp", None, None),
        P("dp", None),
        P("dp", "space", None, None),
        P(),
        P(),
        P(),
        P(),
    )
    out_specs = (P("dp", "space", None, None), P(), P(), P(), P())
    return jax.shard_map(local, mesh=mesh, in_specs=in_specs, out_specs=out_specs, check_vma=False)
```
